32 devices in a mesh: grp: 8 (over y, x, core), seq: 4 (over z).
Axes of the slice: x: 2, y: 2, z: 4, core: 2. Of those that a mesh axis runs over, the one named last changes fastest.
Arguments:
- q_space: bfloat16 [32, 256, 576], P(('grp', 'seq')), may hold values from -96 to 96
- k_space: bfloat16 [32, 256, 576], P(('grp', 'seq')), may hold values from -96 to 96
- v_space: bfloat16 [32, 256, 576], P(('grp', 'seq')), may hold values from -6 to 6
- cot_space: bfloat16 [32, 256, 576], P(('grp', 'seq')), may hold values from -6 to 6
- q_time: bfloat16 [32, 256, 576], P(('grp', 'seq')), may hold values from -96 to 96
- k_time: bfloat16 [32, 256, 576], P(('grp', 'seq')), may hold values from -96 to 96
- v_time: bfloat16 [32, 256, 576], P(('grp', 'seq')), may hold values from -6 to 6
- cot_time: bfloat16 [32, 256, 576], P(('grp', 'seq')), may hold values from -6 to 6
- clip_len: int32 [16], replicated, may hold values from 1 to 4, 32 in all
Outputs:
- grad_q_space: bfloat16 [32, 256, 576], P(('grp', 'seq'))
- grad_k_space: bfloat16 [32, 256, 576], P(('grp', 'seq'))
- grad_v_space: bfloat16 [32, 256, 576], P(('grp', 'seq'))
- grad_q_time: bfloat16 [32, 256, 576], P(('grp', 'seq'))
- grad_k_time: bfloat16 [32, 256, 576], P(('grp', 'seq'))
- grad_v_time: bfloat16 [32, 256, 576], P(('grp', 'seq'))
The draws below stay inside these ranges and needn't reach their ends.
Inputs may be any that keep to these rules, and one draw needn't show every extreme that they name: `clip_len`: the 16 frame counts sum to 32; some clip has exactly 4 frames.
All inputs are finite; a program needn't handle non-finite values.
Results may differ from the reference program's by a relative error of at most 0.013.
Values may be sent and summed in bfloat16 or wider, within the bound.
No kernel may reach another device: no remote copies, remote signals or barrier semaphores. Data moves between devices by JAX's collectives and lax.ppermute only.
A program may use at most 64 MiB of HBM per device.

```python
import math
import jax
import jax.numpy as jnp
import numpy as np
from jax import lax

HEADS = 8
HDIM = 72
S = 256
WIN = 4
FRAMES = 32
CLIPS = 16
N_GRP = 8


def paired(key, salt):
    key = jax.random.fold_in(key, salt)
    full_shape = (FRAMES, S, HEADS * HDIM)
    pieces = jax.random.split(key, 2)
    queries = jnp.clip(jax.random.normal(pieces[0], full_shape, jnp.float32), -6.0, 6.0)
    keys = jnp.clip(jax.random.normal(pieces[1], full_shape, jnp.float32), -6.0, 6.0)
    return (queries, keys)


def draw_q_space(key, part):
    queries, keys = paired(key, 11)
    return queries.astype(jnp.bfloat16)


def draw_k_space(key, part):
    queries, keys = paired(key, 11)
    return keys.astype(jnp.bfloat16)


def draw_q_time(key, part):
    queries, keys = paired(key, 12)
    return queries.astype(jnp.bfloat16)


def draw_k_time(key, part):
    queries, keys = paired(key, 12)
    return keys.astype(jnp.bfloat16)


def steps_of(stream_key, dims, cuts, low, largest):
    loudness = 1.0
    for dim, parts in cuts:
        steps = jax.random.uniform(jax.random.fold_in(jax.random.fold_in(stream_key, 6), dim), (parts,), jnp.float32, low / len(cuts), largest / len(cuts))
        loudness = loudness * jnp.repeat(jnp.exp(steps), dims[dim] // parts).reshape((-1,) + (1,) * (len(dims) - 1 - dim))
    return loudness


def profile(number_of, total, reach, slope):
    loads = [(1 << 20) // math.isqrt(standing ** slope) + 1 for standing in range(2, number_of + 1)]
    rest, given = total - reach - (number_of - 1), [1] * (number_of - 1)
    while rest > 0:
        candidates = [i for i in range(number_of - 1) if given[i] < reach]
        whole, remaining = sum([loads[i] for i in candidates]), rest
        for i in candidates:
            extra = min(reach - given[i], max(1, remaining * loads[i] // whole), rest)
            given[i] = given[i] + extra
            rest = rest - extra
    return np.array([reach] + given)


def ragged_sizes(own_key, amount, total, bound, lean):
    if amount == 2:
        one = jax.random.randint(own_key, (), max(1, total - bound), min(bound, total - 1) + 1)
        return jnp.stack([one, total - one])
    tallies = jnp.asarray(profile(amount, total, bound, lean), jnp.int32)
    pairs = (amount - 1) // 2
    giver, receiver = tallies[1:1 + 2 * pairs:2], tallies[2:2 + 2 * pairs:2]
    slack = jnp.minimum(giver - 1, bound - receiver)
    passed = jax.random.randint(jax.random.fold_in(own_key, 1), (pairs,), 0, 1 << 20) % (slack + 1)
    tallies = tallies.at[1:1 + 2 * pairs:2].set(giver - passed).at[2:2 + 2 * pairs:2].set(receiver + passed)
    return tallies[jax.random.permutation(jax.random.fold_in(own_key, 2), amount)]


def gaussian(own_key, shape, width, bound, cuts=(), kind=jnp.bfloat16):
    entries = jax.random.normal(own_key, shape, jnp.float32) * width
    if len(cuts) > 0:
        entries = steps_of(own_key, shape, cuts, -0.22, 0.18) * entries
    return jnp.clip(entries, min=-bound, max=bound).astype(kind)


def setup_inputs(seed: int = 0) -> dict:
    key_list = jax.random.split(jax.random.key(seed), 10)
    q_space = draw_q_space(jax.random.fold_in(key_list[9], 71), 0)
    k_space = draw_k_space(jax.random.fold_in(key_list[9], 71), 0)
    v_space = gaussian(key_list[2], (FRAMES, S, HEADS * HDIM), 1.0, 6.0, ((0, 32),))
    cot_space = gaussian(key_list[3], (FRAMES, S, HEADS * HDIM), 1.0, 6.0, ((0, 32),))
    q_time = draw_q_time(jax.random.fold_in(key_list[9], 71), 0)
    k_time = draw_k_time(jax.random.fold_in(key_list[9], 71), 0)
    v_time = gaussian(key_list[6], (FRAMES, S, HEADS * HDIM), 1.0, 6.0, ((0, 32),))
    cot_time = gaussian(key_list[7], (FRAMES, S, HEADS * HDIM), 1.0, 6.0, ((0, 32),))
    clip_len = ragged_sizes(key_list[8], CLIPS, FRAMES, WIN, 2).astype(jnp.int32)
    return {"q_space": q_space, "k_space": k_space, "v_space": v_space, "cot_space": cot_space, "q_time": q_time, "k_time": k_time, "v_time": v_time, "cot_time": cot_time, "clip_len": clip_len}


masked_score = -1e+30

def rounded(array):
    return lax.optimization_barrier(array.astype(jnp.bfloat16)).astype(jnp.float32)

def split_heads(array):
    return array.astype(jnp.float32).reshape(array.shape[0], array.shape[1], HEADS, HDIM)

def clip_labels(clip_len, first_frame, count, frame_total):
    frame_ids = first_frame + jnp.arange(count, dtype=jnp.int32)
    clip_ends = jnp.cumsum(clip_len).astype(jnp.int32)
    labels = lax.optimization_barrier(jnp.sum((clip_ends[None, :] <= frame_ids[:, None]).astype(jnp.int32), axis=1))
    inside = (frame_ids >= 0) & (frame_ids < frame_total)
    return (labels, inside)

def frame_grads(operands):
    queries, keys, values, cotangent = operands
    scaling = 1.0 / math.sqrt(HDIM)
    q_heads = queries.astype(jnp.float32).reshape(S, HEADS, HDIM)
    k_heads = keys.astype(jnp.float32).reshape(S, HEADS, HDIM)
    v_heads = values.astype(jnp.float32).reshape(S, HEADS, HDIM)
    g_heads = cotangent.astype(jnp.float32).reshape(S, HEADS, HDIM)
    scores = jnp.einsum('qhd,khd->hqk', q_heads, k_heads) * scaling
    row_max = lax.optimization_barrier(jnp.max(scores, axis=-1, keepdims=True))
    log_total = row_max + jnp.log(lax.optimization_barrier(jnp.sum(jnp.exp(scores - row_max), axis=-1, keepdims=True)))
    weights = jnp.exp(scores - log_total)
    weights_low = rounded(weights)
    attended = jnp.einsum('hqk,khd->qhd', weights_low, v_heads)
    row_dot = jnp.einsum('qhd,qhd->hq', g_heads, attended)
    weight_grad = jnp.einsum('qhd,khd->hqk', g_heads, v_heads)
    score_grad = rounded(weights * (weight_grad - row_dot[:, :, None]))
    grad_query = jnp.einsum('hqk,khd->qhd', score_grad, k_heads) * scaling
    grad_key = jnp.einsum('hqk,qhd->khd', score_grad, q_heads) * scaling
    grad_value = jnp.einsum('hqk,qhd->khd', weights_low, g_heads)
    flat_shape = (S, HEADS * HDIM)
    return (grad_query.reshape(flat_shape).astype(jnp.bfloat16), grad_key.reshape(flat_shape).astype(jnp.bfloat16), grad_value.reshape(flat_shape).astype(jnp.bfloat16))

def time_grads(q_time, k_time, v_time, cot_time, clip_len):
    scaling = 1.0 / math.sqrt(HDIM)
    margin = ((WIN, WIN), (0, 0), (0, 0))
    key_pad = jnp.pad(k_time, margin)
    value_pad = jnp.pad(v_time, margin)
    query_pad = jnp.pad(q_time, margin)
    cot_pad = jnp.pad(cot_time, margin)

    def query_side(group_id):
        first_frame = group_id * WIN
        q_own = split_heads(lax.dynamic_slice_in_dim(q_time, first_frame, WIN, 0))
        g_own = split_heads(lax.dynamic_slice_in_dim(cot_time, first_frame, WIN, 0))
        k_ext = split_heads(lax.dynamic_slice_in_dim(key_pad, first_frame, 3 * WIN, 0))
        v_ext = split_heads(lax.dynamic_slice_in_dim(value_pad, first_frame, 3 * WIN, 0))
        own_label, own_inside = clip_labels(clip_len, first_frame, WIN, FRAMES)
        ext_label, ext_inside = clip_labels(clip_len, first_frame - WIN, 3 * WIN, FRAMES)
        allowed = (own_label[:, None] == ext_label[None, :]) & ext_inside[None, :]
        scores = jnp.einsum('iphd,jphd->phij', q_own, k_ext) * scaling
        scores = jnp.where(allowed, scores, masked_score)
        row_max = lax.optimization_barrier(jnp.max(scores, axis=-1))
        log_total = row_max + jnp.log(lax.optimization_barrier(jnp.sum(jnp.exp(scores - row_max[..., None]), axis=-1)))
        weights = jnp.where(allowed, jnp.exp(scores - log_total[..., None]), 0.0)
        weights_low = rounded(weights)
        attended = jnp.einsum('phij,jphd->iphd', weights_low, v_ext)
        row_dot = jnp.einsum('iphd,iphd->phi', g_own, attended)
        weight_grad = jnp.einsum('iphd,jphd->phij', g_own, v_ext)
        score_grad = rounded(weights * (weight_grad - row_dot[..., None]))
        grad_query = jnp.einsum('phij,jphd->iphd', score_grad, k_ext) * scaling
        return (grad_query.reshape(WIN, S, HEADS * HDIM).astype(jnp.bfloat16), log_total, row_dot)
    groups = jnp.arange(N_GRP, dtype=jnp.int32)
    grad_q, log_totals, row_dots = lax.map(query_side, groups)

    def frame_major(stat):
        return jnp.pad(stat.transpose(0, 3, 1, 2).reshape(FRAMES, S, HEADS), margin)
    total_pad = frame_major(log_totals)
    dot_pad = frame_major(row_dots)

    def key_side(group_id):
        first_frame = group_id * WIN
        k_own = split_heads(lax.dynamic_slice_in_dim(k_time, first_frame, WIN, 0))
        v_own = split_heads(lax.dynamic_slice_in_dim(v_time, first_frame, WIN, 0))
        q_ext = split_heads(lax.dynamic_slice_in_dim(query_pad, first_frame, 3 * WIN, 0))
        g_ext = split_heads(lax.dynamic_slice_in_dim(cot_pad, first_frame, 3 * WIN, 0))
        total_ext = lax.dynamic_slice_in_dim(total_pad, first_frame, 3 * WIN, 0).transpose(1, 2, 0)
        dot_ext = lax.dynamic_slice_in_dim(dot_pad, first_frame, 3 * WIN, 0).transpose(1, 2, 0)
        own_label, own_inside = clip_labels(clip_len, first_frame, WIN, FRAMES)
        ext_label, ext_inside = clip_labels(clip_len, first_frame - WIN, 3 * WIN, FRAMES)
        allowed = ext_inside[:, None] & (ext_label[:, None] == own_label[None, :])
        scores = jnp.einsum('iphd,jphd->phij', q_ext, k_own) * scaling
        weights = jnp.where(allowed, jnp.exp(jnp.where(allowed, scores, masked_score) - total_ext[..., None]), 0.0)
        weights_low = rounded(weights)
        weight_grad = jnp.einsum('iphd,jphd->phij', g_ext, v_own)
        score_grad = rounded(weights * (weight_grad - dot_ext[..., None]))
        grad_key = jnp.einsum('phij,iphd->jphd', score_grad, q_ext) * scaling
        grad_value = jnp.einsum('phij,iphd->jphd', weights_low, g_ext)
        flat_shape = (WIN, S, HEADS * HDIM)
        return (grad_key.reshape(flat_shape).astype(jnp.bfloat16), grad_value.reshape(flat_shape).astype(jnp.bfloat16))
    grad_k, grad_v = lax.map(key_side, groups)
    full_shape = (FRAMES, S, HEADS * HDIM)
    return (grad_q.reshape(full_shape), grad_k.reshape(full_shape), grad_v.reshape(full_shape))

def reference(q_space, k_space, v_space, cot_space, q_time, k_time, v_time, cot_time, clip_len):
    grad_qs, grad_ks, grad_vs = lax.map(frame_grads, (q_space, k_space, v_space, cot_space))
    grad_qt, grad_kt, grad_vt = time_grads(q_time, k_time, v_time, cot_time, clip_len)
    return (grad_qs, grad_ks, grad_vs, grad_qt, grad_kt, grad_vt)
```

```python
import functools
import math

import jax
import jax.numpy as jnp
from jax import lax
from jax.experimental import pallas as pl
from jax.experimental.pallas import tpu as pltpu
from jax.sharding import PartitionSpec as P

HEADS = 8
HDIM = 72
WIDTH = HEADS * HDIM
LANES = 128
REST = WIDTH % LANES
FULL = WIDTH // LANES
SCALING = 1.0 / math.sqrt(HDIM)
NEAR = 16
masked_score = -1e30
PARTS = 1


def shifted(value, axis, by):
    count = lax.axis_size(axis)
    pairs = [(i, i + by) for i in range(count) if 0 <= i + by < count]
    return lax.ppermute(value, axis, pairs)


def head_window(head):
    low, high = head * HDIM, (head + 1) * HDIM
    first = low // LANES * LANES
    last = min(-(-high // LANES) * LANES, WIDTH)
    lane = lax.broadcasted_iota(jnp.int32, (1, last - first), 1) + first
    mask = ((lane >= low) & (lane < high)).astype(jnp.float32).astype(jnp.bfloat16)
    return first, last, mask


def dot_nt(left, right):
    return lax.dot_general(
        left, right, (((1,), (1,)), ((), ())), preferred_element_type=jnp.float32
    )


def dot_nn(left, right):
    return lax.dot_general(
        left, right, (((1,), (0,)), ((), ())), preferred_element_type=jnp.float32
    )


def dot_tn(left, right):
    return lax.dot_general(
        left, right, (((0,), (0,)), ((), ())), preferred_element_type=jnp.float32
    )


def weights_and_grads(queries, keys, values, cotangent, bias=None, valid=None):
    scores = dot_nt(keys, queries) * SCALING
    if bias is not None:
        scores = scores + bias
    raised = jnp.exp(scores - jnp.max(scores, axis=0, keepdims=True))
    inverse = 1.0 / jnp.sum(raised, axis=0, keepdims=True)
    if valid is not None:
        inverse = inverse * valid
    weights = raised * inverse
    weights_low = weights.astype(jnp.bfloat16)
    weight_grad = dot_nt(values, cotangent)
    dots = jnp.sum(weights_low.astype(jnp.float32) * weight_grad, axis=0, keepdims=True)
    score_grad = (weights * (weight_grad - dots)).astype(jnp.bfloat16)
    return weights_low, score_grad


def add_tiles(tiles, term, first):
    for at in range(0, term.shape[1], LANES):
        piece = term[:, at : at + LANES]
        tile = (first + at) // LANES
        tiles[tile] = piece if tiles[tile] is None else tiles[tile] + piece


def frame_kernel(q_ref, k_ref, v_ref, g_ref, dq_ref, dk_ref, dv_ref):
    tiles = [[None] * (FULL + 1) for _ in range(3)]
    outs = (dq_ref, dk_ref, dv_ref)
    scales = (SCALING, SCALING, 1.0)
    done = 0
    for head in range(HEADS):
        first, last, mask = head_window(head)
        span = slice(first, last)
        queries, keys = q_ref[0, :, span], k_ref[0, :, span]
        q_own, k_own = queries * mask, keys * mask
        g_own = g_ref[0, :, span] * mask
        weights_low, score_grad = weights_and_grads(queries, k_own, v_ref[0, :, span], g_own)
        add_tiles(tiles[0], dot_tn(score_grad, k_own), first)
        add_tiles(tiles[1], dot_nn(score_grad, q_own), first)
        add_tiles(tiles[2], dot_nn(weights_low, g_own), first)
        finished = (head + 1) * HDIM // LANES if head < HEADS - 1 else FULL + 1
        for tile in range(done, finished):
            at = tile * LANES
            size = min(LANES, WIDTH - at)
            for out, held, scale in zip(outs, tiles, scales):
                out[0, :, at : at + size] = (held[tile] * scale).astype(jnp.bfloat16)
                held[tile] = None
        done = finished


def frame_grads(queries, keys, values, cotangent):
    tokens = queries.shape[1]
    shape = jax.ShapeDtypeStruct(queries.shape, jnp.bfloat16)
    return pl.pallas_call(
        frame_kernel,
        out_shape=(shape, shape, shape),
        compiler_params=pltpu.CompilerParams(vmem_limit_bytes=40 * 2**20),
        cost_estimate=pl.CostEstimate(
            flops=12 * tokens * tokens * 256 * HEADS,
            bytes_accessed=14 * tokens * WIDTH,
            transcendentals=tokens * tokens * HEADS,
        ),
        name="space",
    )(queries, keys, values, cotangent)


def pack_rows(load, store, count, places):
    for which in range(count):
        for tile in range(FULL):
            row = (which * FULL + tile) * places
            store(row, places, load(which, tile * LANES, LANES))
    for which in range(0, count, 2):
        row = (count * FULL + which // 2) * places
        left = load(which, FULL * LANES, REST)
        if which + 1 < count:
            right = load(which + 1, FULL * LANES, REST)
        else:
            right = jnp.zeros_like(left)
        store(row, places, jnp.concatenate([left, right], axis=1))


def packed_rows(count, places):
    return (count * FULL + (count + 1) // 2) * places


def split_kernel(parts, n, places, *refs):
    ins, outs = refs[:4], refs[4:]
    per = places // parts
    for part in range(parts):
        for target in range(n):
            begin = target * places + part * per

            def load(which, lane, size):
                return ins[which][0, begin : begin + per, lane : lane + size]

            def store(row, rows, value):
                outs[part][target, row : row + rows, :] = value

            pack_rows(load, store, 4, per)


def split(arrays, parts, n):
    places = arrays[0].shape[1] // n
    rows = packed_rows(4, places // parts)
    shape = jax.ShapeDtypeStruct((n, rows, LANES), jnp.bfloat16)
    return pl.pallas_call(
        functools.partial(split_kernel, parts, n, places),
        out_shape=(shape,) * parts,
        compiler_params=pltpu.CompilerParams(vmem_limit_bytes=32 * 2**20),
        name="pack",
    )(*arrays)


def join_kernel(parts, n, places, *refs):
    ins, outs = refs[:parts], refs[parts:]
    per = places // parts
    for part in range(parts):
        for source in range(n):
            begin = source * places + part * per
            for which in range(3):
                for tile in range(FULL):
                    row = (which * FULL + tile) * per
                    outs[which][0, begin : begin + per, tile * LANES : (tile + 1) * LANES] = ins[
                        part
                    ][source, row : row + per, :]
                row = (3 * FULL + which // 2) * per
                lane = which % 2 * REST
                outs[which][0, begin : begin + per, FULL * LANES :] = ins[part][
                    source, row : row + per, lane : lane + REST
                ]


def join(packed, parts, n, places):
    shape = jax.ShapeDtypeStruct((1, n * places, WIDTH), jnp.bfloat16)
    return pl.pallas_call(
        functools.partial(join_kernel, parts, n, places),
        out_shape=(shape,) * 3,
        compiler_params=pltpu.CompilerParams(vmem_limit_bytes=32 * 2**20),
        name="unpack",
    )(*packed)


def token_bias(labels, frames, near):
    tokens = len(frames) * near
    shape = (tokens, tokens)
    rows = lax.broadcasted_iota(jnp.int32, shape, 0)
    columns = lax.broadcasted_iota(jnp.int32, shape, 1)
    row_label = jnp.zeros(shape, jnp.int32)
    column_label = jnp.zeros(shape, jnp.int32)
    for place, frame in enumerate(frames):
        row_label = jnp.where(rows // near == place, labels[frame], row_label)
        column_label = jnp.where(columns // near == place, labels[frame], column_label)
    same = (row_label == column_label) & (rows % near == columns % near)
    return jnp.where(same, 0.0, masked_score), column_label[:1]


def clip_kernel(window, per, near, labels, own_ref, low_ref, high_ref, out_ref, bias_a, bias_b, full):
    halo = window - 1
    own_frames = list(range(halo, halo + window))
    low_frames = list(range(halo))
    high_frames = list(range(halo + window, halo + window + halo))
    frames_a = own_frames + high_frames
    frames_b = own_frames[:halo] + low_frames
    crossing = labels[halo - 1]
    first_bias, label_a = token_bias(labels, frames_a, near)
    bias_a[...] = first_bias
    valid_a = jnp.where(label_a == crossing, 0.0, 1.0)
    second_bias, label_b = token_bias(labels, frames_b, near)
    bias_b[...] = second_bias
    valid_b = jnp.where(label_b == crossing, 1.0, 0.0)
    own_tokens = window * near
    few_tokens = halo * near

    def block(step, carry):
        begin = pl.multiple_of(step * near, near)

        def load(ref, count, which, tile):
            if tile < FULL:
                row = (which * FULL + tile) * per
                value = ref[:count, pl.ds(row + begin, near), :]
                return value.reshape(count * near, LANES)
            row = (4 * FULL + which // 2) * per
            value = ref[:count, pl.ds(row + begin, near), :].reshape(count * near, LANES)
            lane = which % 2 * REST
            return value[:, lane : lane + REST]

        def tiles_of(which):
            own = [load(own_ref, window, which, t) for t in range(FULL + 1)]
            low = [load(low_ref, halo, which, t) for t in range(FULL + 1)]
            high = [load(high_ref, halo, which, t) for t in range(FULL + 1)]
            whole = jnp.concatenate
            a = [whole([x, y], axis=0) for x, y in zip(own, high)]
            b = [whole([x[:few_tokens], y], axis=0) for x, y in zip(own, low)]
            return a, b

        arrays = [tiles_of(which) for which in range(4)]
        for which in range(4):
            for part in range(2):
                rows = arrays[which][part][0].shape[0]
                for t in range(FULL + 1):
                    size = LANES if t < FULL else REST
                    full[part, which, :rows, t * LANES : t * LANES + size] = arrays[which][part][t]
        grads = [[None] * (FULL + 1) for _ in range(3)]
        for head in range(HEADS):
            first, last, mask = head_window(head)
            span = slice(first, last)
            for part, bias, valid in ((0, bias_a, valid_a), (1, bias_b, valid_b)):
                rows = bias.shape[0]
                kept = own_tokens if part == 0 else few_tokens
                queries, keys, values, cot = [full[part, i, :rows, span] for i in range(4)]
                q_own, k_own, g_own = queries * mask, keys * mask, cot * mask
                weights_low, score_grad = weights_and_grads(
                    queries, k_own, values, g_own, bias[...], valid
                )
                terms = (
                    dot_tn(score_grad[:, :kept], k_own),
                    dot_nn(score_grad[:kept], q_own),
                    dot_nn(weights_low[:kept], g_own),
                )
                for held, term in zip(grads, terms):
                    if part == 1:
                        gap = jnp.zeros((own_tokens - few_tokens, term.shape[1]), jnp.float32)
                        term = jnp.concatenate([term, gap], axis=0)
                    add_tiles(held, term, first)

        def give(which, lane, size):
            scale = 1.0 if which == 2 else SCALING
            return (grads[which][lane // LANES] * scale).astype(jnp.bfloat16)

        def store(row, rows, value):
            out_ref[:, pl.ds(row * (per // near) + begin, near), :] = value.reshape(
                window, near, LANES
            )

        pack_rows(give, store, 3, near)
        return carry

    lax.fori_loop(0, per // near, block, 0)


def clip_grads(labels, own, low, high):
    window, rows, _ = own.shape
    per = rows // packed_rows(4, 1)
    near = min(NEAR, per)
    halo = window - 1
    tokens_a = (window + halo) * near
    tokens_b = 2 * halo * near
    vmem = pl.BlockSpec(memory_space=pltpu.VMEM)
    pairs = (tokens_a * tokens_a + tokens_b * tokens_b) * (per // near) * HEADS
    return pl.pallas_call(
        functools.partial(clip_kernel, window, per, near),
        out_shape=jax.ShapeDtypeStruct((window, packed_rows(3, per), LANES), jnp.bfloat16),
        in_specs=[pl.BlockSpec(memory_space=pltpu.SMEM), vmem, vmem, vmem],
        out_specs=vmem,
        scratch_shapes=[
            pltpu.VMEM((tokens_a, tokens_a), jnp.float32),
            pltpu.VMEM((tokens_b, tokens_b), jnp.float32),
            pltpu.VMEM((2, 4, tokens_a, WIDTH), jnp.bfloat16),
        ],
        compiler_params=pltpu.CompilerParams(vmem_limit_bytes=48 * 2**20),
        cost_estimate=pl.CostEstimate(
            flops=12 * pairs * LANES,
            bytes_accessed=2 * (own.size + low.size + high.size),
            transcendentals=pairs,
        ),
        name="clips",
    )(labels, own, low, high)


def frame_labels(clip_len, window):
    halo = window - 1
    total = window * lax.axis_size("grp")
    frames = lax.axis_index("grp") * window - halo + jnp.arange(window + 2 * halo, dtype=jnp.int32)
    order = jnp.arange(clip_len.shape[0])
    ends = jnp.sum(jnp.where(order[:, None] <= order[None, :], clip_len[:, None], 0), axis=0)
    labels = jnp.sum((ends[None, :] <= frames[:, None]).astype(jnp.int32), axis=1)
    outside = jnp.where(frames < 0, -1, clip_len.shape[0])
    return jnp.where((frames >= 0) & (frames < total), labels, outside).astype(jnp.int32)


def shards(q_space, k_space, v_space, cot_space, q_time, k_time, v_time, cot_time, clip_len):
    n = lax.axis_size("seq")
    window = q_time.shape[0] * n
    places = q_time.shape[1] // n
    parts = PARTS
    labels = frame_labels(clip_len, window)
    packed = split((q_time, k_time, v_time, cot_time), parts, n)
    back = []
    for part in range(parts):
        own = lax.all_to_all(packed[part], "seq", split_axis=0, concat_axis=0, tiled=True)
        low = shifted(own[1:], "grp", 1)
        high = shifted(own[: window - 1], "grp", -1)
        grads = clip_grads(labels, own, low, high)
        back.append(lax.all_to_all(grads, "seq", split_axis=0, concat_axis=0, tiled=True))
    grad_qs, grad_ks, grad_vs = frame_grads(q_space, k_space, v_space, cot_space)
    grad_qt, grad_kt, grad_vt = join(back, parts, n, places)
    return (grad_qs, grad_ks, grad_vs, grad_qt, grad_kt, grad_vt)


def solution(mesh):
    split_spec = P(("grp", "seq"), None, None)
    return jax.shard_map(
        shards,
        mesh=mesh,
        in_specs=(split_spec,) * 8 + (P(),),
        out_specs=(split_spec,) * 6,
        check_vma=False,
    )
```

```python
import functools
import math

import jax
import jax.numpy as jnp
from jax import lax
from jax.experimental import pallas as pl
from jax.experimental.pallas import tpu as pltpu
from jax.sharding import PartitionSpec as P

HEADS = 8
HDIM = 72
WIDTH = HEADS * HDIM
SCALING = 1.0 / math.sqrt(HDIM)
CHUNKS = (4, 4)
masked_score = -1e30


def shifted(value, axis, by):
    count = lax.axis_size(axis)
    pairs = [(i, i + by) for i in range(count) if 0 <= i + by < count]
    return lax.ppermute(value, axis, pairs)


def dot(left, right, left_dim, right_dim):
    dims = (((left_dim,), (right_dim,)), ((), ()))
    return lax.dot_general(left, right, dims, preferred_element_type=jnp.float32)


def rounded(value):
    return value.astype(jnp.bfloat16).astype(jnp.float32)


def swapped(value):
    half = value.shape[1] // 2
    if 2 * half == 128:
        return pltpu.roll(value, half, 1)
    return jnp.concatenate([value[:, half:], value[:, :half]], axis=1)


def frame_kernel(q_ref, k_ref, v_ref, g_ref, dq_ref, dk_ref, dv_ref):
    pair = 2 * HDIM
    reach = -(-HDIM // 16) * 16
    row = lax.broadcasted_iota(jnp.int32, (reach, 1), 0)
    for begin in range(0, WIDTH, pair):
        found = [[], [], []]
        for low, own in ((0, 0), (pair - reach, reach - HDIM)):
            span = slice(begin + low, begin + low + reach)
            mask = ((row >= own) & (row < own + HDIM)).astype(jnp.float32).astype(jnp.bfloat16)
            queries, keys = q_ref[0, span, :], k_ref[0, span, :]
            cotangent = g_ref[0, span, :]
            scores = dot(keys * mask, queries, 0, 0) * SCALING
            weight_grad = dot(v_ref[0, span, :] * mask, cotangent, 0, 0)
            raised = jnp.exp(scores - jnp.max(scores, axis=0, keepdims=True))
            weights = raised * (1.0 / jnp.sum(raised, axis=0, keepdims=True))
            weights_low = weights.astype(jnp.bfloat16)
            dots = jnp.sum(weights_low.astype(jnp.float32) * weight_grad, axis=0, keepdims=True)
            score_grad = (weights * (weight_grad - dots)).astype(jnp.bfloat16)
            rows = slice(own, own + HDIM)
            found[0].append(dot(keys, score_grad, 1, 0)[rows] * SCALING)
            found[1].append(dot(queries, score_grad, 1, 1)[rows] * SCALING)
            found[2].append(dot(cotangent, weights_low, 1, 1)[rows])
        for out, parts in zip((dq_ref, dk_ref, dv_ref), found):
            out[0, begin : begin + pair, :] = jnp.concatenate(parts, axis=0).astype(jnp.bfloat16)


def frame_grads(queries, keys, values, cotangent):
    tokens = queries.shape[2]
    shape = jax.ShapeDtypeStruct(queries.shape, jnp.bfloat16)
    return pl.pallas_call(
        frame_kernel,
        out_shape=(shape, shape, shape),
        compiler_params=pltpu.CompilerParams(vmem_limit_bytes=60 * 2**20),
        cost_estimate=pl.CostEstimate(
            flops=12 * tokens * tokens * 256 * HEADS,
            bytes_accessed=14 * tokens * WIDTH,
            transcendentals=tokens * tokens * HEADS,
        ),
        name="space",
    )(queries, keys, values, cotangent)


def split_kernel(rows, n, q_ref, k_ref, v_ref, g_ref, out_ref):
    places = q_ref.shape[2] // n
    for target in range(n):
        lanes = slice(target * places, (target + 1) * places)
        for at, (left, right) in enumerate(((q_ref, g_ref), (k_ref, v_ref))):
            both = [left[0, rows, lanes], right[0, rows, lanes]]
            out_ref[target, at] = jnp.concatenate(both, axis=1)


def split(arrays, rows, n):
    places = arrays[0].shape[2] // n
    shape = (n, 2, rows.stop - rows.start, 2 * places)
    return pl.pallas_call(
        functools.partial(split_kernel, rows, n),
        out_shape=jax.ShapeDtypeStruct(shape, jnp.bfloat16),
        compiler_params=pltpu.CompilerParams(vmem_limit_bytes=32 * 2**20),
        name="pack",
    )(*arrays)


def join_kernel(spans, n, *refs):
    ins, (dq_ref, dk_ref, dv_ref) = refs[: len(spans)], refs[len(spans) :]
    for packed, span in zip(ins, spans):
        count = span.stop - span.start
        half = count // 2
        places = packed.shape[2] // 2

        def gather(rows, lanes):
            return jnp.concatenate([packed[source, rows, lanes] for source in range(n)], axis=1)

        left, right = slice(0, places), slice(places, 2 * places)
        dk_ref[0, span, :] = gather(slice(0, count), left)
        dv_ref[0, span, :] = gather(slice(0, count), right)
        rest = slice(count, count + half)
        dq_ref[0, span.start : span.start + half, :] = gather(rest, left)
        dq_ref[0, span.start + half : span.stop, :] = gather(rest, right)


def join(packed, spans, tokens):
    n = packed[0].shape[0]
    shape = jax.ShapeDtypeStruct((1, WIDTH, tokens), jnp.bfloat16)
    return pl.pallas_call(
        functools.partial(join_kernel, spans, n),
        out_shape=(shape,) * 3,
        compiler_params=pltpu.CompilerParams(vmem_limit_bytes=60 * 2**20),
        name="unpack",
    )(*packed)


def clip_kernel(window, heads, bounds, own_ref, low_ref, high_ref, out_ref, x_ref, y_ref, coef_ref):
    halo = window - 1
    extent = window + 2 * halo
    lanes = out_ref.shape[2]
    places = lanes // 2
    rows = heads * HDIM
    is_left = lax.broadcasted_iota(jnp.int32, (1, lanes), 1) < places
    lowest, highest = bounds[0, halo], bounds[1, halo + window - 1]

    def widen(ref, at, frame):
        x_ref[frame] = ref[at, 0].astype(jnp.float32)
        y_ref[frame] = ref[at, 1].astype(jnp.float32)

    for at in range(window):
        widen(own_ref, at, halo + at)
    for at in range(halo):
        pl.when(at >= lowest)(functools.partial(widen, low_ref, at, at))
        frame = halo + window + at
        pl.when(frame < highest)(functools.partial(widen, high_ref, at, frame))

    def partners(frame):
        first, last = bounds[0, frame], bounds[1, frame]
        return first, last - first, [jnp.minimum(first + t, last - 1) for t in range(window)]

    def weigh(frame, carry):
        first, count, others = partners(frame)
        sums = [[] for _ in range(window)]
        for head in range(heads):
            span = slice(head * HDIM, (head + 1) * HDIM)
            mine = x_ref[frame, span, :]
            for t, other in enumerate(others):
                sums[t].append(jnp.sum(mine * y_ref[other, span, :], axis=0, keepdims=True))
        sums = [jnp.concatenate(parts, axis=0) for parts in sums]
        scores = [
            part * SCALING + jnp.where(t < count, 0.0, masked_score) for t, part in enumerate(sums)
        ]
        peak = functools.reduce(jnp.maximum, scores)
        raised = [jnp.exp(score - peak) for score in scores]
        inverse = 1.0 / functools.reduce(jnp.add, raised)
        weights = [part * inverse for part in raised]
        weights_low = [rounded(part) for part in weights]
        weight_grad = [swapped(part) for part in sums]
        dots = functools.reduce(jnp.add, [w * d for w, d in zip(weights_low, weight_grad)])
        for t in range(window):
            score_grad = rounded(weights[t] * (weight_grad[t] - dots))
            coef_ref[frame, t] = jnp.where(is_left, score_grad, swapped(weights_low[t]))
        return carry

    lax.fori_loop(lowest, highest, weigh, 0)

    def gradients(at, carry):
        frame = halo + at
        first, count, others = partners(frame)
        place = frame - first
        by_key, by_query = [], []
        for head in range(heads):
            span = slice(head * HDIM, (head + 1) * HDIM)
            key_sum, query_sum = None, None
            for t, other in enumerate(others):
                back = coef_ref[other, place, head : head + 1, :]
                back = jnp.where(t < count, back, 0.0)
                ahead = coef_ref[frame, t, head : head + 1, :]
                key_term = back * x_ref[other, span, :]
                query_term = ahead * y_ref[other, span, :]
                key_sum = key_term if t == 0 else key_sum + key_term
                query_sum = query_term if t == 0 else query_sum + query_term
            by_key.append(key_sum * jnp.where(is_left, SCALING, 1.0))
            by_query.append(query_sum * SCALING)
            if head % 2 == 1:
                span = slice((head - 1) * HDIM, (head + 1) * HDIM)
                value = jnp.concatenate(by_key[head - 1 :], axis=0)
                out_ref[at, span, :] = value.astype(jnp.bfloat16)
        half = heads // 2
        folded = [
            jnp.where(is_left, by_query[head], swapped(by_query[head + half]))
            for head in range(half)
        ]
        value = jnp.concatenate(folded, axis=0)
        out_ref[at, rows:, :] = value.astype(jnp.bfloat16)
        return carry

    lax.fori_loop(0, window, gradients, 0)


def clip_grads(bounds, own, low, high):
    window, _, rows, lanes = own.shape
    heads = rows // HDIM
    extent = 3 * window - 2
    vmem = pl.BlockSpec(memory_space=pltpu.VMEM)
    work = extent * window * rows * lanes
    return pl.pallas_call(
        functools.partial(clip_kernel, window, heads),
        out_shape=jax.ShapeDtypeStruct((window, rows + rows // 2, lanes), jnp.bfloat16),
        in_specs=[pl.BlockSpec(memory_space=pltpu.SMEM), vmem, vmem, vmem],
        out_specs=vmem,
        scratch_shapes=[
            pltpu.VMEM((extent, rows, lanes), jnp.float32),
            pltpu.VMEM((extent, rows, lanes), jnp.float32),
            pltpu.VMEM((extent, window, heads, lanes), jnp.float32),
        ],
        compiler_params=pltpu.CompilerParams(vmem_limit_bytes=48 * 2**20),
        cost_estimate=pl.CostEstimate(
            flops=400 * work,
            bytes_accessed=2 * (own.size + low.size + high.size),
            transcendentals=extent * window * heads * lanes,
        ),
        name="clips",
    )(bounds, own, low, high)


def clip_bounds(clip_len, window):
    halo = window - 1
    extent = window + 2 * halo
    start = lax.axis_index("grp") * window - halo
    frames = start + jnp.arange(extent, dtype=jnp.int32)
    order = jnp.arange(clip_len.shape[0])
    ends = jnp.sum(jnp.where(order[:, None] <= order[None, :], clip_len[:, None], 0), axis=0)
    begins = ends - clip_len
    holds = (begins[None, :] <= frames[:, None]) & (frames[:, None] < ends[None, :])
    first = jnp.sum(jnp.where(holds, begins[None, :], 0), axis=1) - start
    last = jnp.sum(jnp.where(holds, ends[None, :], 0), axis=1) - start
    return jnp.stack([first, last]).astype(jnp.int32)


def shards(q_space, k_space, v_space, cot_space, q_time, k_time, v_time, cot_time, clip_len):
    def turned(*arrays):
        return tuple(array.transpose(0, 2, 1) for array in arrays)

    n = lax.axis_size("seq")
    window = q_time.shape[0] * n
    tokens = q_time.shape[1]
    bounds = clip_bounds(clip_len, window)
    time = turned(q_time, k_time, v_time, cot_time)
    spans, back = [], []
    head = 0
    for heads in CHUNKS:
        span = slice(head * HDIM, (head + heads) * HDIM)
        head += heads
        packed = split(time, span, n)
        own = lax.all_to_all(packed, "seq", split_axis=0, concat_axis=0, tiled=True)
        low = shifted(own[1:], "grp", 1)
        high = shifted(own[: window - 1], "grp", -1)
        grads = clip_grads(bounds, own, low, high)
        back.append(lax.all_to_all(grads, "seq", split_axis=0, concat_axis=0, tiled=True))
        spans.append(span)
    space = frame_grads(*turned(q_space, k_space, v_space, cot_space))
    return turned(*space, *join(back, spans, tokens))


def solution(mesh):
    split_spec = P(("grp", "seq"), None, None)
    return jax.shard_map(
        shards,
        mesh=mesh,
        in_specs=(split_spec,) * 8 + (P(),),
        out_specs=(split_spec,) * 6,
        check_vma=False,
    )
```

```python
import functools
import math

import jax
import jax.numpy as jnp
from jax import lax
from jax.experimental import pallas as pl
from jax.experimental.pallas import tpu as pltpu
from jax.sharding import PartitionSpec as P

HEADS = 8
HDIM = 72
WIDTH = HEADS * HDIM
SCALING = 1.0 / math.sqrt(HDIM)
CHUNKS = 2
masked_score = -1e30


def shifted(value, axis, by):
    count = lax.axis_size(axis)
    pairs = [(i, i + by) for i in range(count) if 0 <= i + by < count]
    return lax.ppermute(value, axis, pairs)


def dot(left, right, left_dim, right_dim):
    dims = (((left_dim,), (right_dim,)), ((), ()))
    return lax.dot_general(left, right, dims, preferred_element_type=jnp.float32)


def rounded(value):
    return value.astype(jnp.bfloat16).astype(jnp.float32)


def swapped(value):
    half = value.shape[1] // 2
    if 2 * half == 128:
        return pltpu.roll(value, half, 1)
    return jnp.concatenate([value[:, half:], value[:, :half]], axis=1)


def frame_kernel(q_ref, k_ref, v_ref, g_ref, dq_ref, dk_ref, dv_ref):
    pair = 2 * HDIM
    reach = -(-HDIM // 16) * 16
    row = lax.broadcasted_iota(jnp.int32, (reach, 1), 0)
    for begin in range(0, WIDTH, pair):
        found = [[], [], []]
        for low, own in ((0, 0), (pair - reach, reach - HDIM)):
            span = slice(begin + low, begin + low + reach)
            mask = ((row >= own) & (row < own + HDIM)).astype(jnp.float32).astype(jnp.bfloat16)
            queries, keys = q_ref[0, span, :], k_ref[0, span, :]
            cotangent = g_ref[0, span, :]
            scores = dot(keys * mask, queries, 0, 0) * SCALING
            weight_grad = dot(v_ref[0, span, :] * mask, cotangent, 0, 0)
            raised = jnp.exp(scores - jnp.max(scores, axis=0, keepdims=True))
            weights = raised * (1.0 / jnp.sum(raised, axis=0, keepdims=True))
            weights_low = weights.astype(jnp.bfloat16)
            dots = jnp.sum(weights_low.astype(jnp.float32) * weight_grad, axis=0, keepdims=True)
            score_grad = (weights * (weight_grad - dots)).astype(jnp.bfloat16)
            rows = slice(own, own + HDIM)
            found[0].append(dot(keys, score_grad, 1, 0)[rows] * SCALING)
            found[1].append(dot(queries, score_grad, 1, 1)[rows] * SCALING)
            found[2].append(dot(cotangent, weights_low, 1, 1)[rows])
        for out, parts in zip((dq_ref, dk_ref, dv_ref), found):
            out[0, begin : begin + pair, :] = jnp.concatenate(parts, axis=0).astype(jnp.bfloat16)


def frame_grads(queries, keys, values, cotangent):
    tokens = queries.shape[2]
    shape = jax.ShapeDtypeStruct(queries.shape, jnp.bfloat16)
    return pl.pallas_call(
        frame_kernel,
        out_shape=(shape, shape, shape),
        compiler_params=pltpu.CompilerParams(vmem_limit_bytes=60 * 2**20),
        cost_estimate=pl.CostEstimate(
            flops=12 * tokens * tokens * 256 * HEADS,
            bytes_accessed=14 * tokens * WIDTH,
            transcendentals=tokens * tokens * HEADS,
        ),
        name="space",
    )(queries, keys, values, cotangent)


def split_kernel(n, place_ref, q_ref, k_ref, v_ref, g_ref, *refs):
    outs, held = refs[:n], refs[n]
    places = q_ref.shape[2] // n
    for target in range(n):
        lanes = slice(target * places, (target + 1) * places)
        for at, (left, right) in enumerate(((q_ref, g_ref), (k_ref, v_ref))):
            held[target, at] = jnp.concatenate([left[0, :, lanes], right[0, :, lanes]], axis=1)
    for step, out in enumerate(outs):
        out[...] = held[place_ref[0] ^ step]


def split(place, arrays, chunk, rows, n):
    tokens = arrays[0].shape[2]
    shape = (2, rows, 2 * tokens // n)
    block = pl.BlockSpec((1, rows, tokens), lambda i: (0, chunk, 0))
    return pl.pallas_call(
        functools.partial(split_kernel, n),
        grid=(1,),
        in_specs=[pl.BlockSpec(memory_space=pltpu.SMEM)] + [block] * 4,
        out_specs=[pl.BlockSpec(shape, lambda i: (0, 0, 0))] * n,
        out_shape=[jax.ShapeDtypeStruct(shape, jnp.bfloat16)] * n,
        scratch_shapes=[pltpu.VMEM((n, *shape), jnp.bfloat16)],
        compiler_params=pltpu.CompilerParams(vmem_limit_bytes=60 * 2**20),
        name="pack",
    )(place, *arrays)


def exchange(blocks):
    n = len(blocks)
    moved = [blocks[0]]
    for step in range(1, n):
        moved.append(lax.ppermute(blocks[step], "seq", [(i, i ^ step) for i in range(n)]))
    return moved


def sides_kernel(n, place_ref, *refs):
    ins, (first_ref, last_ref) = refs[:n], refs[n:]
    for step, block in enumerate(ins):
        frame = place_ref[0] ^ step

        @pl.when(frame < n - 1)
        def _():
            first_ref[jnp.minimum(frame, n - 2)] = block[...]

        @pl.when(frame > 0)
        def _():
            last_ref[jnp.maximum(frame - 1, 0)] = block[...]


def sides(place, blocks):
    n = len(blocks)
    shape = jax.ShapeDtypeStruct((n - 1, *blocks[0].shape), jnp.bfloat16)
    vmem = pl.BlockSpec(memory_space=pltpu.VMEM)
    return pl.pallas_call(
        functools.partial(sides_kernel, n),
        in_specs=[pl.BlockSpec(memory_space=pltpu.SMEM)] + [vmem] * n,
        out_specs=[vmem] * 2,
        out_shape=[shape] * 2,
        compiler_params=pltpu.CompilerParams(vmem_limit_bytes=32 * 2**20),
        name="sides",
    )(place, *blocks)


def join_kernel(n, place_ref, *refs):
    ins, (dq_ref, dk_ref, dv_ref, held) = refs[:n], refs[-4:]
    for step, block in enumerate(ins):
        held[place_ref[0] ^ step] = block[...]
    count = dq_ref.shape[1]
    half = count // 2
    places = held.shape[2] // 2

    def gather(rows, lanes):
        return jnp.concatenate([held[source, rows, lanes] for source in range(n)], axis=1)

    left, right = slice(0, places), slice(places, 2 * places)
    dk_ref[0] = gather(slice(0, count), left)
    dv_ref[0] = gather(slice(0, count), right)
    rest = slice(count, count + half)
    dq_ref[0, :half, :] = gather(rest, left)
    dq_ref[0, half:, :] = gather(rest, right)


def join(place, blocks, chunk, rows, tokens, earlier):
    n = len(blocks)
    shape = jax.ShapeDtypeStruct((1, WIDTH, tokens), jnp.bfloat16)
    vmem = pl.BlockSpec(memory_space=pltpu.VMEM)
    whole = pl.BlockSpec(memory_space=pl.ANY)
    earlier = [] if earlier is None else list(earlier)
    return pl.pallas_call(
        functools.partial(join_kernel, n),
        grid=(1,),
        in_specs=[pl.BlockSpec(memory_space=pltpu.SMEM)] + [vmem] * n + [whole] * len(earlier),
        out_specs=[pl.BlockSpec((1, rows, tokens), lambda i: (0, chunk, 0))] * 3,
        out_shape=[shape] * 3,
        scratch_shapes=[pltpu.VMEM((n, *blocks[0].shape), jnp.bfloat16)],
        input_output_aliases={1 + n + i: i for i in range(len(earlier))},
        compiler_params=pltpu.CompilerParams(vmem_limit_bytes=24 * 2**20),
        name="unpack",
    )(place, *blocks, *earlier)


def clip_kernel(window, heads, place_ref, bounds, *refs):
    own, low_ref, high_ref = refs[:window], refs[window], refs[window + 1]
    outs, (x_ref, y_ref, coef_ref, grad_ref) = refs[window + 2 : 2 * window + 2], refs[-4:]
    halo = window - 1
    extent = window + 2 * halo
    lanes = grad_ref.shape[2]
    places = lanes // 2
    rows = heads * HDIM
    is_left = lax.broadcasted_iota(jnp.int32, (1, lanes), 1) < places
    lowest, highest = bounds[0, halo], bounds[1, halo + window - 1]

    def widen(ref, frame):
        x_ref[frame] = ref[0].astype(jnp.float32)
        y_ref[frame] = ref[1].astype(jnp.float32)

    for step, block in enumerate(own):
        widen(block, halo + (place_ref[0] ^ step))
    for at in range(halo):
        pl.when(at >= lowest)(functools.partial(widen, low_ref.at[at], at))
        frame = halo + window + at
        pl.when(frame < highest)(functools.partial(widen, high_ref.at[at], frame))

    def partners(frame):
        first, last = bounds[0, frame], bounds[1, frame]
        return first, last - first, [jnp.minimum(first + t, last - 1) for t in range(window)]

    def weigh(frame, carry):
        first, count, others = partners(frame)
        sums = [[] for _ in range(window)]
        for head in range(heads):
            span = slice(head * HDIM, (head + 1) * HDIM)
            mine = x_ref[frame, span, :]
            for t, other in enumerate(others):
                sums[t].append(jnp.sum(mine * y_ref[other, span, :], axis=0, keepdims=True))
        sums = [jnp.concatenate(parts, axis=0) for parts in sums]
        scores = [
            part * SCALING + jnp.where(t < count, 0.0, masked_score) for t, part in enumerate(sums)
        ]
        peak = functools.reduce(jnp.maximum, scores)
        raised = [jnp.exp(score - peak) for score in scores]
        inverse = 1.0 / functools.reduce(jnp.add, raised)
        weights = [part * inverse for part in raised]
        weights_low = [rounded(part) for part in weights]
        weight_grad = [swapped(part) for part in sums]
        dots = functools.reduce(jnp.add, [w * d for w, d in zip(weights_low, weight_grad)])
        for t in range(window):
            score_grad = rounded(weights[t] * (weight_grad[t] - dots))
            coef_ref[frame, t] = jnp.where(is_left, score_grad, swapped(weights_low[t]))
        return carry

    lax.fori_loop(lowest, highest, weigh, 0)

    def gradients(at, carry):
        frame = halo + at
        first, count, others = partners(frame)
        place = frame - first
        by_key, by_query = [], []
        for head in range(heads):
            span = slice(head * HDIM, (head + 1) * HDIM)
            key_sum, query_sum = None, None
            for t, other in enumerate(others):
                back = coef_ref[other, place, head : head + 1, :]
                back = jnp.where(t < count, back, 0.0)
                ahead = coef_ref[frame, t, head : head + 1, :]
                key_term = back * x_ref[other, span, :]
                query_term = ahead * y_ref[other, span, :]
                key_sum = key_term if t == 0 else key_sum + key_term
                query_sum = query_term if t == 0 else query_sum + query_term
            by_key.append(key_sum * jnp.where(is_left, SCALING, 1.0))
            by_query.append(query_sum * SCALING)
            if head % 2 == 1:
                span = slice((head - 1) * HDIM, (head + 1) * HDIM)
                value = jnp.concatenate(by_key[head - 1 :], axis=0)
                grad_ref[at, span, :] = value.astype(jnp.bfloat16)
        half = heads // 2
        folded = [
            jnp.where(is_left, by_query[head], swapped(by_query[head + half]))
            for head in range(half)
        ]
        value = jnp.concatenate(folded, axis=0)
        grad_ref[at, rows:, :] = value.astype(jnp.bfloat16)
        return carry

    lax.fori_loop(0, window, gradients, 0)
    for step, out in enumerate(outs):
        out[...] = grad_ref[place_ref[0] ^ step]


def clip_grads(place, bounds, own, low, high):
    window = len(own)
    _, rows, lanes = own[0].shape
    heads = rows // HDIM
    extent = 3 * window - 2
    vmem = pl.BlockSpec(memory_space=pltpu.VMEM)
    smem = pl.BlockSpec(memory_space=pltpu.SMEM)
    work = extent * window * rows * lanes
    shape = (rows + rows // 2, lanes)
    return pl.pallas_call(
        functools.partial(clip_kernel, window, heads),
        out_shape=[jax.ShapeDtypeStruct(shape, jnp.bfloat16)] * window,
        in_specs=[smem, smem] + [vmem] * (window + 2),
        out_specs=[vmem] * window,
        scratch_shapes=[
            pltpu.VMEM((extent, rows, lanes), jnp.float32),
            pltpu.VMEM((extent, rows, lanes), jnp.float32),
            pltpu.VMEM((extent, window, heads, lanes), jnp.float32),
            pltpu.VMEM((window, *shape), jnp.bfloat16),
        ],
        compiler_params=pltpu.CompilerParams(vmem_limit_bytes=48 * 2**20),
        cost_estimate=pl.CostEstimate(
            flops=400 * work,
            bytes_accessed=2 * (window * own[0].size + low.size + high.size),
            transcendentals=extent * window * heads * lanes,
        ),
        name="clips",
    )(place, bounds, *own, low, high)


def clip_bounds(clip_len, window):
    halo = window - 1
    extent = window + 2 * halo
    start = lax.axis_index("grp") * window - halo
    frames = start + jnp.arange(extent, dtype=jnp.int32)
    order = jnp.arange(clip_len.shape[0])
    ends = jnp.sum(jnp.where(order[:, None] <= order[None, :], clip_len[:, None], 0), axis=0)
    begins = ends - clip_len
    holds = (begins[None, :] <= frames[:, None]) & (frames[:, None] < ends[None, :])
    first = jnp.sum(jnp.where(holds, begins[None, :], 0), axis=1) - start
    last = jnp.sum(jnp.where(holds, ends[None, :], 0), axis=1) - start
    return jnp.stack([first, last]).astype(jnp.int32)


def shards(q_space, k_space, v_space, cot_space, q_time, k_time, v_time, cot_time, clip_len):
    def turned(*arrays):
        return tuple(array.transpose(0, 2, 1) for array in arrays)

    n = lax.axis_size("seq")
    window = q_time.shape[0] * n
    tokens = q_time.shape[1]
    bounds = clip_bounds(clip_len, window)
    place = lax.axis_index("seq").astype(jnp.int32).reshape(1)
    time = turned(q_time, k_time, v_time, cot_time)
    rows = WIDTH // CHUNKS
    back = []
    for chunk in range(CHUNKS):
        own = exchange(split(place, time, chunk, rows, n))
        first, last = sides(place, own)
        low = shifted(last, "grp", 1)
        high = shifted(first, "grp", -1)
        back.append(exchange(clip_grads(place, bounds, own, low, high)))
    grads = None
    for chunk, blocks in enumerate(back):
        grads = join(place, blocks, chunk, rows, tokens, grads)
    space = frame_grads(*turned(q_space, k_space, v_space, cot_space))
    return turned(*space, *grads)


def solution(mesh):
    split_spec = P(("grp", "seq"), None, None)
    return jax.shard_map(
        shards,
        mesh=mesh,
        in_specs=(split_spec,) * 8 + (P(),),
        out_specs=(split_spec,) * 6,
        check_vma=False,
    )
```

```python
import functools
import math

import jax
import jax.numpy as jnp
from jax import lax
from jax.experimental import pallas as pl
from jax.experimental.pallas import tpu as pltpu
from jax.sharding import PartitionSpec as P

HEADS = 8
HDIM = 72
WIDTH = HEADS * HDIM
SCALING = 1.0 / math.sqrt(HDIM)
CHUNKS = (4, 4)
masked_score = -1e30


def shifted(value, axis, by):
    count = lax.axis_size(axis)
    pairs = [(i, i + by) for i in range(count) if 0 <= i + by < count]
    return lax.ppermute(value, axis, pairs)


def dot(left, right, left_dim, right_dim):
    dims = (((left_dim,), (right_dim,)), ((), ()))
    return lax.dot_general(left, right, dims, preferred_element_type=jnp.float32)


def rounded(value):
    return value.astype(jnp.bfloat16).astype(jnp.float32)


def swapped(value):
    half = value.shape[1] // 2
    if 2 * half == 128:
        return pltpu.roll(value, half, 1)
    return jnp.concatenate([value[:, half:], value[:, :half]], axis=1)


def frame_kernel(q_ref, k_ref, v_ref, g_ref, dq_ref, dk_ref, dv_ref):
    pair = 2 * HDIM
    reach = -(-HDIM // 16) * 16
    row = lax.broadcasted_iota(jnp.int32, (reach, 1), 0)
    for begin in range(0, WIDTH, pair):
        found = [[], [], []]
        for low, own in ((0, 0), (pair - reach, reach - HDIM)):
            span = slice(begin + low, begin + low + reach)
            mask = ((row >= own) & (row < own + HDIM)).astype(jnp.float32).astype(jnp.bfloat16)
            queries, keys = q_ref[0, span, :], k_ref[0, span, :]
            cotangent = g_ref[0, span, :]
            scores = dot(keys * mask, queries, 0, 0) * SCALING
            weight_grad = dot(v_ref[0, span, :] * mask, cotangent, 0, 0)
            raised = jnp.exp(scores - jnp.max(scores, axis=0, keepdims=True))
            weights = raised * (1.0 / jnp.sum(raised, axis=0, keepdims=True))
            weights_low = weights.astype(jnp.bfloat16)
            dots = jnp.sum(weights_low.astype(jnp.float32) * weight_grad, axis=0, keepdims=True)
            score_grad = (weights * (weight_grad - dots)).astype(jnp.bfloat16)
            rows = slice(own, own + HDIM)
            found[0].append(dot(keys, score_grad, 1, 0)[rows] * SCALING)
            found[1].append(dot(queries, score_grad, 1, 1)[rows] * SCALING)
            found[2].append(dot(cotangent, weights_low, 1, 1)[rows])
        for out, parts in zip((dq_ref, dk_ref, dv_ref), found):
            out[0, begin : begin + pair, :] = jnp.concatenate(parts, axis=0).astype(jnp.bfloat16)


def frame_grads(queries, keys, values, cotangent):
    tokens = queries.shape[2]
    shape = jax.ShapeDtypeStruct(queries.shape, jnp.bfloat16)
    return pl.pallas_call(
        frame_kernel,
        out_shape=(shape, shape, shape),
        compiler_params=pltpu.CompilerParams(vmem_limit_bytes=60 * 2**20),
        cost_estimate=pl.CostEstimate(
            flops=12 * tokens * tokens * 256 * HEADS,
            bytes_accessed=14 * tokens * WIDTH,
            transcendentals=tokens * tokens * HEADS,
        ),
        name="space",
    )(queries, keys, values, cotangent)


def split_kernel(n, span, place_ref, *refs):
    ins, outs, (loaded, held, arrived, left_off) = refs[:4], refs[4 : 4 + n], refs[-4:]
    loads = [
        pltpu.make_async_copy(array.at[0, span, :], loaded.at[i], arrived.at[i])
        for i, array in enumerate(ins)
    ]
    for copy in loads:
        copy.start()
    places = ins[0].shape[2] // n
    for at in range(2):
        loads[2 * at].wait()
        loads[2 * at + 1].wait()
        for target in range(n):
            lanes = slice(target * places, (target + 1) * places)
            both = [loaded[2 * at, :, lanes], loaded[2 * at + 1, :, lanes]]
            held[target, at] = jnp.concatenate(both, axis=1)
    stores = [
        pltpu.make_async_copy(held.at[place_ref[0] ^ step], out, left_off.at[step])
        for step, out in enumerate(outs)
    ]
    for copy in stores:
        copy.start()
    for copy in stores:
        copy.wait()


def split(place, arrays, span, n):
    rows, tokens = span.stop - span.start, arrays[0].shape[2]
    shape = (2, rows, 2 * tokens // n)
    hbm = pl.BlockSpec(memory_space=pltpu.HBM)
    return pl.pallas_call(
        functools.partial(split_kernel, n, span),
        in_specs=[pl.BlockSpec(memory_space=pltpu.SMEM)] + [hbm] * 4,
        out_specs=[hbm] * n,
        out_shape=[jax.ShapeDtypeStruct(shape, jnp.bfloat16)] * n,
        scratch_shapes=[
            pltpu.VMEM((4, rows, tokens), jnp.bfloat16),
            pltpu.VMEM((n, *shape), jnp.bfloat16),
            pltpu.SemaphoreType.DMA((4,)),
            pltpu.SemaphoreType.DMA((n,)),
        ],
        compiler_params=pltpu.CompilerParams(vmem_limit_bytes=60 * 2**20),
        name="pack",
    )(place, *arrays)


def exchange(blocks):
    n = len(blocks)
    moved = [blocks[0]]
    for step in range(1, n):
        moved.append(lax.ppermute(blocks[step], "seq", [(i, i ^ step) for i in range(n)]))
    return moved


def sides_kernel(n, place_ref, *refs):
    ins, (first_ref, last_ref) = refs[:n], refs[n:]
    for step, block in enumerate(ins):
        frame = place_ref[0] ^ step

        @pl.when(frame < n - 1)
        def _():
            first_ref[jnp.minimum(frame, n - 2)] = block[...]

        @pl.when(frame > 0)
        def _():
            last_ref[jnp.maximum(frame - 1, 0)] = block[...]


def sides(place, blocks):
    n = len(blocks)
    shape = jax.ShapeDtypeStruct((n - 1, *blocks[0].shape), jnp.bfloat16)
    vmem = pl.BlockSpec(memory_space=pltpu.VMEM)
    return pl.pallas_call(
        functools.partial(sides_kernel, n),
        in_specs=[pl.BlockSpec(memory_space=pltpu.SMEM)] + [vmem] * n,
        out_specs=[vmem] * 2,
        out_shape=[shape] * 2,
        compiler_params=pltpu.CompilerParams(vmem_limit_bytes=32 * 2**20),
        name="sides",
    )(place, *blocks)


def join_kernel(n, span, place_ref, *refs):
    ins, outs, (held, ready, left_off) = refs[:n], refs[-6:-3], refs[-3:]
    for step, block in enumerate(ins):
        held[place_ref[0] ^ step] = block[...]
    count = span.stop - span.start
    half = count // 2
    places = held.shape[2] // 2

    def gather(rows, lanes):
        return jnp.concatenate([held[source, rows, lanes] for source in range(n)], axis=1)

    left, right = slice(0, places), slice(places, 2 * places)
    rest = slice(count, count + half)
    ready[1] = gather(slice(0, count), left)
    ready[2] = gather(slice(0, count), right)
    ready[0, :half, :] = gather(rest, left)
    ready[0, half:, :] = gather(rest, right)
    copies = [
        pltpu.make_async_copy(ready.at[i], out.at[0, span, :], left_off.at[i])
        for i, out in enumerate(outs)
    ]
    for copy in copies:
        copy.start()
    for copy in copies:
        copy.wait()


def join(place, blocks, span, tokens, earlier):
    n = len(blocks)
    rows = span.stop - span.start
    shape = jax.ShapeDtypeStruct((1, WIDTH, tokens), jnp.bfloat16)
    vmem = pl.BlockSpec(memory_space=pltpu.VMEM)
    hbm = pl.BlockSpec(memory_space=pltpu.HBM)
    earlier = [] if earlier is None else list(earlier)
    return pl.pallas_call(
        functools.partial(join_kernel, n, span),
        in_specs=[pl.BlockSpec(memory_space=pltpu.SMEM)] + [vmem] * n + [hbm] * len(earlier),
        out_specs=[hbm] * 3,
        out_shape=[shape] * 3,
        scratch_shapes=[
            pltpu.VMEM((n, *blocks[0].shape), jnp.bfloat16),
            pltpu.VMEM((3, rows, tokens), jnp.bfloat16),
            pltpu.SemaphoreType.DMA((3,)),
        ],
        input_output_aliases={1 + n + i: i for i in range(len(earlier))},
        compiler_params=pltpu.CompilerParams(vmem_limit_bytes=24 * 2**20),
        name="unpack",
    )(place, *blocks, *earlier)


def clip_kernel(window, heads, place_ref, bounds, *refs):
    own, low_ref, high_ref = refs[:window], refs[window], refs[window + 1]
    outs, (x_ref, y_ref, coef_ref, grad_ref) = refs[window + 2 : 2 * window + 2], refs[-4:]
    halo = window - 1
    extent = window + 2 * halo
    lanes = grad_ref.shape[2]
    places = lanes // 2
    rows = heads * HDIM
    is_left = lax.broadcasted_iota(jnp.int32, (1, lanes), 1) < places
    lowest, highest = bounds[0, halo], bounds[1, halo + window - 1]

    def widen(ref, frame):
        x_ref[frame] = ref[0].astype(jnp.float32)
        y_ref[frame] = ref[1].astype(jnp.float32)

    for step, block in enumerate(own):
        widen(block, halo + (place_ref[0] ^ step))
    for at in range(halo):
        pl.when(at >= lowest)(functools.partial(widen, low_ref.at[at], at))
        frame = halo + window + at
        pl.when(frame < highest)(functools.partial(widen, high_ref.at[at], frame))

    def partners(frame):
        first, last = bounds[0, frame], bounds[1, frame]
        return first, last - first, [jnp.minimum(first + t, last - 1) for t in range(window)]

    def weigh(frame, carry):
        first, count, others = partners(frame)
        sums = [[] for _ in range(window)]
        for head in range(heads):
            span = slice(head * HDIM, (head + 1) * HDIM)
            mine = x_ref[frame, span, :]
            for t, other in enumerate(others):
                sums[t].append(jnp.sum(mine * y_ref[other, span, :], axis=0, keepdims=True))
        sums = [jnp.concatenate(parts, axis=0) for parts in sums]
        scores = [
            part * SCALING + jnp.where(t < count, 0.0, masked_score) for t, part in enumerate(sums)
        ]
        peak = functools.reduce(jnp.maximum, scores)
        raised = [jnp.exp(score - peak) for score in scores]
        inverse = 1.0 / functools.reduce(jnp.add, raised)
        weights = [part * inverse for part in raised]
        weights_low = [rounded(part) for part in weights]
        weight_grad = [swapped(part) for part in sums]
        dots = functools.reduce(jnp.add, [w * d for w, d in zip(weights_low, weight_grad)])
        for t in range(window):
            score_grad = rounded(weights[t] * (weight_grad[t] - dots))
            coef_ref[frame, t] = jnp.where(is_left, score_grad, swapped(weights_low[t]))
        return carry

    lax.fori_loop(lowest, highest, weigh, 0)

    def gradients(at, carry):
        frame = halo + at
        first, count, others = partners(frame)
        place = frame - first
        by_key, by_query = [], []
        for head in range(heads):
            span = slice(head * HDIM, (head + 1) * HDIM)
            key_sum, query_sum = None, None
            for t, other in enumerate(others):
                back = coef_ref[other, place, head : head + 1, :]
                back = jnp.where(t < count, back, 0.0)
                ahead = coef_ref[frame, t, head : head + 1, :]
                key_term = back * x_ref[other, span, :]
                query_term = ahead * y_ref[other, span, :]
                key_sum = key_term if t == 0 else key_sum + key_term
                query_sum = query_term if t == 0 else query_sum + query_term
            by_key.append(key_sum * jnp.where(is_left, SCALING, 1.0))
            by_query.append(query_sum * SCALING)
            if head % 2 == 1:
                span = slice((head - 1) * HDIM, (head + 1) * HDIM)
                value = jnp.concatenate(by_key[head - 1 :], axis=0)
                grad_ref[at, span, :] = value.astype(jnp.bfloat16)
        half = heads // 2
        folded = [
            jnp.where(is_left, by_query[head], swapped(by_query[head + half]))
            for head in range(half)
        ]
        value = jnp.concatenate(folded, axis=0)
        grad_ref[at, rows:, :] = value.astype(jnp.bfloat16)
        return carry

    lax.fori_loop(0, window, gradients, 0)
    for step, out in enumerate(outs):
        out[...] = grad_ref[place_ref[0] ^ step]


def clip_grads(place, bounds, own, low, high):
    window = len(own)
    _, rows, lanes = own[0].shape
    heads = rows // HDIM
    extent = 3 * window - 2
    vmem = pl.BlockSpec(memory_space=pltpu.VMEM)
    smem = pl.BlockSpec(memory_space=pltpu.SMEM)
    work = extent * window * rows * lanes
    shape = (rows + rows // 2, lanes)
    return pl.pallas_call(
        functools.partial(clip_kernel, window, heads),
        out_shape=[jax.ShapeDtypeStruct(shape, jnp.bfloat16)] * window,
        in_specs=[smem, smem] + [vmem] * (window + 2),
        out_specs=[vmem] * window,
        scratch_shapes=[
            pltpu.VMEM((extent, rows, lanes), jnp.float32),
            pltpu.VMEM((extent, rows, lanes), jnp.float32),
            pltpu.VMEM((extent, window, heads, lanes), jnp.float32),
            pltpu.VMEM((window, *shape), jnp.bfloat16),
        ],
        compiler_params=pltpu.CompilerParams(vmem_limit_bytes=48 * 2**20),
        cost_estimate=pl.CostEstimate(
            flops=400 * work,
            bytes_accessed=2 * (window * own[0].size + low.size + high.size),
            transcendentals=extent * window * heads * lanes,
        ),
        name="clips",
    )(place, bounds, *own, low, high)


def clip_bounds(clip_len, window):
    halo = window - 1
    extent = window + 2 * halo
    start = lax.axis_index("grp") * window - halo
    frames = start + jnp.arange(extent, dtype=jnp.int32)
    order = jnp.arange(clip_len.shape[0])
    ends = jnp.sum(jnp.where(order[:, None] <= order[None, :], clip_len[:, None], 0), axis=0)
    begins = ends - clip_len
    holds = (begins[None, :] <= frames[:, None]) & (frames[:, None] < ends[None, :])
    first = jnp.sum(jnp.where(holds, begins[None, :], 0), axis=1) - start
    last = jnp.sum(jnp.where(holds, ends[None, :], 0), axis=1) - start
    return jnp.stack([first, last]).astype(jnp.int32)


def shards(q_space, k_space, v_space, cot_space, q_time, k_time, v_time, cot_time, clip_len):
    def turned(*arrays):
        return tuple(array.transpose(0, 2, 1) for array in arrays)

    n = lax.axis_size("seq")
    window = q_time.shape[0] * n
    tokens = q_time.shape[1]
    bounds = clip_bounds(clip_len, window)
    place = lax.axis_index("seq").astype(jnp.int32).reshape(1)
    time = turned(q_time, cot_time, k_time, v_time)
    spans = []
    head = 0
    for heads in CHUNKS:
        spans.append(slice(head * HDIM, (head + heads) * HDIM))
        head += heads
    space = frame_grads(*turned(q_space, k_space, v_space, cot_space))
    back = []
    own = None
    for span in spans:
        packed = list(split(place, time, span, n))
        if own is not None:
            packed[2:], own[2] = lax.optimization_barrier((packed[2:], own[2]))
        own = exchange(packed)
        first, last = sides(place, own)
        low = shifted(last, "grp", 1)
        high = shifted(first, "grp", -1)
        back.append(exchange(clip_grads(place, bounds, own, low, high)))
    grads = None
    for span, blocks in zip(spans, back):
        grads = join(place, blocks, span, tokens, grads)
    return turned(*space, *grads)


def solution(mesh):
    split_spec = P(("grp", "seq"), None, None)
    return jax.shard_map(
        shards,
        mesh=mesh,
        in_specs=(split_spec,) * 8 + (P(),),
        out_specs=(split_spec,) * 6,
        check_vma=False,
    )
```

```python
import functools
import math

import jax
import jax.numpy as jnp
from jax import lax
from jax.experimental import pallas as pl
from jax.experimental.pallas import tpu as pltpu
from jax.sharding import PartitionSpec as P

HEADS = 8
HDIM = 72
WIDTH = HEADS * HDIM
SCALING = 1.0 / math.sqrt(HDIM)
CHUNKS = (4, 4)
GATHER_SEQ = True
GATHER_GRP = True
masked_score = -1e30


def dot(left, right, left_dim, right_dim):
    dims = (((left_dim,), (right_dim,)), ((), ()))
    return lax.dot_general(left, right, dims, preferred_element_type=jnp.float32)


def rounded(value):
    return value.astype(jnp.bfloat16).astype(jnp.float32)


def swapped(value):
    half = value.shape[1] // 2
    if 2 * half == 128:
        return pltpu.roll(value, half, 1)
    return jnp.concatenate([value[:, half:], value[:, :half]], axis=1)


def frame_kernel(q_ref, k_ref, v_ref, g_ref, dq_ref, dk_ref, dv_ref):
    pair = 2 * HDIM
    reach = -(-HDIM // 16) * 16
    row = lax.broadcasted_iota(jnp.int32, (reach, 1), 0)
    for begin in range(0, WIDTH, pair):
        found = [[], [], []]
        for low, own in ((0, 0), (pair - reach, reach - HDIM)):
            span = slice(begin + low, begin + low + reach)
            mask = ((row >= own) & (row < own + HDIM)).astype(jnp.float32).astype(jnp.bfloat16)
            queries, keys = q_ref[0, span, :], k_ref[0, span, :]
            cotangent = g_ref[0, span, :]
            scores = dot(keys * mask, queries, 0, 0) * SCALING
            weight_grad = dot(v_ref[0, span, :] * mask, cotangent, 0, 0)
            raised = jnp.exp(scores - jnp.max(scores, axis=0, keepdims=True))
            weights = raised * (1.0 / jnp.sum(raised, axis=0, keepdims=True))
            weights_low = weights.astype(jnp.bfloat16)
            dots = jnp.sum(weights_low.astype(jnp.float32) * weight_grad, axis=0, keepdims=True)
            score_grad = (weights * (weight_grad - dots)).astype(jnp.bfloat16)
            rows = slice(own, own + HDIM)
            found[0].append(dot(keys, score_grad, 1, 0)[rows] * SCALING)
            found[1].append(dot(queries, score_grad, 1, 1)[rows] * SCALING)
            found[2].append(dot(cotangent, weights_low, 1, 1)[rows])
        for out, parts in zip((dq_ref, dk_ref, dv_ref), found):
            out[0, begin : begin + pair, :] = jnp.concatenate(parts, axis=0).astype(jnp.bfloat16)


def frame_grads(queries, keys, values, cotangent):
    tokens = queries.shape[2]
    shape = jax.ShapeDtypeStruct(queries.shape, jnp.bfloat16)
    return pl.pallas_call(
        frame_kernel,
        out_shape=(shape, shape, shape),
        compiler_params=pltpu.CompilerParams(vmem_limit_bytes=60 * 2**20),
        cost_estimate=pl.CostEstimate(
            flops=12 * tokens * tokens * 256 * HEADS,
            bytes_accessed=14 * tokens * WIDTH,
            transcendentals=tokens * tokens * HEADS,
        ),
        name="space",
    )(queries, keys, values, cotangent)


def split_kernel(n, span, place_ref, *refs):
    ins, outs, (loaded, held, arrived, left_off) = refs[:4], refs[4 : 4 + n], refs[-4:]
    loads = [
        pltpu.make_async_copy(array.at[0, span, :], loaded.at[i], arrived.at[i])
        for i, array in enumerate(ins)
    ]
    for copy in loads:
        copy.start()
    places = ins[0].shape[2] // n
    for at in range(2):
        loads[2 * at].wait()
        loads[2 * at + 1].wait()
        for target in range(n):
            lanes = slice(target * places, (target + 1) * places)
            both = [loaded[2 * at, :, lanes], loaded[2 * at + 1, :, lanes]]
            held[target, at] = jnp.concatenate(both, axis=1)
    stores = [
        pltpu.make_async_copy(held.at[place_ref[0] ^ step], out, left_off.at[step])
        for step, out in enumerate(outs)
    ]
    for copy in stores:
        copy.start()
    for copy in stores:
        copy.wait()


def split(place, arrays, span, n):
    rows, tokens = span.stop - span.start, arrays[0].shape[2]
    shape = (2, rows, 2 * tokens // n)
    hbm = pl.BlockSpec(memory_space=pltpu.HBM)
    return pl.pallas_call(
        functools.partial(split_kernel, n, span),
        in_specs=[pl.BlockSpec(memory_space=pltpu.SMEM)] + [hbm] * 4,
        out_specs=[hbm] * n,
        out_shape=[jax.ShapeDtypeStruct(shape, jnp.bfloat16)] * n,
        scratch_shapes=[
            pltpu.VMEM((4, rows, tokens), jnp.bfloat16),
            pltpu.VMEM((n, *shape), jnp.bfloat16),
            pltpu.SemaphoreType.DMA((4,)),
            pltpu.SemaphoreType.DMA((n,)),
        ],
        compiler_params=pltpu.CompilerParams(vmem_limit_bytes=60 * 2**20),
        name="pack",
    )(place, *arrays)


def swap(block, axis, pairs, gathered):
    if gathered:
        return lax.all_gather(block, axis, axis_index_groups=pairs)
    return lax.ppermute(block, axis, [(i, j) for i, j in pairs] + [(j, i) for i, j in pairs])


def exchange(blocks):
    n = len(blocks)
    moved = [blocks[0]]
    for step in range(1, n):
        pairs = [[i, i ^ step] for i in range(n) if i < i ^ step]
        moved.append(swap(blocks[step], "seq", pairs, GATHER_SEQ))
    return moved


def from_partner(ref, is_second):
    return ref.at[is_second] if GATHER_SEQ else ref


def seq_block(ref, step, place_ref):
    if step == 0:
        return ref
    return from_partner(ref, jnp.int32(place_ref[0] < place_ref[0] ^ step))


def sides_kernel(n, place_ref, *refs):
    ins, outs = refs[:n], refs[n:]
    is_odd = place_ref[1]
    for step, ref in enumerate(ins):
        block = seq_block(ref, step, place_ref)
        frame = place_ref[0] ^ step
        for start, out in enumerate(outs):
            at = frame - jnp.where(is_odd == start, 1, 0)

            @pl.when((at >= 0) & (at < n - 1))
            def _():
                out[jnp.clip(at, 0, n - 2)] = block[...]


def sides(place, blocks):
    n = len(blocks)
    shape = jax.ShapeDtypeStruct((n - 1, *blocks[0].shape), jnp.bfloat16)
    vmem = pl.BlockSpec(memory_space=pltpu.VMEM)
    return pl.pallas_call(
        functools.partial(sides_kernel, n),
        in_specs=[pl.BlockSpec(memory_space=pltpu.SMEM)] + [vmem] * n,
        out_specs=[vmem] * 2,
        out_shape=[shape] * 2,
        compiler_params=pltpu.CompilerParams(vmem_limit_bytes=60 * 2**20),
        name="sides",
    )(place, *blocks)


def neighbours(blocks):
    count = lax.axis_size("grp")
    moved = []
    for start, block in enumerate(blocks):
        pairs = [[i, (i + 1) % count] for i in range(start, count, 2)]
        if not GATHER_GRP:
            pairs = [pair for pair in pairs if pair[0] < pair[1]]
        moved.append(swap(block, "grp", pairs, GATHER_GRP))
    return moved


def join_kernel(n, span, place_ref, *refs):
    ins, outs, (held, ready, left_off) = refs[:n], refs[-6:-3], refs[-3:]
    for step, ref in enumerate(ins):
        held[place_ref[0] ^ step] = seq_block(ref, step, place_ref)[...]
    count = span.stop - span.start
    half = count // 2
    places = held.shape[2] // 2

    def gather(rows, lanes):
        return jnp.concatenate([held[source, rows, lanes] for source in range(n)], axis=1)

    left, right = slice(0, places), slice(places, 2 * places)
    rest = slice(count, count + half)
    ready[1] = gather(slice(0, count), left)
    ready[2] = gather(slice(0, count), right)
    ready[0, :half, :] = gather(rest, left)
    ready[0, half:, :] = gather(rest, right)
    copies = [
        pltpu.make_async_copy(ready.at[i], out.at[0, span, :], left_off.at[i])
        for i, out in enumerate(outs)
    ]
    for copy in copies:
        copy.start()
    for copy in copies:
        copy.wait()


def join(place, blocks, span, tokens, earlier):
    n = len(blocks)
    rows = span.stop - span.start
    shape = jax.ShapeDtypeStruct((1, WIDTH, tokens), jnp.bfloat16)
    vmem = pl.BlockSpec(memory_space=pltpu.VMEM)
    hbm = pl.BlockSpec(memory_space=pltpu.HBM)
    earlier = [] if earlier is None else list(earlier)
    return pl.pallas_call(
        functools.partial(join_kernel, n, span),
        in_specs=[pl.BlockSpec(memory_space=pltpu.SMEM)] + [vmem] * n + [hbm] * len(earlier),
        out_specs=[hbm] * 3,
        out_shape=[shape] * 3,
        scratch_shapes=[
            pltpu.VMEM((n, *blocks[0].shape), jnp.bfloat16),
            pltpu.VMEM((3, rows, tokens), jnp.bfloat16),
            pltpu.SemaphoreType.DMA((3,)),
        ],
        input_output_aliases={1 + n + i: i for i in range(len(earlier))},
        compiler_params=pltpu.CompilerParams(vmem_limit_bytes=60 * 2**20),
        name="unpack",
    )(place, *blocks, *earlier)


def clip_kernel(window, heads, place_ref, bounds, *refs):
    own, sides_of = refs[:window], refs[window : window + 2]
    outs, (x_ref, y_ref, coef_ref, grad_ref) = refs[window + 2 : 2 * window + 2], refs[-4:]
    halo = window - 1
    extent = window + 2 * halo
    lanes = grad_ref.shape[2]
    places = lanes // 2
    rows = heads * HDIM
    is_left = lax.broadcasted_iota(jnp.int32, (1, lanes), 1) < places
    lowest, highest = bounds[0, halo], bounds[1, halo + window - 1]

    def widen(ref, frame):
        x_ref[frame] = ref[0].astype(jnp.float32)
        y_ref[frame] = ref[1].astype(jnp.float32)

    for step, ref in enumerate(own):
        widen(seq_block(ref, step, place_ref), halo + (place_ref[0] ^ step))
    for start, ref in enumerate(sides_of):
        is_next = place_ref[1] == start
        if GATHER_GRP:
            ref = ref.at[jnp.int32(is_next)]
        for at in range(halo):
            frame = at + jnp.where(is_next, halo + window, 0)
            needed = (frame >= lowest) & (frame < highest)
            pl.when(needed)(functools.partial(widen, ref.at[at], frame))

    def partners(frame):
        first, last = bounds[0, frame], bounds[1, frame]
        return first, last - first, [jnp.minimum(first + t, last - 1) for t in range(window)]

    def weigh(frame, carry):
        first, count, others = partners(frame)
        sums = [[] for _ in range(window)]
        for head in range(heads):
            span = slice(head * HDIM, (head + 1) * HDIM)
            mine = x_ref[frame, span, :]
            for t, other in enumerate(others):
                sums[t].append(jnp.sum(mine * y_ref[other, span, :], axis=0, keepdims=True))
        sums = [jnp.concatenate(parts, axis=0) for parts in sums]
        scores = [
            part * SCALING + jnp.where(t < count, 0.0, masked_score) for t, part in enumerate(sums)
        ]
        peak = functools.reduce(jnp.maximum, scores)
        raised = [jnp.exp(score - peak) for score in scores]
        inverse = 1.0 / functools.reduce(jnp.add, raised)
        weights = [part * inverse for part in raised]
        weights_low = [rounded(part) for part in weights]
        weight_grad = [swapped(part) for part in sums]
        dots = functools.reduce(jnp.add, [w * d for w, d in zip(weights_low, weight_grad)])
        for t in range(window):
            score_grad = rounded(weights[t] * (weight_grad[t] - dots))
            coef_ref[frame, t] = jnp.where(is_left, score_grad, swapped(weights_low[t]))
        return carry

    lax.fori_loop(lowest, highest, weigh, 0)

    def gradients(at, carry):
        frame = halo + at
        first, count, others = partners(frame)
        place = frame - first
        by_key, by_query = [], []
        for head in range(heads):
            span = slice(head * HDIM, (head + 1) * HDIM)
            key_sum, query_sum = None, None
            for t, other in enumerate(others):
                back = coef_ref[other, place, head : head + 1, :]
                back = jnp.where(t < count, back, 0.0)
                ahead = coef_ref[frame, t, head : head + 1, :]
                key_term = back * x_ref[other, span, :]
                query_term = ahead * y_ref[other, span, :]
                key_sum = key_term if t == 0 else key_sum + key_term
                query_sum = query_term if t == 0 else query_sum + query_term
            by_key.append(key_sum * jnp.where(is_left, SCALING, 1.0))
            by_query.append(query_sum * SCALING)
            if head % 2 == 1:
                span = slice((head - 1) * HDIM, (head + 1) * HDIM)
                value = jnp.concatenate(by_key[head - 1 :], axis=0)
                grad_ref[at, span, :] = value.astype(jnp.bfloat16)
        half = heads // 2
        folded = [
            jnp.where(is_left, by_query[head], swapped(by_query[head + half]))
            for head in range(half)
        ]
        value = jnp.concatenate(folded, axis=0)
        grad_ref[at, rows:, :] = value.astype(jnp.bfloat16)
        return carry

    lax.fori_loop(0, window, gradients, 0)
    for step, out in enumerate(outs):
        out[...] = grad_ref[place_ref[0] ^ step]


def clip_grads(place, bounds, own, beside):
    window = len(own)
    _, rows, lanes = own[0].shape
    beside = list(beside)
    heads = rows // HDIM
    extent = 3 * window - 2
    vmem = pl.BlockSpec(memory_space=pltpu.VMEM)
    smem = pl.BlockSpec(memory_space=pltpu.SMEM)
    work = extent * window * rows * lanes
    shape = (rows + rows // 2, lanes)
    return pl.pallas_call(
        functools.partial(clip_kernel, window, heads),
        out_shape=[jax.ShapeDtypeStruct(shape, jnp.bfloat16)] * window,
        in_specs=[smem, smem] + [vmem] * (window + 2),
        out_specs=[vmem] * window,
        scratch_shapes=[
            pltpu.VMEM((extent, rows, lanes), jnp.float32),
            pltpu.VMEM((extent, rows, lanes), jnp.float32),
            pltpu.VMEM((extent, window, heads, lanes), jnp.float32),
            pltpu.VMEM((window, *shape), jnp.bfloat16),
        ],
        compiler_params=pltpu.CompilerParams(vmem_limit_bytes=60 * 2**20),
        cost_estimate=pl.CostEstimate(
            flops=400 * work,
            bytes_accessed=2 * sum(block.size for block in (*own, *beside)),
            transcendentals=extent * window * heads * lanes,
        ),
        name="clips",
    )(place, bounds, *own, *beside)


def clip_bounds(clip_len, window):
    halo = window - 1
    extent = window + 2 * halo
    start = lax.axis_index("grp") * window - halo
    frames = start + jnp.arange(extent, dtype=jnp.int32)
    order = jnp.arange(clip_len.shape[0])
    ends = jnp.sum(jnp.where(order[:, None] <= order[None, :], clip_len[:, None], 0), axis=0)
    begins = ends - clip_len
    holds = (begins[None, :] <= frames[:, None]) & (frames[:, None] < ends[None, :])
    first = jnp.sum(jnp.where(holds, begins[None, :], 0), axis=1) - start
    last = jnp.sum(jnp.where(holds, ends[None, :], 0), axis=1) - start
    return jnp.stack([first, last]).astype(jnp.int32)


def shards(q_space, k_space, v_space, cot_space, q_time, k_time, v_time, cot_time, clip_len):
    def turned(*arrays):
        return tuple(array.transpose(0, 2, 1) for array in arrays)

    n = lax.axis_size("seq")
    window = q_time.shape[0] * n
    tokens = q_time.shape[1]
    bounds = clip_bounds(clip_len, window)
    place = jnp.stack([lax.axis_index("seq"), lax.axis_index("grp") % 2]).astype(jnp.int32)
    time = turned(q_time, cot_time, k_time, v_time)
    spans = []
    head = 0
    for heads in CHUNKS:
        spans.append(slice(head * HDIM, (head + heads) * HDIM))
        head += heads
    space = frame_grads(*turned(q_space, k_space, v_space, cot_space))
    back = []
    own = None
    for span in spans:
        packed = list(split(place, time, span, n))
        if own is not None:
            packed[2:], own[2] = lax.optimization_barrier((packed[2:], own[2]))
        own = exchange(packed)
        beside = neighbours(sides(place, own))
        back.append(exchange(clip_grads(place, bounds, own, beside)))
    grads = None
    for span, blocks in zip(spans, back):
        grads = join(place, blocks, span, tokens, grads)
    return turned(*space, *grads)


def solution(mesh):
    split_spec = P(("grp", "seq"), None, None)
    return jax.shard_map(
        shards,
        mesh=mesh,
        in_specs=(split_spec,) * 8 + (P(),),
        out_specs=(split_spec,) * 6,
        check_vma=False,
    )
```

```python
import functools
import math

import jax
import jax.numpy as jnp
from jax import lax
from jax.experimental import pallas as pl
from jax.experimental.pallas import tpu as pltpu
from jax.sharding import PartitionSpec as P

HEADS = 8
HDIM = 72
WIDTH = HEADS * HDIM
SCALING = 1.0 / math.sqrt(HDIM)
CHUNKS = (4, 4)
masked_score = -1e30


def dot(left, right, left_dim, right_dim):
    dims = (((left_dim,), (right_dim,)), ((), ()))
    return lax.dot_general(left, right, dims, preferred_element_type=jnp.float32)


def rounded(value):
    return value.astype(jnp.bfloat16).astype(jnp.float32)


def swapped(value):
    half = value.shape[1] // 2
    if 2 * half == 128:
        return pltpu.roll(value, half, 1)
    return jnp.concatenate([value[:, half:], value[:, :half]], axis=1)


def frame_kernel(q_ref, k_ref, v_ref, g_ref, dq_ref, dk_ref, dv_ref):
    pair = 2 * HDIM
    reach = -(-HDIM // 16) * 16
    row = lax.broadcasted_iota(jnp.int32, (reach, 1), 0)
    for begin in range(0, WIDTH, pair):
        found = [[], [], []]
        for low, own in ((0, 0), (pair - reach, reach - HDIM)):
            span = slice(begin + low, begin + low + reach)
            mask = ((row >= own) & (row < own + HDIM)).astype(jnp.float32).astype(jnp.bfloat16)
            queries, keys = q_ref[0, span, :], k_ref[0, span, :]
            cotangent = g_ref[0, span, :]
            scores = dot(keys * mask, queries, 0, 0) * SCALING
            weight_grad = dot(v_ref[0, span, :] * mask, cotangent, 0, 0)
            raised = jnp.exp(scores - jnp.max(scores, axis=0, keepdims=True))
            weights = raised * (1.0 / jnp.sum(raised, axis=0, keepdims=True))
            weights_low = weights.astype(jnp.bfloat16)
            dots = jnp.sum(weights_low.astype(jnp.float32) * weight_grad, axis=0, keepdims=True)
            score_grad = (weights * (weight_grad - dots)).astype(jnp.bfloat16)
            rows = slice(own, own + HDIM)
            found[0].append(dot(keys, score_grad, 1, 0)[rows] * SCALING)
            found[1].append(dot(queries, score_grad, 1, 1)[rows] * SCALING)
            found[2].append(dot(cotangent, weights_low, 1, 1)[rows])
        for out, parts in zip((dq_ref, dk_ref, dv_ref), found):
            out[0, begin : begin + pair, :] = jnp.concatenate(parts, axis=0).astype(jnp.bfloat16)


def frame_grads(queries, keys, values, cotangent):
    tokens = queries.shape[2]
    shape = jax.ShapeDtypeStruct(queries.shape, jnp.bfloat16)
    return pl.pallas_call(
        frame_kernel,
        out_shape=(shape, shape, shape),
        compiler_params=pltpu.CompilerParams(vmem_limit_bytes=60 * 2**20),
        cost_estimate=pl.CostEstimate(
            flops=12 * tokens * tokens * 256 * HEADS,
            bytes_accessed=14 * tokens * WIDTH,
            transcendentals=tokens * tokens * HEADS,
        ),
        name="space",
    )(queries, keys, values, cotangent)


def split_kernel(n, span, place_ref, *refs):
    ins, outs, (loaded, held, arrived, left_off) = refs[:4], refs[4 : 4 + n], refs[-4:]
    loads = [
        pltpu.make_async_copy(array.at[0, span, :], loaded.at[i], arrived.at[i])
        for i, array in enumerate(ins)
    ]
    for copy in loads:
        copy.start()
    places = ins[0].shape[2] // n
    for at in range(2):
        loads[2 * at].wait()
        loads[2 * at + 1].wait()
        for target in range(n):
            lanes = slice(target * places, (target + 1) * places)
            both = [loaded[2 * at, :, lanes], loaded[2 * at + 1, :, lanes]]
            held[target, at] = jnp.concatenate(both, axis=1)
    stores = [
        pltpu.make_async_copy(held.at[place_ref[0] ^ step], out, left_off.at[step])
        for step, out in enumerate(outs)
    ]
    for copy in stores:
        copy.start()
    for copy in stores:
        copy.wait()


def split(place, arrays, span, n):
    rows, tokens = span.stop - span.start, arrays[0].shape[2]
    shape = (2, rows, 2 * tokens // n)
    hbm = pl.BlockSpec(memory_space=pltpu.HBM)
    return pl.pallas_call(
        functools.partial(split_kernel, n, span),
        in_specs=[pl.BlockSpec(memory_space=pltpu.SMEM)] + [hbm] * 4,
        out_specs=[hbm] * n,
        out_shape=[jax.ShapeDtypeStruct(shape, jnp.bfloat16)] * n,
        scratch_shapes=[
            pltpu.VMEM((4, rows, tokens), jnp.bfloat16),
            pltpu.VMEM((n, *shape), jnp.bfloat16),
            pltpu.SemaphoreType.DMA((4,)),
            pltpu.SemaphoreType.DMA((n,)),
        ],
        compiler_params=pltpu.CompilerParams(vmem_limit_bytes=60 * 2**20),
        name="pack",
    )(place, *arrays)


def swap(block, axis, pairs):
    return lax.ppermute(block, axis, [(i, j) for i, j in pairs] + [(j, i) for i, j in pairs])


def exchange(blocks):
    n = len(blocks)
    moved = [blocks[0]]
    for step in range(1, n):
        pairs = [[i, i ^ step] for i in range(n) if i < i ^ step]
        moved.append(swap(blocks[step], "seq", pairs))
    return moved


def sides_kernel(n, place_ref, *refs):
    ins, outs = refs[:n], refs[n:]
    is_odd = place_ref[1]
    for step, ref in enumerate(ins):
        frame = place_ref[0] ^ step
        for start, out in enumerate(outs):
            at = frame - jnp.where(is_odd == start, 1, 0)

            @pl.when((at >= 0) & (at < n - 1))
            def _():
                out[jnp.clip(at, 0, n - 2)] = ref[...]


def sides(place, blocks):
    n = len(blocks)
    shape = jax.ShapeDtypeStruct((n - 1, *blocks[0].shape), jnp.bfloat16)
    vmem = pl.BlockSpec(memory_space=pltpu.VMEM)
    return pl.pallas_call(
        functools.partial(sides_kernel, n),
        in_specs=[pl.BlockSpec(memory_space=pltpu.SMEM)] + [vmem] * n,
        out_specs=[vmem] * 2,
        out_shape=[shape] * 2,
        compiler_params=pltpu.CompilerParams(vmem_limit_bytes=24 * 2**20),
        name="sides",
    )(place, *blocks)


def neighbours(blocks):
    count = lax.axis_size("grp")
    moved = []
    for start, block in enumerate(blocks):
        moved.append(swap(block, "grp", [(i, i + 1) for i in range(start, count - 1, 2)]))
    return moved


def join_kernel(n, span, place_ref, *refs):
    ins, outs, (held, ready, left_off) = refs[:n], refs[-6:-3], refs[-3:]
    for step, ref in enumerate(ins):
        held[place_ref[0] ^ step] = ref[...]
    count = span.stop - span.start
    half = count // 2
    places = held.shape[2] // 2

    def gather(rows, lanes):
        return jnp.concatenate([held[source, rows, lanes] for source in range(n)], axis=1)

    left, right = slice(0, places), slice(places, 2 * places)
    rest = slice(count, count + half)
    ready[1] = gather(slice(0, count), left)
    ready[2] = gather(slice(0, count), right)
    ready[0, :half, :] = gather(rest, left)
    ready[0, half:, :] = gather(rest, right)
    copies = [
        pltpu.make_async_copy(ready.at[i], out.at[0, span, :], left_off.at[i])
        for i, out in enumerate(outs)
    ]
    for copy in copies:
        copy.start()
    for copy in copies:
        copy.wait()


def join(place, blocks, span, tokens, earlier):
    n = len(blocks)
    rows = span.stop - span.start
    shape = jax.ShapeDtypeStruct((1, WIDTH, tokens), jnp.bfloat16)
    vmem = pl.BlockSpec(memory_space=pltpu.VMEM)
    hbm = pl.BlockSpec(memory_space=pltpu.HBM)
    earlier = [] if earlier is None else list(earlier)
    return pl.pallas_call(
        functools.partial(join_kernel, n, span),
        in_specs=[pl.BlockSpec(memory_space=pltpu.SMEM)] + [vmem] * n + [hbm] * len(earlier),
        out_specs=[hbm] * 3,
        out_shape=[shape] * 3,
        scratch_shapes=[
            pltpu.VMEM((n, *blocks[0].shape), jnp.bfloat16),
            pltpu.VMEM((3, rows, tokens), jnp.bfloat16),
            pltpu.SemaphoreType.DMA((3,)),
        ],
        input_output_aliases={1 + n + i: i for i in range(len(earlier))},
        compiler_params=pltpu.CompilerParams(vmem_limit_bytes=24 * 2**20),
        name="unpack",
    )(place, *blocks, *earlier)


def clip_kernel(window, heads, place_ref, bounds, *refs):
    own, sides_of = refs[:window], refs[window : window + 2]
    outs, (x_ref, y_ref, coef_ref, grad_ref) = refs[window + 2 : 2 * window + 2], refs[-4:]
    halo = window - 1
    extent = window + 2 * halo
    lanes = grad_ref.shape[2]
    places = lanes // 2
    rows = heads * HDIM
    is_left = lax.broadcasted_iota(jnp.int32, (1, lanes), 1) < places
    lowest, highest = bounds[0, halo], bounds[1, halo + window - 1]

    def widen(ref, frame):
        x_ref[frame] = ref[0].astype(jnp.float32)
        y_ref[frame] = ref[1].astype(jnp.float32)

    for step, ref in enumerate(own):
        widen(ref, halo + (place_ref[0] ^ step))
    for start, ref in enumerate(sides_of):
        is_next = place_ref[1] == start
        for at in range(halo):
            frame = at + jnp.where(is_next, halo + window, 0)
            needed = (frame >= lowest) & (frame < highest)
            pl.when(needed)(functools.partial(widen, ref.at[at], frame))

    def partners(frame):
        first, last = bounds[0, frame], bounds[1, frame]
        return first, last - first, [jnp.minimum(first + t, last - 1) for t in range(window)]

    def weigh(frame, carry):
        first, count, others = partners(frame)
        sums = [[] for _ in range(window)]
        for head in range(heads):
            span = slice(head * HDIM, (head + 1) * HDIM)
            mine = x_ref[frame, span, :]
            for t, other in enumerate(others):
                sums[t].append(jnp.sum(mine * y_ref[other, span, :], axis=0, keepdims=True))
        sums = [jnp.concatenate(parts, axis=0) for parts in sums]
        scores = [
            part * SCALING + jnp.where(t < count, 0.0, masked_score) for t, part in enumerate(sums)
        ]
        peak = functools.reduce(jnp.maximum, scores)
        raised = [jnp.exp(score - peak) for score in scores]
        inverse = 1.0 / functools.reduce(jnp.add, raised)
        weights = [part * inverse for part in raised]
        weights_low = [rounded(part) for part in weights]
        weight_grad = [swapped(part) for part in sums]
        dots = functools.reduce(jnp.add, [w * d for w, d in zip(weights_low, weight_grad)])
        for t in range(window):
            score_grad = rounded(weights[t] * (weight_grad[t] - dots))
            coef_ref[frame, t] = jnp.where(is_left, score_grad, swapped(weights_low[t]))
        return carry

    lax.fori_loop(lowest, highest, weigh, 0)

    def gradients(at, carry):
        frame = halo + at
        first, count, others = partners(frame)
        place = frame - first
        by_key, by_query = [], []
        for head in range(heads):
            span = slice(head * HDIM, (head + 1) * HDIM)
            key_sum, query_sum = None, None
            for t, other in enumerate(others):
                back = coef_ref[other, place, head : head + 1, :]
                back = jnp.where(t < count, back, 0.0)
                ahead = coef_ref[frame, t, head : head + 1, :]
                key_term = back * x_ref[other, span, :]
                query_term = ahead * y_ref[other, span, :]
                key_sum = key_term if t == 0 else key_sum + key_term
                query_sum = query_term if t == 0 else query_sum + query_term
            by_key.append(key_sum * jnp.where(is_left, SCALING, 1.0))
            by_query.append(query_sum * SCALING)
            if head % 2 == 1:
                span = slice((head - 1) * HDIM, (head + 1) * HDIM)
                value = jnp.concatenate(by_key[head - 1 :], axis=0)
                grad_ref[at, span, :] = value.astype(jnp.bfloat16)
        half = heads // 2
        folded = [
            jnp.where(is_left, by_query[head], swapped(by_query[head + half]))
            for head in range(half)
        ]
        value = jnp.concatenate(folded, axis=0)
        grad_ref[at, rows:, :] = value.astype(jnp.bfloat16)
        return carry

    lax.fori_loop(0, window, gradients, 0)
    for step, out in enumerate(outs):
        out[...] = grad_ref[place_ref[0] ^ step]


def clip_grads(place, bounds, own, beside):
    window = len(own)
    _, rows, lanes = own[0].shape
    beside = list(beside)
    heads = rows // HDIM
    extent = 3 * window - 2
    vmem = pl.BlockSpec(memory_space=pltpu.VMEM)
    smem = pl.BlockSpec(memory_space=pltpu.SMEM)
    work = extent * window * rows * lanes
    shape = (rows + rows // 2, lanes)
    return pl.pallas_call(
        functools.partial(clip_kernel, window, heads),
        out_shape=[jax.ShapeDtypeStruct(shape, jnp.bfloat16)] * window,
        in_specs=[smem, smem] + [vmem] * (window + 2),
        out_specs=[vmem] * window,
        scratch_shapes=[
            pltpu.VMEM((extent, rows, lanes), jnp.float32),
            pltpu.VMEM((extent, rows, lanes), jnp.float32),
            pltpu.VMEM((extent, window, heads, lanes), jnp.float32),
            pltpu.VMEM((window, *shape), jnp.bfloat16),
        ],
        compiler_params=pltpu.CompilerParams(vmem_limit_bytes=48 * 2**20),
        cost_estimate=pl.CostEstimate(
            flops=400 * work,
            bytes_accessed=2 * sum(block.size for block in (*own, *beside)),
            transcendentals=extent * window * heads * lanes,
        ),
        name="clips",
    )(place, bounds, *own, *beside)


def clip_bounds(clip_len, window):
    halo = window - 1
    extent = window + 2 * halo
    start = lax.axis_index("grp") * window - halo
    frames = start + jnp.arange(extent, dtype=jnp.int32)
    order = jnp.arange(clip_len.shape[0])
    ends = jnp.sum(jnp.where(order[:, None] <= order[None, :], clip_len[:, None], 0), axis=0)
    begins = ends - clip_len
    holds = (begins[None, :] <= frames[:, None]) & (frames[:, None] < ends[None, :])
    first = jnp.sum(jnp.where(holds, begins[None, :], 0), axis=1) - start
    last = jnp.sum(jnp.where(holds, ends[None, :], 0), axis=1) - start
    return jnp.stack([first, last]).astype(jnp.int32)


def shards(q_space, k_space, v_space, cot_space, q_time, k_time, v_time, cot_time, clip_len):
    def turned(*arrays):
        return tuple(array.transpose(0, 2, 1) for array in arrays)

    n = lax.axis_size("seq")
    window = q_time.shape[0] * n
    tokens = q_time.shape[1]
    bounds = clip_bounds(clip_len, window)
    place = jnp.stack([lax.axis_index("seq"), lax.axis_index("grp") % 2]).astype(jnp.int32)
    time = turned(q_time, cot_time, k_time, v_time)
    spans = []
    head = 0
    for heads in CHUNKS:
        spans.append(slice(head * HDIM, (head + heads) * HDIM))
        head += heads
    space = frame_grads(*turned(q_space, k_space, v_space, cot_space))
    back = []
    for span in spans:
        own = exchange(split(place, time, span, n))
        beside = neighbours(sides(place, own))
        back.append(exchange(clip_grads(place, bounds, own, beside)))
    grads = None
    for span, blocks in zip(spans, back):
        grads = join(place, blocks, span, tokens, grads)
    return turned(*space, *grads)


def solution(mesh):
    split_spec = P(("grp", "seq"), None, None)
    return jax.shard_map(
        shards,
        mesh=mesh,
        in_specs=(split_spec,) * 8 + (P(),),
        out_specs=(split_spec,) * 6,
        check_vma=False,
    )
```

```python
import functools
import math

import jax
import jax.numpy as jnp
from jax import lax
from jax.experimental import pallas as pl
from jax.experimental.pallas import tpu as pltpu
from jax.sharding import PartitionSpec as P

HEADS = 8
HDIM = 72
WIDTH = HEADS * HDIM
SCALING = 1.0 / math.sqrt(HDIM)
CHUNKS = (2, 4, 2)
masked_score = -1e30


def dot(left, right, left_dim, right_dim):
    dims = (((left_dim,), (right_dim,)), ((), ()))
    return lax.dot_general(left, right, dims, preferred_element_type=jnp.float32)


def rounded(value):
    return value.astype(jnp.bfloat16).astype(jnp.float32)


def swapped(value):
    half = value.shape[1] // 2
    if 2 * half == 128:
        return pltpu.roll(value, half, 1)
    return jnp.concatenate([value[:, half:], value[:, :half]], axis=1)


def frame_kernel(q_ref, k_ref, v_ref, g_ref, dq_ref, dk_ref, dv_ref):
    pair = 2 * HDIM
    reach = -(-HDIM // 16) * 16
    row = lax.broadcasted_iota(jnp.int32, (reach, 1), 0)
    for begin in range(0, WIDTH, pair):
        found = [[], [], []]
        for low, own in ((0, 0), (pair - reach, reach - HDIM)):
            span = slice(begin + low, begin + low + reach)
            mask = ((row >= own) & (row < own + HDIM)).astype(jnp.float32).astype(jnp.bfloat16)
            queries, keys = q_ref[0, span, :], k_ref[0, span, :]
            cotangent = g_ref[0, span, :]
            scores = dot(keys * mask, queries, 0, 0) * SCALING
            weight_grad = dot(v_ref[0, span, :] * mask, cotangent, 0, 0)
            raised = jnp.exp(scores - jnp.max(scores, axis=0, keepdims=True))
            weights = raised * (1.0 / jnp.sum(raised, axis=0, keepdims=True))
            weights_low = weights.astype(jnp.bfloat16)
            dots = jnp.sum(weights_low.astype(jnp.float32) * weight_grad, axis=0, keepdims=True)
            score_grad = (weights * (weight_grad - dots)).astype(jnp.bfloat16)
            rows = slice(own, own + HDIM)
            found[0].append(dot(keys, score_grad, 1, 0)[rows] * SCALING)
            found[1].append(dot(queries, score_grad, 1, 1)[rows] * SCALING)
            found[2].append(dot(cotangent, weights_low, 1, 1)[rows])
        for out, parts in zip((dq_ref, dk_ref, dv_ref), found):
            out[0, begin : begin + pair, :] = jnp.concatenate(parts, axis=0).astype(jnp.bfloat16)


def frame_grads(queries, keys, values, cotangent):
    tokens = queries.shape[2]
    shape = jax.ShapeDtypeStruct(queries.shape, jnp.bfloat16)
    return pl.pallas_call(
        frame_kernel,
        out_shape=(shape, shape, shape),
        compiler_params=pltpu.CompilerParams(vmem_limit_bytes=60 * 2**20),
        cost_estimate=pl.CostEstimate(
            flops=12 * tokens * tokens * 256 * HEADS,
            bytes_accessed=14 * tokens * WIDTH,
            transcendentals=tokens * tokens * HEADS,
        ),
        name="space",
    )(queries, keys, values, cotangent)


def split_kernel(n, span, *refs):
    ins, outs, (loaded, held, arrived, left_off) = refs[:4], refs[4 : 4 + n], refs[-4:]
    loads = [
        pltpu.make_async_copy(array.at[0, span, :], loaded.at[i], arrived.at[i])
        for i, array in enumerate(ins)
    ]
    for copy in loads:
        copy.start()
    places = ins[0].shape[2] // n
    for at in range(2):
        loads[2 * at].wait()
        loads[2 * at + 1].wait()
        for target in range(n):
            lanes = slice(target * places, (target + 1) * places)
            both = [loaded[2 * at, :, lanes], loaded[2 * at + 1, :, lanes]]
            held[target, at] = jnp.concatenate(both, axis=1)
    stores = [
        pltpu.make_async_copy(held.at[(lax.axis_index("seq") ^ step)], out, left_off.at[step])
        for step, out in enumerate(outs)
    ]
    for copy in stores:
        copy.start()
    for copy in stores:
        copy.wait()


def split(arrays, span, n):
    rows, tokens = span.stop - span.start, arrays[0].shape[2]
    shape = (2, rows, 2 * tokens // n)
    hbm = pl.BlockSpec(memory_space=pltpu.HBM)
    return pl.pallas_call(
        functools.partial(split_kernel, n, span),
        in_specs=[hbm] * 4,
        out_specs=[hbm] * n,
        out_shape=[jax.ShapeDtypeStruct(shape, jnp.bfloat16)] * n,
        scratch_shapes=[
            pltpu.VMEM((4, rows, tokens), jnp.bfloat16),
            pltpu.VMEM((n, *shape), jnp.bfloat16),
            pltpu.SemaphoreType.DMA((4,)),
            pltpu.SemaphoreType.DMA((n,)),
        ],
        compiler_params=pltpu.CompilerParams(vmem_limit_bytes=60 * 2**20),
        name="pack",
    )(*arrays)


def swap(block, axis, pairs):
    return lax.ppermute(block, axis, [(i, j) for i, j in pairs] + [(j, i) for i, j in pairs])


def exchange(blocks):
    n = len(blocks)
    moved = [blocks[0]]
    for step in range(1, n):
        pairs = [[i, i ^ step] for i in range(n) if i < i ^ step]
        moved.append(swap(blocks[step], "seq", pairs))
    return moved


def sides_kernel(n, *refs):
    ins, outs = refs[:n], refs[n:]
    is_odd = lax.axis_index("grp") & 1
    for step, ref in enumerate(ins):
        frame = (lax.axis_index("seq") ^ step)
        for start, out in enumerate(outs):
            at = frame - jnp.where(is_odd == start, 1, 0)

            @pl.when((at >= 0) & (at < n - 1))
            def _():
                out[jnp.clip(at, 0, n - 2)] = ref[...]


def sides(blocks):
    n = len(blocks)
    shape = jax.ShapeDtypeStruct((n - 1, *blocks[0].shape), jnp.bfloat16)
    vmem = pl.BlockSpec(memory_space=pltpu.VMEM)
    return pl.pallas_call(
        functools.partial(sides_kernel, n),
        in_specs=[vmem] * n,
        out_specs=[vmem] * 2,
        out_shape=[shape] * 2,
        compiler_params=pltpu.CompilerParams(vmem_limit_bytes=24 * 2**20),
        name="sides",
    )(*blocks)


def neighbours(blocks):
    count = lax.axis_size("grp")
    moved = []
    for start, block in enumerate(blocks):
        moved.append(swap(block, "grp", [(i, i + 1) for i in range(start, count - 1, 2)]))
    return moved


def join_kernel(n, span, *refs):
    ins, outs, (held, ready, left_off) = refs[:n], refs[-6:-3], refs[-3:]
    for step, ref in enumerate(ins):
        held[(lax.axis_index("seq") ^ step)] = ref[...]
    count = span.stop - span.start
    half = count // 2
    places = held.shape[2] // 2

    def gather(rows, lanes):
        return jnp.concatenate([held[source, rows, lanes] for source in range(n)], axis=1)

    left, right = slice(0, places), slice(places, 2 * places)
    rest = slice(count, count + half)
    ready[1] = gather(slice(0, count), left)
    ready[2] = gather(slice(0, count), right)
    ready[0, :half, :] = gather(rest, left)
    ready[0, half:, :] = gather(rest, right)
    copies = [
        pltpu.make_async_copy(ready.at[i], out.at[0, span, :], left_off.at[i])
        for i, out in enumerate(outs)
    ]
    for copy in copies:
        copy.start()
    for copy in copies:
        copy.wait()


def join(blocks, span, tokens, earlier):
    n = len(blocks)
    rows = span.stop - span.start
    shape = jax.ShapeDtypeStruct((1, WIDTH, tokens), jnp.bfloat16)
    vmem = pl.BlockSpec(memory_space=pltpu.VMEM)
    hbm = pl.BlockSpec(memory_space=pltpu.HBM)
    earlier = [] if earlier is None else list(earlier)
    return pl.pallas_call(
        functools.partial(join_kernel, n, span),
        in_specs=[vmem] * n + [hbm] * len(earlier),
        out_specs=[hbm] * 3,
        out_shape=[shape] * 3,
        scratch_shapes=[
            pltpu.VMEM((n, *blocks[0].shape), jnp.bfloat16),
            pltpu.VMEM((3, rows, tokens), jnp.bfloat16),
            pltpu.SemaphoreType.DMA((3,)),
        ],
        input_output_aliases={n + i: i for i in range(len(earlier))},
        compiler_params=pltpu.CompilerParams(vmem_limit_bytes=24 * 2**20),
        name="unpack",
    )(*blocks, *earlier)


def clip_kernel(window, heads, bounds, *refs):
    own, sides_of = refs[:window], refs[window : window + 2]
    outs, (x_ref, y_ref, coef_ref, grad_ref) = refs[window + 2 : 2 * window + 2], refs[-4:]
    halo = window - 1
    extent = window + 2 * halo
    lanes = grad_ref.shape[2]
    places = lanes // 2
    rows = heads * HDIM
    is_left = lax.broadcasted_iota(jnp.int32, (1, lanes), 1) < places
    lowest, highest = bounds[0, halo], bounds[1, halo + window - 1]

    def widen(ref, frame):
        x_ref[frame] = ref[0].astype(jnp.float32)
        y_ref[frame] = ref[1].astype(jnp.float32)

    for step, ref in enumerate(own):
        widen(ref, halo + ((lax.axis_index("seq") ^ step)))
    for start, ref in enumerate(sides_of):
        is_next = (lax.axis_index("grp") & 1) == start
        for at in range(halo):
            frame = at + jnp.where(is_next, halo + window, 0)
            needed = (frame >= lowest) & (frame < highest)
            pl.when(needed)(functools.partial(widen, ref.at[at], frame))

    def partners(frame):
        first, last = bounds[0, frame], bounds[1, frame]
        return first, last - first, [jnp.minimum(first + t, last - 1) for t in range(window)]

    def weigh(frame, carry):
        first, count, others = partners(frame)
        sums = [[] for _ in range(window)]
        for head in range(heads):
            span = slice(head * HDIM, (head + 1) * HDIM)
            mine = x_ref[frame, span, :]
            for t, other in enumerate(others):
                sums[t].append(jnp.sum(mine * y_ref[other, span, :], axis=0, keepdims=True))
        sums = [jnp.concatenate(parts, axis=0) for parts in sums]
        scores = [
            part * SCALING + jnp.where(t < count, 0.0, masked_score) for t, part in enumerate(sums)
        ]
        peak = functools.reduce(jnp.maximum, scores)
        raised = [jnp.exp(score - peak) for score in scores]
        inverse = 1.0 / functools.reduce(jnp.add, raised)
        weights = [part * inverse for part in raised]
        weights_low = [rounded(part) for part in weights]
        weight_grad = [swapped(part) for part in sums]
        dots = functools.reduce(jnp.add, [w * d for w, d in zip(weights_low, weight_grad)])
        for t in range(window):
            score_grad = rounded(weights[t] * (weight_grad[t] - dots))
            coef_ref[frame, t] = jnp.where(is_left, score_grad, swapped(weights_low[t]))
        return carry

    lax.fori_loop(lowest, highest, weigh, 0)

    def gradients(at, carry):
        frame = halo + at
        first, count, others = partners(frame)
        place = frame - first
        by_key, by_query = [], []
        for head in range(heads):
            span = slice(head * HDIM, (head + 1) * HDIM)
            key_sum, query_sum = None, None
            for t, other in enumerate(others):
                back = coef_ref[other, place, head : head + 1, :]
                back = jnp.where(t < count, back, 0.0)
                ahead = coef_ref[frame, t, head : head + 1, :]
                key_term = back * x_ref[other, span, :]
                query_term = ahead * y_ref[other, span, :]
                key_sum = key_term if t == 0 else key_sum + key_term
                query_sum = query_term if t == 0 else query_sum + query_term
            by_key.append(key_sum * jnp.where(is_left, SCALING, 1.0))
            by_query.append(query_sum * SCALING)
            if head % 2 == 1:
                span = slice((head - 1) * HDIM, (head + 1) * HDIM)
                value = jnp.concatenate(by_key[head - 1 :], axis=0)
                grad_ref[at, span, :] = value.astype(jnp.bfloat16)
        half = heads // 2
        folded = [
            jnp.where(is_left, by_query[head], swapped(by_query[head + half]))
            for head in range(half)
        ]
        value = jnp.concatenate(folded, axis=0)
        grad_ref[at, rows:, :] = value.astype(jnp.bfloat16)
        return carry

    lax.fori_loop(0, window, gradients, 0)
    for step, out in enumerate(outs):
        out[...] = grad_ref[(lax.axis_index("seq") ^ step)]


def clip_grads(bounds, own, beside):
    window = len(own)
    _, rows, lanes = own[0].shape
    beside = list(beside)
    heads = rows // HDIM
    extent = 3 * window - 2
    vmem = pl.BlockSpec(memory_space=pltpu.VMEM)
    smem = pl.BlockSpec(memory_space=pltpu.SMEM)
    work = extent * window * rows * lanes
    shape = (rows + rows // 2, lanes)
    return pl.pallas_call(
        functools.partial(clip_kernel, window, heads),
        out_shape=[jax.ShapeDtypeStruct(shape, jnp.bfloat16)] * window,
        in_specs=[smem] + [vmem] * (window + 2),
        out_specs=[vmem] * window,
        scratch_shapes=[
            pltpu.VMEM((extent, rows, lanes), jnp.float32),
            pltpu.VMEM((extent, rows, lanes), jnp.float32),
            pltpu.VMEM((extent, window, heads, lanes), jnp.float32),
            pltpu.VMEM((window, *shape), jnp.bfloat16),
        ],
        compiler_params=pltpu.CompilerParams(vmem_limit_bytes=48 * 2**20),
        cost_estimate=pl.CostEstimate(
            flops=400 * work,
            bytes_accessed=2 * sum(block.size for block in (*own, *beside)),
            transcendentals=extent * window * heads * lanes,
        ),
        name="clips",
    )(bounds, *own, *beside)


def clip_bounds(clip_len, window):
    halo = window - 1
    extent = window + 2 * halo
    start = lax.axis_index("grp") * window - halo
    frames = start + jnp.arange(extent, dtype=jnp.int32)
    order = jnp.arange(clip_len.shape[0])
    ends = jnp.sum(jnp.where(order[:, None] <= order[None, :], clip_len[:, None], 0), axis=0)
    begins = ends - clip_len
    holds = (begins[None, :] <= frames[:, None]) & (frames[:, None] < ends[None, :])
    first = jnp.sum(jnp.where(holds, begins[None, :], 0), axis=1) - start
    last = jnp.sum(jnp.where(holds, ends[None, :], 0), axis=1) - start
    return jnp.stack([first, last]).astype(jnp.int32)


def shards(q_space, k_space, v_space, cot_space, q_time, k_time, v_time, cot_time, clip_len):
    def turned(*arrays):
        return tuple(array.transpose(0, 2, 1) for array in arrays)

    n = lax.axis_size("seq")
    window = q_time.shape[0] * n
    tokens = q_time.shape[1]
    bounds = clip_bounds(clip_len, window)
    time = turned(q_time, cot_time, k_time, v_time)
    spans = []
    head = 0
    for heads in CHUNKS:
        spans.append(slice(head * HDIM, (head + heads) * HDIM))
        head += heads
    space_in = turned(q_space, k_space, v_space, cot_space)
    packed = [split(time, span, n) for span in spans]

    def gated(values, *earlier):
        return lax.optimization_barrier((values, *earlier))

    back, grads, own, beside = [], None, [], []
    own.append(exchange(packed[0]))
    own.append(exchange(packed[1]))
    ends = sides(own[0])
    space_in, ends = gated(space_in, ends)
    beside.append(neighbours(ends))
    space = frame_grads(*space_in)
    packed[2], space, beside[0], own[1][1] = gated(packed[2], space, beside[0], own[1][1])
    own.append(exchange(packed[2]))
    own[1], own[2][1] = gated(own[1], own[2][1])
    ends, beside[0] = gated(sides(own[1]), beside[0])
    beside.append(neighbours(ends))
    back.append(exchange(clip_grads(bounds, own[0], beside[0])))
    ends, beside[1], back[0][1] = gated(sides(own[2]), beside[1], back[0][1])
    beside.append(neighbours(ends))
    back.append(exchange(clip_grads(bounds, own[1], beside[1])))
    grads = join(back[0], spans[0], tokens, grads)
    beside[2], grads = gated(beside[2], grads)
    back.append(exchange(clip_grads(bounds, own[2], beside[2])))
    grads = join(back[1], spans[1], tokens, grads)
    grads = join(back[2], spans[2], tokens, grads)
    return turned(*space, *grads)


def solution(mesh):
    split_spec = P(("grp", "seq"), None, None)
    return jax.shard_map(
        shards,
        mesh=mesh,
        in_specs=(split_spec,) * 8 + (P(),),
        out_specs=(split_spec,) * 6,
        check_vma=False,
    )
```

```python
import functools
import math

import jax
import jax.numpy as jnp
from jax import lax
from jax.experimental import pallas as pl
from jax.experimental.pallas import tpu as pltpu
from jax.sharding import PartitionSpec as P

HEADS = 8
HDIM = 72
WIDTH = HEADS * HDIM
SCALING = 1.0 / math.sqrt(HDIM)
CHUNKS = (4, 4)
masked_score = -1e30


def dot(left, right, left_dim, right_dim):
    dims = (((left_dim,), (right_dim,)), ((), ()))
    return lax.dot_general(left, right, dims, preferred_element_type=jnp.float32)


def rounded(value):
    return value.astype(jnp.bfloat16).astype(jnp.float32)


def swapped(value):
    half = value.shape[1] // 2
    if 2 * half == 128:
        return pltpu.roll(value, half, 1)
    return jnp.concatenate([value[:, half:], value[:, :half]], axis=1)


def frame_kernel(q_ref, k_ref, v_ref, g_ref, dq_ref, dk_ref, dv_ref):
    pair = 2 * HDIM
    reach = -(-HDIM // 16) * 16
    row = lax.broadcasted_iota(jnp.int32, (reach, 1), 0)
    for begin in range(0, WIDTH, pair):
        found = [[], [], []]
        for low, own in ((0, 0), (pair - reach, reach - HDIM)):
            span = slice(begin + low, begin + low + reach)
            mask = ((row >= own) & (row < own + HDIM)).astype(jnp.float32).astype(jnp.bfloat16)
            queries, keys = q_ref[0, span, :], k_ref[0, span, :]
            cotangent = g_ref[0, span, :]
            scores = dot(keys * mask, queries, 0, 0) * SCALING
            weight_grad = dot(v_ref[0, span, :] * mask, cotangent, 0, 0)
            raised = jnp.exp(scores - jnp.max(scores, axis=0, keepdims=True))
            weights = raised * (1.0 / jnp.sum(raised, axis=0, keepdims=True))
            weights_low = weights.astype(jnp.bfloat16)
            dots = jnp.sum(weights_low.astype(jnp.float32) * weight_grad, axis=0, keepdims=True)
            score_grad = (weights * (weight_grad - dots)).astype(jnp.bfloat16)
            rows = slice(own, own + HDIM)
            found[0].append(dot(keys, score_grad, 1, 0)[rows] * SCALING)
            found[1].append(dot(queries, score_grad, 1, 1)[rows] * SCALING)
            found[2].append(dot(cotangent, weights_low, 1, 1)[rows])
        for out, parts in zip((dq_ref, dk_ref, dv_ref), found):
            out[0, begin : begin + pair, :] = jnp.concatenate(parts, axis=0).astype(jnp.bfloat16)


def frame_grads(queries, keys, values, cotangent):
    tokens = queries.shape[2]
    shape = jax.ShapeDtypeStruct(queries.shape, jnp.bfloat16)
    return pl.pallas_call(
        frame_kernel,
        out_shape=(shape, shape, shape),
        compiler_params=pltpu.CompilerParams(vmem_limit_bytes=60 * 2**20),
        cost_estimate=pl.CostEstimate(
            flops=12 * tokens * tokens * 256 * HEADS,
            bytes_accessed=14 * tokens * WIDTH,
            transcendentals=tokens * tokens * HEADS,
        ),
        name="space",
    )(queries, keys, values, cotangent)


def split_kernel(n, span, *refs):
    ins, outs, (loaded, held, arrived, left_off) = refs[:4], refs[4 : 4 + n], refs[-4:]
    loads = [
        pltpu.make_async_copy(array.at[0, span, :], loaded.at[i], arrived.at[i])
        for i, array in enumerate(ins)
    ]
    for copy in loads:
        copy.start()
    places = ins[0].shape[2] // n
    stores = []
    for at in range(2):
        loads[2 * at].wait()
        loads[2 * at + 1].wait()
        for target in range(n):
            lanes = slice(target * places, (target + 1) * places)
            both = [loaded[2 * at, :, lanes], loaded[2 * at + 1, :, lanes]]
            held[at, target] = jnp.concatenate(both, axis=1)
        for step, out in enumerate(outs):
            block = held.at[at, lax.axis_index("seq") ^ step]
            stores.append(pltpu.make_async_copy(block, out.at[at], left_off.at[at, step]))
            stores[-1].start()
    for copy in stores:
        copy.wait()


def split(arrays, span, n):
    rows, tokens = span.stop - span.start, arrays[0].shape[2]
    shape = (2, rows, 2 * tokens // n)
    hbm = pl.BlockSpec(memory_space=pltpu.HBM)
    return pl.pallas_call(
        functools.partial(split_kernel, n, span),
        in_specs=[hbm] * 4,
        out_specs=[hbm] * n,
        out_shape=[jax.ShapeDtypeStruct(shape, jnp.bfloat16)] * n,
        scratch_shapes=[
            pltpu.VMEM((4, rows, tokens), jnp.bfloat16),
            pltpu.VMEM((2, n, *shape[1:]), jnp.bfloat16),
            pltpu.SemaphoreType.DMA((4,)),
            pltpu.SemaphoreType.DMA((2, n)),
        ],
        compiler_params=pltpu.CompilerParams(vmem_limit_bytes=60 * 2**20),
        name="pack",
    )(*arrays)


def swap(block, axis, pairs):
    return lax.ppermute(block, axis, [(i, j) for i, j in pairs] + [(j, i) for i, j in pairs])


def exchange(blocks):
    n = len(blocks)
    moved = list(blocks)
    for step in reversed(range(1, n)):
        pairs = [[i, i ^ step] for i in range(n) if i < i ^ step]
        moved[step] = swap(blocks[step], "seq", pairs)
    return moved


def sides_kernel(n, *refs):
    ins, outs = refs[:n], refs[n:]
    is_odd = lax.axis_index("grp") & 1
    for step, ref in enumerate(ins):
        frame = (lax.axis_index("seq") ^ step)
        for start, out in enumerate(outs):
            at = frame - jnp.where(is_odd == start, 1, 0)

            @pl.when((at >= 0) & (at < n - 1))
            def _():
                out[jnp.clip(at, 0, n - 2)] = ref[...]


def sides(blocks):
    n = len(blocks)
    shape = jax.ShapeDtypeStruct((n - 1, *blocks[0].shape), jnp.bfloat16)
    vmem = pl.BlockSpec(memory_space=pltpu.VMEM)
    return pl.pallas_call(
        functools.partial(sides_kernel, n),
        in_specs=[vmem] * n,
        out_specs=[vmem] * 2,
        out_shape=[shape] * 2,
        compiler_params=pltpu.CompilerParams(vmem_limit_bytes=24 * 2**20),
        name="sides",
    )(*blocks)


def neighbours(blocks):
    count = lax.axis_size("grp")
    moved = list(blocks)
    for start in (1, 0):
        moved[start] = swap(blocks[start], "grp", [(i, i + 1) for i in range(start, count - 1, 2)])
    return moved


def join_kernel(n, span, *refs):
    ins, outs, (held, ready, left_off) = refs[:n], refs[-6:-3], refs[-3:]
    for step, ref in enumerate(ins):
        held[(lax.axis_index("seq") ^ step)] = ref[...]
    count = span.stop - span.start
    half = count // 2
    places = held.shape[2] // 2

    def gather(rows, lanes):
        return jnp.concatenate([held[source, rows, lanes] for source in range(n)], axis=1)

    left, right = slice(0, places), slice(places, 2 * places)
    rest = slice(count, count + half)
    ready[1] = gather(slice(0, count), left)
    ready[2] = gather(slice(0, count), right)
    ready[0, :half, :] = gather(rest, left)
    ready[0, half:, :] = gather(rest, right)
    copies = [
        pltpu.make_async_copy(ready.at[i], out.at[0, span, :], left_off.at[i])
        for i, out in enumerate(outs)
    ]
    for copy in copies:
        copy.start()
    for copy in copies:
        copy.wait()


def join(blocks, span, tokens, earlier):
    n = len(blocks)
    rows = span.stop - span.start
    shape = jax.ShapeDtypeStruct((1, WIDTH, tokens), jnp.bfloat16)
    vmem = pl.BlockSpec(memory_space=pltpu.VMEM)
    hbm = pl.BlockSpec(memory_space=pltpu.HBM)
    earlier = [] if earlier is None else list(earlier)
    return pl.pallas_call(
        functools.partial(join_kernel, n, span),
        in_specs=[vmem] * n + [hbm] * len(earlier),
        out_specs=[hbm] * 3,
        out_shape=[shape] * 3,
        scratch_shapes=[
            pltpu.VMEM((n, *blocks[0].shape), jnp.bfloat16),
            pltpu.VMEM((3, rows, tokens), jnp.bfloat16),
            pltpu.SemaphoreType.DMA((3,)),
        ],
        input_output_aliases={n + i: i for i in range(len(earlier))},
        compiler_params=pltpu.CompilerParams(vmem_limit_bytes=24 * 2**20),
        name="unpack",
    )(*blocks, *earlier)


def clip_kernel(window, heads, given_bounds, *refs):
    own, sides_of = refs[:window], refs[window : window + 2]
    outs, (x_ref, y_ref, coef_ref, grad_ref) = refs[window + 2 : 2 * window + 2], refs[-6:-2]
    bounds, arrived = refs[-2:]
    copy = pltpu.make_async_copy(given_bounds, bounds, arrived)
    copy.start()
    halo = window - 1
    extent = window + 2 * halo
    lanes = grad_ref.shape[2]
    places = lanes // 2
    rows = heads * HDIM
    is_left = lax.broadcasted_iota(jnp.int32, (1, lanes), 1) < places

    def widen(ref, frame):
        x_ref[frame] = ref[0].astype(jnp.float32)
        y_ref[frame] = ref[1].astype(jnp.float32)

    for step, ref in enumerate(own):
        widen(ref, halo + (lax.axis_index("seq") ^ step))
    copy.wait()
    lowest, highest = bounds[0, halo], bounds[1, halo + window - 1]
    for start, ref in enumerate(sides_of):
        is_next = (lax.axis_index("grp") & 1) == start
        for at in range(halo):
            frame = at + jnp.where(is_next, halo + window, 0)
            needed = (frame >= lowest) & (frame < highest)
            pl.when(needed)(functools.partial(widen, ref.at[at], frame))

    def partners(frame):
        first, last = bounds[0, frame], bounds[1, frame]
        return first, last - first, [jnp.minimum(first + t, last - 1) for t in range(window)]

    def weigh(frame, carry):
        first, count, others = partners(frame)
        sums = [[] for _ in range(window)]
        for head in range(heads):
            span = slice(head * HDIM, (head + 1) * HDIM)
            mine = x_ref[frame, span, :]
            for t, other in enumerate(others):
                sums[t].append(jnp.sum(mine * y_ref[other, span, :], axis=0, keepdims=True))
        sums = [jnp.concatenate(parts, axis=0) for parts in sums]
        scores = [
            part * SCALING + jnp.where(t < count, 0.0, masked_score) for t, part in enumerate(sums)
        ]
        peak = functools.reduce(jnp.maximum, scores)
        raised = [jnp.exp(score - peak) for score in scores]
        inverse = 1.0 / functools.reduce(jnp.add, raised)
        weights = [part * inverse for part in raised]
        weights_low = [rounded(part) for part in weights]
        weight_grad = [swapped(part) for part in sums]
        dots = functools.reduce(jnp.add, [w * d for w, d in zip(weights_low, weight_grad)])
        for t in range(window):
            score_grad = rounded(weights[t] * (weight_grad[t] - dots))
            coef_ref[frame, t] = jnp.where(is_left, score_grad, swapped(weights_low[t]))
        return carry

    lax.fori_loop(lowest, highest, weigh, 0)

    def gradients(at, carry):
        frame = halo + at
        first, count, others = partners(frame)
        place = frame - first
        by_key, by_query = [], []
        for head in range(heads):
            span = slice(head * HDIM, (head + 1) * HDIM)
            key_sum, query_sum = None, None
            for t, other in enumerate(others):
                back = coef_ref[other, place, head : head + 1, :]
                back = jnp.where(t < count, back, 0.0)
                ahead = coef_ref[frame, t, head : head + 1, :]
                key_term = back * x_ref[other, span, :]
                query_term = ahead * y_ref[other, span, :]
                key_sum = key_term if t == 0 else key_sum + key_term
                query_sum = query_term if t == 0 else query_sum + query_term
            by_key.append(key_sum * jnp.where(is_left, SCALING, 1.0))
            by_query.append(query_sum * SCALING)
            if head % 2 == 1:
                span = slice((head - 1) * HDIM, (head + 1) * HDIM)
                value = jnp.concatenate(by_key[head - 1 :], axis=0)
                grad_ref[at, span, :] = value.astype(jnp.bfloat16)
        half = heads // 2
        folded = [
            jnp.where(is_left, by_query[head], swapped(by_query[head + half]))
            for head in range(half)
        ]
        value = jnp.concatenate(folded, axis=0)
        grad_ref[at, rows:, :] = value.astype(jnp.bfloat16)
        return carry

    lax.fori_loop(0, window, gradients, 0)
    for step, out in enumerate(outs):
        out[...] = grad_ref[(lax.axis_index("seq") ^ step)]


def clip_grads(bounds, own, beside):
    window = len(own)
    _, rows, lanes = own[0].shape
    beside = list(beside)
    heads = rows // HDIM
    extent = 3 * window - 2
    vmem = pl.BlockSpec(memory_space=pltpu.VMEM)
    work = extent * window * rows * lanes
    shape = (rows + rows // 2, lanes)
    return pl.pallas_call(
        functools.partial(clip_kernel, window, heads),
        out_shape=[jax.ShapeDtypeStruct(shape, jnp.bfloat16)] * window,
        in_specs=[pl.BlockSpec(memory_space=pl.ANY)] + [vmem] * (window + 2),
        out_specs=[vmem] * window,
        scratch_shapes=[
            pltpu.VMEM((extent, rows, lanes), jnp.float32),
            pltpu.VMEM((extent, rows, lanes), jnp.float32),
            pltpu.VMEM((extent, window, heads, lanes), jnp.float32),
            pltpu.VMEM((window, *shape), jnp.bfloat16),
            pltpu.SMEM(bounds.shape, jnp.int32),
            pltpu.SemaphoreType.DMA,
        ],
        compiler_params=pltpu.CompilerParams(vmem_limit_bytes=48 * 2**20),
        cost_estimate=pl.CostEstimate(
            flops=400 * work,
            bytes_accessed=2 * sum(block.size for block in (*own, *beside)),
            transcendentals=extent * window * heads * lanes,
        ),
        name="clips",
    )(bounds, *own, *beside)


def clip_bounds(clip_len, window):
    halo = window - 1
    extent = window + 2 * halo
    start = lax.axis_index("grp") * window - halo
    frames = start + jnp.arange(extent, dtype=jnp.int32)
    order = jnp.arange(clip_len.shape[0])
    ends = jnp.sum(jnp.where(order[:, None] <= order[None, :], clip_len[:, None], 0), axis=0)
    begins = ends - clip_len
    holds = (begins[None, :] <= frames[:, None]) & (frames[:, None] < ends[None, :])
    first = jnp.sum(jnp.where(holds, begins[None, :], 0), axis=1) - start
    last = jnp.sum(jnp.where(holds, ends[None, :], 0), axis=1) - start
    return jnp.stack([first, last]).astype(jnp.int32)


def shards(q_space, k_space, v_space, cot_space, q_time, k_time, v_time, cot_time, clip_len):
    def turned(*arrays):
        return tuple(array.transpose(0, 2, 1) for array in arrays)

    n = lax.axis_size("seq")
    window = q_time.shape[0] * n
    tokens = q_time.shape[1]
    bounds = clip_bounds(clip_len, window)
    time = turned(q_time, cot_time, k_time, v_time)
    spans = []
    head = 0
    for heads in CHUNKS:
        spans.append(slice(head * HDIM, (head + heads) * HDIM))
        head += heads
    space_in = turned(q_space, k_space, v_space, cot_space)
    packed = [split(time, span, n) for span in spans]

    def gated(values, *earlier):
        return lax.optimization_barrier((values, *earlier))

    own = [exchange(blocks) for blocks in packed]
    ends = sides(own[0])
    space_in, ends = gated(space_in, ends)
    beside = [neighbours(ends)]
    space = frame_grads(*space_in)
    own[1], space = gated(own[1], space)
    beside.append(neighbours(sides(own[1])))
    back, grads = [], None
    for blocks, near in zip(own, beside):
        back.append(exchange(clip_grads(bounds, blocks, near)))
    for span, blocks in zip(spans, back):
        grads = join(blocks, span, tokens, grads)
    return turned(*space, *grads)


def solution(mesh):
    split_spec = P(("grp", "seq"), None, None)
    return jax.shard_map(
        shards,
        mesh=mesh,
        in_specs=(split_spec,) * 8 + (P(),),
        out_specs=(split_spec,) * 6,
        check_vma=False,
    )
```

```python
import functools
import math

import jax
import jax.numpy as jnp
from jax import lax
from jax.experimental import pallas as pl
from jax.experimental.pallas import tpu as pltpu
from jax.sharding import PartitionSpec as P

HEADS = 8
HDIM = 72
WIDTH = HEADS * HDIM
SCALING = 1.0 / math.sqrt(HDIM)
CHUNKS = (4, 4)
masked_score = -1e30


def dot(left, right, left_dim, right_dim):
    dims = (((left_dim,), (right_dim,)), ((), ()))
    return lax.dot_general(left, right, dims, preferred_element_type=jnp.float32)


def rounded(value):
    return value.astype(jnp.bfloat16).astype(jnp.float32)


def swapped(value):
    half = value.shape[1] // 2
    if 2 * half == 128:
        return pltpu.roll(value, half, 1)
    return jnp.concatenate([value[:, half:], value[:, :half]], axis=1)


def frame_kernel(q_ref, k_ref, v_ref, g_ref, dq_ref, dk_ref, dv_ref):
    pair = 2 * HDIM
    reach = -(-HDIM // 16) * 16
    row = lax.broadcasted_iota(jnp.int32, (reach, 1), 0)
    for begin in range(0, WIDTH, pair):
        found = [[], [], []]
        for low, own in ((0, 0), (pair - reach, reach - HDIM)):
            span = slice(begin + low, begin + low + reach)
            mask = ((row >= own) & (row < own + HDIM)).astype(jnp.float32).astype(jnp.bfloat16)
            queries, keys = q_ref[0, span, :], k_ref[0, span, :]
            cotangent = g_ref[0, span, :]
            scores = dot(keys * mask, queries, 0, 0) * SCALING
            weight_grad = dot(v_ref[0, span, :] * mask, cotangent, 0, 0)
            raised = jnp.exp(scores - jnp.max(scores, axis=0, keepdims=True))
            weights = raised * (1.0 / jnp.sum(raised, axis=0, keepdims=True))
            weights_low = weights.astype(jnp.bfloat16)
            dots = jnp.sum(weights_low.astype(jnp.float32) * weight_grad, axis=0, keepdims=True)
            score_grad = (weights * (weight_grad - dots)).astype(jnp.bfloat16)
            rows = slice(own, own + HDIM)
            found[0].append(dot(keys, score_grad, 1, 0)[rows] * SCALING)
            found[1].append(dot(queries, score_grad, 1, 1)[rows] * SCALING)
            found[2].append(dot(cotangent, weights_low, 1, 1)[rows])
        for out, parts in zip((dq_ref, dk_ref, dv_ref), found):
            out[0, begin : begin + pair, :] = jnp.concatenate(parts, axis=0).astype(jnp.bfloat16)


def frame_grads(queries, keys, values, cotangent):
    tokens = queries.shape[2]
    shape = jax.ShapeDtypeStruct(queries.shape, jnp.bfloat16)
    return pl.pallas_call(
        frame_kernel,
        out_shape=(shape, shape, shape),
        compiler_params=pltpu.CompilerParams(vmem_limit_bytes=60 * 2**20),
        cost_estimate=pl.CostEstimate(
            flops=12 * tokens * tokens * 256 * HEADS,
            bytes_accessed=14 * tokens * WIDTH,
            transcendentals=tokens * tokens * HEADS,
        ),
        name="space",
    )(queries, keys, values, cotangent)


def split_kernel(n, span, *refs):
    ins, outs, (loaded, held, arrived, left_off) = refs[:4], refs[4 : 4 + n], refs[-4:]
    loads = [
        pltpu.make_async_copy(array.at[0, span, :], loaded.at[i], arrived.at[i])
        for i, array in enumerate(ins)
    ]
    for copy in loads:
        copy.start()
    places = ins[0].shape[2] // n
    stores = []
    for at in range(2):
        loads[2 * at].wait()
        loads[2 * at + 1].wait()
        for target in range(n):
            lanes = slice(target * places, (target + 1) * places)
            both = [loaded[2 * at, :, lanes], loaded[2 * at + 1, :, lanes]]
            held[at, target] = jnp.concatenate(both, axis=1)
        for step, out in enumerate(outs):
            block = held.at[at, lax.axis_index("seq") ^ step]
            stores.append(pltpu.make_async_copy(block, out.at[at], left_off.at[at, step]))
            stores[-1].start()
    for copy in stores:
        copy.wait()


def split(arrays, span, n):
    rows, tokens = span.stop - span.start, arrays[0].shape[2]
    shape = (2, rows, 2 * tokens // n)
    hbm = pl.BlockSpec(memory_space=pltpu.HBM)
    return pl.pallas_call(
        functools.partial(split_kernel, n, span),
        in_specs=[hbm] * 4,
        out_specs=[hbm] * n,
        out_shape=[jax.ShapeDtypeStruct(shape, jnp.bfloat16)] * n,
        scratch_shapes=[
            pltpu.VMEM((4, rows, tokens), jnp.bfloat16),
            pltpu.VMEM((2, n, *shape[1:]), jnp.bfloat16),
            pltpu.SemaphoreType.DMA((4,)),
            pltpu.SemaphoreType.DMA((2, n)),
        ],
        compiler_params=pltpu.CompilerParams(vmem_limit_bytes=60 * 2**20),
        name="pack",
    )(*arrays)


def swap(block, axis, pairs):
    return lax.ppermute(block, axis, [(i, j) for i, j in pairs] + [(j, i) for i, j in pairs])


def exchange(blocks):
    n = len(blocks)
    moved = list(blocks)
    for step in reversed(range(1, n)):
        pairs = [[i, i ^ step] for i in range(n) if i < i ^ step]
        moved[step] = swap(blocks[step], "seq", pairs)
    return moved


def sides_kernel(n, *refs):
    ins, outs = refs[:n], refs[n:]
    is_odd = lax.axis_index("grp") & 1
    for step, ref in enumerate(ins):
        frame = (lax.axis_index("seq") ^ step)
        for start, out in enumerate(outs):
            at = frame - jnp.where(is_odd == start, 1, 0)

            @pl.when((at >= 0) & (at < n - 1))
            def _():
                out[jnp.clip(at, 0, n - 2)] = ref[...]


def sides(blocks):
    n = len(blocks)
    shape = jax.ShapeDtypeStruct((n - 1, *blocks[0].shape), jnp.bfloat16)
    vmem = pl.BlockSpec(memory_space=pltpu.VMEM)
    return pl.pallas_call(
        functools.partial(sides_kernel, n),
        in_specs=[vmem] * n,
        out_specs=[vmem] * 2,
        out_shape=[shape] * 2,
        compiler_params=pltpu.CompilerParams(vmem_limit_bytes=24 * 2**20),
        name="sides",
    )(*blocks)


def neighbours(blocks):
    count = lax.axis_size("grp")
    moved = list(blocks)
    for start in (1, 0):
        moved[start] = swap(blocks[start], "grp", [(i, i + 1) for i in range(start, count - 1, 2)])
    return moved


def join_kernel(n, span, *refs):
    ins, outs, (held, ready, left_off) = refs[:n], refs[-6:-3], refs[-3:]
    for step, ref in enumerate(ins):
        held[(lax.axis_index("seq") ^ step)] = ref[...]
    count = span.stop - span.start
    half = count // 2
    places = held.shape[2] // 2

    def gather(rows, lanes):
        return jnp.concatenate([held[source, rows, lanes] for source in range(n)], axis=1)

    left, right = slice(0, places), slice(places, 2 * places)
    rest = slice(count, count + half)
    ready[1] = gather(slice(0, count), left)
    ready[2] = gather(slice(0, count), right)
    ready[0, :half, :] = gather(rest, left)
    ready[0, half:, :] = gather(rest, right)
    copies = [
        pltpu.make_async_copy(ready.at[i], out.at[0, span, :], left_off.at[i])
        for i, out in enumerate(outs)
    ]
    for copy in copies:
        copy.start()
    for copy in copies:
        copy.wait()


def join(blocks, span, tokens, earlier):
    n = len(blocks)
    rows = span.stop - span.start
    shape = jax.ShapeDtypeStruct((1, WIDTH, tokens), jnp.bfloat16)
    vmem = pl.BlockSpec(memory_space=pltpu.VMEM)
    hbm = pl.BlockSpec(memory_space=pltpu.HBM)
    earlier = [] if earlier is None else list(earlier)
    return pl.pallas_call(
        functools.partial(join_kernel, n, span),
        in_specs=[vmem] * n + [hbm] * len(earlier),
        out_specs=[hbm] * 3,
        out_shape=[shape] * 3,
        scratch_shapes=[
            pltpu.VMEM((n, *blocks[0].shape), jnp.bfloat16),
            pltpu.VMEM((3, rows, tokens), jnp.bfloat16),
            pltpu.SemaphoreType.DMA((3,)),
        ],
        input_output_aliases={n + i: i for i in range(len(earlier))},
        compiler_params=pltpu.CompilerParams(vmem_limit_bytes=24 * 2**20),
        name="unpack",
    )(*blocks, *earlier)


def clip_kernel(window, heads, given_bounds, *refs):
    own, sides_of = refs[:window], refs[window : window + 2]
    outs, (x_ref, y_ref, coef_ref, grad_ref) = refs[window + 2 : 2 * window + 2], refs[-6:-2]
    bounds, arrived = refs[-2:]
    copy = pltpu.make_async_copy(given_bounds, bounds, arrived)
    copy.start()
    halo = window - 1
    extent = window + 2 * halo
    lanes = grad_ref.shape[2]
    places = lanes // 2
    rows = heads * HDIM
    is_left = lax.broadcasted_iota(jnp.int32, (1, lanes), 1) < places

    def widen(ref, frame):
        x_ref[frame] = ref[0].astype(jnp.float32)
        y_ref[frame] = ref[1].astype(jnp.float32)

    for step, ref in enumerate(own):
        widen(ref, halo + (lax.axis_index("seq") ^ step))
    copy.wait()
    lowest, highest = bounds[0, halo], bounds[1, halo + window - 1]
    for start, ref in enumerate(sides_of):
        is_next = (lax.axis_index("grp") & 1) == start
        for at in range(halo):
            frame = at + jnp.where(is_next, halo + window, 0)
            needed = (frame >= lowest) & (frame < highest)
            pl.when(needed)(functools.partial(widen, ref.at[at], frame))

    def partners(frame):
        first, last = bounds[0, frame], bounds[1, frame]
        return first, last - first, [jnp.minimum(first + t, last - 1) for t in range(window)]

    def weigh(frame, carry):
        first, count, others = partners(frame)
        sums = [[] for _ in range(window)]
        for head in range(heads):
            span = slice(head * HDIM, (head + 1) * HDIM)
            mine = x_ref[frame, span, :]
            for t, other in enumerate(others):
                sums[t].append(jnp.sum(mine * y_ref[other, span, :], axis=0, keepdims=True))
        sums = [jnp.concatenate(parts, axis=0) for parts in sums]
        scores = [
            part * SCALING + jnp.where(t < count, 0.0, masked_score) for t, part in enumerate(sums)
        ]
        peak = functools.reduce(jnp.maximum, scores)
        raised = [jnp.exp(score - peak) for score in scores]
        inverse = 1.0 / functools.reduce(jnp.add, raised)
        weights = [part * inverse for part in raised]
        weights_low = [rounded(part) for part in weights]
        weight_grad = [swapped(part) for part in sums]
        dots = functools.reduce(jnp.add, [w * d for w, d in zip(weights_low, weight_grad)])
        for t in range(window):
            score_grad = rounded(weights[t] * (weight_grad[t] - dots))
            coef_ref[frame, t] = jnp.where(is_left, score_grad, swapped(weights_low[t]))
        return carry

    lax.fori_loop(lowest, highest, weigh, 0)

    def gradients(at, carry):
        frame = halo + at
        first, count, others = partners(frame)
        place = frame - first
        by_key, by_query = [], []
        for head in range(heads):
            span = slice(head * HDIM, (head + 1) * HDIM)
            key_sum, query_sum = None, None
            for t, other in enumerate(others):
                back = coef_ref[other, place, head : head + 1, :]
                back = jnp.where(t < count, back, 0.0)
                ahead = coef_ref[frame, t, head : head + 1, :]
                key_term = back * x_ref[other, span, :]
                query_term = ahead * y_ref[other, span, :]
                key_sum = key_term if t == 0 else key_sum + key_term
                query_sum = query_term if t == 0 else query_sum + query_term
            by_key.append(key_sum * jnp.where(is_left, SCALING, 1.0))
            by_query.append(query_sum * SCALING)
            if head % 2 == 1:
                span = slice((head - 1) * HDIM, (head + 1) * HDIM)
                value = jnp.concatenate(by_key[head - 1 :], axis=0)
                grad_ref[at, span, :] = value.astype(jnp.bfloat16)
        half = heads // 2
        folded = [
            jnp.where(is_left, by_query[head], swapped(by_query[head + half]))
            for head in range(half)
        ]
        value = jnp.concatenate(folded, axis=0)
        grad_ref[at, rows:, :] = value.astype(jnp.bfloat16)
        return carry

    lax.fori_loop(0, window, gradients, 0)
    for step, out in enumerate(outs):
        out[...] = grad_ref[(lax.axis_index("seq") ^ step)]


def clip_grads(bounds, own, beside):
    window = len(own)
    _, rows, lanes = own[0].shape
    beside = list(beside)
    heads = rows // HDIM
    extent = 3 * window - 2
    vmem = pl.BlockSpec(memory_space=pltpu.VMEM)
    work = extent * window * rows * lanes
    shape = (rows + rows // 2, lanes)
    return pl.pallas_call(
        functools.partial(clip_kernel, window, heads),
        out_shape=[jax.ShapeDtypeStruct(shape, jnp.bfloat16)] * window,
        in_specs=[pl.BlockSpec(memory_space=pl.ANY)] + [vmem] * (window + 2),
        out_specs=[vmem] * window,
        scratch_shapes=[
            pltpu.VMEM((extent, rows, lanes), jnp.float32),
            pltpu.VMEM((extent, rows, lanes), jnp.float32),
            pltpu.VMEM((extent, window, heads, lanes), jnp.float32),
            pltpu.VMEM((window, *shape), jnp.bfloat16),
            pltpu.SMEM(bounds.shape, jnp.int32),
            pltpu.SemaphoreType.DMA,
        ],
        compiler_params=pltpu.CompilerParams(vmem_limit_bytes=48 * 2**20),
        cost_estimate=pl.CostEstimate(
            flops=400 * work,
            bytes_accessed=2 * sum(block.size for block in (*own, *beside)),
            transcendentals=extent * window * heads * lanes,
        ),
        name="clips",
    )(bounds, *own, *beside)


def clip_bounds(clip_len, window):
    halo = window - 1
    extent = window + 2 * halo
    start = lax.axis_index("grp") * window - halo
    frames = start + jnp.arange(extent, dtype=jnp.int32)
    order = jnp.arange(clip_len.shape[0])
    ends = jnp.sum(jnp.where(order[:, None] <= order[None, :], clip_len[:, None], 0), axis=0)
    begins = ends - clip_len
    holds = (begins[None, :] <= frames[:, None]) & (frames[:, None] < ends[None, :])
    first = jnp.sum(jnp.where(holds, begins[None, :], 0), axis=1) - start
    last = jnp.sum(jnp.where(holds, ends[None, :], 0), axis=1) - start
    return jnp.stack([first, last]).astype(jnp.int32)


def shards(q_space, k_space, v_space, cot_space, q_time, k_time, v_time, cot_time, clip_len):
    def turned(*arrays):
        return tuple(array.transpose(0, 2, 1) for array in arrays)

    n = lax.axis_size("seq")
    window = q_time.shape[0] * n
    tokens = q_time.shape[1]
    bounds = clip_bounds(clip_len, window)
    time = turned(q_time, cot_time, k_time, v_time)
    spans = []
    head = 0
    for heads in CHUNKS:
        spans.append(slice(head * HDIM, (head + heads) * HDIM))
        head += heads
    space_in = turned(q_space, k_space, v_space, cot_space)
    packed = [list(split(time, span, n)) for span in spans]

    def gated(values, *earlier):
        return lax.optimization_barrier((values, *earlier))

    own = [exchange(packed[0])]
    space = frame_grads(*space_in)
    packed[1][2:], own[0][2], space = gated(packed[1][2:], own[0][2], space)
    own.append(exchange(packed[1]))
    beside = [neighbours(sides(blocks)) for blocks in own]
    back, grads = [], None
    for blocks, near in zip(own, beside):
        back.append(exchange(clip_grads(bounds, blocks, near)))
    for span, blocks in zip(spans, back):
        grads = join(blocks, span, tokens, grads)
    return turned(*space, *grads)


def solution(mesh):
    split_spec = P(("grp", "seq"), None, None)
    return jax.shard_map(
        shards,
        mesh=mesh,
        in_specs=(split_spec,) * 8 + (P(),),
        out_specs=(split_spec,) * 6,
        check_vma=False,
    )
```

```python
import functools
import math

import jax
import jax.numpy as jnp
from jax import lax
from jax.experimental import pallas as pl
from jax.experimental.pallas import tpu as pltpu
from jax.sharding import PartitionSpec as P

HEADS = 8
HDIM = 72
WIDTH = HEADS * HDIM
SCALING = 1.0 / math.sqrt(HDIM)
CHUNKS = (4, 4)
PARTS = 2
masked_score = -1e30


def dot(left, right, left_dim, right_dim):
    dims = (((left_dim,), (right_dim,)), ((), ()))
    return lax.dot_general(left, right, dims, preferred_element_type=jnp.float32)


def rounded(value):
    return value.astype(jnp.bfloat16).astype(jnp.float32)


def swapped(value):
    half = value.shape[1] // 2
    if 2 * half == 128:
        return pltpu.roll(value, half, 1)
    return jnp.concatenate([value[:, half:], value[:, :half]], axis=1)


def frame_kernel(q_ref, k_ref, v_ref, g_ref, dq_ref, dk_ref, dv_ref):
    pair = 2 * HDIM
    reach = -(-HDIM // 16) * 16
    row = lax.broadcasted_iota(jnp.int32, (reach, 1), 0)
    for begin in range(0, WIDTH, pair):
        found = [[], [], []]
        for low, own in ((0, 0), (pair - reach, reach - HDIM)):
            span = slice(begin + low, begin + low + reach)
            mask = ((row >= own) & (row < own + HDIM)).astype(jnp.float32).astype(jnp.bfloat16)
            queries, keys = q_ref[0, span, :], k_ref[0, span, :]
            cotangent = g_ref[0, span, :]
            scores = dot(keys * mask, queries, 0, 0) * SCALING
            weight_grad = dot(v_ref[0, span, :] * mask, cotangent, 0, 0)
            raised = jnp.exp(scores - jnp.max(scores, axis=0, keepdims=True))
            weights = raised * (1.0 / jnp.sum(raised, axis=0, keepdims=True))
            weights_low = weights.astype(jnp.bfloat16)
            dots = jnp.sum(weights_low.astype(jnp.float32) * weight_grad, axis=0, keepdims=True)
            score_grad = (weights * (weight_grad - dots)).astype(jnp.bfloat16)
            rows = slice(own, own + HDIM)
            found[0].append(dot(keys, score_grad, 1, 0)[rows] * SCALING)
            found[1].append(dot(queries, score_grad, 1, 1)[rows] * SCALING)
            found[2].append(dot(cotangent, weights_low, 1, 1)[rows])
        for out, parts in zip((dq_ref, dk_ref, dv_ref), found):
            out[0, begin : begin + pair, :] = jnp.concatenate(parts, axis=0).astype(jnp.bfloat16)


def frame_grads(queries, keys, values, cotangent):
    tokens = queries.shape[2]
    shape = jax.ShapeDtypeStruct(queries.shape, jnp.bfloat16)
    return pl.pallas_call(
        frame_kernel,
        out_shape=(shape, shape, shape),
        compiler_params=pltpu.CompilerParams(vmem_limit_bytes=60 * 2**20),
        cost_estimate=pl.CostEstimate(
            flops=12 * tokens * tokens * 256 * HEADS,
            bytes_accessed=14 * tokens * WIDTH,
            transcendentals=tokens * tokens * HEADS,
        ),
        name="space",
    )(queries, keys, values, cotangent)


def split_kernel(n, span, *refs):
    ins, outs, (loaded, held, arrived, left_off) = refs[:4], refs[4 : 4 + n], refs[-4:]
    count = (span.stop - span.start) // PARTS
    places = ins[0].shape[2] // n
    loads, stores = [], []
    for part in range(PARTS):
        rows = slice(part * count, (part + 1) * count)
        given = slice(span.start + rows.start, span.start + rows.stop)
        for i, array in enumerate(ins):
            copy = pltpu.make_async_copy(
                array.at[0, given, :], loaded.at[i, rows, :], arrived.at[part, i]
            )
            copy.start()
            loads.append(copy)
    for part in range(PARTS):
        rows = slice(part * count, (part + 1) * count)
        for at in range(2):
            for i in (2 * at, 2 * at + 1):
                loads[4 * part + i].wait()
            for target in range(n):
                lanes = slice(target * places, (target + 1) * places)
                both = [loaded[2 * at, rows, lanes], loaded[2 * at + 1, rows, lanes]]
                held[at, target, rows, :] = jnp.concatenate(both, axis=1)
            for step, out in enumerate(outs):
                block = held.at[at, lax.axis_index("seq") ^ step, rows, :]
                copy = pltpu.make_async_copy(block, out.at[at, rows, :], left_off.at[part, at, step])
                copy.start()
                stores.append(copy)
    for copy in stores:
        copy.wait()


def split(arrays, span, n):
    rows, tokens = span.stop - span.start, arrays[0].shape[2]
    shape = (2, rows, 2 * tokens // n)
    hbm = pl.BlockSpec(memory_space=pltpu.HBM)
    return pl.pallas_call(
        functools.partial(split_kernel, n, span),
        in_specs=[hbm] * 4,
        out_specs=[hbm] * n,
        out_shape=[jax.ShapeDtypeStruct(shape, jnp.bfloat16)] * n,
        scratch_shapes=[
            pltpu.VMEM((4, rows, tokens), jnp.bfloat16),
            pltpu.VMEM((2, n, *shape[1:]), jnp.bfloat16),
            pltpu.SemaphoreType.DMA((PARTS, 4)),
            pltpu.SemaphoreType.DMA((PARTS, 2, n)),
        ],
        compiler_params=pltpu.CompilerParams(vmem_limit_bytes=60 * 2**20),
        name="pack",
    )(*arrays)


def swap(block, axis, pairs):
    return lax.ppermute(block, axis, [(i, j) for i, j in pairs] + [(j, i) for i, j in pairs])


def exchange(blocks):
    n = len(blocks)
    moved = list(blocks)
    for step in reversed(range(1, n)):
        pairs = [[i, i ^ step] for i in range(n) if i < i ^ step]
        moved[step] = swap(blocks[step], "seq", pairs)
    return moved


def sides_kernel(n, *refs):
    ins, outs = refs[:n], refs[n:]
    is_odd = lax.axis_index("grp") & 1
    for step, ref in enumerate(ins):
        frame = (lax.axis_index("seq") ^ step)
        for start, out in zip((1, 0), outs):
            at = frame - jnp.where(is_odd == start, 1, 0)

            @pl.when((at >= 0) & (at < n - 1))
            def _():
                out[jnp.clip(at, 0, n - 2)] = ref[...]


def sides(blocks):
    n = len(blocks)
    shape = jax.ShapeDtypeStruct((n - 1, *blocks[0].shape), jnp.bfloat16)
    vmem = pl.BlockSpec(memory_space=pltpu.VMEM)
    return pl.pallas_call(
        functools.partial(sides_kernel, n),
        in_specs=[vmem] * n,
        out_specs=[vmem] * 2,
        out_shape=[shape] * 2,
        compiler_params=pltpu.CompilerParams(vmem_limit_bytes=24 * 2**20),
        name="sides",
    )(*blocks)


def gated(values, *earlier):
    return lax.optimization_barrier((values, *earlier))


def neighbours(blocks):
    count = lax.axis_size("grp")
    pairs = [[(i, i + 1) for i in range(start, count - 1, 2)] for start in (1, 0)]
    return [swap(block, "grp", links) for block, links in zip(blocks, pairs)]


def join_kernel(near, far, span, *refs):
    ins, outs, (held, ready, left_off) = refs[:near], refs[-6:-3], refs[-3:]
    place = lax.axis_index("seq")
    for step, ref in enumerate(ins):
        held[(place ^ step) & (near - 1)] = ref[...]
    count = span.stop - span.start
    half = count // 2
    places = held.shape[2] // 2

    def gather(rows, lanes):
        return jnp.concatenate([held[source, rows, lanes] for source in range(near)], axis=1)

    left, right = slice(0, places), slice(places, 2 * places)
    rest = slice(count, count + half)
    ready[1] = gather(slice(0, count), left)
    ready[2] = gather(slice(0, count), right)
    ready[0, :half, :] = gather(rest, left)
    ready[0, half:, :] = gather(rest, right)
    width = near * places
    tokens = pl.ds(pl.multiple_of((place // near ^ far) * width, width), width)
    copies = [
        pltpu.make_async_copy(ready.at[i], out.at[0, span, tokens], left_off.at[i])
        for i, out in enumerate(outs)
    ]
    for copy in copies:
        copy.start()
    for copy in copies:
        copy.wait()


def join(blocks, span, tokens, far, earlier):
    near = len(blocks) // 2
    blocks = blocks[near:] if far else blocks[:near]
    rows = span.stop - span.start
    shape = jax.ShapeDtypeStruct((1, WIDTH, tokens), jnp.bfloat16)
    vmem = pl.BlockSpec(memory_space=pltpu.VMEM)
    hbm = pl.BlockSpec(memory_space=pltpu.HBM)
    earlier = [] if earlier is None else list(earlier)
    return pl.pallas_call(
        functools.partial(join_kernel, near, far, span),
        in_specs=[vmem] * near + [hbm] * len(earlier),
        out_specs=[hbm] * 3,
        out_shape=[shape] * 3,
        scratch_shapes=[
            pltpu.VMEM((near, *blocks[0].shape), jnp.bfloat16),
            pltpu.VMEM((3, rows, tokens // 2), jnp.bfloat16),
            pltpu.SemaphoreType.DMA((3,)),
        ],
        input_output_aliases={near + i: i for i in range(len(earlier))},
        compiler_params=pltpu.CompilerParams(vmem_limit_bytes=24 * 2**20),
        name="unpack",
    )(*blocks, *earlier)


def clip_kernel(window, heads, given_bounds, *refs):
    own, sides_of = refs[:window], refs[window : window + 2]
    outs, (x_ref, y_ref, coef_ref, grad_ref) = refs[window + 2 : 2 * window + 2], refs[-6:-2]
    bounds, arrived = refs[-2:]
    copy = pltpu.make_async_copy(given_bounds, bounds, arrived)
    copy.start()
    halo = window - 1
    extent = window + 2 * halo
    lanes = grad_ref.shape[2]
    places = lanes // 2
    rows = heads * HDIM
    is_left = lax.broadcasted_iota(jnp.int32, (1, lanes), 1) < places

    def widen(ref, frame):
        x_ref[frame] = ref[0].astype(jnp.float32)
        y_ref[frame] = ref[1].astype(jnp.float32)

    for step, ref in enumerate(own):
        widen(ref, halo + (lax.axis_index("seq") ^ step))
    copy.wait()
    lowest, highest = bounds[0, halo], bounds[1, halo + window - 1]
    for start, ref in zip((1, 0), sides_of):
        is_next = (lax.axis_index("grp") & 1) == start
        for at in range(halo):
            frame = at + jnp.where(is_next, halo + window, 0)
            needed = (frame >= lowest) & (frame < highest)
            pl.when(needed)(functools.partial(widen, ref.at[at], frame))

    def partners(frame):
        first, last = bounds[0, frame], bounds[1, frame]
        return first, last - first, [jnp.minimum(first + t, last - 1) for t in range(window)]

    def weigh(frame, carry):
        first, count, others = partners(frame)
        sums = [[] for _ in range(window)]
        for head in range(heads):
            span = slice(head * HDIM, (head + 1) * HDIM)
            mine = x_ref[frame, span, :]
            for t, other in enumerate(others):
                sums[t].append(jnp.sum(mine * y_ref[other, span, :], axis=0, keepdims=True))
        sums = [jnp.concatenate(parts, axis=0) for parts in sums]
        scores = [
            part * SCALING + jnp.where(t < count, 0.0, masked_score) for t, part in enumerate(sums)
        ]
        peak = functools.reduce(jnp.maximum, scores)
        raised = [jnp.exp(score - peak) for score in scores]
        inverse = 1.0 / functools.reduce(jnp.add, raised)
        weights = [part * inverse for part in raised]
        weights_low = [rounded(part) for part in weights]
        weight_grad = [swapped(part) for part in sums]
        dots = functools.reduce(jnp.add, [w * d for w, d in zip(weights_low, weight_grad)])
        for t in range(window):
            score_grad = rounded(weights[t] * (weight_grad[t] - dots))
            coef_ref[frame, t] = jnp.where(is_left, score_grad, swapped(weights_low[t]))
        return carry

    lax.fori_loop(lowest, highest, weigh, 0)

    def gradients(at, carry):
        frame = halo + at
        first, count, others = partners(frame)
        place = frame - first
        by_key, by_query = [], []
        for head in range(heads):
            span = slice(head * HDIM, (head + 1) * HDIM)
            key_sum, query_sum = None, None
            for t, other in enumerate(others):
                back = coef_ref[other, place, head : head + 1, :]
                back = jnp.where(t < count, back, 0.0)
                ahead = coef_ref[frame, t, head : head + 1, :]
                key_term = back * x_ref[other, span, :]
                query_term = ahead * y_ref[other, span, :]
                key_sum = key_term if t == 0 else key_sum + key_term
                query_sum = query_term if t == 0 else query_sum + query_term
            by_key.append(key_sum * jnp.where(is_left, SCALING, 1.0))
            by_query.append(query_sum * SCALING)
            if head % 2 == 1:
                span = slice((head - 1) * HDIM, (head + 1) * HDIM)
                value = jnp.concatenate(by_key[head - 1 :], axis=0)
                grad_ref[at, span, :] = value.astype(jnp.bfloat16)
        half = heads // 2
        folded = [
            jnp.where(is_left, by_query[head], swapped(by_query[head + half]))
            for head in range(half)
        ]
        value = jnp.concatenate(folded, axis=0)
        grad_ref[at, rows:, :] = value.astype(jnp.bfloat16)
        return carry

    lax.fori_loop(0, window, gradients, 0)
    for step, out in enumerate(outs):
        out[...] = grad_ref[(lax.axis_index("seq") ^ step)]


def clip_grads(bounds, own, beside):
    window = len(own)
    _, rows, lanes = own[0].shape
    beside = list(beside)
    heads = rows // HDIM
    extent = 3 * window - 2
    vmem = pl.BlockSpec(memory_space=pltpu.VMEM)
    work = extent * window * rows * lanes
    shape = (rows + rows // 2, lanes)
    return pl.pallas_call(
        functools.partial(clip_kernel, window, heads),
        out_shape=[jax.ShapeDtypeStruct(shape, jnp.bfloat16)] * window,
        in_specs=[pl.BlockSpec(memory_space=pl.ANY)] + [vmem] * (window + 2),
        out_specs=[vmem] * window,
        scratch_shapes=[
            pltpu.VMEM((extent, rows, lanes), jnp.float32),
            pltpu.VMEM((extent, rows, lanes), jnp.float32),
            pltpu.VMEM((extent, window, heads, lanes), jnp.float32),
            pltpu.VMEM((window, *shape), jnp.bfloat16),
            pltpu.SMEM(bounds.shape, jnp.int32),
            pltpu.SemaphoreType.DMA,
        ],
        compiler_params=pltpu.CompilerParams(vmem_limit_bytes=48 * 2**20),
        cost_estimate=pl.CostEstimate(
            flops=400 * work,
            bytes_accessed=2 * sum(block.size for block in (*own, *beside)),
            transcendentals=extent * window * heads * lanes,
        ),
        name="clips",
    )(bounds, *own, *beside)


def clip_bounds(clip_len, window):
    halo = window - 1
    extent = window + 2 * halo
    start = lax.axis_index("grp") * window - halo
    frames = start + jnp.arange(extent, dtype=jnp.int32)
    order = jnp.arange(clip_len.shape[0])
    ends = jnp.sum(jnp.where(order[:, None] <= order[None, :], clip_len[:, None], 0), axis=0)
    begins = ends - clip_len
    holds = (begins[None, :] <= frames[:, None]) & (frames[:, None] < ends[None, :])
    first = jnp.sum(jnp.where(holds, begins[None, :], 0), axis=1) - start
    last = jnp.sum(jnp.where(holds, ends[None, :], 0), axis=1) - start
    return jnp.stack([first, last]).astype(jnp.int32)


def shards(q_space, k_space, v_space, cot_space, q_time, k_time, v_time, cot_time, clip_len):
    def turned(*arrays):
        return tuple(array.transpose(0, 2, 1) for array in arrays)

    n = lax.axis_size("seq")
    window = q_time.shape[0] * n
    tokens = q_time.shape[1]
    bounds = clip_bounds(clip_len, window)
    time = turned(q_time, cot_time, k_time, v_time)
    spans = []
    head = 0
    for heads in CHUNKS:
        spans.append(slice(head * HDIM, (head + heads) * HDIM))
        head += heads
    space_in = turned(q_space, k_space, v_space, cot_space)
    packed = [list(split(time, span, n)) for span in spans]

    own = [exchange(packed[0])]
    space = frame_grads(*space_in)
    packed[1][2:], own[0][2], space = gated(packed[1][2:], own[0][2], space)
    own.append(exchange(packed[1]))
    beside = [neighbours(sides(blocks)) for blocks in own]
    back, grads = [], None
    for blocks, near in zip(own, beside):
        back.append(exchange(clip_grads(bounds, blocks, near)))
    for span, blocks in zip(spans, back):
        for far in (1, 0):
            grads = join(blocks, span, tokens, far, grads)
    return turned(*space, *grads)


def solution(mesh):
    split_spec = P(("grp", "seq"), None, None)
    return jax.shard_map(
        shards,
        mesh=mesh,
        in_specs=(split_spec,) * 8 + (P(),),
        out_specs=(split_spec,) * 6,
        check_vma=False,
    )
```

```python
import functools
import math

import jax
import jax.numpy as jnp
from jax import lax
from jax.experimental import pallas as pl
from jax.experimental.pallas import tpu as pltpu
from jax.sharding import PartitionSpec as P

HEADS = 8
HDIM = 72
WIDTH = HEADS * HDIM
SCALING = 1.0 / math.sqrt(HDIM)
CHUNKS = (4, 4)
PARTS = 2
masked_score = -1e30


def dot(left, right, left_dim, right_dim):
    dims = (((left_dim,), (right_dim,)), ((), ()))
    return lax.dot_general(left, right, dims, preferred_element_type=jnp.float32)


def rounded(value):
    return value.astype(jnp.bfloat16).astype(jnp.float32)


def swapped(value):
    half = value.shape[1] // 2
    if 2 * half == 128:
        return pltpu.roll(value, half, 1)
    return jnp.concatenate([value[:, half:], value[:, :half]], axis=1)


def frame_kernel(q_ref, k_ref, v_ref, g_ref, dq_ref, dk_ref, dv_ref):
    pair = 2 * HDIM
    reach = -(-HDIM // 16) * 16
    row = lax.broadcasted_iota(jnp.int32, (reach, 1), 0)
    for begin in range(0, WIDTH, pair):
        found = [[], [], []]
        for low, own in ((0, 0), (pair - reach, reach - HDIM)):
            span = slice(begin + low, begin + low + reach)
            mask = ((row >= own) & (row < own + HDIM)).astype(jnp.float32).astype(jnp.bfloat16)
            queries, keys = q_ref[0, span, :], k_ref[0, span, :]
            cotangent = g_ref[0, span, :]
            scores = dot(keys * mask, queries, 0, 0) * SCALING
            weight_grad = dot(v_ref[0, span, :] * mask, cotangent, 0, 0)
            raised = jnp.exp(scores - jnp.max(scores, axis=0, keepdims=True))
            weights = raised * (1.0 / jnp.sum(raised, axis=0, keepdims=True))
            weights_low = weights.astype(jnp.bfloat16)
            dots = jnp.sum(weights_low.astype(jnp.float32) * weight_grad, axis=0, keepdims=True)
            score_grad = (weights * (weight_grad - dots)).astype(jnp.bfloat16)
            rows = slice(own, own + HDIM)
            found[0].append(dot(keys, score_grad, 1, 0)[rows] * SCALING)
            found[1].append(dot(queries, score_grad, 1, 1)[rows] * SCALING)
            found[2].append(dot(cotangent, weights_low, 1, 1)[rows])
        for out, parts in zip((dq_ref, dk_ref, dv_ref), found):
            out[0, begin : begin + pair, :] = jnp.concatenate(parts, axis=0).astype(jnp.bfloat16)


def frame_grads(queries, keys, values, cotangent):
    tokens = queries.shape[2]
    shape = jax.ShapeDtypeStruct(queries.shape, jnp.bfloat16)
    return pl.pallas_call(
        frame_kernel,
        out_shape=(shape, shape, shape),
        compiler_params=pltpu.CompilerParams(vmem_limit_bytes=60 * 2**20),
        cost_estimate=pl.CostEstimate(
            flops=12 * tokens * tokens * 256 * HEADS,
            bytes_accessed=14 * tokens * WIDTH,
            transcendentals=tokens * tokens * HEADS,
        ),
        name="space",
    )(queries, keys, values, cotangent)


def split_kernel(n, span, *refs):
    ins, outs, (loaded, held, arrived, left_off) = refs[:4], refs[4 : 4 + n], refs[-4:]
    count = (span.stop - span.start) // PARTS
    places = ins[0].shape[2] // n
    loads, stores = [], []
    for part in range(PARTS):
        rows = slice(part * count, (part + 1) * count)
        given = slice(span.start + rows.start, span.start + rows.stop)
        for i, array in enumerate(ins):
            copy = pltpu.make_async_copy(
                array.at[0, given, :], loaded.at[i, rows, :], arrived.at[part, i]
            )
            copy.start()
            loads.append(copy)
    for part in range(PARTS):
        rows = slice(part * count, (part + 1) * count)
        for at in range(2):
            for i in (2 * at, 2 * at + 1):
                loads[4 * part + i].wait()
            for target in range(n):
                lanes = slice(target * places, (target + 1) * places)
                both = [loaded[2 * at, rows, lanes], loaded[2 * at + 1, rows, lanes]]
                held[at, target, rows, :] = jnp.concatenate(both, axis=1)
            for step, out in enumerate(outs):
                block = held.at[at, lax.axis_index("seq") ^ step, rows, :]
                copy = pltpu.make_async_copy(block, out.at[at, rows, :], left_off.at[part, at, step])
                copy.start()
                stores.append(copy)
    for copy in stores:
        copy.wait()


def split(arrays, span, n):
    rows, tokens = span.stop - span.start, arrays[0].shape[2]
    shape = (2, rows, 2 * tokens // n)
    hbm = pl.BlockSpec(memory_space=pltpu.HBM)
    return pl.pallas_call(
        functools.partial(split_kernel, n, span),
        in_specs=[hbm] * 4,
        out_specs=[hbm] * n,
        out_shape=[jax.ShapeDtypeStruct(shape, jnp.bfloat16)] * n,
        scratch_shapes=[
            pltpu.VMEM((4, rows, tokens), jnp.bfloat16),
            pltpu.VMEM((2, n, *shape[1:]), jnp.bfloat16),
            pltpu.SemaphoreType.DMA((PARTS, 4)),
            pltpu.SemaphoreType.DMA((PARTS, 2, n)),
        ],
        compiler_params=pltpu.CompilerParams(vmem_limit_bytes=60 * 2**20),
        name="pack",
    )(*arrays)


def swap(block, axis, pairs):
    return lax.ppermute(block, axis, [(i, j) for i, j in pairs] + [(j, i) for i, j in pairs])


def exchange(blocks):
    n = len(blocks)
    moved = list(blocks)
    for step in reversed(range(1, n)):
        pairs = [[i, i ^ step] for i in range(n) if i < i ^ step]
        moved[step] = swap(blocks[step], "seq", pairs)
    return moved


def sides_kernel(n, *refs):
    ins, outs = refs[:n], refs[n:]
    is_odd = lax.axis_index("grp") & 1
    for step, ref in enumerate(ins):
        frame = (lax.axis_index("seq") ^ step)
        for start, out in zip((1, 0), outs):
            at = frame - jnp.where(is_odd == start, 1, 0)

            @pl.when((at >= 0) & (at < n - 1))
            def _():
                out[jnp.clip(at, 0, n - 2)] = ref[...]


def sides(blocks):
    n = len(blocks)
    shape = jax.ShapeDtypeStruct((n - 1, *blocks[0].shape), jnp.bfloat16)
    vmem = pl.BlockSpec(memory_space=pltpu.VMEM)
    return pl.pallas_call(
        functools.partial(sides_kernel, n),
        in_specs=[vmem] * n,
        out_specs=[vmem] * 2,
        out_shape=[shape] * 2,
        compiler_params=pltpu.CompilerParams(vmem_limit_bytes=24 * 2**20),
        name="sides",
    )(*blocks)


def gated(values, *earlier):
    return lax.optimization_barrier((values, *earlier))


def neighbours(blocks):
    count = lax.axis_size("grp")
    pairs = [[(i, i + 1) for i in range(start, count - 1, 2)] for start in (1, 0)]
    return [swap(block, "grp", links) for block, links in zip(blocks, pairs)]


def join_kernel(near, far, span, *refs):
    ins, outs, (held, ready, left_off) = refs[:near], refs[-6:-3], refs[-3:]
    place = lax.axis_index("seq")
    for step, ref in enumerate(ins):
        held[(place ^ step) & (near - 1)] = ref[...]
    count = span.stop - span.start
    half = count // 2
    places = held.shape[2] // 2

    def gather(rows, lanes):
        return jnp.concatenate([held[source, rows, lanes] for source in range(near)], axis=1)

    left, right = slice(0, places), slice(places, 2 * places)
    rest = slice(count, count + half)
    ready[1] = gather(slice(0, count), left)
    ready[2] = gather(slice(0, count), right)
    ready[0, :half, :] = gather(rest, left)
    ready[0, half:, :] = gather(rest, right)
    width = near * places
    tokens = pl.ds(pl.multiple_of((place // near ^ far) * width, width), width)
    copies = [
        pltpu.make_async_copy(ready.at[i], out.at[0, span, tokens], left_off.at[i])
        for i, out in enumerate(outs)
    ]
    for copy in copies:
        copy.start()
    for copy in copies:
        copy.wait()


def join(blocks, span, tokens, far, earlier):
    near = len(blocks) // 2
    blocks = blocks[near:] if far else blocks[:near]
    rows = span.stop - span.start
    shape = jax.ShapeDtypeStruct((1, WIDTH, tokens), jnp.bfloat16)
    vmem = pl.BlockSpec(memory_space=pltpu.VMEM)
    hbm = pl.BlockSpec(memory_space=pltpu.HBM)
    earlier = [] if earlier is None else list(earlier)
    return pl.pallas_call(
        functools.partial(join_kernel, near, far, span),
        in_specs=[vmem] * near + [hbm] * len(earlier),
        out_specs=[hbm] * 3,
        out_shape=[shape] * 3,
        scratch_shapes=[
            pltpu.VMEM((near, *blocks[0].shape), jnp.bfloat16),
            pltpu.VMEM((3, rows, tokens // 2), jnp.bfloat16),
            pltpu.SemaphoreType.DMA((3,)),
        ],
        input_output_aliases={near + i: i for i in range(len(earlier))},
        compiler_params=pltpu.CompilerParams(vmem_limit_bytes=24 * 2**20),
        name="unpack",
    )(*blocks, *earlier)


def clip_kernel(window, heads, given_bounds, *refs):
    own, sides_of = refs[:window], refs[window : window + 2]
    outs, (x_ref, y_ref, coef_ref, grad_ref) = refs[window + 2 : 2 * window + 2], refs[-6:-2]
    bounds, arrived = refs[-2:]
    copy = pltpu.make_async_copy(given_bounds, bounds, arrived)
    copy.start()
    halo = window - 1
    extent = window + 2 * halo
    lanes = grad_ref.shape[2]
    places = lanes // 2
    rows = heads * HDIM
    is_left = lax.broadcasted_iota(jnp.int32, (1, lanes), 1) < places

    def widen(ref, frame):
        x_ref[frame] = ref[0].astype(jnp.float32)
        y_ref[frame] = ref[1].astype(jnp.float32)

    for step, ref in enumerate(own):
        widen(ref, halo + (lax.axis_index("seq") ^ step))
    copy.wait()
    lowest, highest = bounds[0, halo], bounds[1, halo + window - 1]
    for start, ref in zip((1, 0), sides_of):
        is_next = (lax.axis_index("grp") & 1) == start
        for at in range(halo):
            frame = at + jnp.where(is_next, halo + window, 0)
            needed = (frame >= lowest) & (frame < highest)
            pl.when(needed)(functools.partial(widen, ref.at[at], frame))

    def partners(frame):
        first, last = bounds[0, frame], bounds[1, frame]
        return first, last - first, [jnp.minimum(first + t, last - 1) for t in range(window)]

    def weigh(frame, carry):
        first, count, others = partners(frame)
        sums = [[] for _ in range(window)]
        for head in range(heads):
            span = slice(head * HDIM, (head + 1) * HDIM)
            mine = x_ref[frame, span, :]
            for t, other in enumerate(others):
                sums[t].append(jnp.sum(mine * y_ref[other, span, :], axis=0, keepdims=True))
        sums = [jnp.concatenate(parts, axis=0) for parts in sums]
        scores = [
            part * SCALING + jnp.where(t < count, 0.0, masked_score) for t, part in enumerate(sums)
        ]
        peak = functools.reduce(jnp.maximum, scores)
        raised = [jnp.exp(score - peak) for score in scores]
        inverse = 1.0 / functools.reduce(jnp.add, raised)
        weights = [part * inverse for part in raised]
        weights_low = [rounded(part) for part in weights]
        weight_grad = [swapped(part) for part in sums]
        dots = functools.reduce(jnp.add, [w * d for w, d in zip(weights_low, weight_grad)])
        for t in range(window):
            score_grad = rounded(weights[t] * (weight_grad[t] - dots))
            coef_ref[frame, t] = jnp.where(is_left, score_grad, swapped(weights_low[t]))
        return carry

    lax.fori_loop(lowest, highest, weigh, 0)

    def gradients(at, carry):
        frame = halo + at
        first, count, others = partners(frame)
        place = frame - first
        by_key, by_query = [], []
        for head in range(heads):
            span = slice(head * HDIM, (head + 1) * HDIM)
            key_sum, query_sum = None, None
            for t, other in enumerate(others):
                back = coef_ref[other, place, head : head + 1, :]
                back = jnp.where(t < count, back, 0.0)
                ahead = coef_ref[frame, t, head : head + 1, :]
                key_term = back * x_ref[other, span, :]
                query_term = ahead * y_ref[other, span, :]
                key_sum = key_term if t == 0 else key_sum + key_term
                query_sum = query_term if t == 0 else query_sum + query_term
            by_key.append(key_sum * jnp.where(is_left, SCALING, 1.0))
            by_query.append(query_sum * SCALING)
            if head % 2 == 1:
                span = slice((head - 1) * HDIM, (head + 1) * HDIM)
                value = jnp.concatenate(by_key[head - 1 :], axis=0)
                grad_ref[at, span, :] = value.astype(jnp.bfloat16)
        half = heads // 2
        folded = [
            jnp.where(is_left, by_query[head], swapped(by_query[head + half]))
            for head in range(half)
        ]
        value = jnp.concatenate(folded, axis=0)
        grad_ref[at, rows:, :] = value.astype(jnp.bfloat16)
        return carry

    lax.fori_loop(0, window, gradients, 0)
    for step, out in enumerate(outs):
        out[...] = grad_ref[(lax.axis_index("seq") ^ step)]


def clip_grads(bounds, own, beside):
    window = len(own)
    _, rows, lanes = own[0].shape
    beside = list(beside)
    heads = rows // HDIM
    extent = 3 * window - 2
    vmem = pl.BlockSpec(memory_space=pltpu.VMEM)
    work = extent * window * rows * lanes
    shape = (rows + rows // 2, lanes)
    return pl.pallas_call(
        functools.partial(clip_kernel, window, heads),
        out_shape=[jax.ShapeDtypeStruct(shape, jnp.bfloat16)] * window,
        in_specs=[pl.BlockSpec(memory_space=pl.ANY)] + [vmem] * (window + 2),
        out_specs=[vmem] * window,
        scratch_shapes=[
            pltpu.VMEM((extent, rows, lanes), jnp.float32),
            pltpu.VMEM((extent, rows, lanes), jnp.float32),
            pltpu.VMEM((extent, window, heads, lanes), jnp.float32),
            pltpu.VMEM((window, *shape), jnp.bfloat16),
            pltpu.SMEM(bounds.shape, jnp.int32),
            pltpu.SemaphoreType.DMA,
        ],
        compiler_params=pltpu.CompilerParams(vmem_limit_bytes=48 * 2**20),
        cost_estimate=pl.CostEstimate(
            flops=400 * work,
            bytes_accessed=2 * sum(block.size for block in (*own, *beside)),
            transcendentals=extent * window * heads * lanes,
        ),
        name="clips",
    )(bounds, *own, *beside)


def transposed_groups(tiles):
    count = len(tiles)
    size = tiles[0].shape[1] // count
    group = lax.broadcasted_iota(jnp.int32, (1, tiles[0].shape[1]), 1) // size
    step = count // 2
    while step:
        upper = (group & step) != 0
        moved = list(tiles)
        for a in range(count):
            if not a & step:
                low, high = tiles[a], tiles[a | step]
                moved[a] = jnp.where(upper, pltpu.roll(high, step * size, 1), low)
                moved[a | step] = jnp.where(upper, high, pltpu.roll(low, (count - step) * size, 1))
        tiles = moved
        step //= 2
    return tiles


def deal_kernel(q_ref, g_ref, k_ref, v_ref, out_ref, wide, turned):
    for i, ref in enumerate((q_ref, g_ref, k_ref, v_ref)):
        wide[i] = ref[0].astype(jnp.float32)
    groups = 2 * HEADS

    def rows_of(step, carry):
        begin = pl.multiple_of(step * 8, 8)
        for pair in range(2):
            for tile in range(wide.shape[2] // 128):
                lanes = slice(tile * 128, (tile + 1) * 128)
                parts = [
                    wide[2 * pair + i, pl.ds(head * HDIM + begin, 8), lanes]
                    for head in range(HEADS)
                    for i in range(2)
                ]
                for d, part in enumerate(transposed_groups(parts)):
                    turned[tile * groups + d, pl.ds(pair * HDIM + begin, 8), :] = part
        return carry

    lax.fori_loop(0, HDIM // 8, rows_of, 0)
    for target in range(out_ref.shape[0]):
        out_ref[target] = turned[target].astype(jnp.bfloat16)


def deal(arrays, count):
    shape = (count, 2 * HDIM, 128)
    return pl.pallas_call(
        deal_kernel,
        out_shape=jax.ShapeDtypeStruct(shape, jnp.bfloat16),
        scratch_shapes=[
            pltpu.VMEM((4, *arrays[0].shape[1:]), jnp.float32),
            pltpu.VMEM(shape, jnp.float32),
        ],
        compiler_params=pltpu.CompilerParams(vmem_limit_bytes=60 * 2**20),
        name="pack",
    )(*arrays)


FOLD = 40


def all_frames_kernel(slots, given_bounds, in_ref, out_ref, both, sums_ref, bias_ref, coef_ref, bounds, arrived):
    copy = pltpu.make_async_copy(given_bounds, bounds, arrived)
    copy.start()
    count = in_ref.shape[0]
    for frame in range(count):
        both[frame] = in_ref[frame].astype(jnp.float32)
    copy.wait()
    lane = lax.broadcasted_iota(jnp.int32, (1, 128), 1)
    is_left = (lane & 8) == 0
    x_rows, y_rows = slice(0, HDIM), slice(HDIM, 2 * HDIM)
    together = 4

    def partners(frame):
        first, last = bounds[0, frame], bounds[1, frame]
        return first, last - first, [jnp.minimum(first + t, last - 1) for t in range(slots)]

    def products(step, carry):
        for i in range(together):
            frame = step * together + i
            first, size, others = partners(frame)
            mine = both[frame, x_rows, :]
            for t, other in enumerate(others):
                total = jnp.sum(mine * both[other, y_rows, :], axis=0, keepdims=True)
                sums_ref[t, pl.ds(frame, 1), :] = total
                bias = jnp.where(t < size, 0.0, masked_score)
                bias_ref[t, pl.ds(frame, 1), :] = jnp.full((1, 128), bias, jnp.float32)
        return carry

    lax.fori_loop(0, count // together, products, 0)
    sums = [sums_ref[t] for t in range(slots)]
    scores = [sums[t] * SCALING + bias_ref[t] for t in range(slots)]
    peak = functools.reduce(jnp.maximum, scores)
    raised = [jnp.exp(score - peak) for score in scores]
    inverse = 1.0 / functools.reduce(jnp.add, raised)
    weights = [part * inverse for part in raised]
    weights_low = [rounded(part) for part in weights]
    weight_grad = [pltpu.roll(part, 120, 1) for part in sums]
    dots = functools.reduce(jnp.add, [w * d for w, d in zip(weights_low, weight_grad)])
    for t in range(slots):
        score_grad = rounded(weights[t] * (weight_grad[t] - dots))
        coef_ref[t] = jnp.where(is_left, score_grad, pltpu.roll(weights_low[t], 8, 1))

    def gradients(step, carry):
        for i in range(together):
            frame = step * together + i
            first, size, others = partners(frame)
            key_sum, query_sum = None, None
            for t, other in enumerate(others):
                back = coef_ref[frame - first, pl.ds(other, 1), :]
                back = jnp.where(t < size, back, 0.0)
                key_term = back * both[other, x_rows, :]
                query_term = coef_ref[t, pl.ds(frame, 1), :] * both[other, y_rows, :]
                key_sum = key_term if t == 0 else key_sum + key_term
                query_sum = query_term if t == 0 else query_sum + query_term
            query_sum = query_sum * SCALING
            rest = pltpu.roll(query_sum[FOLD:], 8, 1)
            rest = jnp.concatenate([rest, jnp.zeros((2 * FOLD - HDIM, 128), jnp.float32)], axis=0)
            folded = jnp.where(is_left, query_sum[:FOLD], rest)
            value = jnp.concatenate([key_sum * jnp.where(is_left, SCALING, 1.0), folded], axis=0)
            out_ref[frame] = value.astype(jnp.bfloat16)
        return carry

    lax.fori_loop(0, count // together, gradients, 0)


def all_frames_grads(bounds, blocks, slots):
    count = blocks.shape[0]
    rows = pltpu.VMEM((slots, count, 128), jnp.float32)
    return pl.pallas_call(
        functools.partial(all_frames_kernel, slots),
        out_shape=jax.ShapeDtypeStruct((count, HDIM + FOLD, 128), jnp.bfloat16),
        in_specs=[pl.BlockSpec(memory_space=pl.ANY), pl.BlockSpec(memory_space=pltpu.VMEM)],
        out_specs=pl.BlockSpec(memory_space=pltpu.VMEM),
        scratch_shapes=[
            pltpu.VMEM(blocks.shape, jnp.float32),
            rows,
            rows,
            rows,
            pltpu.SMEM(bounds.shape, jnp.int32),
            pltpu.SemaphoreType.DMA,
        ],
        compiler_params=pltpu.CompilerParams(vmem_limit_bytes=48 * 2**20),
        name="clips",
    )(bounds, blocks)


def collect_kernel(in_ref, dq_ref, dk_ref, dv_ref, wide, turned):
    count = in_ref.shape[0]
    groups = 2 * HEADS
    for source in range(count):
        wide[source] = in_ref[source].astype(jnp.float32)
    lane = lax.broadcasted_iota(jnp.int32, (1, 128), 1)
    is_left = (lane & 8) == 0
    for begin in range(0, HDIM, 8):
        for tile in range(count // groups):
            lanes = slice(tile * 128, (tile + 1) * 128)
            parts = [wide[tile * groups + d, begin : begin + 8, :] for d in range(groups)]
            for s, part in enumerate(transposed_groups(parts)):
                row = s // 2 * HDIM + begin
                turned[1 + s % 2, row : row + 8, lanes] = part
        parts = []
        row = HDIM + begin % FOLD
        for d in range(groups):
            low, high = wide[d, row : row + 8, :], wide[groups + d, row : row + 8, :]
            if begin < FOLD:
                high = pltpu.roll(high, 8, 1)
            else:
                low = pltpu.roll(low, 120, 1)
            parts.append(jnp.where(is_left, low, high))
        for s, part in enumerate(transposed_groups(parts)):
            row = s // 2 * HDIM + begin
            turned[0, row : row + 8, s % 2 * 128 : (s % 2 + 1) * 128] = part
    for i, out in enumerate((dq_ref, dk_ref, dv_ref)):
        out[0] = turned[i].astype(jnp.bfloat16)


def collect(blocks, tokens):
    shape = jax.ShapeDtypeStruct((1, WIDTH, tokens), jnp.bfloat16)
    return pl.pallas_call(
        collect_kernel,
        out_shape=[shape] * 3,
        scratch_shapes=[
            pltpu.VMEM(blocks.shape, jnp.float32),
            pltpu.VMEM((3, WIDTH, tokens), jnp.float32),
        ],
        compiler_params=pltpu.CompilerParams(vmem_limit_bytes=60 * 2**20),
        name="unpack",
    )(blocks)


def all_frames(time, clip_len, slots):
    axes = ("grp", "seq")
    count = lax.axis_size("grp") * lax.axis_size("seq")
    begins, ends = clip_edges(clip_len)
    bounds = clip_bounds(begins, ends, 0, count)
    blocks = lax.all_to_all(deal(time, count), axes, split_axis=0, concat_axis=0, tiled=True)
    grads = all_frames_grads(bounds, blocks, slots)
    grads = lax.all_to_all(grads, axes, split_axis=0, concat_axis=0, tiled=True)
    return collect(grads, time[0].shape[2])


def clip_edges(clip_len):
    order = jnp.arange(clip_len.shape[0])
    ends = jnp.sum(jnp.where(order[:, None] <= order[None, :], clip_len[:, None], 0), axis=0)
    return ends - clip_len, ends


def clip_bounds(begins, ends, start, count):
    frames = start + jnp.arange(count, dtype=jnp.int32)
    holds = (begins[None, :] <= frames[:, None]) & (frames[:, None] < ends[None, :])
    first = jnp.sum(jnp.where(holds, begins[None, :], 0), axis=1) - start
    last = jnp.sum(jnp.where(holds, ends[None, :], 0), axis=1) - start
    return jnp.stack([first, last]).astype(jnp.int32)


def shards(q_space, k_space, v_space, cot_space, q_time, k_time, v_time, cot_time, clip_len):
    def turned(*arrays):
        return tuple(array.transpose(0, 2, 1) for array in arrays)

    n = lax.axis_size("seq")
    window = q_time.shape[0] * n
    tokens = q_time.shape[1]
    time = turned(q_time, cot_time, k_time, v_time)
    space_in = turned(q_space, k_space, v_space, cot_space)
    if tokens * 2 * HEADS == 128 * n * lax.axis_size("grp"):
        grads = all_frames(time, clip_len, window)
        return turned(*frame_grads(*space_in), *grads)
    halo = window - 1
    begins, ends = clip_edges(clip_len)
    start = lax.axis_index("grp") * window - halo
    bounds = clip_bounds(begins, ends, start, window + 2 * halo)
    spans = []
    head = 0
    for heads in CHUNKS:
        spans.append(slice(head * HDIM, (head + heads) * HDIM))
        head += heads
    packed = [list(split(time, span, n)) for span in spans]

    own = [exchange(packed[0])]
    space = frame_grads(*space_in)
    packed[1][2:], own[0][2], space = gated(packed[1][2:], own[0][2], space)
    own.append(exchange(packed[1]))
    beside = [neighbours(sides(blocks)) for blocks in own]
    back, grads = [], None
    for blocks, near in zip(own, beside):
        back.append(exchange(clip_grads(bounds, blocks, near)))
    for span, blocks in zip(spans, back):
        for far in (1, 0):
            grads = join(blocks, span, tokens, far, grads)
    return turned(*space, *grads)


def solution(mesh):
    split_spec = P(("grp", "seq"), None, None)
    return jax.shard_map(
        shards,
        mesh=mesh,
        in_specs=(split_spec,) * 8 + (P(),),
        out_specs=(split_spec,) * 6,
        check_vma=False,
    )
```

```python
import functools
import math

import jax
import jax.numpy as jnp
from jax import lax
from jax.experimental import pallas as pl
from jax.experimental.pallas import tpu as pltpu
from jax.sharding import PartitionSpec as P

HEADS = 8
HDIM = 72
WIDTH = HEADS * HDIM
SCALING = 1.0 / math.sqrt(HDIM)
CHUNKS = (4, 4)
PARTS = 1
masked_score = -1e30


def dot(left, right, left_dim, right_dim):
    dims = (((left_dim,), (right_dim,)), ((), ()))
    return lax.dot_general(left, right, dims, preferred_element_type=jnp.float32)


def rounded(value):
    return value.astype(jnp.bfloat16).astype(jnp.float32)


def swapped(value):
    half = value.shape[1] // 2
    if 2 * half == 128:
        return pltpu.roll(value, half, 1)
    return jnp.concatenate([value[:, half:], value[:, :half]], axis=1)


def frame_kernel(q_ref, k_ref, v_ref, g_ref, dq_ref, dk_ref, dv_ref):
    pair = 2 * HDIM
    reach = -(-HDIM // 16) * 16
    row = lax.broadcasted_iota(jnp.int32, (reach, 1), 0)
    for begin in range(0, WIDTH, pair):
        found = [[], [], []]
        for low, own in ((0, 0), (pair - reach, reach - HDIM)):
            span = slice(begin + low, begin + low + reach)
            mask = ((row >= own) & (row < own + HDIM)).astype(jnp.float32).astype(jnp.bfloat16)
            queries, keys = q_ref[0, span, :], k_ref[0, span, :]
            cotangent = g_ref[0, span, :]
            scores = dot(keys * mask, queries, 0, 0) * SCALING
            weight_grad = dot(v_ref[0, span, :] * mask, cotangent, 0, 0)
            raised = jnp.exp(scores - jnp.max(scores, axis=0, keepdims=True))
            weights = raised * (1.0 / jnp.sum(raised, axis=0, keepdims=True))
            weights_low = weights.astype(jnp.bfloat16)
            dots = jnp.sum(weights_low.astype(jnp.float32) * weight_grad, axis=0, keepdims=True)
            score_grad = (weights * (weight_grad - dots)).astype(jnp.bfloat16)
            rows = slice(own, own + HDIM)
            found[0].append(dot(keys, score_grad, 1, 0)[rows] * SCALING)
            found[1].append(dot(queries, score_grad, 1, 1)[rows] * SCALING)
            found[2].append(dot(cotangent, weights_low, 1, 1)[rows])
        for out, parts in zip((dq_ref, dk_ref, dv_ref), found):
            out[0, begin : begin + pair, :] = jnp.concatenate(parts, axis=0).astype(jnp.bfloat16)


def frame_grads(queries, keys, values, cotangent):
    tokens = queries.shape[2]
    shape = jax.ShapeDtypeStruct(queries.shape, jnp.bfloat16)
    return pl.pallas_call(
        frame_kernel,
        out_shape=(shape, shape, shape),
        compiler_params=pltpu.CompilerParams(vmem_limit_bytes=60 * 2**20),
        cost_estimate=pl.CostEstimate(
            flops=12 * tokens * tokens * 256 * HEADS,
            bytes_accessed=14 * tokens * WIDTH,
            transcendentals=tokens * tokens * HEADS,
        ),
        name="space",
    )(queries, keys, values, cotangent)


def split_kernel(n, span, *refs):
    ins, outs, (loaded, held, arrived, left_off) = refs[:4], refs[4 : 4 + n], refs[-4:]
    count = (span.stop - span.start) // PARTS
    places = ins[0].shape[2] // n
    loads, stores = [], []
    for part in range(PARTS):
        rows = slice(part * count, (part + 1) * count)
        given = slice(span.start + rows.start, span.start + rows.stop)
        for i, array in enumerate(ins):
            copy = pltpu.make_async_copy(
                array.at[0, given, :], loaded.at[i, rows, :], arrived.at[part, i]
            )
            copy.start()
            loads.append(copy)
    for part in range(PARTS):
        rows = slice(part * count, (part + 1) * count)
        for at in range(2):
            for i in (2 * at, 2 * at + 1):
                loads[4 * part + i].wait()
            for target in range(n):
                lanes = slice(target * places, (target + 1) * places)
                both = [loaded[2 * at, rows, lanes], loaded[2 * at + 1, rows, lanes]]
                held[at, target, rows, :] = jnp.concatenate(both, axis=1)
            for step, out in enumerate(outs):
                block = held.at[at, lax.axis_index("seq") ^ step, rows, :]
                copy = pltpu.make_async_copy(block, out.at[at, rows, :], left_off.at[part, at, step])
                copy.start()
                stores.append(copy)
    for copy in stores:
        copy.wait()


def split(arrays, span, n):
    rows, tokens = span.stop - span.start, arrays[0].shape[2]
    shape = (2, rows, 2 * tokens // n)
    hbm = pl.BlockSpec(memory_space=pltpu.HBM)
    return pl.pallas_call(
        functools.partial(split_kernel, n, span),
        in_specs=[hbm] * 4,
        out_specs=[hbm] * n,
        out_shape=[jax.ShapeDtypeStruct(shape, jnp.bfloat16)] * n,
        scratch_shapes=[
            pltpu.VMEM((4, rows, tokens), jnp.bfloat16),
            pltpu.VMEM((2, n, *shape[1:]), jnp.bfloat16),
            pltpu.SemaphoreType.DMA((PARTS, 4)),
            pltpu.SemaphoreType.DMA((PARTS, 2, n)),
        ],
        compiler_params=pltpu.CompilerParams(vmem_limit_bytes=60 * 2**20),
        name="pack",
    )(*arrays)


def swap(block, axis, pairs):
    return lax.ppermute(block, axis, [(i, j) for i, j in pairs] + [(j, i) for i, j in pairs])


def exchange(blocks):
    n = len(blocks)
    moved = list(blocks)
    for step in reversed(range(1, n)):
        pairs = [[i, i ^ step] for i in range(n) if i < i ^ step]
        moved[step] = swap(blocks[step], "seq", pairs)
    return moved


def sides_kernel(n, *refs):
    ins, outs = refs[:n], refs[n:]
    is_odd = lax.axis_index("grp") & 1
    for step, ref in enumerate(ins):
        frame = (lax.axis_index("seq") ^ step)
        for start, out in zip((1, 0), outs):
            at = frame - jnp.where(is_odd == start, 1, 0)

            @pl.when((at >= 0) & (at < n - 1))
            def _():
                out[jnp.clip(at, 0, n - 2)] = ref[...]


def sides(blocks):
    n = len(blocks)
    shape = jax.ShapeDtypeStruct((n - 1, *blocks[0].shape), jnp.bfloat16)
    vmem = pl.BlockSpec(memory_space=pltpu.VMEM)
    return pl.pallas_call(
        functools.partial(sides_kernel, n),
        in_specs=[vmem] * n,
        out_specs=[vmem] * 2,
        out_shape=[shape] * 2,
        compiler_params=pltpu.CompilerParams(vmem_limit_bytes=24 * 2**20),
        name="sides",
    )(*blocks)


def gated(values, *earlier):
    return lax.optimization_barrier((values, *earlier))


def neighbours(block, start):
    count = lax.axis_size("grp")
    return swap(block, "grp", [(i, i + 1) for i in range(start, count - 1, 2)])


def far_first(n):
    return [*range(n // 2, n), *range(n // 2)]


def join_kernel(n, span, *refs):
    ins, outs, (held, ready, left_off) = refs[:n], refs[-6:-3], refs[-3:]
    for step, ref in zip(far_first(n), ins):
        held[lax.axis_index("seq") ^ step] = ref[...]
    count = span.stop - span.start
    half = count // 2
    places = held.shape[2] // 2

    def gather(rows, lanes):
        return jnp.concatenate([held[source, rows, lanes] for source in range(n)], axis=1)

    left, right = slice(0, places), slice(places, 2 * places)
    rest = slice(count, count + half)
    ready[1] = gather(slice(0, count), left)
    ready[2] = gather(slice(0, count), right)
    ready[0, :half, :] = gather(rest, left)
    ready[0, half:, :] = gather(rest, right)
    copies = [
        pltpu.make_async_copy(ready.at[i], out.at[0, span, :], left_off.at[i])
        for i, out in enumerate(outs)
    ]
    for copy in copies:
        copy.start()
    for copy in copies:
        copy.wait()


def join(blocks, span, tokens, earlier):
    n = len(blocks)
    rows = span.stop - span.start
    shape = jax.ShapeDtypeStruct((1, WIDTH, tokens), jnp.bfloat16)
    vmem = pl.BlockSpec(memory_space=pltpu.VMEM)
    hbm = pl.BlockSpec(memory_space=pltpu.HBM)
    earlier = [] if earlier is None else list(earlier)
    return pl.pallas_call(
        functools.partial(join_kernel, n, span),
        in_specs=[vmem] * n + [hbm] * len(earlier),
        out_specs=[hbm] * 3,
        out_shape=[shape] * 3,
        scratch_shapes=[
            pltpu.VMEM((n, *blocks[0].shape), jnp.bfloat16),
            pltpu.VMEM((3, rows, tokens), jnp.bfloat16),
            pltpu.SemaphoreType.DMA((3,)),
        ],
        input_output_aliases={n + i: i for i in range(len(earlier))},
        compiler_params=pltpu.CompilerParams(vmem_limit_bytes=24 * 2**20),
        name="unpack",
    )(*(blocks[step] for step in far_first(n)), *earlier)


def clip_kernel(window, heads, given_bounds, *refs):
    own, sides_of = refs[:window], refs[window : window + 2]
    outs, (x_ref, y_ref) = refs[window + 2 : 2 * window + 2], refs[-8:-6]
    sums_ref, score_ref, coef_ref, grad_ref = refs[-6:-2]
    bounds, arrived = refs[-2:]
    copy = pltpu.make_async_copy(given_bounds, bounds, arrived)
    copy.start()
    halo = window - 1
    extent = window + 2 * halo
    lanes = grad_ref.shape[2]
    places = lanes // 2
    rows = heads * HDIM
    is_left = lax.broadcasted_iota(jnp.int32, (1, lanes), 1) < places

    def widen(ref, frame):
        x_ref[frame] = ref[0].astype(jnp.float32)
        y_ref[frame] = ref[1].astype(jnp.float32)

    for step, ref in enumerate(own):
        widen(ref, halo + (lax.axis_index("seq") ^ step))
    copy.wait()
    lowest, highest = bounds[0, halo], bounds[1, halo + window - 1]
    for start, ref in zip((1, 0), sides_of):
        is_next = (lax.axis_index("grp") & 1) == start
        for at in range(halo):
            frame = at + jnp.where(is_next, halo + window, 0)
            needed = (frame >= lowest) & (frame < highest)
            pl.when(needed)(functools.partial(widen, ref.at[at], frame))

    def partners(frame):
        first, last = bounds[0, frame], bounds[1, frame]
        return first, last - first, [jnp.minimum(first + t, last - 1) for t in range(window)]

    def products(frame, carry):
        first, count, others = partners(frame)
        sums = [[] for _ in range(window)]
        for head in range(heads):
            span = slice(head * HDIM, (head + 1) * HDIM)
            mine = x_ref[frame, span, :]
            for t, other in enumerate(others):
                sums[t].append(jnp.sum(mine * y_ref[other, span, :], axis=0, keepdims=True))
        for t, parts in enumerate(sums):
            total = jnp.concatenate(parts, axis=0)
            sums_ref[t, frame] = total
            score_ref[t, frame] = total * SCALING + jnp.where(t < count, 0.0, masked_score)
        return carry

    lax.fori_loop(lowest, highest, products, 0)
    flat = (extent * heads, lanes)
    scores = [score_ref[t].reshape(flat) for t in range(window)]
    sums = [sums_ref[t].reshape(flat) for t in range(window)]
    peak = functools.reduce(jnp.maximum, scores)
    raised = [jnp.exp(score - peak) for score in scores]
    inverse = 1.0 / functools.reduce(jnp.add, raised)
    weights = [part * inverse for part in raised]
    weights_low = [rounded(part) for part in weights]
    weight_grad = [swapped(part) for part in sums]
    dots = functools.reduce(jnp.add, [w * d for w, d in zip(weights_low, weight_grad)])
    for t in range(window):
        score_grad = rounded(weights[t] * (weight_grad[t] - dots))
        coef = jnp.where(is_left, score_grad, swapped(weights_low[t]))
        coef_ref[t] = coef.reshape(extent, heads, lanes)

    def gradients(at, carry):
        frame = halo + at
        first, count, others = partners(frame)
        place = frame - first
        by_key, by_query = [], []
        for head in range(heads):
            span = slice(head * HDIM, (head + 1) * HDIM)
            key_sum, query_sum = None, None
            for t, other in enumerate(others):
                back = coef_ref[place, other, head : head + 1, :]
                back = jnp.where(t < count, back, 0.0)
                ahead = coef_ref[t, frame, head : head + 1, :]
                key_term = back * x_ref[other, span, :]
                query_term = ahead * y_ref[other, span, :]
                key_sum = key_term if t == 0 else key_sum + key_term
                query_sum = query_term if t == 0 else query_sum + query_term
            by_key.append(key_sum * jnp.where(is_left, SCALING, 1.0))
            by_query.append(query_sum * SCALING)
            if head % 2 == 1:
                span = slice((head - 1) * HDIM, (head + 1) * HDIM)
                value = jnp.concatenate(by_key[head - 1 :], axis=0)
                grad_ref[at, span, :] = value.astype(jnp.bfloat16)
        half = heads // 2
        folded = [
            jnp.where(is_left, by_query[head], swapped(by_query[head + half]))
            for head in range(half)
        ]
        value = jnp.concatenate(folded, axis=0)
        grad_ref[at, rows:, :] = value.astype(jnp.bfloat16)
        return carry

    lax.fori_loop(0, window, gradients, 0)
    for step, out in enumerate(outs):
        out[...] = grad_ref[(lax.axis_index("seq") ^ step)]


def clip_grads(bounds, own, beside):
    window = len(own)
    _, rows, lanes = own[0].shape
    beside = list(beside)
    heads = rows // HDIM
    extent = 3 * window - 2
    vmem = pl.BlockSpec(memory_space=pltpu.VMEM)
    work = extent * window * rows * lanes
    shape = (rows + rows // 2, lanes)
    return pl.pallas_call(
        functools.partial(clip_kernel, window, heads),
        out_shape=[jax.ShapeDtypeStruct(shape, jnp.bfloat16)] * window,
        in_specs=[pl.BlockSpec(memory_space=pl.ANY)] + [vmem] * (window + 2),
        out_specs=[vmem] * window,
        scratch_shapes=[
            pltpu.VMEM((extent, rows, lanes), jnp.float32),
            pltpu.VMEM((extent, rows, lanes), jnp.float32),
            pltpu.VMEM((window, extent, heads, lanes), jnp.float32),
            pltpu.VMEM((window, extent, heads, lanes), jnp.float32),
            pltpu.VMEM((window, extent, heads, lanes), jnp.float32),
            pltpu.VMEM((window, *shape), jnp.bfloat16),
            pltpu.SMEM(bounds.shape, jnp.int32),
            pltpu.SemaphoreType.DMA,
        ],
        compiler_params=pltpu.CompilerParams(vmem_limit_bytes=48 * 2**20),
        cost_estimate=pl.CostEstimate(
            flops=400 * work,
            bytes_accessed=2 * sum(block.size for block in (*own, *beside)),
            transcendentals=extent * window * heads * lanes,
        ),
        name="clips",
    )(bounds, *own, *beside)


def clip_bounds(clip_len, window):
    halo = window - 1
    extent = window + 2 * halo
    start = lax.axis_index("grp") * window - halo
    frames = start + jnp.arange(extent, dtype=jnp.int32)
    order = jnp.arange(clip_len.shape[0])
    ends = jnp.sum(jnp.where(order[:, None] <= order[None, :], clip_len[:, None], 0), axis=0)
    begins = ends - clip_len
    holds = (begins[None, :] <= frames[:, None]) & (frames[:, None] < ends[None, :])
    first = jnp.sum(jnp.where(holds, begins[None, :], 0), axis=1) - start
    last = jnp.sum(jnp.where(holds, ends[None, :], 0), axis=1) - start
    return jnp.stack([first, last]).astype(jnp.int32)


def shards(q_space, k_space, v_space, cot_space, q_time, k_time, v_time, cot_time, clip_len):
    def turned(*arrays):
        return tuple(array.transpose(0, 2, 1) for array in arrays)

    n = lax.axis_size("seq")
    window = q_time.shape[0] * n
    tokens = q_time.shape[1]
    bounds = clip_bounds(clip_len, window)
    time = turned(q_time, cot_time, k_time, v_time)
    spans = []
    head = 0
    for heads in CHUNKS:
        spans.append(slice(head * HDIM, (head + heads) * HDIM))
        head += heads
    space_in = turned(q_space, k_space, v_space, cot_space)
    packed = [list(split(time, span, n)) for span in spans]

    own = [exchange(packed[0])]
    space = frame_grads(*space_in)
    packed[1][2:], own[0][2], space = gated(packed[1][2:], own[0][2], space)
    own.append(exchange(packed[1]))
    ends = [sides(blocks) for blocks in own]
    beside = [neighbours(ends[0][0], 1), neighbours(ends[0][1], 0)]
    far = neighbours(ends[1][0], 1)
    found = list(clip_grads(bounds, own[0], beside))
    waiting = ends[1][1]
    back = [exchange(found)]
    found = clip_grads(bounds, own[1], [far, neighbours(waiting, 0)])
    back.append(exchange(found))
    grads = None
    for span, blocks in zip(spans, back):
        grads = join(blocks, span, tokens, grads)
    return turned(*space, *grads)


def solution(mesh):
    split_spec = P(("grp", "seq"), None, None)
    return jax.shard_map(
        shards,
        mesh=mesh,
        in_specs=(split_spec,) * 8 + (P(),),
        out_specs=(split_spec,) * 6,
        check_vma=False,
    )
```

```python
import functools
import math

import jax
import jax.numpy as jnp
from jax import lax
from jax.experimental import pallas as pl
from jax.experimental.pallas import tpu as pltpu
from jax.sharding import PartitionSpec as P

HEADS = 8
HDIM = 72
WIDTH = HEADS * HDIM
LANES = 128
SCALING = 1.0 / math.sqrt(HDIM)
CHUNKS = (4, 4)
masked_score = -1e30


def dot(left, right, left_dim, right_dim):
    dims = (((left_dim,), (right_dim,)), ((), ()))
    return lax.dot_general(left, right, dims, preferred_element_type=jnp.float32)


def rounded(value):
    return value.astype(jnp.bfloat16).astype(jnp.float32)


def frame_kernel(q_ref, k_ref, v_ref, g_ref, dq_ref, dk_ref, dv_ref):
    pair = 2 * HDIM
    reach = -(-HDIM // 16) * 16
    row = lax.broadcasted_iota(jnp.int32, (reach, 1), 0)
    for begin in range(0, WIDTH, pair):
        found = [[], [], []]
        for low, own in ((0, 0), (pair - reach, reach - HDIM)):
            span = slice(begin + low, begin + low + reach)
            mask = ((row >= own) & (row < own + HDIM)).astype(jnp.float32).astype(jnp.bfloat16)
            queries, keys = q_ref[0, span, :], k_ref[0, span, :]
            cotangent = g_ref[0, span, :]
            scores = dot(keys * mask, queries, 0, 0) * SCALING
            weight_grad = dot(v_ref[0, span, :] * mask, cotangent, 0, 0)
            raised = jnp.exp(scores - jnp.max(scores, axis=0, keepdims=True))
            weights = raised * (1.0 / jnp.sum(raised, axis=0, keepdims=True))
            weights_low = weights.astype(jnp.bfloat16)
            dots = jnp.sum(weights_low.astype(jnp.float32) * weight_grad, axis=0, keepdims=True)
            score_grad = (weights * (weight_grad - dots)).astype(jnp.bfloat16)
            rows = slice(own, own + HDIM)
            found[0].append(dot(keys, score_grad, 1, 0)[rows] * SCALING)
            found[1].append(dot(queries, score_grad, 1, 1)[rows] * SCALING)
            found[2].append(dot(cotangent, weights_low, 1, 1)[rows])
        for out, parts in zip((dq_ref, dk_ref, dv_ref), found):
            out[0, begin : begin + pair, :] = jnp.concatenate(parts, axis=0).astype(jnp.bfloat16)


def space_grads(queries, keys, values, cotangent):
    tokens = queries.shape[2]
    shape = jax.ShapeDtypeStruct(queries.shape, jnp.bfloat16)
    return pl.pallas_call(
        frame_kernel,
        out_shape=(shape, shape, shape),
        compiler_params=pltpu.CompilerParams(vmem_limit_bytes=60 * 2**20),
        cost_estimate=pl.CostEstimate(
            flops=12 * tokens * tokens * 256 * HEADS,
            bytes_accessed=14 * tokens * WIDTH,
            transcendentals=tokens * tokens * HEADS,
        ),
        name="space",
    )(queries, keys, values, cotangent)


def part_of(device, sharing, rows):
    row = pl.multiple_of(device % sharing * rows, 16)
    return row, pl.ds(pl.multiple_of(device // sharing * LANES, LANES), LANES)


def split_kernel(sharing, rows, span, *refs):
    ins, outs, sent = refs[:4], refs[4:-1], refs[-1]
    copies = []
    for step in far_first(len(outs)):
        row, tokens = part_of(lax.axis_index("seq") ^ step, sharing, rows)
        for i, array in enumerate(ins):
            given = array.at[0, pl.ds(span.start + row, rows), tokens]
            copies.append(pltpu.make_async_copy(given, outs[step].at[i], sent.at[step, i]))
            copies[-1].start()
    for copy in copies:
        copy.wait()


def split(arrays, span, n, sharing):
    rows = (span.stop - span.start) // sharing
    hbm = pl.BlockSpec(memory_space=pltpu.HBM)
    return pl.pallas_call(
        functools.partial(split_kernel, sharing, rows, span),
        in_specs=[hbm] * 4,
        out_specs=[hbm] * n,
        out_shape=[jax.ShapeDtypeStruct((4, rows, LANES), jnp.bfloat16)] * n,
        scratch_shapes=[pltpu.SemaphoreType.DMA((n, 4))],
        compiler_params=pltpu.CompilerParams(vmem_limit_bytes=60 * 2**20),
        name="pack",
    )(*arrays)


def far_first(n):
    return [*range(n // 2, n), *range(n // 2)]


def swap(block, axis, pairs):
    return lax.ppermute(block, axis, [(i, j) for i, j in pairs] + [(j, i) for i, j in pairs])


def exchange(blocks):
    n = len(blocks)
    moved = list(blocks)
    for step in reversed(range(1, n)):
        pairs = [[i, i ^ step] for i in range(n) if i < i ^ step]
        moved[step] = swap(blocks[step], "seq", pairs)
    return moved


def sides_kernel(n, *refs):
    ins, outs = refs[:n], refs[n:]
    is_odd = lax.axis_index("grp") & 1
    for step, ref in enumerate(ins):
        frame = lax.axis_index("seq") ^ step
        for start, out in zip((1, 0), outs):
            at = frame - jnp.where(is_odd == start, 1, 0)

            @pl.when((at >= 0) & (at < n - 1))
            def _():
                out[jnp.clip(at, 0, n - 2)] = ref[...]


def sides(blocks):
    n = len(blocks)
    shape = jax.ShapeDtypeStruct((n - 1, *blocks[0].shape), jnp.bfloat16)
    vmem = pl.BlockSpec(memory_space=pltpu.VMEM)
    return pl.pallas_call(
        functools.partial(sides_kernel, n),
        in_specs=[vmem] * n,
        out_specs=[vmem] * 2,
        out_shape=[shape] * 2,
        compiler_params=pltpu.CompilerParams(vmem_limit_bytes=24 * 2**20),
        name="sides",
    )(*blocks)


def gated(values, *earlier):
    return lax.optimization_barrier((values, *earlier))


def neighbours(block, start):
    count = lax.axis_size("grp")
    return swap(block, "grp", [(i, i + 1) for i in range(start, count - 1, 2)])


def join_kernel(sharing, span, *refs):
    outs, sent = refs[-4:-1], refs[-1]
    rows = refs[0].shape[1]
    n = sent.shape[0]
    copies = []
    for at, step in enumerate(far_first(n)):
        row, tokens = part_of(lax.axis_index("seq") ^ step, sharing, rows)
        for i, out in enumerate(outs):
            given = out.at[0, pl.ds(span.start + row, rows), tokens]
            copies.append(pltpu.make_async_copy(refs[at].at[i], given, sent.at[step, i]))
            copies[-1].start()
    for copy in copies:
        copy.wait()


def join(blocks, span, tokens, sharing, earlier):
    n = len(blocks)
    shape = jax.ShapeDtypeStruct((1, WIDTH, tokens), jnp.bfloat16)
    hbm = pl.BlockSpec(memory_space=pltpu.HBM)
    earlier = [] if earlier is None else list(earlier)
    return pl.pallas_call(
        functools.partial(join_kernel, sharing, span),
        in_specs=[pl.BlockSpec(memory_space=pltpu.VMEM)] * n + [hbm] * len(earlier),
        out_specs=[hbm] * 3,
        out_shape=[shape] * 3,
        scratch_shapes=[pltpu.SemaphoreType.DMA((n, 3))],
        input_output_aliases={n + i: i for i in range(len(earlier))},
        compiler_params=pltpu.CompilerParams(vmem_limit_bytes=24 * 2**20),
        name="unpack",
    )(*(blocks[step] for step in far_first(n)), *earlier)


def clip_kernel(window, heads, given_bounds, *refs):
    own, sides_of = refs[:window], refs[window : window + 2]
    outs, refs = refs[window + 2 : 2 * window + 2], refs[2 * window + 2 :]
    wide, score_ref, grad_ref, weight_ref, found, bounds, arrived = refs
    copy = pltpu.make_async_copy(given_bounds, bounds, arrived)
    copy.start()
    halo = window - 1
    extent = window + 2 * halo
    queries, keys, values, cotangent = range(4)

    def widen(ref, frame):
        for i in range(4):
            wide[i, frame] = ref[i].astype(jnp.float32)

    for step, ref in enumerate(own):
        widen(ref, halo + (lax.axis_index("seq") ^ step))
    copy.wait()
    lowest, highest = bounds[0, halo], bounds[1, halo + window - 1]
    for start, ref in zip((1, 0), sides_of):
        is_next = (lax.axis_index("grp") & 1) == start
        for at in range(halo):
            frame = at + jnp.where(is_next, halo + window, 0)
            needed = (frame >= lowest) & (frame < highest)
            pl.when(needed)(functools.partial(widen, ref.at[at], frame))

    def partners(frame):
        first, last = bounds[0, frame], bounds[1, frame]
        return first, last - first, [jnp.minimum(first + t, last - 1) for t in range(window)]

    def products(frame, carry):
        first, count, others = partners(frame)
        scores, grads = [[] for _ in others], [[] for _ in others]
        for head in range(heads):
            span = slice(head * HDIM, (head + 1) * HDIM)
            query, cot = wide[queries, frame, span, :], wide[cotangent, frame, span, :]
            for t, other in enumerate(others):
                score = jnp.sum(query * wide[keys, other, span, :], axis=0, keepdims=True)
                grad = jnp.sum(cot * wide[values, other, span, :], axis=0, keepdims=True)
                scores[t].append(score)
                grads[t].append(grad)
        for t in range(window):
            bias = jnp.where(t < count, 0.0, masked_score)
            score_ref[t, frame] = jnp.concatenate(scores[t], axis=0) * SCALING + bias
            grad_ref[t, frame] = jnp.concatenate(grads[t], axis=0)
        return carry

    lax.fori_loop(lowest, highest, products, 0)
    scores, grads = [score_ref[t] for t in range(window)], [grad_ref[t] for t in range(window)]
    peak = functools.reduce(jnp.maximum, scores)
    raised = [jnp.exp(score - peak) for score in scores]
    inverse = 1.0 / functools.reduce(jnp.add, raised)
    weights = [part * inverse for part in raised]
    weights_low = [rounded(part) for part in weights]
    dots = functools.reduce(jnp.add, [w * d for w, d in zip(weights_low, grads)])
    for t in range(window):
        weight_ref[t] = weights_low[t]
        score_ref[t] = rounded(weights[t] * (grads[t] - dots))

    def gradients(at, carry):
        frame = halo + at
        first, count, others = partners(frame)
        place = frame - first
        sums = [[], [], []]
        for head in range(heads):
            span, row = slice(head * HDIM, (head + 1) * HDIM), slice(head, head + 1)
            totals = [None] * 3
            for t, other in enumerate(others):
                score_back = jnp.where(t < count, score_ref[place, other, row, :], 0.0)
                weight_back = jnp.where(t < count, weight_ref[place, other, row, :], 0.0)
                terms = (
                    score_ref[t, frame, row, :] * wide[keys, other, span, :],
                    score_back * wide[queries, other, span, :],
                    weight_back * wide[cotangent, other, span, :],
                )
                totals = [x if y is None else y + x for x, y in zip(terms, totals)]
            for held, total, scale in zip(sums, totals, (SCALING, SCALING, None)):
                held.append(total if scale is None else total * scale)
        for i, parts in enumerate(sums):
            found[at, i] = jnp.concatenate(parts, axis=0).astype(jnp.bfloat16)
        return carry

    lax.fori_loop(0, window, gradients, 0)
    for step, out in enumerate(outs):
        out[...] = found[lax.axis_index("seq") ^ step]


def clip_grads(bounds, own, beside):
    window = len(own)
    _, rows, lanes = own[0].shape
    heads = rows // HDIM
    extent = 3 * window - 2
    vmem = pl.BlockSpec(memory_space=pltpu.VMEM)
    shape = (3, rows, lanes)
    slots = pltpu.VMEM((window, extent, heads, lanes), jnp.float32)
    return pl.pallas_call(
        functools.partial(clip_kernel, window, heads),
        out_shape=[jax.ShapeDtypeStruct(shape, jnp.bfloat16)] * window,
        in_specs=[pl.BlockSpec(memory_space=pl.ANY)] + [vmem] * (window + 2),
        out_specs=[vmem] * window,
        scratch_shapes=[
            pltpu.VMEM((4, extent, rows, lanes), jnp.float32),
            slots,
            slots,
            slots,
            pltpu.VMEM((window, *shape), jnp.bfloat16),
            pltpu.SMEM(bounds.shape, jnp.int32),
            pltpu.SemaphoreType.DMA,
        ],
        compiler_params=pltpu.CompilerParams(vmem_limit_bytes=48 * 2**20),
        cost_estimate=pl.CostEstimate(
            flops=800 * extent * window * rows * lanes,
            bytes_accessed=2 * sum(block.size for block in (*own, *beside)),
            transcendentals=extent * window * heads * lanes,
        ),
        name="clips",
    )(bounds, *own, *beside)


def clip_bounds(clip_len, window):
    halo = window - 1
    extent = window + 2 * halo
    start = lax.axis_index("grp") * window - halo
    frames = start + jnp.arange(extent, dtype=jnp.int32)
    order = jnp.arange(clip_len.shape[0])
    ends = jnp.sum(jnp.where(order[:, None] <= order[None, :], clip_len[:, None], 0), axis=0)
    begins = ends - clip_len
    holds = (begins[None, :] <= frames[:, None]) & (frames[:, None] < ends[None, :])
    first = jnp.sum(jnp.where(holds, begins[None, :], 0), axis=1) - start
    last = jnp.sum(jnp.where(holds, ends[None, :], 0), axis=1) - start
    return jnp.stack([first, last]).astype(jnp.int32)


def tile_shards(q_space, k_space, v_space, cot_space, q_time, k_time, v_time, cot_time, clip_len):
    def turned(*arrays):
        return tuple(array.transpose(0, 2, 1) for array in arrays)

    n = lax.axis_size("seq")
    window = q_time.shape[0] * n
    tokens = q_time.shape[1]
    sharing = n * LANES // tokens
    bounds = clip_bounds(clip_len, window)
    time = turned(q_time, k_time, v_time, cot_time)
    spans = []
    head = 0
    for heads in CHUNKS:
        spans.append(slice(head * HDIM, (head + heads) * HDIM))
        head += heads
    space_in = turned(q_space, k_space, v_space, cot_space)
    packed = [list(split(time, span, n, sharing)) for span in spans]
    own = [exchange(packed[0])]
    space = space_grads(*space_in)
    packed[1][2:], own[0][2], space = gated(packed[1][2:], own[0][2], space)
    own.append(exchange(packed[1]))
    beside = [
        [neighbours(ends, start) for ends, start in zip(sides(blocks), (1, 0))] for blocks in own
    ]
    back, grads = [], None
    for blocks, near in zip(own, beside):
        back.append(exchange(clip_grads(bounds, blocks, near)))
    for span, blocks in zip(spans, back):
        grads = join(blocks, span, tokens, sharing, grads)
    return turned(*space, *grads)


def whole_tiles(mesh, tokens):
    n = mesh.shape["seq"]
    sharing = n * LANES // tokens
    return (
        tokens % LANES == 0
        and n % 4 == 0
        and n & (n - 1) == 0
        and sharing * tokens == n * LANES
        and all(heads % sharing == 0 and heads // sharing * HDIM % 16 == 0 for heads in CHUNKS)
    )


def padded(block, sides, width):
    for axis, dim in sides:
        count = lax.axis_size(axis)
        forward = [(i, i + 1) for i in range(count - 1)]
        backward = [(target, source) for source, target in forward]
        low = lax.ppermute(
            lax.slice_in_dim(block, block.shape[dim] - width, None, axis=dim), axis, forward
        )
        high = lax.ppermute(lax.slice_in_dim(block, 0, width, axis=dim), axis, backward)
        block = jnp.concatenate([low, block, high], axis=dim)
    return block


def shifted(value, axis, by):
    count = lax.axis_size(axis)
    pairs = [(i, i + by) for i in range(count) if 0 <= i + by < count]
    return lax.ppermute(value, axis, pairs)


def clip_labels(clip_len, first_frame, count, frame_total):
    frame_ids = first_frame + jnp.arange(count, dtype=jnp.int32)
    clip_ends = jnp.cumsum(clip_len)
    labels = jnp.sum((clip_ends[None, :] <= frame_ids[:, None]).astype(jnp.int32), axis=1)
    inside = (frame_ids >= 0) & (frame_ids < frame_total)
    return (labels, inside)


def frame_grads(queries, keys, values, cotangent):
    scaling = 1.0 / math.sqrt(HDIM)
    tokens = queries.shape[0]
    q_heads = queries.reshape(tokens, HEADS, HDIM)
    k_heads = keys.reshape(tokens, HEADS, HDIM)
    v_heads = values.reshape(tokens, HEADS, HDIM)
    g_heads = cotangent.reshape(tokens, HEADS, HDIM)
    scores = (
        jnp.einsum("qhd,khd->hqk", q_heads, k_heads, preferred_element_type=jnp.float32) * scaling
    )
    row_max = jnp.max(scores, axis=-1, keepdims=True)
    log_total = row_max + jnp.log(jnp.sum(jnp.exp(scores - row_max), axis=-1, keepdims=True))
    weights = jnp.exp(scores - log_total)
    weights_low = weights.astype(jnp.bfloat16)
    attended = jnp.einsum("hqk,khd->qhd", weights_low, v_heads, preferred_element_type=jnp.float32)
    row_dot = jnp.einsum("qhd,qhd->hq", g_heads.astype(jnp.float32), attended)
    weight_grad = jnp.einsum("qhd,khd->hqk", g_heads, v_heads, preferred_element_type=jnp.float32)
    score_grad = (weights * (weight_grad - row_dot[:, :, None])).astype(jnp.bfloat16)
    grad_query = (
        jnp.einsum("hqk,khd->qhd", score_grad, k_heads, preferred_element_type=jnp.float32)
        * scaling
    )
    grad_key = (
        jnp.einsum("hqk,qhd->khd", score_grad, q_heads, preferred_element_type=jnp.float32)
        * scaling
    )
    grad_value = jnp.einsum(
        "hqk,qhd->khd", weights_low, g_heads, preferred_element_type=jnp.float32
    )
    flat_shape = (1, tokens, HEADS * HDIM)
    return (
        grad_query.reshape(flat_shape).astype(jnp.bfloat16),
        grad_key.reshape(flat_shape).astype(jnp.bfloat16),
        grad_value.reshape(flat_shape).astype(jnp.bfloat16),
    )


def shards(q_space, k_space, v_space, cot_space, q_time, k_time, v_time, cot_time, clip_len):
    scaling = 1.0 / math.sqrt(HDIM)
    grad_qs, grad_ks, grad_vs = frame_grads(q_space[0], k_space[0], v_space[0], cot_space[0])
    moved = (
        lax.all_to_all(q_time, "seq", split_axis=1, concat_axis=0, tiled=True),
        lax.all_to_all(k_time, "seq", split_axis=1, concat_axis=0, tiled=True),
        lax.all_to_all(v_time, "seq", split_axis=1, concat_axis=0, tiled=True),
        lax.all_to_all(cot_time, "seq", split_axis=1, concat_axis=0, tiled=True),
    )
    query_win, key_win, value_win, cot_win = moved
    window = query_win.shape[0]
    places = query_win.shape[1]
    channels = query_win.shape[2]
    group_id = lax.axis_index("grp")
    frame_total = window * lax.axis_size("grp")
    first_frame = group_id * window

    def split_heads(array):
        return array.reshape(array.shape[0], places, HEADS, HDIM)

    key_pair = padded(jnp.stack([key_win, value_win]), (("grp", 1),), window)
    q_own = split_heads(query_win)
    g_own = split_heads(cot_win)
    k_ext = split_heads(key_pair[0])
    v_ext = split_heads(key_pair[1])
    own_label, own_inside = clip_labels(clip_len, first_frame, window, frame_total)
    ext_label, ext_inside = clip_labels(clip_len, first_frame - window, 3 * window, frame_total)
    allowed = (own_label[:, None] == ext_label[None, :]) & ext_inside[None, :]
    scores = (
        jnp.einsum("iphd,jphd->phij", q_own, k_ext, preferred_element_type=jnp.float32) * scaling
    )
    scores = jnp.where(allowed, scores, masked_score)
    row_max = jnp.max(scores, axis=-1)
    log_total = row_max + jnp.log(jnp.sum(jnp.exp(scores - row_max[..., None]), axis=-1))
    weights = jnp.where(allowed, jnp.exp(scores - log_total[..., None]), 0.0)
    weights_low = weights.astype(jnp.bfloat16)
    attended = jnp.einsum("phij,jphd->iphd", weights_low, v_ext, preferred_element_type=jnp.float32)
    row_dot = jnp.einsum("iphd,iphd->phi", g_own.astype(jnp.float32), attended)
    weight_grad = jnp.einsum("iphd,jphd->phij", g_own, v_ext, preferred_element_type=jnp.float32)
    score_grad = (weights * (weight_grad - row_dot[..., None])).astype(jnp.bfloat16)
    grad_query = (
        jnp.einsum("phij,jphd->iphd", score_grad, k_ext, preferred_element_type=jnp.float32)
        * scaling
    )
    key_terms = (
        jnp.einsum("phij,iphd->jphd", score_grad, q_own, preferred_element_type=jnp.float32)
        * scaling
    )
    value_terms = jnp.einsum(
        "phij,iphd->jphd", weights_low, g_own, preferred_element_type=jnp.float32
    )
    both_terms = jnp.stack([key_terms, value_terms]).reshape(2, 3 * window, places, channels)
    from_after = shifted(both_terms[:, :window], "grp", -1)
    from_before = shifted(both_terms[:, 2 * window :], "grp", 1)
    summed = both_terms[:, window : 2 * window] + from_after + from_before
    grad_key = summed[0]
    grad_value = summed[1]
    grad_qt, grad_kt, grad_vt = (
        lax.all_to_all(
            grad_query.reshape(window, places, channels).astype(jnp.bfloat16),
            "seq",
            split_axis=0,
            concat_axis=1,
            tiled=True,
        ),
        lax.all_to_all(
            grad_key.astype(jnp.bfloat16), "seq", split_axis=0, concat_axis=1, tiled=True
        ),
        lax.all_to_all(
            grad_value.astype(jnp.bfloat16), "seq", split_axis=0, concat_axis=1, tiled=True
        ),
    )
    return (grad_qs, grad_ks, grad_vs, grad_qt, grad_kt, grad_vt)


def solution(mesh):
    split_spec = P(("grp", "seq"), None, None)

    def mapped(body):
        return jax.shard_map(
            body,
            mesh=mesh,
            in_specs=(split_spec,) * 8 + (P(),),
            out_specs=(split_spec,) * 6,
            check_vma=False,
        )

    def grads(*arrays):
        return mapped(tile_shards if whole_tiles(mesh, arrays[0].shape[1]) else shards)(*arrays)

    return grads
```

```python
import functools
import math

import jax
import jax.numpy as jnp
from jax import lax
from jax.experimental import pallas as pl
from jax.experimental.pallas import tpu as pltpu
from jax.sharding import PartitionSpec as P

HEADS = 8
HDIM = 72
WIDTH = HEADS * HDIM
LANES = 128
SCALING = 1.0 / math.sqrt(HDIM)
CHUNKS = (4, 4)
masked_score = -1e30


def dot(left, right, left_dim, right_dim):
    dims = (((left_dim,), (right_dim,)), ((), ()))
    return lax.dot_general(left, right, dims, preferred_element_type=jnp.float32)


def rounded(value):
    return value.astype(jnp.bfloat16).astype(jnp.float32)


def frame_kernel(q_ref, k_ref, v_ref, g_ref, dq_ref, dk_ref, dv_ref):
    pair = 2 * HDIM
    reach = -(-HDIM // 16) * 16
    row = lax.broadcasted_iota(jnp.int32, (reach, 1), 0)
    for begin in range(0, WIDTH, pair):
        found = [[], [], []]
        for low, own in ((0, 0), (pair - reach, reach - HDIM)):
            span = slice(begin + low, begin + low + reach)
            mask = ((row >= own) & (row < own + HDIM)).astype(jnp.float32).astype(jnp.bfloat16)
            queries, keys = q_ref[0, span, :], k_ref[0, span, :]
            cotangent = g_ref[0, span, :]
            scores = dot(keys * mask, queries, 0, 0) * SCALING
            weight_grad = dot(v_ref[0, span, :] * mask, cotangent, 0, 0)
            raised = jnp.exp(scores - jnp.max(scores, axis=0, keepdims=True))
            weights = raised * (1.0 / jnp.sum(raised, axis=0, keepdims=True))
            weights_low = weights.astype(jnp.bfloat16)
            dots = jnp.sum(weights_low.astype(jnp.float32) * weight_grad, axis=0, keepdims=True)
            score_grad = (weights * (weight_grad - dots)).astype(jnp.bfloat16)
            rows = slice(own, own + HDIM)
            found[0].append(dot(keys, score_grad, 1, 0)[rows] * SCALING)
            found[1].append(dot(queries, score_grad, 1, 1)[rows] * SCALING)
            found[2].append(dot(cotangent, weights_low, 1, 1)[rows])
        for out, parts in zip((dq_ref, dk_ref, dv_ref), found):
            out[0, begin : begin + pair, :] = jnp.concatenate(parts, axis=0).astype(jnp.bfloat16)


def space_grads(queries, keys, values, cotangent):
    tokens = queries.shape[2]
    shape = jax.ShapeDtypeStruct(queries.shape, jnp.bfloat16)
    return pl.pallas_call(
        frame_kernel,
        out_shape=(shape, shape, shape),
        compiler_params=pltpu.CompilerParams(vmem_limit_bytes=60 * 2**20),
        cost_estimate=pl.CostEstimate(
            flops=12 * tokens * tokens * 256 * HEADS,
            bytes_accessed=14 * tokens * WIDTH,
            transcendentals=tokens * tokens * HEADS,
        ),
        name="space",
    )(queries, keys, values, cotangent)


def part_of(device, sharing, rows):
    row = pl.multiple_of(device % sharing * rows, 16)
    return row, pl.ds(pl.multiple_of(device // sharing * LANES, LANES), LANES)


def split_kernel(sharing, rows, span, *refs):
    ins, outs, (held, arrived, sent) = refs[:4], refs[4:-3], refs[-3:]
    loads, stores = {}, []
    for step in far_first(len(outs)):
        row, tokens = part_of(lax.axis_index("seq") ^ step, sharing, rows)
        for i, array in enumerate(ins):
            given = array.at[0, pl.ds(span.start + row, rows), tokens]
            loads[step, i] = pltpu.make_async_copy(given, held.at[step, i], arrived.at[step, i])
            loads[step, i].start()
    for step in far_first(len(outs)):
        for i in range(len(ins)):
            loads[step, i].wait()
        stores.append(pltpu.make_async_copy(held.at[step], outs[step], sent.at[step]))
        stores[-1].start()
    for copy in stores:
        copy.wait()


def split(arrays, span, n, sharing):
    rows = (span.stop - span.start) // sharing
    hbm = pl.BlockSpec(memory_space=pltpu.HBM)
    return pl.pallas_call(
        functools.partial(split_kernel, sharing, rows, span),
        in_specs=[hbm] * 4,
        out_specs=[hbm] * n,
        out_shape=[jax.ShapeDtypeStruct((4, rows, LANES), jnp.bfloat16)] * n,
        scratch_shapes=[
            pltpu.VMEM((n, 4, rows, LANES), jnp.bfloat16),
            pltpu.SemaphoreType.DMA((n, 4)),
            pltpu.SemaphoreType.DMA((n,)),
        ],
        compiler_params=pltpu.CompilerParams(vmem_limit_bytes=60 * 2**20),
        name="pack",
    )(*arrays)


def far_first(n):
    return [*range(n // 2, n), *range(n // 2)]


def swap(block, axis, pairs):
    return lax.ppermute(block, axis, [(i, j) for i, j in pairs] + [(j, i) for i, j in pairs])


def exchange(blocks):
    n = len(blocks)
    moved = list(blocks)
    for step in reversed(range(1, n)):
        pairs = [[i, i ^ step] for i in range(n) if i < i ^ step]
        moved[step] = swap(blocks[step], "seq", pairs)
    return moved


def sides_kernel(n, *refs):
    ins, outs = refs[:n], refs[n:]
    is_odd = lax.axis_index("grp") & 1
    for step, ref in enumerate(ins):
        frame = lax.axis_index("seq") ^ step
        for start, out in zip((1, 0), outs):
            at = frame - jnp.where(is_odd == start, 1, 0)

            @pl.when((at >= 0) & (at < n - 1))
            def _():
                out[jnp.clip(at, 0, n - 2)] = ref[...]


def sides(blocks):
    n = len(blocks)
    shape = jax.ShapeDtypeStruct((n - 1, *blocks[0].shape), jnp.bfloat16)
    vmem = pl.BlockSpec(memory_space=pltpu.VMEM)
    return pl.pallas_call(
        functools.partial(sides_kernel, n),
        in_specs=[vmem] * n,
        out_specs=[vmem] * 2,
        out_shape=[shape] * 2,
        compiler_params=pltpu.CompilerParams(vmem_limit_bytes=24 * 2**20),
        name="sides",
    )(*blocks)


def gated(values, *earlier):
    return lax.optimization_barrier((values, *earlier))


def neighbours(block, start):
    count = lax.axis_size("grp")
    return swap(block, "grp", [(i, i + 1) for i in range(start, count - 1, 2)])


def join_kernel(sharing, span, *refs):
    outs, sent = refs[-4:-1], refs[-1]
    rows = refs[0].shape[1]
    n = sent.shape[0]
    copies = []
    for at, step in enumerate(far_first(n)):
        row, tokens = part_of(lax.axis_index("seq") ^ step, sharing, rows)
        for i, out in enumerate(outs):
            given = out.at[0, pl.ds(span.start + row, rows), tokens]
            copies.append(pltpu.make_async_copy(refs[at].at[i], given, sent.at[step, i]))
            copies[-1].start()
    for copy in copies:
        copy.wait()


def join(blocks, span, tokens, sharing, earlier):
    n = len(blocks)
    shape = jax.ShapeDtypeStruct((1, WIDTH, tokens), jnp.bfloat16)
    hbm = pl.BlockSpec(memory_space=pltpu.HBM)
    earlier = [] if earlier is None else list(earlier)
    return pl.pallas_call(
        functools.partial(join_kernel, sharing, span),
        in_specs=[pl.BlockSpec(memory_space=pltpu.VMEM)] * n + [hbm] * len(earlier),
        out_specs=[hbm] * 3,
        out_shape=[shape] * 3,
        scratch_shapes=[pltpu.SemaphoreType.DMA((n, 3))],
        input_output_aliases={n + i: i for i in range(len(earlier))},
        compiler_params=pltpu.CompilerParams(vmem_limit_bytes=24 * 2**20),
        name="unpack",
    )(*(blocks[step] for step in far_first(n)), *earlier)


def clip_kernel(window, heads, given_bounds, *refs):
    own, sides_of = refs[:window], refs[window : window + 2]
    outs, refs = refs[window + 2 : 2 * window + 2], refs[2 * window + 2 :]
    wide, score_ref, grad_ref, weight_ref, found, bounds, arrived = refs
    copy = pltpu.make_async_copy(given_bounds, bounds, arrived)
    copy.start()
    halo = window - 1
    extent = window + 2 * halo
    queries, keys, values, cotangent = range(4)

    def widen(ref, frame):
        for i in range(4):
            wide[i, frame] = ref[i].astype(jnp.float32)

    for step, ref in enumerate(own):
        widen(ref, halo + (lax.axis_index("seq") ^ step))
    copy.wait()
    lowest, highest = bounds[0, halo], bounds[1, halo + window - 1]
    for start, ref in zip((1, 0), sides_of):
        is_next = (lax.axis_index("grp") & 1) == start
        for at in range(halo):
            frame = at + jnp.where(is_next, halo + window, 0)
            needed = (frame >= lowest) & (frame < highest)
            pl.when(needed)(functools.partial(widen, ref.at[at], frame))

    def partners(frame):
        first, last = bounds[0, frame], bounds[1, frame]
        return first, last - first, [jnp.minimum(first + t, last - 1) for t in range(window)]

    def products(frame, carry):
        first, count, others = partners(frame)
        scores, grads = [[] for _ in others], [[] for _ in others]
        for head in range(heads):
            span = slice(head * HDIM, (head + 1) * HDIM)
            query, cot = wide[queries, frame, span, :], wide[cotangent, frame, span, :]
            for t, other in enumerate(others):
                score = jnp.sum(query * wide[keys, other, span, :], axis=0, keepdims=True)
                grad = jnp.sum(cot * wide[values, other, span, :], axis=0, keepdims=True)
                scores[t].append(score)
                grads[t].append(grad)
        for t in range(window):
            bias = jnp.where(t < count, 0.0, masked_score)
            score_ref[t, frame] = jnp.concatenate(scores[t], axis=0) * SCALING + bias
            grad_ref[t, frame] = jnp.concatenate(grads[t], axis=0)
        return carry

    lax.fori_loop(lowest, highest, products, 0)
    scores, grads = [score_ref[t] for t in range(window)], [grad_ref[t] for t in range(window)]
    peak = functools.reduce(jnp.maximum, scores)
    raised = [jnp.exp(score - peak) for score in scores]
    inverse = 1.0 / functools.reduce(jnp.add, raised)
    weights = [part * inverse for part in raised]
    weights_low = [rounded(part) for part in weights]
    dots = functools.reduce(jnp.add, [w * d for w, d in zip(weights_low, grads)])
    for t in range(window):
        weight_ref[t] = weights_low[t]
        score_ref[t] = rounded(weights[t] * (grads[t] - dots))

    def gradients(at, carry):
        frame = halo + at
        first, count, others = partners(frame)
        place = frame - first
        sums = [[], [], []]
        for head in range(heads):
            span, row = slice(head * HDIM, (head + 1) * HDIM), slice(head, head + 1)
            totals = [None] * 3
            for t, other in enumerate(others):
                score_back = jnp.where(t < count, score_ref[place, other, row, :], 0.0)
                weight_back = jnp.where(t < count, weight_ref[place, other, row, :], 0.0)
                terms = (
                    score_ref[t, frame, row, :] * wide[keys, other, span, :],
                    score_back * wide[queries, other, span, :],
                    weight_back * wide[cotangent, other, span, :],
                )
                totals = [x if y is None else y + x for x, y in zip(terms, totals)]
            for held, total, scale in zip(sums, totals, (SCALING, SCALING, None)):
                held.append(total if scale is None else total * scale)
        for i, parts in enumerate(sums):
            found[at, i] = jnp.concatenate(parts, axis=0).astype(jnp.bfloat16)
        return carry

    lax.fori_loop(0, window, gradients, 0)
    for step, out in enumerate(outs):
        out[...] = found[lax.axis_index("seq") ^ step]


def clip_grads(bounds, own, beside):
    window = len(own)
    _, rows, lanes = own[0].shape
    heads = rows // HDIM
    extent = 3 * window - 2
    vmem = pl.BlockSpec(memory_space=pltpu.VMEM)
    shape = (3, rows, lanes)
    slots = pltpu.VMEM((window, extent, heads, lanes), jnp.float32)
    return pl.pallas_call(
        functools.partial(clip_kernel, window, heads),
        out_shape=[jax.ShapeDtypeStruct(shape, jnp.bfloat16)] * window,
        in_specs=[pl.BlockSpec(memory_space=pl.ANY)] + [vmem] * (window + 2),
        out_specs=[vmem] * window,
        scratch_shapes=[
            pltpu.VMEM((4, extent, rows, lanes), jnp.float32),
            slots,
            slots,
            slots,
            pltpu.VMEM((window, *shape), jnp.bfloat16),
            pltpu.SMEM(bounds.shape, jnp.int32),
            pltpu.SemaphoreType.DMA,
        ],
        compiler_params=pltpu.CompilerParams(vmem_limit_bytes=48 * 2**20),
        cost_estimate=pl.CostEstimate(
            flops=800 * extent * window * rows * lanes,
            bytes_accessed=2 * sum(block.size for block in (*own, *beside)),
            transcendentals=extent * window * heads * lanes,
        ),
        name="clips",
    )(bounds, *own, *beside)


def clip_bounds(clip_len, window):
    halo = window - 1
    extent = window + 2 * halo
    start = lax.axis_index("grp") * window - halo
    frames = start + jnp.arange(extent, dtype=jnp.int32)
    order = jnp.arange(clip_len.shape[0])
    ends = jnp.sum(jnp.where(order[:, None] <= order[None, :], clip_len[:, None], 0), axis=0)
    begins = ends - clip_len
    holds = (begins[None, :] <= frames[:, None]) & (frames[:, None] < ends[None, :])
    first = jnp.sum(jnp.where(holds, begins[None, :], 0), axis=1) - start
    last = jnp.sum(jnp.where(holds, ends[None, :], 0), axis=1) - start
    return jnp.stack([first, last]).astype(jnp.int32)


def tile_shards(q_space, k_space, v_space, cot_space, q_time, k_time, v_time, cot_time, clip_len):
    def turned(*arrays):
        return tuple(array.transpose(0, 2, 1) for array in arrays)

    n = lax.axis_size("seq")
    window = q_time.shape[0] * n
    tokens = q_time.shape[1]
    sharing = n * LANES // tokens
    bounds = clip_bounds(clip_len, window)
    time = turned(q_time, k_time, v_time, cot_time)
    spans = []
    head = 0
    for heads in CHUNKS:
        spans.append(slice(head * HDIM, (head + heads) * HDIM))
        head += heads
    space_in = turned(q_space, k_space, v_space, cot_space)
    packed = [list(split(time, span, n, sharing)) for span in spans]
    own = [exchange(packed[0])]
    space = space_grads(*space_in)
    packed[1][2:], own[0][2], space = gated(packed[1][2:], own[0][2], space)
    own.append(exchange(packed[1]))
    beside = [
        [neighbours(ends, start) for ends, start in zip(sides(blocks), (1, 0))] for blocks in own
    ]
    back, grads = [], None
    for blocks, near in zip(own, beside):
        back.append(exchange(clip_grads(bounds, blocks, near)))
    for span, blocks in zip(spans, back):
        grads = join(blocks, span, tokens, sharing, grads)
    return turned(*space, *grads)


def whole_tiles(mesh, tokens):
    n = mesh.shape["seq"]
    sharing = n * LANES // tokens
    return (
        tokens % LANES == 0
        and n % 4 == 0
        and n & (n - 1) == 0
        and sharing * tokens == n * LANES
        and all(heads % sharing == 0 and heads // sharing * HDIM % 16 == 0 for heads in CHUNKS)
    )


def padded(block, sides, width):
    for axis, dim in sides:
        count = lax.axis_size(axis)
        forward = [(i, i + 1) for i in range(count - 1)]
        backward = [(target, source) for source, target in forward]
        low = lax.ppermute(
            lax.slice_in_dim(block, block.shape[dim] - width, None, axis=dim), axis, forward
        )
        high = lax.ppermute(lax.slice_in_dim(block, 0, width, axis=dim), axis, backward)
        block = jnp.concatenate([low, block, high], axis=dim)
    return block


def shifted(value, axis, by):
    count = lax.axis_size(axis)
    pairs = [(i, i + by) for i in range(count) if 0 <= i + by < count]
    return lax.ppermute(value, axis, pairs)


def clip_labels(clip_len, first_frame, count, frame_total):
    frame_ids = first_frame + jnp.arange(count, dtype=jnp.int32)
    clip_ends = jnp.cumsum(clip_len)
    labels = jnp.sum((clip_ends[None, :] <= frame_ids[:, None]).astype(jnp.int32), axis=1)
    inside = (frame_ids >= 0) & (frame_ids < frame_total)
    return (labels, inside)


def frame_grads(queries, keys, values, cotangent):
    scaling = 1.0 / math.sqrt(HDIM)
    tokens = queries.shape[0]
    q_heads = queries.reshape(tokens, HEADS, HDIM)
    k_heads = keys.reshape(tokens, HEADS, HDIM)
    v_heads = values.reshape(tokens, HEADS, HDIM)
    g_heads = cotangent.reshape(tokens, HEADS, HDIM)
    scores = (
        jnp.einsum("qhd,khd->hqk", q_heads, k_heads, preferred_element_type=jnp.float32) * scaling
    )
    row_max = jnp.max(scores, axis=-1, keepdims=True)
    log_total = row_max + jnp.log(jnp.sum(jnp.exp(scores - row_max), axis=-1, keepdims=True))
    weights = jnp.exp(scores - log_total)
    weights_low = weights.astype(jnp.bfloat16)
    attended = jnp.einsum("hqk,khd->qhd", weights_low, v_heads, preferred_element_type=jnp.float32)
    row_dot = jnp.einsum("qhd,qhd->hq", g_heads.astype(jnp.float32), attended)
    weight_grad = jnp.einsum("qhd,khd->hqk", g_heads, v_heads, preferred_element_type=jnp.float32)
    score_grad = (weights * (weight_grad - row_dot[:, :, None])).astype(jnp.bfloat16)
    grad_query = (
        jnp.einsum("hqk,khd->qhd", score_grad, k_heads, preferred_element_type=jnp.float32)
        * scaling
    )
    grad_key = (
        jnp.einsum("hqk,qhd->khd", score_grad, q_heads, preferred_element_type=jnp.float32)
        * scaling
    )
    grad_value = jnp.einsum(
        "hqk,qhd->khd", weights_low, g_heads, preferred_element_type=jnp.float32
    )
    flat_shape = (1, tokens, HEADS * HDIM)
    return (
        grad_query.reshape(flat_shape).astype(jnp.bfloat16),
        grad_key.reshape(flat_shape).astype(jnp.bfloat16),
        grad_value.reshape(flat_shape).astype(jnp.bfloat16),
    )


def shards(q_space, k_space, v_space, cot_space, q_time, k_time, v_time, cot_time, clip_len):
    scaling = 1.0 / math.sqrt(HDIM)
    grad_qs, grad_ks, grad_vs = frame_grads(q_space[0], k_space[0], v_space[0], cot_space[0])
    moved = (
        lax.all_to_all(q_time, "seq", split_axis=1, concat_axis=0, tiled=True),
        lax.all_to_all(k_time, "seq", split_axis=1, concat_axis=0, tiled=True),
        lax.all_to_all(v_time, "seq", split_axis=1, concat_axis=0, tiled=True),
        lax.all_to_all(cot_time, "seq", split_axis=1, concat_axis=0, tiled=True),
    )
    query_win, key_win, value_win, cot_win = moved
    window = query_win.shape[0]
    places = query_win.shape[1]
    channels = query_win.shape[2]
    group_id = lax.axis_index("grp")
    frame_total = window * lax.axis_size("grp")
    first_frame = group_id * window

    def split_heads(array):
        return array.reshape(array.shape[0], places, HEADS, HDIM)

    key_pair = padded(jnp.stack([key_win, value_win]), (("grp", 1),), window)
    q_own = split_heads(query_win)
    g_own = split_heads(cot_win)
    k_ext = split_heads(key_pair[0])
    v_ext = split_heads(key_pair[1])
    own_label, own_inside = clip_labels(clip_len, first_frame, window, frame_total)
    ext_label, ext_inside = clip_labels(clip_len, first_frame - window, 3 * window, frame_total)
    allowed = (own_label[:, None] == ext_label[None, :]) & ext_inside[None, :]
    scores = (
        jnp.einsum("iphd,jphd->phij", q_own, k_ext, preferred_element_type=jnp.float32) * scaling
    )
    scores = jnp.where(allowed, scores, masked_score)
    row_max = jnp.max(scores, axis=-1)
    log_total = row_max + jnp.log(jnp.sum(jnp.exp(scores - row_max[..., None]), axis=-1))
    weights = jnp.where(allowed, jnp.exp(scores - log_total[..., None]), 0.0)
    weights_low = weights.astype(jnp.bfloat16)
    attended = jnp.einsum("phij,jphd->iphd", weights_low, v_ext, preferred_element_type=jnp.float32)
    row_dot = jnp.einsum("iphd,iphd->phi", g_own.astype(jnp.float32), attended)
    weight_grad = jnp.einsum("iphd,jphd->phij", g_own, v_ext, preferred_element_type=jnp.float32)
    score_grad = (weights * (weight_grad - row_dot[..., None])).astype(jnp.bfloat16)
    grad_query = (
        jnp.einsum("phij,jphd->iphd", score_grad, k_ext, preferred_element_type=jnp.float32)
        * scaling
    )
    key_terms = (
        jnp.einsum("phij,iphd->jphd", score_grad, q_own, preferred_element_type=jnp.float32)
        * scaling
    )
    value_terms = jnp.einsum(
        "phij,iphd->jphd", weights_low, g_own, preferred_element_type=jnp.float32
    )
    both_terms = jnp.stack([key_terms, value_terms]).reshape(2, 3 * window, places, channels)
    from_after = shifted(both_terms[:, :window], "grp", -1)
    from_before = shifted(both_terms[:, 2 * window :], "grp", 1)
    summed = both_terms[:, window : 2 * window] + from_after + from_before
    grad_key = summed[0]
    grad_value = summed[1]
    grad_qt, grad_kt, grad_vt = (
        lax.all_to_all(
            grad_query.reshape(window, places, channels).astype(jnp.bfloat16),
            "seq",
            split_axis=0,
            concat_axis=1,
            tiled=True,
        ),
        lax.all_to_all(
            grad_key.astype(jnp.bfloat16), "seq", split_axis=0, concat_axis=1, tiled=True
        ),
        lax.all_to_all(
            grad_value.astype(jnp.bfloat16), "seq", split_axis=0, concat_axis=1, tiled=True
        ),
    )
    return (grad_qs, grad_ks, grad_vs, grad_qt, grad_kt, grad_vt)


def solution(mesh):
    split_spec = P(("grp", "seq"), None, None)

    def mapped(body):
        return jax.shard_map(
            body,
            mesh=mesh,
            in_specs=(split_spec,) * 8 + (P(),),
            out_specs=(split_spec,) * 6,
            check_vma=False,
        )

    def grads(*arrays):
        return mapped(tile_shards if whole_tiles(mesh, arrays[0].shape[1]) else shards)(*arrays)

    return grads
```

```python
import functools
import math

import jax
import jax.numpy as jnp
from jax import lax
from jax.experimental import pallas as pl
from jax.experimental.pallas import tpu as pltpu
from jax.sharding import PartitionSpec as P

HEADS = 8
HDIM = 72
WIDTH = HEADS * HDIM
LANES = 128
SCALING = 1.0 / math.sqrt(HDIM)
CHUNKS = (4, 4)
masked_score = -1e30


def dot(left, right, left_dim, right_dim):
    dims = (((left_dim,), (right_dim,)), ((), ()))
    return lax.dot_general(left, right, dims, preferred_element_type=jnp.float32)


def rounded(value):
    return value.astype(jnp.bfloat16).astype(jnp.float32)


def frame_kernel(q_ref, k_ref, v_ref, g_ref, dq_ref, dk_ref, dv_ref):
    pair = 2 * HDIM
    reach = -(-HDIM // 16) * 16
    row = lax.broadcasted_iota(jnp.int32, (reach, 1), 0)
    for begin in range(0, WIDTH, pair):
        found = [[], [], []]
        for low, own in ((0, 0), (pair - reach, reach - HDIM)):
            span = slice(begin + low, begin + low + reach)
            mask = ((row >= own) & (row < own + HDIM)).astype(jnp.float32).astype(jnp.bfloat16)
            queries, keys = q_ref[0, span, :], k_ref[0, span, :]
            cotangent = g_ref[0, span, :]
            scores = dot(keys * mask, queries, 0, 0) * SCALING
            weight_grad = dot(v_ref[0, span, :] * mask, cotangent, 0, 0)
            raised = jnp.exp(scores - jnp.max(scores, axis=0, keepdims=True))
            weights = raised * (1.0 / jnp.sum(raised, axis=0, keepdims=True))
            weights_low = weights.astype(jnp.bfloat16)
            dots = jnp.sum(weights_low.astype(jnp.float32) * weight_grad, axis=0, keepdims=True)
            score_grad = (weights * (weight_grad - dots)).astype(jnp.bfloat16)
            rows = slice(own, own + HDIM)
            found[0].append(dot(keys, score_grad, 1, 0)[rows] * SCALING)
            found[1].append(dot(queries, score_grad, 1, 1)[rows] * SCALING)
            found[2].append(dot(cotangent, weights_low, 1, 1)[rows])
        for out, parts in zip((dq_ref, dk_ref, dv_ref), found):
            out[0, begin : begin + pair, :] = jnp.concatenate(parts, axis=0).astype(jnp.bfloat16)


def space_grads(queries, keys, values, cotangent):
    tokens = queries.shape[2]
    shape = jax.ShapeDtypeStruct(queries.shape, jnp.bfloat16)
    return pl.pallas_call(
        frame_kernel,
        out_shape=(shape, shape, shape),
        compiler_params=pltpu.CompilerParams(vmem_limit_bytes=60 * 2**20),
        cost_estimate=pl.CostEstimate(
            flops=12 * tokens * tokens * 256 * HEADS,
            bytes_accessed=14 * tokens * WIDTH,
            transcendentals=tokens * tokens * HEADS,
        ),
        name="space",
    )(queries, keys, values, cotangent)


def part_of(device, sharing, rows):
    row = pl.multiple_of(device % sharing * rows, 16)
    return row, pl.ds(pl.multiple_of(device // sharing * LANES, LANES), LANES)


def split_kernel(sharing, rows, span, *refs):
    ins, outs, (held, arrived, sent) = refs[:4], refs[4:-3], refs[-3:]
    loads, stores = {}, []
    for step in far_first(len(outs)):
        row, tokens = part_of(lax.axis_index("seq") ^ step, sharing, rows)
        for i, array in enumerate(ins):
            given = array.at[0, pl.ds(span.start + row, rows), tokens]
            loads[step, i] = pltpu.make_async_copy(given, held.at[step, i], arrived.at[step, i])
            loads[step, i].start()
    for step in far_first(len(outs)):
        for i in range(len(ins)):
            loads[step, i].wait()
        stores.append(pltpu.make_async_copy(held.at[step], outs[step], sent.at[step]))
        stores[-1].start()
    for copy in stores:
        copy.wait()


def split(arrays, span, n, sharing):
    rows = (span.stop - span.start) // sharing
    hbm = pl.BlockSpec(memory_space=pltpu.HBM)
    return pl.pallas_call(
        functools.partial(split_kernel, sharing, rows, span),
        in_specs=[hbm] * 4,
        out_specs=[hbm] * n,
        out_shape=[jax.ShapeDtypeStruct((4, rows, LANES), jnp.bfloat16)] * n,
        scratch_shapes=[
            pltpu.VMEM((n, 4, rows, LANES), jnp.bfloat16),
            pltpu.SemaphoreType.DMA((n, 4)),
            pltpu.SemaphoreType.DMA((n,)),
        ],
        compiler_params=pltpu.CompilerParams(vmem_limit_bytes=60 * 2**20),
        name="pack",
    )(*arrays)


def far_first(n):
    return [*reversed(range(n // 2, n)), *range(n // 2)]


def swap(block, axis, pairs):
    return lax.ppermute(block, axis, [(i, j) for i, j in pairs] + [(j, i) for i, j in pairs])


def exchange(blocks):
    n = len(blocks)
    moved = list(blocks)
    for step in reversed(range(1, n)):
        pairs = [[i, i ^ step] for i in range(n) if i < i ^ step]
        moved[step] = swap(blocks[step], "seq", pairs)
    return moved


def sides_kernel(n, *refs):
    ins, outs = refs[:n], refs[n:]
    is_odd = lax.axis_index("grp") & 1
    for step, ref in enumerate(ins):
        frame = lax.axis_index("seq") ^ step
        for start, out in zip((1, 0), outs):
            at = frame - jnp.where(is_odd == start, 1, 0)

            @pl.when((at >= 0) & (at < n - 1))
            def _():
                out[jnp.clip(at, 0, n - 2)] = ref[...]


def sides(blocks):
    n = len(blocks)
    shape = jax.ShapeDtypeStruct((n - 1, *blocks[0].shape), jnp.bfloat16)
    vmem = pl.BlockSpec(memory_space=pltpu.VMEM)
    return pl.pallas_call(
        functools.partial(sides_kernel, n),
        in_specs=[vmem] * n,
        out_specs=[vmem] * 2,
        out_shape=[shape] * 2,
        compiler_params=pltpu.CompilerParams(vmem_limit_bytes=24 * 2**20),
        name="sides",
    )(*blocks)


def gated(values, *earlier):
    return lax.optimization_barrier((values, *earlier))


def neighbours(block, start):
    count = lax.axis_size("grp")
    return swap(block, "grp", [(i, i + 1) for i in range(start, count - 1, 2)])


def join_kernel(sharing, span, *refs):
    outs, sent = refs[-4:-1], refs[-1]
    rows = refs[0].shape[1]
    n = sent.shape[0]
    copies = []
    for at, step in enumerate(far_first(n)):
        row, tokens = part_of(lax.axis_index("seq") ^ step, sharing, rows)
        for i, out in enumerate(outs):
            given = out.at[0, pl.ds(span.start + row, rows), tokens]
            copies.append(pltpu.make_async_copy(refs[at].at[i], given, sent.at[step, i]))
            copies[-1].start()
    for copy in copies:
        copy.wait()


def join(blocks, span, tokens, sharing, earlier):
    n = len(blocks)
    shape = jax.ShapeDtypeStruct((1, WIDTH, tokens), jnp.bfloat16)
    hbm = pl.BlockSpec(memory_space=pltpu.HBM)
    earlier = [] if earlier is None else list(earlier)
    return pl.pallas_call(
        functools.partial(join_kernel, sharing, span),
        in_specs=[pl.BlockSpec(memory_space=pltpu.VMEM)] * n + [hbm] * len(earlier),
        out_specs=[hbm] * 3,
        out_shape=[shape] * 3,
        scratch_shapes=[pltpu.SemaphoreType.DMA((n, 3))],
        input_output_aliases={n + i: i for i in range(len(earlier))},
        compiler_params=pltpu.CompilerParams(vmem_limit_bytes=24 * 2**20),
        name="unpack",
    )(*(blocks[step] for step in far_first(n)), *earlier)


def clip_kernel(window, heads, given_bounds, *refs):
    own, sides_of = refs[:window], refs[window : window + 2]
    outs, refs = refs[window + 2 : 2 * window + 2], refs[2 * window + 2 :]
    wide, score_ref, grad_ref, weight_ref, found, bounds, arrived = refs
    copy = pltpu.make_async_copy(given_bounds, bounds, arrived)
    copy.start()
    halo = window - 1
    extent = window + 2 * halo
    queries, keys, values, cotangent = range(4)

    def widen(ref, frame):
        for i in range(4):
            wide[i, frame] = ref[i].astype(jnp.float32)

    for step, ref in enumerate(own):
        widen(ref, halo + (lax.axis_index("seq") ^ step))
    copy.wait()
    lowest, highest = bounds[0, halo], bounds[1, halo + window - 1]
    for start, ref in zip((1, 0), sides_of):
        is_next = (lax.axis_index("grp") & 1) == start
        for at in range(halo):
            frame = at + jnp.where(is_next, halo + window, 0)
            needed = (frame >= lowest) & (frame < highest)
            pl.when(needed)(functools.partial(widen, ref.at[at], frame))

    def partners(frame):
        first, last = bounds[0, frame], bounds[1, frame]
        return first, last - first, [jnp.minimum(first + t, last - 1) for t in range(window)]

    def products(frame, carry):
        first, count, others = partners(frame)
        scores, grads = [[] for _ in others], [[] for _ in others]
        for head in range(heads):
            span = slice(head * HDIM, (head + 1) * HDIM)
            query, cot = wide[queries, frame, span, :], wide[cotangent, frame, span, :]
            for t, other in enumerate(others):
                score = jnp.sum(query * wide[keys, other, span, :], axis=0, keepdims=True)
                grad = jnp.sum(cot * wide[values, other, span, :], axis=0, keepdims=True)
                scores[t].append(score)
                grads[t].append(grad)
        for t in range(window):
            bias = jnp.where(t < count, 0.0, masked_score)
            score_ref[t, frame] = jnp.concatenate(scores[t], axis=0) * SCALING + bias
            grad_ref[t, frame] = jnp.concatenate(grads[t], axis=0)
        return carry

    lax.fori_loop(lowest, highest, products, 0)
    scores, grads = [score_ref[t] for t in range(window)], [grad_ref[t] for t in range(window)]
    peak = functools.reduce(jnp.maximum, scores)
    raised = [jnp.exp(score - peak) for score in scores]
    inverse = 1.0 / functools.reduce(jnp.add, raised)
    weights = [part * inverse for part in raised]
    weights_low = [rounded(part) for part in weights]
    dots = functools.reduce(jnp.add, [w * d for w, d in zip(weights_low, grads)])
    for t in range(window):
        weight_ref[t] = weights_low[t]
        score_ref[t] = rounded(weights[t] * (grads[t] - dots))

    def gradients(at, carry):
        frame = halo + at
        first, count, others = partners(frame)
        place = frame - first
        sums = [[], [], []]
        for head in range(heads):
            span, row = slice(head * HDIM, (head + 1) * HDIM), slice(head, head + 1)
            totals = [None] * 3
            for t, other in enumerate(others):
                score_back = jnp.where(t < count, score_ref[place, other, row, :], 0.0)
                weight_back = jnp.where(t < count, weight_ref[place, other, row, :], 0.0)
                terms = (
                    score_ref[t, frame, row, :] * wide[keys, other, span, :],
                    score_back * wide[queries, other, span, :],
                    weight_back * wide[cotangent, other, span, :],
                )
                totals = [x if y is None else y + x for x, y in zip(terms, totals)]
            for held, total, scale in zip(sums, totals, (SCALING, SCALING, None)):
                held.append(total if scale is None else total * scale)
        for i, parts in enumerate(sums):
            found[at, i] = jnp.concatenate(parts, axis=0).astype(jnp.bfloat16)
        return carry

    lax.fori_loop(0, window, gradients, 0)
    for step, out in enumerate(outs):
        out[...] = found[lax.axis_index("seq") ^ step]


def clip_grads(bounds, own, beside):
    window = len(own)
    _, rows, lanes = own[0].shape
    heads = rows // HDIM
    extent = 3 * window - 2
    vmem = pl.BlockSpec(memory_space=pltpu.VMEM)
    shape = (3, rows, lanes)
    slots = pltpu.VMEM((window, extent, heads, lanes), jnp.float32)
    return pl.pallas_call(
        functools.partial(clip_kernel, window, heads),
        out_shape=[jax.ShapeDtypeStruct(shape, jnp.bfloat16)] * window,
        in_specs=[pl.BlockSpec(memory_space=pl.ANY)] + [vmem] * (window + 2),
        out_specs=[vmem] * window,
        scratch_shapes=[
            pltpu.VMEM((4, extent, rows, lanes), jnp.float32),
            slots,
            slots,
            slots,
            pltpu.VMEM((window, *shape), jnp.bfloat16),
            pltpu.SMEM(bounds.shape, jnp.int32),
            pltpu.SemaphoreType.DMA,
        ],
        compiler_params=pltpu.CompilerParams(vmem_limit_bytes=48 * 2**20),
        cost_estimate=pl.CostEstimate(
            flops=800 * extent * window * rows * lanes,
            bytes_accessed=2 * sum(block.size for block in (*own, *beside)),
            transcendentals=extent * window * heads * lanes,
        ),
        name="clips",
    )(bounds, *own, *beside)


def clip_bounds(clip_len, window):
    halo = window - 1
    extent = window + 2 * halo
    start = lax.axis_index("grp") * window - halo
    frames = start + jnp.arange(extent, dtype=jnp.int32)
    order = jnp.arange(clip_len.shape[0])
    ends = jnp.sum(jnp.where(order[:, None] <= order[None, :], clip_len[:, None], 0), axis=0)
    begins = ends - clip_len
    holds = (begins[None, :] <= frames[:, None]) & (frames[:, None] < ends[None, :])
    first = jnp.sum(jnp.where(holds, begins[None, :], 0), axis=1) - start
    last = jnp.sum(jnp.where(holds, ends[None, :], 0), axis=1) - start
    return jnp.stack([first, last]).astype(jnp.int32)


def tile_shards(q_space, k_space, v_space, cot_space, q_time, k_time, v_time, cot_time, clip_len):
    def turned(*arrays):
        return tuple(array.transpose(0, 2, 1) for array in arrays)

    n = lax.axis_size("seq")
    window = q_time.shape[0] * n
    tokens = q_time.shape[1]
    sharing = n * LANES // tokens
    bounds = clip_bounds(clip_len, window)
    time = turned(q_time, k_time, v_time, cot_time)
    spans = []
    head = 0
    for heads in CHUNKS:
        spans.append(slice(head * HDIM, (head + heads) * HDIM))
        head += heads
    space_in = turned(q_space, k_space, v_space, cot_space)
    packed = [list(split(time, span, n, sharing)) for span in spans]
    own = [exchange(packed[0])]
    space = space_grads(*space_in)
    packed[1][2:], own[0][2], space = gated(packed[1][2:], own[0][2], space)
    own.append(exchange(packed[1]))
    beside = [
        [neighbours(ends, start) for ends, start in zip(sides(blocks), (1, 0))] for blocks in own
    ]
    back, grads = [], None
    for blocks, near in zip(own, beside):
        back.append(exchange(clip_grads(bounds, blocks, near)))
    for span, blocks in zip(spans, back):
        grads = join(blocks, span, tokens, sharing, grads)
    return turned(*space, *grads)


def whole_tiles(mesh, tokens):
    n = mesh.shape["seq"]
    sharing = n * LANES // tokens
    return (
        tokens % LANES == 0
        and n % 4 == 0
        and n & (n - 1) == 0
        and sharing * tokens == n * LANES
        and all(heads % sharing == 0 and heads // sharing * HDIM % 16 == 0 for heads in CHUNKS)
    )


def padded(block, sides, width):
    for axis, dim in sides:
        count = lax.axis_size(axis)
        forward = [(i, i + 1) for i in range(count - 1)]
        backward = [(target, source) for source, target in forward]
        low = lax.ppermute(
            lax.slice_in_dim(block, block.shape[dim] - width, None, axis=dim), axis, forward
        )
        high = lax.ppermute(lax.slice_in_dim(block, 0, width, axis=dim), axis, backward)
        block = jnp.concatenate([low, block, high], axis=dim)
    return block


def shifted(value, axis, by):
    count = lax.axis_size(axis)
    pairs = [(i, i + by) for i in range(count) if 0 <= i + by < count]
    return lax.ppermute(value, axis, pairs)


def clip_labels(clip_len, first_frame, count, frame_total):
    frame_ids = first_frame + jnp.arange(count, dtype=jnp.int32)
    clip_ends = jnp.cumsum(clip_len)
    labels = jnp.sum((clip_ends[None, :] <= frame_ids[:, None]).astype(jnp.int32), axis=1)
    inside = (frame_ids >= 0) & (frame_ids < frame_total)
    return (labels, inside)


def frame_grads(queries, keys, values, cotangent):
    scaling = 1.0 / math.sqrt(HDIM)
    tokens = queries.shape[0]
    q_heads = queries.reshape(tokens, HEADS, HDIM)
    k_heads = keys.reshape(tokens, HEADS, HDIM)
    v_heads = values.reshape(tokens, HEADS, HDIM)
    g_heads = cotangent.reshape(tokens, HEADS, HDIM)
    scores = (
        jnp.einsum("qhd,khd->hqk", q_heads, k_heads, preferred_element_type=jnp.float32) * scaling
    )
    row_max = jnp.max(scores, axis=-1, keepdims=True)
    log_total = row_max + jnp.log(jnp.sum(jnp.exp(scores - row_max), axis=-1, keepdims=True))
    weights = jnp.exp(scores - log_total)
    weights_low = weights.astype(jnp.bfloat16)
    attended = jnp.einsum("hqk,khd->qhd", weights_low, v_heads, preferred_element_type=jnp.float32)
    row_dot = jnp.einsum("qhd,qhd->hq", g_heads.astype(jnp.float32), attended)
    weight_grad = jnp.einsum("qhd,khd->hqk", g_heads, v_heads, preferred_element_type=jnp.float32)
    score_grad = (weights * (weight_grad - row_dot[:, :, None])).astype(jnp.bfloat16)
    grad_query = (
        jnp.einsum("hqk,khd->qhd", score_grad, k_heads, preferred_element_type=jnp.float32)
        * scaling
    )
    grad_key = (
        jnp.einsum("hqk,qhd->khd", score_grad, q_heads, preferred_element_type=jnp.float32)
        * scaling
    )
    grad_value = jnp.einsum(
        "hqk,qhd->khd", weights_low, g_heads, preferred_element_type=jnp.float32
    )
    flat_shape = (1, tokens, HEADS * HDIM)
    return (
        grad_query.reshape(flat_shape).astype(jnp.bfloat16),
        grad_key.reshape(flat_shape).astype(jnp.bfloat16),
        grad_value.reshape(flat_shape).astype(jnp.bfloat16),
    )


def shards(q_space, k_space, v_space, cot_space, q_time, k_time, v_time, cot_time, clip_len):
    scaling = 1.0 / math.sqrt(HDIM)
    grad_qs, grad_ks, grad_vs = frame_grads(q_space[0], k_space[0], v_space[0], cot_space[0])
    moved = (
        lax.all_to_all(q_time, "seq", split_axis=1, concat_axis=0, tiled=True),
        lax.all_to_all(k_time, "seq", split_axis=1, concat_axis=0, tiled=True),
        lax.all_to_all(v_time, "seq", split_axis=1, concat_axis=0, tiled=True),
        lax.all_to_all(cot_time, "seq", split_axis=1, concat_axis=0, tiled=True),
    )
    query_win, key_win, value_win, cot_win = moved
    window = query_win.shape[0]
    places = query_win.shape[1]
    channels = query_win.shape[2]
    group_id = lax.axis_index("grp")
    frame_total = window * lax.axis_size("grp")
    first_frame = group_id * window

    def split_heads(array):
        return array.reshape(array.shape[0], places, HEADS, HDIM)

    key_pair = padded(jnp.stack([key_win, value_win]), (("grp", 1),), window)
    q_own = split_heads(query_win)
    g_own = split_heads(cot_win)
    k_ext = split_heads(key_pair[0])
    v_ext = split_heads(key_pair[1])
    own_label, own_inside = clip_labels(clip_len, first_frame, window, frame_total)
    ext_label, ext_inside = clip_labels(clip_len, first_frame - window, 3 * window, frame_total)
    allowed = (own_label[:, None] == ext_label[None, :]) & ext_inside[None, :]
    scores = (
        jnp.einsum("iphd,jphd->phij", q_own, k_ext, preferred_element_type=jnp.float32) * scaling
    )
    scores = jnp.where(allowed, scores, masked_score)
    row_max = jnp.max(scores, axis=-1)
    log_total = row_max + jnp.log(jnp.sum(jnp.exp(scores - row_max[..., None]), axis=-1))
    weights = jnp.where(allowed, jnp.exp(scores - log_total[..., None]), 0.0)
    weights_low = weights.astype(jnp.bfloat16)
    attended = jnp.einsum("phij,jphd->iphd", weights_low, v_ext, preferred_element_type=jnp.float32)
    row_dot = jnp.einsum("iphd,iphd->phi", g_own.astype(jnp.float32), attended)
    weight_grad = jnp.einsum("iphd,jphd->phij", g_own, v_ext, preferred_element_type=jnp.float32)
    score_grad = (weights * (weight_grad - row_dot[..., None])).astype(jnp.bfloat16)
    grad_query = (
        jnp.einsum("phij,jphd->iphd", score_grad, k_ext, preferred_element_type=jnp.float32)
        * scaling
    )
    key_terms = (
        jnp.einsum("phij,iphd->jphd", score_grad, q_own, preferred_element_type=jnp.float32)
        * scaling
    )
    value_terms = jnp.einsum(
        "phij,iphd->jphd", weights_low, g_own, preferred_element_type=jnp.float32
    )
    both_terms = jnp.stack([key_terms, value_terms]).reshape(2, 3 * window, places, channels)
    from_after = shifted(both_terms[:, :window], "grp", -1)
    from_before = shifted(both_terms[:, 2 * window :], "grp", 1)
    summed = both_terms[:, window : 2 * window] + from_after + from_before
    grad_key = summed[0]
    grad_value = summed[1]
    grad_qt, grad_kt, grad_vt = (
        lax.all_to_all(
            grad_query.reshape(window, places, channels).astype(jnp.bfloat16),
            "seq",
            split_axis=0,
            concat_axis=1,
            tiled=True,
        ),
        lax.all_to_all(
            grad_key.astype(jnp.bfloat16), "seq", split_axis=0, concat_axis=1, tiled=True
        ),
        lax.all_to_all(
            grad_value.astype(jnp.bfloat16), "seq", split_axis=0, concat_axis=1, tiled=True
        ),
    )
    return (grad_qs, grad_ks, grad_vs, grad_qt, grad_kt, grad_vt)


def solution(mesh):
    split_spec = P(("grp", "seq"), None, None)

    def mapped(body):
        return jax.shard_map(
            body,
            mesh=mesh,
            in_specs=(split_spec,) * 8 + (P(),),
            out_specs=(split_spec,) * 6,
            check_vma=False,
        )

    def grads(*arrays):
        return mapped(tile_shards if whole_tiles(mesh, arrays[0].shape[1]) else shards)(*arrays)

    return grads
```

```python
import functools
import math

import jax
import jax.numpy as jnp
from jax import lax
from jax.experimental import pallas as pl
from jax.experimental.pallas import tpu as pltpu
from jax.sharding import PartitionSpec as P

HEADS = 8
HDIM = 72
WIDTH = HEADS * HDIM
LANES = 128
SCALING = 1.0 / math.sqrt(HDIM)
CHUNKS = (4, 4)
masked_score = -1e30


def dot(left, right, left_dim, right_dim):
    dims = (((left_dim,), (right_dim,)), ((), ()))
    return lax.dot_general(left, right, dims, preferred_element_type=jnp.float32)


def rounded(value):
    return value.astype(jnp.bfloat16).astype(jnp.float32)


def frame_kernel(q_ref, k_ref, v_ref, g_ref, dq_ref, dk_ref, dv_ref):
    pair = 2 * HDIM
    reach = -(-HDIM // 16) * 16
    row = lax.broadcasted_iota(jnp.int32, (reach, 1), 0)
    for begin in range(0, WIDTH, pair):
        found = [[], [], []]
        for low, own in ((0, 0), (pair - reach, reach - HDIM)):
            span = slice(begin + low, begin + low + reach)
            mask = ((row >= own) & (row < own + HDIM)).astype(jnp.float32).astype(jnp.bfloat16)
            queries, keys = q_ref[0, span, :], k_ref[0, span, :]
            cotangent = g_ref[0, span, :]
            scores = dot(keys * mask, queries, 0, 0) * SCALING
            weight_grad = dot(v_ref[0, span, :] * mask, cotangent, 0, 0)
            raised = jnp.exp(scores - jnp.max(scores, axis=0, keepdims=True))
            weights = raised * (1.0 / jnp.sum(raised, axis=0, keepdims=True))
            weights_low = weights.astype(jnp.bfloat16)
            dots = jnp.sum(weights_low.astype(jnp.float32) * weight_grad, axis=0, keepdims=True)
            score_grad = (weights * (weight_grad - dots)).astype(jnp.bfloat16)
            rows = slice(own, own + HDIM)
            found[0].append(dot(keys, score_grad, 1, 0)[rows] * SCALING)
            found[1].append(dot(queries, score_grad, 1, 1)[rows] * SCALING)
            found[2].append(dot(cotangent, weights_low, 1, 1)[rows])
        for out, parts in zip((dq_ref, dk_ref, dv_ref), found):
            out[0, begin : begin + pair, :] = jnp.concatenate(parts, axis=0).astype(jnp.bfloat16)


def space_grads(queries, keys, values, cotangent):
    tokens = queries.shape[2]
    shape = jax.ShapeDtypeStruct(queries.shape, jnp.bfloat16)
    return pl.pallas_call(
        frame_kernel,
        out_shape=(shape, shape, shape),
        compiler_params=pltpu.CompilerParams(vmem_limit_bytes=60 * 2**20),
        cost_estimate=pl.CostEstimate(
            flops=12 * tokens * tokens * 256 * HEADS,
            bytes_accessed=14 * tokens * WIDTH,
            transcendentals=tokens * tokens * HEADS,
        ),
        name="space",
    )(queries, keys, values, cotangent)


def part_of(device, sharing, rows):
    row = pl.multiple_of(device % sharing * rows, 16)
    return row, pl.ds(pl.multiple_of(device // sharing * LANES, LANES), LANES)


def split_kernel(sharing, rows, span, *refs):
    ins, outs, (held, arrived, sent) = refs[:4], refs[4:-3], refs[-3:]
    loads, stores = {}, []
    for step in far_first(len(outs)):
        row, tokens = part_of(lax.axis_index("seq") ^ step, sharing, rows)
        for i, array in enumerate(ins):
            given = array.at[0, pl.ds(span.start + row, rows), tokens]
            loads[step, i] = pltpu.make_async_copy(given, held.at[step, i], arrived.at[step, i])
            loads[step, i].start()
    for step in far_first(len(outs)):
        for i in range(len(ins)):
            loads[step, i].wait()
        stores.append(pltpu.make_async_copy(held.at[step], outs[step], sent.at[step]))
        stores[-1].start()
    for copy in stores:
        copy.wait()


def split(arrays, span, n, sharing):
    rows = (span.stop - span.start) // sharing
    hbm = pl.BlockSpec(memory_space=pltpu.HBM)
    return pl.pallas_call(
        functools.partial(split_kernel, sharing, rows, span),
        in_specs=[hbm] * 4,
        out_specs=[hbm] * n,
        out_shape=[jax.ShapeDtypeStruct((4, rows, LANES), jnp.bfloat16)] * n,
        scratch_shapes=[
            pltpu.VMEM((n, 4, rows, LANES), jnp.bfloat16),
            pltpu.SemaphoreType.DMA((n, 4)),
            pltpu.SemaphoreType.DMA((n,)),
        ],
        compiler_params=pltpu.CompilerParams(vmem_limit_bytes=60 * 2**20),
        name="pack",
    )(*arrays)


def far_first(n):
    return [*reversed(range(n // 2, n)), *range(n // 2)]


def swap(block, axis, pairs):
    return lax.ppermute(block, axis, [(i, j) for i, j in pairs] + [(j, i) for i, j in pairs])


def exchange(blocks):
    n = len(blocks)
    moved = list(blocks)
    for step in reversed(range(1, n)):
        pairs = [[i, i ^ step] for i in range(n) if i < i ^ step]
        moved[step] = swap(blocks[step], "seq", pairs)
    return moved


def sides_kernel(n, *refs):
    ins, outs = refs[:n], refs[n:]
    is_odd = lax.axis_index("grp") & 1
    for step, ref in enumerate(ins):
        frame = lax.axis_index("seq") ^ step
        for start, out in zip((1, 0), outs):
            at = frame - jnp.where(is_odd == start, 1, 0)

            @pl.when((at >= 0) & (at < n - 1))
            def _():
                out[jnp.clip(at, 0, n - 2)] = ref[...]


def sides(blocks):
    n = len(blocks)
    shape = jax.ShapeDtypeStruct((n - 1, *blocks[0].shape), jnp.bfloat16)
    vmem = pl.BlockSpec(memory_space=pltpu.VMEM)
    return pl.pallas_call(
        functools.partial(sides_kernel, n),
        in_specs=[vmem] * n,
        out_specs=[vmem] * 2,
        out_shape=[shape] * 2,
        compiler_params=pltpu.CompilerParams(vmem_limit_bytes=24 * 2**20),
        name="sides",
    )(*blocks)


def gated(values, *earlier):
    return lax.optimization_barrier((values, *earlier))


def neighbours(block, start):
    count = lax.axis_size("grp")
    return swap(block, "grp", [(i, i + 1) for i in range(start, count - 1, 2)])


def join_kernel(sharing, span, *refs):
    outs, sent = refs[-4:-1], refs[-1]
    rows = refs[0].shape[1]
    n = sent.shape[0]
    copies = []
    for at, step in enumerate(far_first(n)):
        row, tokens = part_of(lax.axis_index("seq") ^ step, sharing, rows)
        for i, out in enumerate(outs):
            given = out.at[0, pl.ds(span.start + row, rows), tokens]
            copies.append(pltpu.make_async_copy(refs[at].at[i], given, sent.at[step, i]))
            copies[-1].start()
    for copy in copies:
        copy.wait()


def join(blocks, span, tokens, sharing, earlier):
    n = len(blocks)
    shape = jax.ShapeDtypeStruct((1, WIDTH, tokens), jnp.bfloat16)
    hbm = pl.BlockSpec(memory_space=pltpu.HBM)
    earlier = [] if earlier is None else list(earlier)
    return pl.pallas_call(
        functools.partial(join_kernel, sharing, span),
        in_specs=[pl.BlockSpec(memory_space=pltpu.VMEM)] * n + [hbm] * len(earlier),
        out_specs=[hbm] * 3,
        out_shape=[shape] * 3,
        scratch_shapes=[pltpu.SemaphoreType.DMA((n, 3))],
        input_output_aliases={n + i: i for i in range(len(earlier))},
        compiler_params=pltpu.CompilerParams(vmem_limit_bytes=24 * 2**20),
        name="unpack",
    )(*(blocks[step] for step in far_first(n)), *earlier)


def clip_kernel(window, heads, given_bounds, *refs):
    own, sides_of = refs[:window], refs[window : window + 2]
    outs, refs = refs[window + 2 : 2 * window + 2], refs[2 * window + 2 :]
    wide, score_ref, grad_ref, weight_ref, found, bounds, arrived = refs
    copy = pltpu.make_async_copy(given_bounds, bounds, arrived)
    copy.start()
    halo = window - 1
    extent = window + 2 * halo
    queries, keys, values, cotangent = range(4)

    def widen(ref, frame):
        for i in range(4):
            wide[i, frame] = ref[i].astype(jnp.float32)

    for step, ref in enumerate(own):
        widen(ref, halo + (lax.axis_index("seq") ^ step))
    copy.wait()
    lowest, highest = bounds[0, halo], bounds[1, halo + window - 1]
    for start, ref in zip((1, 0), sides_of):
        is_next = (lax.axis_index("grp") & 1) == start
        for at in range(halo):
            frame = at + jnp.where(is_next, halo + window, 0)
            needed = (frame >= lowest) & (frame < highest)
            pl.when(needed)(functools.partial(widen, ref.at[at], frame))

    def partners(frame):
        first, last = bounds[0, frame], bounds[1, frame]
        return first, last - first, [jnp.minimum(first + t, last - 1) for t in range(window)]

    def products(frame, carry):
        first, count, others = partners(frame)
        scores, grads = [[] for _ in others], [[] for _ in others]
        for head in range(heads):
            span = slice(head * HDIM, (head + 1) * HDIM)
            query, cot = wide[queries, frame, span, :], wide[cotangent, frame, span, :]
            for t, other in enumerate(others):
                score = jnp.sum(query * wide[keys, other, span, :], axis=0, keepdims=True)
                grad = jnp.sum(cot * wide[values, other, span, :], axis=0, keepdims=True)
                scores[t].append(score)
                grads[t].append(grad)
        for t in range(window):
            bias = jnp.where(t < count, 0.0, masked_score)
            score_ref[t, frame] = jnp.concatenate(scores[t], axis=0) * SCALING + bias
            grad_ref[t, frame] = jnp.concatenate(grads[t], axis=0)
        return carry

    lax.fori_loop(lowest, highest, products, 0)
    scores, grads = [score_ref[t] for t in range(window)], [grad_ref[t] for t in range(window)]
    peak = functools.reduce(jnp.maximum, scores)
    raised = [jnp.exp(score - peak) for score in scores]
    inverse = 1.0 / functools.reduce(jnp.add, raised)
    weights = [part * inverse for part in raised]
    weights_low = [rounded(part) for part in weights]
    dots = functools.reduce(jnp.add, [w * d for w, d in zip(weights_low, grads)])
    for t in range(window):
        weight_ref[t] = weights_low[t]
        score_ref[t] = rounded(weights[t] * (grads[t] - dots))

    def gradients(at, carry):
        frame = halo + at
        first, count, others = partners(frame)
        place = frame - first
        sums = [[], [], []]
        for head in range(heads):
            span, row = slice(head * HDIM, (head + 1) * HDIM), slice(head, head + 1)
            totals = [None] * 3
            for t, other in enumerate(others):
                score_back = jnp.where(t < count, score_ref[place, other, row, :], 0.0)
                weight_back = jnp.where(t < count, weight_ref[place, other, row, :], 0.0)
                terms = (
                    score_ref[t, frame, row, :] * wide[keys, other, span, :],
                    score_back * wide[queries, other, span, :],
                    weight_back * wide[cotangent, other, span, :],
                )
                totals = [x if y is None else y + x for x, y in zip(terms, totals)]
            for held, total, scale in zip(sums, totals, (SCALING, SCALING, None)):
                held.append(total if scale is None else total * scale)
        for i, parts in enumerate(sums):
            found[at, i] = jnp.concatenate(parts, axis=0).astype(jnp.bfloat16)
        return carry

    lax.fori_loop(0, window, gradients, 0)
    for step, out in enumerate(outs):
        out[...] = found[lax.axis_index("seq") ^ step]


def clip_grads(bounds, own, beside):
    window = len(own)
    _, rows, lanes = own[0].shape
    heads = rows // HDIM
    extent = 3 * window - 2
    vmem = pl.BlockSpec(memory_space=pltpu.VMEM)
    shape = (3, rows, lanes)
    slots = pltpu.VMEM((window, extent, heads, lanes), jnp.float32)
    return pl.pallas_call(
        functools.partial(clip_kernel, window, heads),
        out_shape=[jax.ShapeDtypeStruct(shape, jnp.bfloat16)] * window,
        in_specs=[pl.BlockSpec(memory_space=pl.ANY)] + [vmem] * (window + 2),
        out_specs=[vmem] * window,
        scratch_shapes=[
            pltpu.VMEM((4, extent, rows, lanes), jnp.float32),
            slots,
            slots,
            slots,
            pltpu.VMEM((window, *shape), jnp.bfloat16),
            pltpu.SMEM(bounds.shape, jnp.int32),
            pltpu.SemaphoreType.DMA,
        ],
        compiler_params=pltpu.CompilerParams(vmem_limit_bytes=48 * 2**20),
        cost_estimate=pl.CostEstimate(
            flops=800 * extent * window * rows * lanes,
            bytes_accessed=2 * sum(block.size for block in (*own, *beside)),
            transcendentals=extent * window * heads * lanes,
        ),
        name="clips",
    )(bounds, *own, *beside)


def clip_bounds(clip_len, window):
    halo = window - 1
    extent = window + 2 * halo
    start = lax.axis_index("grp") * window - halo
    frames = start + jnp.arange(extent, dtype=jnp.int32)
    order = jnp.arange(clip_len.shape[0])
    ends = jnp.sum(jnp.where(order[:, None] <= order[None, :], clip_len[:, None], 0), axis=0)
    begins = ends - clip_len
    holds = (begins[None, :] <= frames[:, None]) & (frames[:, None] < ends[None, :])
    first = jnp.sum(jnp.where(holds, begins[None, :], 0), axis=1) - start
    last = jnp.sum(jnp.where(holds, ends[None, :], 0), axis=1) - start
    return jnp.stack([first, last]).astype(jnp.int32)


def tile_shards(q_space, k_space, v_space, cot_space, q_time, k_time, v_time, cot_time, clip_len):
    def turned(*arrays):
        return tuple(array.transpose(0, 2, 1) for array in arrays)

    n = lax.axis_size("seq")
    window = q_time.shape[0] * n
    tokens = q_time.shape[1]
    sharing = n * LANES // tokens
    bounds = clip_bounds(clip_len, window)
    time = turned(q_time, k_time, v_time, cot_time)
    spans = []
    head = 0
    for heads in CHUNKS:
        spans.append(slice(head * HDIM, (head + heads) * HDIM))
        head += heads
    space_in = turned(q_space, k_space, v_space, cot_space)
    packed = [split(time, span, n, sharing) for span in spans]
    own = [exchange(blocks) for blocks in packed]
    space = space_grads(*space_in)
    beside = [
        [neighbours(ends, start) for ends, start in zip(sides(blocks), (1, 0))] for blocks in own
    ]
    back, grads = [], None
    for blocks, near in zip(own, beside):
        back.append(exchange(clip_grads(bounds, blocks, near)))
    for span, blocks in zip(spans, back):
        grads = join(blocks, span, tokens, sharing, grads)
    return turned(*space, *grads)


def whole_tiles(mesh, tokens):
    n = mesh.shape["seq"]
    sharing = n * LANES // tokens
    return (
        tokens % LANES == 0
        and n % 4 == 0
        and n & (n - 1) == 0
        and sharing * tokens == n * LANES
        and all(heads % sharing == 0 and heads // sharing * HDIM % 16 == 0 for heads in CHUNKS)
    )


def padded(block, sides, width):
    for axis, dim in sides:
        count = lax.axis_size(axis)
        forward = [(i, i + 1) for i in range(count - 1)]
        backward = [(target, source) for source, target in forward]
        low = lax.ppermute(
            lax.slice_in_dim(block, block.shape[dim] - width, None, axis=dim), axis, forward
        )
        high = lax.ppermute(lax.slice_in_dim(block, 0, width, axis=dim), axis, backward)
        block = jnp.concatenate([low, block, high], axis=dim)
    return block


def shifted(value, axis, by):
    count = lax.axis_size(axis)
    pairs = [(i, i + by) for i in range(count) if 0 <= i + by < count]
    return lax.ppermute(value, axis, pairs)


def clip_labels(clip_len, first_frame, count, frame_total):
    frame_ids = first_frame + jnp.arange(count, dtype=jnp.int32)
    clip_ends = jnp.cumsum(clip_len)
    labels = jnp.sum((clip_ends[None, :] <= frame_ids[:, None]).astype(jnp.int32), axis=1)
    inside = (frame_ids >= 0) & (frame_ids < frame_total)
    return (labels, inside)


def frame_grads(queries, keys, values, cotangent):
    scaling = 1.0 / math.sqrt(HDIM)
    tokens = queries.shape[0]
    q_heads = queries.reshape(tokens, HEADS, HDIM)
    k_heads = keys.reshape(tokens, HEADS, HDIM)
    v_heads = values.reshape(tokens, HEADS, HDIM)
    g_heads = cotangent.reshape(tokens, HEADS, HDIM)
    scores = (
        jnp.einsum("qhd,khd->hqk", q_heads, k_heads, preferred_element_type=jnp.float32) * scaling
    )
    row_max = jnp.max(scores, axis=-1, keepdims=True)
    log_total = row_max + jnp.log(jnp.sum(jnp.exp(scores - row_max), axis=-1, keepdims=True))
    weights = jnp.exp(scores - log_total)
    weights_low = weights.astype(jnp.bfloat16)
    attended = jnp.einsum("hqk,khd->qhd", weights_low, v_heads, preferred_element_type=jnp.float32)
    row_dot = jnp.einsum("qhd,qhd->hq", g_heads.astype(jnp.float32), attended)
    weight_grad = jnp.einsum("qhd,khd->hqk", g_heads, v_heads, preferred_element_type=jnp.float32)
    score_grad = (weights * (weight_grad - row_dot[:, :, None])).astype(jnp.bfloat16)
    grad_query = (
        jnp.einsum("hqk,khd->qhd", score_grad, k_heads, preferred_element_type=jnp.float32)
        * scaling
    )
    grad_key = (
        jnp.einsum("hqk,qhd->khd", score_grad, q_heads, preferred_element_type=jnp.float32)
        * scaling
    )
    grad_value = jnp.einsum(
        "hqk,qhd->khd", weights_low, g_heads, preferred_element_type=jnp.float32
    )
    flat_shape = (1, tokens, HEADS * HDIM)
    return (
        grad_query.reshape(flat_shape).astype(jnp.bfloat16),
        grad_key.reshape(flat_shape).astype(jnp.bfloat16),
        grad_value.reshape(flat_shape).astype(jnp.bfloat16),
    )


def shards(q_space, k_space, v_space, cot_space, q_time, k_time, v_time, cot_time, clip_len):
    scaling = 1.0 / math.sqrt(HDIM)
    grad_qs, grad_ks, grad_vs = frame_grads(q_space[0], k_space[0], v_space[0], cot_space[0])
    moved = (
        lax.all_to_all(q_time, "seq", split_axis=1, concat_axis=0, tiled=True),
        lax.all_to_all(k_time, "seq", split_axis=1, concat_axis=0, tiled=True),
        lax.all_to_all(v_time, "seq", split_axis=1, concat_axis=0, tiled=True),
        lax.all_to_all(cot_time, "seq", split_axis=1, concat_axis=0, tiled=True),
    )
    query_win, key_win, value_win, cot_win = moved
    window = query_win.shape[0]
    places = query_win.shape[1]
    channels = query_win.shape[2]
    group_id = lax.axis_index("grp")
    frame_total = window * lax.axis_size("grp")
    first_frame = group_id * window

    def split_heads(array):
        return array.reshape(array.shape[0], places, HEADS, HDIM)

    key_pair = padded(jnp.stack([key_win, value_win]), (("grp", 1),), window)
    q_own = split_heads(query_win)
    g_own = split_heads(cot_win)
    k_ext = split_heads(key_pair[0])
    v_ext = split_heads(key_pair[1])
    own_label, own_inside = clip_labels(clip_len, first_frame, window, frame_total)
    ext_label, ext_inside = clip_labels(clip_len, first_frame - window, 3 * window, frame_total)
    allowed = (own_label[:, None] == ext_label[None, :]) & ext_inside[None, :]
    scores = (
        jnp.einsum("iphd,jphd->phij", q_own, k_ext, preferred_element_type=jnp.float32) * scaling
    )
    scores = jnp.where(allowed, scores, masked_score)
    row_max = jnp.max(scores, axis=-1)
    log_total = row_max + jnp.log(jnp.sum(jnp.exp(scores - row_max[..., None]), axis=-1))
    weights = jnp.where(allowed, jnp.exp(scores - log_total[..., None]), 0.0)
    weights_low = weights.astype(jnp.bfloat16)
    attended = jnp.einsum("phij,jphd->iphd", weights_low, v_ext, preferred_element_type=jnp.float32)
    row_dot = jnp.einsum("iphd,iphd->phi", g_own.astype(jnp.float32), attended)
    weight_grad = jnp.einsum("iphd,jphd->phij", g_own, v_ext, preferred_element_type=jnp.float32)
    score_grad = (weights * (weight_grad - row_dot[..., None])).astype(jnp.bfloat16)
    grad_query = (
        jnp.einsum("phij,jphd->iphd", score_grad, k_ext, preferred_element_type=jnp.float32)
        * scaling
    )
    key_terms = (
        jnp.einsum("phij,iphd->jphd", score_grad, q_own, preferred_element_type=jnp.float32)
        * scaling
    )
    value_terms = jnp.einsum(
        "phij,iphd->jphd", weights_low, g_own, preferred_element_type=jnp.float32
    )
    both_terms = jnp.stack([key_terms, value_terms]).reshape(2, 3 * window, places, channels)
    from_after = shifted(both_terms[:, :window], "grp", -1)
    from_before = shifted(both_terms[:, 2 * window :], "grp", 1)
    summed = both_terms[:, window : 2 * window] + from_after + from_before
    grad_key = summed[0]
    grad_value = summed[1]
    grad_qt, grad_kt, grad_vt = (
        lax.all_to_all(
            grad_query.reshape(window, places, channels).astype(jnp.bfloat16),
            "seq",
            split_axis=0,
            concat_axis=1,
            tiled=True,
        ),
        lax.all_to_all(
            grad_key.astype(jnp.bfloat16), "seq", split_axis=0, concat_axis=1, tiled=True
        ),
        lax.all_to_all(
            grad_value.astype(jnp.bfloat16), "seq", split_axis=0, concat_axis=1, tiled=True
        ),
    )
    return (grad_qs, grad_ks, grad_vs, grad_qt, grad_kt, grad_vt)


def solution(mesh):
    split_spec = P(("grp", "seq"), None, None)

    def mapped(body):
        return jax.shard_map(
            body,
            mesh=mesh,
            in_specs=(split_spec,) * 8 + (P(),),
            out_specs=(split_spec,) * 6,
            check_vma=False,
        )

    def grads(*arrays):
        return mapped(tile_shards if whole_tiles(mesh, arrays[0].shape[1]) else shards)(*arrays)

    return grads
```

```python
import functools
import math

import jax
import jax.numpy as jnp
from jax import lax
from jax.experimental import pallas as pl
from jax.experimental.pallas import tpu as pltpu
from jax.sharding import PartitionSpec as P

HEADS = 8
HDIM = 72
WIDTH = HEADS * HDIM
LANES = 128
SCALING = 1.0 / math.sqrt(HDIM)
CHUNKS = (4, 4)
masked_score = -1e30


def dot(left, right, left_dim, right_dim):
    dims = (((left_dim,), (right_dim,)), ((), ()))
    return lax.dot_general(left, right, dims, preferred_element_type=jnp.float32)


def rounded(value):
    return value.astype(jnp.bfloat16).astype(jnp.float32)


def frame_kernel(q_ref, k_ref, v_ref, g_ref, dq_ref, dk_ref, dv_ref):
    pair = 2 * HDIM
    reach = -(-HDIM // 16) * 16
    row = lax.broadcasted_iota(jnp.int32, (reach, 1), 0)
    for begin in range(0, WIDTH, pair):
        found = [[], [], []]
        for low, own in ((0, 0), (pair - reach, reach - HDIM)):
            span = slice(begin + low, begin + low + reach)
            mask = ((row >= own) & (row < own + HDIM)).astype(jnp.float32).astype(jnp.bfloat16)
            queries, keys = q_ref[0, span, :], k_ref[0, span, :]
            cotangent = g_ref[0, span, :]
            scores = dot(keys * mask, queries, 0, 0) * SCALING
            weight_grad = dot(v_ref[0, span, :] * mask, cotangent, 0, 0)
            raised = jnp.exp(scores - jnp.max(scores, axis=0, keepdims=True))
            weights = raised * (1.0 / jnp.sum(raised, axis=0, keepdims=True))
            weights_low = weights.astype(jnp.bfloat16)
            dots = jnp.sum(weights_low.astype(jnp.float32) * weight_grad, axis=0, keepdims=True)
            score_grad = (weights * (weight_grad - dots)).astype(jnp.bfloat16)
            rows = slice(own, own + HDIM)
            found[0].append(dot(keys, score_grad, 1, 0)[rows] * SCALING)
            found[1].append(dot(queries, score_grad, 1, 1)[rows] * SCALING)
            found[2].append(dot(cotangent, weights_low, 1, 1)[rows])
        for out, parts in zip((dq_ref, dk_ref, dv_ref), found):
            out[0, begin : begin + pair, :] = jnp.concatenate(parts, axis=0).astype(jnp.bfloat16)


def space_grads(queries, keys, values, cotangent):
    tokens = queries.shape[2]
    shape = jax.ShapeDtypeStruct(queries.shape, jnp.bfloat16)
    return pl.pallas_call(
        frame_kernel,
        out_shape=(shape, shape, shape),
        compiler_params=pltpu.CompilerParams(vmem_limit_bytes=60 * 2**20),
        cost_estimate=pl.CostEstimate(
            flops=12 * tokens * tokens * 256 * HEADS,
            bytes_accessed=14 * tokens * WIDTH,
            transcendentals=tokens * tokens * HEADS,
        ),
        name="space",
    )(queries, keys, values, cotangent)


def part_of(device, sharing, rows):
    row = pl.multiple_of(device % sharing * rows, 16)
    return row, pl.ds(pl.multiple_of(device // sharing * LANES, LANES), LANES)


def split_kernel(sharing, rows, span, *refs):
    ins, outs, (held, arrived, sent) = refs[:4], refs[4:-3], refs[-3:]
    loads, stores = {}, []
    for step in far_first(len(outs)):
        row, tokens = part_of(lax.axis_index("seq") ^ step, sharing, rows)
        for i, array in enumerate(ins):
            given = array.at[0, pl.ds(span.start + row, rows), tokens]
            loads[step, i] = pltpu.make_async_copy(given, held.at[step, i], arrived.at[step, i])
            loads[step, i].start()
    for step in far_first(len(outs)):
        for i in range(len(ins)):
            loads[step, i].wait()
        stores.append(pltpu.make_async_copy(held.at[step], outs[step], sent.at[step]))
        stores[-1].start()
    for copy in stores:
        copy.wait()


def split(arrays, span, n, sharing):
    rows = (span.stop - span.start) // sharing
    hbm = pl.BlockSpec(memory_space=pltpu.HBM)
    return pl.pallas_call(
        functools.partial(split_kernel, sharing, rows, span),
        in_specs=[hbm] * 4,
        out_specs=[hbm] * n,
        out_shape=[jax.ShapeDtypeStruct((4, rows, LANES), jnp.bfloat16)] * n,
        scratch_shapes=[
            pltpu.VMEM((n, 4, rows, LANES), jnp.bfloat16),
            pltpu.SemaphoreType.DMA((n, 4)),
            pltpu.SemaphoreType.DMA((n,)),
        ],
        compiler_params=pltpu.CompilerParams(vmem_limit_bytes=60 * 2**20),
        name="pack",
    )(*arrays)


def far_first(n):
    return [*reversed(range(n // 2, n)), *range(n // 2)]


def swap(block, axis, pairs):
    return lax.ppermute(block, axis, [(i, j) for i, j in pairs] + [(j, i) for i, j in pairs])


def exchange(blocks):
    n = len(blocks)
    moved = list(blocks)
    for step in reversed(range(1, n)):
        pairs = [[i, i ^ step] for i in range(n) if i < i ^ step]
        moved[step] = swap(blocks[step], "seq", pairs)
    return moved


def sides_kernel(n, *refs):
    ins, outs = refs[:n], refs[n:]
    is_odd = lax.axis_index("grp") & 1
    for step, ref in enumerate(ins):
        frame = lax.axis_index("seq") ^ step
        for start, out in zip((1, 0), outs):
            at = frame - jnp.where(is_odd == start, 1, 0)

            @pl.when((at >= 0) & (at < n - 1))
            def _():
                out[jnp.clip(at, 0, n - 2)] = ref[...]


def sides(blocks):
    n = len(blocks)
    shape = jax.ShapeDtypeStruct((n - 1, *blocks[0].shape), jnp.bfloat16)
    vmem = pl.BlockSpec(memory_space=pltpu.VMEM)
    return pl.pallas_call(
        functools.partial(sides_kernel, n),
        in_specs=[vmem] * n,
        out_specs=[vmem] * 2,
        out_shape=[shape] * 2,
        compiler_params=pltpu.CompilerParams(vmem_limit_bytes=24 * 2**20),
        name="sides",
    )(*blocks)


def gated(values, *earlier):
    return lax.optimization_barrier((values, *earlier))


def neighbours(block, start):
    count = lax.axis_size("grp")
    return swap(block, "grp", [(i, (i + 1) % count) for i in range(start, count, 2)])


def join_kernel(sharing, span, *refs):
    outs, sent = refs[-4:-1], refs[-1]
    rows = refs[0].shape[1]
    n = sent.shape[0]
    copies = []
    for at, step in enumerate(far_first(n)):
        row, tokens = part_of(lax.axis_index("seq") ^ step, sharing, rows)
        for i, out in enumerate(outs):
            given = out.at[0, pl.ds(span.start + row, rows), tokens]
            copies.append(pltpu.make_async_copy(refs[at].at[i], given, sent.at[step, i]))
            copies[-1].start()
    for copy in copies:
        copy.wait()


def join(blocks, span, tokens, sharing, earlier):
    n = len(blocks)
    shape = jax.ShapeDtypeStruct((1, WIDTH, tokens), jnp.bfloat16)
    hbm = pl.BlockSpec(memory_space=pltpu.HBM)
    earlier = [] if earlier is None else list(earlier)
    return pl.pallas_call(
        functools.partial(join_kernel, sharing, span),
        in_specs=[pl.BlockSpec(memory_space=pltpu.VMEM)] * n + [hbm] * len(earlier),
        out_specs=[hbm] * 3,
        out_shape=[shape] * 3,
        scratch_shapes=[pltpu.SemaphoreType.DMA((n, 3))],
        input_output_aliases={n + i: i for i in range(len(earlier))},
        compiler_params=pltpu.CompilerParams(vmem_limit_bytes=24 * 2**20),
        name="unpack",
    )(*(blocks[step] for step in far_first(n)), *earlier)


def clip_kernel(window, heads, given_bounds, *refs):
    own, sides_of = refs[:window], refs[window : window + 2]
    outs, refs = refs[window + 2 : 2 * window + 2], refs[2 * window + 2 :]
    wide, score_ref, grad_ref, weight_ref, found, bounds, arrived = refs
    copy = pltpu.make_async_copy(given_bounds, bounds, arrived)
    copy.start()
    halo = window - 1
    extent = window + 2 * halo
    queries, keys, values, cotangent = range(4)

    def widen(ref, frame):
        for i in range(4):
            wide[i, frame] = ref[i].astype(jnp.float32)

    for step, ref in enumerate(own):
        widen(ref, halo + (lax.axis_index("seq") ^ step))
    copy.wait()
    lowest, highest = bounds[0, halo], bounds[1, halo + window - 1]
    for start, ref in zip((1, 0), sides_of):
        is_next = (lax.axis_index("grp") & 1) == start
        for at in range(halo):
            frame = at + jnp.where(is_next, halo + window, 0)
            needed = (frame >= lowest) & (frame < highest)
            pl.when(needed)(functools.partial(widen, ref.at[at], frame))

    def partners(frame):
        first, last = bounds[0, frame], bounds[1, frame]
        return first, last - first, [jnp.minimum(first + t, last - 1) for t in range(window)]

    def products(frame, carry):
        first, count, others = partners(frame)
        scores, grads = [[] for _ in others], [[] for _ in others]
        for head in range(heads):
            span = slice(head * HDIM, (head + 1) * HDIM)
            query, cot = wide[queries, frame, span, :], wide[cotangent, frame, span, :]
            for t, other in enumerate(others):
                score = jnp.sum(query * wide[keys, other, span, :], axis=0, keepdims=True)
                grad = jnp.sum(cot * wide[values, other, span, :], axis=0, keepdims=True)
                scores[t].append(score)
                grads[t].append(grad)
        for t in range(window):
            bias = jnp.where(t < count, 0.0, masked_score)
            score_ref[t, frame] = jnp.concatenate(scores[t], axis=0) * SCALING + bias
            grad_ref[t, frame] = jnp.concatenate(grads[t], axis=0)
        return carry

    lax.fori_loop(lowest, highest, products, 0)
    scores, grads = [score_ref[t] for t in range(window)], [grad_ref[t] for t in range(window)]
    peak = functools.reduce(jnp.maximum, scores)
    raised = [jnp.exp(score - peak) for score in scores]
    inverse = 1.0 / functools.reduce(jnp.add, raised)
    weights = [part * inverse for part in raised]
    weights_low = [rounded(part) for part in weights]
    dots = functools.reduce(jnp.add, [w * d for w, d in zip(weights_low, grads)])
    for t in range(window):
        weight_ref[t] = weights_low[t]
        score_ref[t] = rounded(weights[t] * (grads[t] - dots))

    def gradients(at, carry):
        frame = halo + at
        first, count, others = partners(frame)
        place = frame - first
        sums = [[], [], []]
        for head in range(heads):
            span, row = slice(head * HDIM, (head + 1) * HDIM), slice(head, head + 1)
            totals = [None] * 3
            for t, other in enumerate(others):
                score_back = jnp.where(t < count, score_ref[place, other, row, :], 0.0)
                weight_back = jnp.where(t < count, weight_ref[place, other, row, :], 0.0)
                terms = (
                    score_ref[t, frame, row, :] * wide[keys, other, span, :],
                    score_back * wide[queries, other, span, :],
                    weight_back * wide[cotangent, other, span, :],
                )
                totals = [x if y is None else y + x for x, y in zip(terms, totals)]
            for held, total, scale in zip(sums, totals, (SCALING, SCALING, None)):
                held.append(total if scale is None else total * scale)
        for i, parts in enumerate(sums):
            found[at, i] = jnp.concatenate(parts, axis=0).astype(jnp.bfloat16)
        return carry

    lax.fori_loop(0, window, gradients, 0)
    for step, out in enumerate(outs):
        out[...] = found[lax.axis_index("seq") ^ step]


def clip_grads(bounds, own, beside):
    window = len(own)
    _, rows, lanes = own[0].shape
    heads = rows // HDIM
    extent = 3 * window - 2
    vmem = pl.BlockSpec(memory_space=pltpu.VMEM)
    shape = (3, rows, lanes)
    slots = pltpu.VMEM((window, extent, heads, lanes), jnp.float32)
    return pl.pallas_call(
        functools.partial(clip_kernel, window, heads),
        out_shape=[jax.ShapeDtypeStruct(shape, jnp.bfloat16)] * window,
        in_specs=[pl.BlockSpec(memory_space=pl.ANY)] + [vmem] * (window + 2),
        out_specs=[vmem] * window,
        scratch_shapes=[
            pltpu.VMEM((4, extent, rows, lanes), jnp.float32),
            slots,
            slots,
            slots,
            pltpu.VMEM((window, *shape), jnp.bfloat16),
            pltpu.SMEM(bounds.shape, jnp.int32),
            pltpu.SemaphoreType.DMA,
        ],
        compiler_params=pltpu.CompilerParams(vmem_limit_bytes=48 * 2**20),
        cost_estimate=pl.CostEstimate(
            flops=800 * extent * window * rows * lanes,
            bytes_accessed=2 * sum(block.size for block in (*own, *beside)),
            transcendentals=extent * window * heads * lanes,
        ),
        name="clips",
    )(bounds, *own, *beside)


def clip_bounds(clip_len, window):
    halo = window - 1
    extent = window + 2 * halo
    start = lax.axis_index("grp") * window - halo
    frames = start + jnp.arange(extent, dtype=jnp.int32)
    order = jnp.arange(clip_len.shape[0])
    ends = jnp.sum(jnp.where(order[:, None] <= order[None, :], clip_len[:, None], 0), axis=0)
    begins = ends - clip_len
    holds = (begins[None, :] <= frames[:, None]) & (frames[:, None] < ends[None, :])
    first = jnp.sum(jnp.where(holds, begins[None, :], 0), axis=1) - start
    last = jnp.sum(jnp.where(holds, ends[None, :], 0), axis=1) - start
    return jnp.stack([first, last]).astype(jnp.int32)


def tile_shards(q_space, k_space, v_space, cot_space, q_time, k_time, v_time, cot_time, clip_len):
    def turned(*arrays):
        return tuple(array.transpose(0, 2, 1) for array in arrays)

    n = lax.axis_size("seq")
    window = q_time.shape[0] * n
    tokens = q_time.shape[1]
    sharing = n * LANES // tokens
    bounds = clip_bounds(clip_len, window)
    time = turned(q_time, k_time, v_time, cot_time)
    spans = []
    head = 0
    for heads in CHUNKS:
        spans.append(slice(head * HDIM, (head + heads) * HDIM))
        head += heads
    space_in = turned(q_space, k_space, v_space, cot_space)
    packed = [list(split(time, span, n, sharing)) for span in spans]
    own = [exchange(packed[0])]
    space = space_grads(*space_in)
    packed[1][2:], own[0][2], space = gated(packed[1][2:], own[0][2], space)
    own.append(exchange(packed[1]))
    beside = [
        [neighbours(ends, start) for ends, start in zip(sides(blocks), (1, 0))] for blocks in own
    ]
    back, grads = [], None
    for blocks, near in zip(own, beside):
        back.append(exchange(clip_grads(bounds, blocks, near)))
    for span, blocks in zip(spans, back):
        grads = join(blocks, span, tokens, sharing, grads)
    return turned(*space, *grads)


def whole_tiles(mesh, tokens):
    n = mesh.shape["seq"]
    sharing = n * LANES // tokens
    return (
        tokens % LANES == 0
        and n % 4 == 0
        and n & (n - 1) == 0
        and mesh.shape["grp"] % 2 == 0
        and mesh.shape["grp"] > 2
        and sharing * tokens == n * LANES
        and all(heads % sharing == 0 and heads // sharing * HDIM % 16 == 0 for heads in CHUNKS)
    )


def padded(block, sides, width):
    for axis, dim in sides:
        count = lax.axis_size(axis)
        forward = [(i, i + 1) for i in range(count - 1)]
        backward = [(target, source) for source, target in forward]
        low = lax.ppermute(
            lax.slice_in_dim(block, block.shape[dim] - width, None, axis=dim), axis, forward
        )
        high = lax.ppermute(lax.slice_in_dim(block, 0, width, axis=dim), axis, backward)
        block = jnp.concatenate([low, block, high], axis=dim)
    return block


def shifted(value, axis, by):
    count = lax.axis_size(axis)
    pairs = [(i, i + by) for i in range(count) if 0 <= i + by < count]
    return lax.ppermute(value, axis, pairs)


def clip_labels(clip_len, first_frame, count, frame_total):
    frame_ids = first_frame + jnp.arange(count, dtype=jnp.int32)
    clip_ends = jnp.cumsum(clip_len)
    labels = jnp.sum((clip_ends[None, :] <= frame_ids[:, None]).astype(jnp.int32), axis=1)
    inside = (frame_ids >= 0) & (frame_ids < frame_total)
    return (labels, inside)


def frame_grads(queries, keys, values, cotangent):
    scaling = 1.0 / math.sqrt(HDIM)
    tokens = queries.shape[0]
    q_heads = queries.reshape(tokens, HEADS, HDIM)
    k_heads = keys.reshape(tokens, HEADS, HDIM)
    v_heads = values.reshape(tokens, HEADS, HDIM)
    g_heads = cotangent.reshape(tokens, HEADS, HDIM)
    scores = (
        jnp.einsum("qhd,khd->hqk", q_heads, k_heads, preferred_element_type=jnp.float32) * scaling
    )
    row_max = jnp.max(scores, axis=-1, keepdims=True)
    log_total = row_max + jnp.log(jnp.sum(jnp.exp(scores - row_max), axis=-1, keepdims=True))
    weights = jnp.exp(scores - log_total)
    weights_low = weights.astype(jnp.bfloat16)
    attended = jnp.einsum("hqk,khd->qhd", weights_low, v_heads, preferred_element_type=jnp.float32)
    row_dot = jnp.einsum("qhd,qhd->hq", g_heads.astype(jnp.float32), attended)
    weight_grad = jnp.einsum("qhd,khd->hqk", g_heads, v_heads, preferred_element_type=jnp.float32)
    score_grad = (weights * (weight_grad - row_dot[:, :, None])).astype(jnp.bfloat16)
    grad_query = (
        jnp.einsum("hqk,khd->qhd", score_grad, k_heads, preferred_element_type=jnp.float32)
        * scaling
    )
    grad_key = (
        jnp.einsum("hqk,qhd->khd", score_grad, q_heads, preferred_element_type=jnp.float32)
        * scaling
    )
    grad_value = jnp.einsum(
        "hqk,qhd->khd", weights_low, g_heads, preferred_element_type=jnp.float32
    )
    flat_shape = (1, tokens, HEADS * HDIM)
    return (
        grad_query.reshape(flat_shape).astype(jnp.bfloat16),
        grad_key.reshape(flat_shape).astype(jnp.bfloat16),
        grad_value.reshape(flat_shape).astype(jnp.bfloat16),
    )


def shards(q_space, k_space, v_space, cot_space, q_time, k_time, v_time, cot_time, clip_len):
    scaling = 1.0 / math.sqrt(HDIM)
    grad_qs, grad_ks, grad_vs = frame_grads(q_space[0], k_space[0], v_space[0], cot_space[0])
    moved = (
        lax.all_to_all(q_time, "seq", split_axis=1, concat_axis=0, tiled=True),
        lax.all_to_all(k_time, "seq", split_axis=1, concat_axis=0, tiled=True),
        lax.all_to_all(v_time, "seq", split_axis=1, concat_axis=0, tiled=True),
        lax.all_to_all(cot_time, "seq", split_axis=1, concat_axis=0, tiled=True),
    )
    query_win, key_win, value_win, cot_win = moved
    window = query_win.shape[0]
    places = query_win.shape[1]
    channels = query_win.shape[2]
    group_id = lax.axis_index("grp")
    frame_total = window * lax.axis_size("grp")
    first_frame = group_id * window

    def split_heads(array):
        return array.reshape(array.shape[0], places, HEADS, HDIM)

    key_pair = padded(jnp.stack([key_win, value_win]), (("grp", 1),), window)
    q_own = split_heads(query_win)
    g_own = split_heads(cot_win)
    k_ext = split_heads(key_pair[0])
    v_ext = split_heads(key_pair[1])
    own_label, own_inside = clip_labels(clip_len, first_frame, window, frame_total)
    ext_label, ext_inside = clip_labels(clip_len, first_frame - window, 3 * window, frame_total)
    allowed = (own_label[:, None] == ext_label[None, :]) & ext_inside[None, :]
    scores = (
        jnp.einsum("iphd,jphd->phij", q_own, k_ext, preferred_element_type=jnp.float32) * scaling
    )
    scores = jnp.where(allowed, scores, masked_score)
    row_max = jnp.max(scores, axis=-1)
    log_total = row_max + jnp.log(jnp.sum(jnp.exp(scores - row_max[..., None]), axis=-1))
    weights = jnp.where(allowed, jnp.exp(scores - log_total[..., None]), 0.0)
    weights_low = weights.astype(jnp.bfloat16)
    attended = jnp.einsum("phij,jphd->iphd", weights_low, v_ext, preferred_element_type=jnp.float32)
    row_dot = jnp.einsum("iphd,iphd->phi", g_own.astype(jnp.float32), attended)
    weight_grad = jnp.einsum("iphd,jphd->phij", g_own, v_ext, preferred_element_type=jnp.float32)
    score_grad = (weights * (weight_grad - row_dot[..., None])).astype(jnp.bfloat16)
    grad_query = (
        jnp.einsum("phij,jphd->iphd", score_grad, k_ext, preferred_element_type=jnp.float32)
        * scaling
    )
    key_terms = (
        jnp.einsum("phij,iphd->jphd", score_grad, q_own, preferred_element_type=jnp.float32)
        * scaling
    )
    value_terms = jnp.einsum(
        "phij,iphd->jphd", weights_low, g_own, preferred_element_type=jnp.float32
    )
    both_terms = jnp.stack([key_terms, value_terms]).reshape(2, 3 * window, places, channels)
    from_after = shifted(both_terms[:, :window], "grp", -1)
    from_before = shifted(both_terms[:, 2 * window :], "grp", 1)
    summed = both_terms[:, window : 2 * window] + from_after + from_before
    grad_key = summed[0]
    grad_value = summed[1]
    grad_qt, grad_kt, grad_vt = (
        lax.all_to_all(
            grad_query.reshape(window, places, channels).astype(jnp.bfloat16),
            "seq",
            split_axis=0,
            concat_axis=1,
            tiled=True,
        ),
        lax.all_to_all(
            grad_key.astype(jnp.bfloat16), "seq", split_axis=0, concat_axis=1, tiled=True
        ),
        lax.all_to_all(
            grad_value.astype(jnp.bfloat16), "seq", split_axis=0, concat_axis=1, tiled=True
        ),
    )
    return (grad_qs, grad_ks, grad_vs, grad_qt, grad_kt, grad_vt)


def solution(mesh):
    split_spec = P(("grp", "seq"), None, None)

    def mapped(body):
        return jax.shard_map(
            body,
            mesh=mesh,
            in_specs=(split_spec,) * 8 + (P(),),
            out_specs=(split_spec,) * 6,
            check_vma=False,
        )

    def grads(*arrays):
        return mapped(tile_shards if whole_tiles(mesh, arrays[0].shape[1]) else shards)(*arrays)

    return grads
```

```python
import functools
import math

import jax
import jax.numpy as jnp
from jax import lax
from jax.experimental import pallas as pl
from jax.experimental.pallas import tpu as pltpu
from jax.sharding import PartitionSpec as P

HEADS = 8
HDIM = 72
WIDTH = HEADS * HDIM
LANES = 128
SCALING = 1.0 / math.sqrt(HDIM)
CHUNKS = (4, 4)
masked_score = -1e30


def dot(left, right, left_dim, right_dim):
    dims = (((left_dim,), (right_dim,)), ((), ()))
    return lax.dot_general(left, right, dims, preferred_element_type=jnp.float32)


def rounded(value):
    return value.astype(jnp.bfloat16).astype(jnp.float32)


def frame_kernel(q_ref, k_ref, v_ref, g_ref, dq_ref, dk_ref, dv_ref):
    pair = 2 * HDIM
    reach = -(-HDIM // 16) * 16
    row = lax.broadcasted_iota(jnp.int32, (reach, 1), 0)
    for begin in range(0, WIDTH, pair):
        found = [[], [], []]
        for low, own in ((0, 0), (pair - reach, reach - HDIM)):
            span = slice(begin + low, begin + low + reach)
            mask = ((row >= own) & (row < own + HDIM)).astype(jnp.float32).astype(jnp.bfloat16)
            queries, keys = q_ref[0, span, :], k_ref[0, span, :]
            cotangent = g_ref[0, span, :]
            scores = dot(keys * mask, queries, 0, 0) * SCALING
            weight_grad = dot(v_ref[0, span, :] * mask, cotangent, 0, 0)
            raised = jnp.exp(scores - jnp.max(scores, axis=0, keepdims=True))
            weights = raised * (1.0 / jnp.sum(raised, axis=0, keepdims=True))
            weights_low = weights.astype(jnp.bfloat16)
            dots = jnp.sum(weights_low.astype(jnp.float32) * weight_grad, axis=0, keepdims=True)
            score_grad = (weights * (weight_grad - dots)).astype(jnp.bfloat16)
            rows = slice(own, own + HDIM)
            found[0].append(dot(keys, score_grad, 1, 0)[rows] * SCALING)
            found[1].append(dot(queries, score_grad, 1, 1)[rows] * SCALING)
            found[2].append(dot(cotangent, weights_low, 1, 1)[rows])
        for out, parts in zip((dq_ref, dk_ref, dv_ref), found):
            out[0, begin : begin + pair, :] = jnp.concatenate(parts, axis=0).astype(jnp.bfloat16)


def space_grads(queries, keys, values, cotangent):
    tokens = queries.shape[2]
    shape = jax.ShapeDtypeStruct(queries.shape, jnp.bfloat16)
    return pl.pallas_call(
        frame_kernel,
        out_shape=(shape, shape, shape),
        compiler_params=pltpu.CompilerParams(vmem_limit_bytes=60 * 2**20),
        cost_estimate=pl.CostEstimate(
            flops=12 * tokens * tokens * 256 * HEADS,
            bytes_accessed=14 * tokens * WIDTH,
            transcendentals=tokens * tokens * HEADS,
        ),
        name="space",
    )(queries, keys, values, cotangent)


def part_of(device, sharing, rows):
    row = pl.multiple_of(device % sharing * rows, 16)
    return row, pl.ds(pl.multiple_of(device // sharing * LANES, LANES), LANES)


def split_kernel(sharing, rows, span, *refs):
    ins, outs, (held, arrived, sent) = refs[:4], refs[4:-3], refs[-3:]
    loads, stores = {}, []
    for step in far_first(len(outs)):
        row, tokens = part_of(lax.axis_index("seq") ^ step, sharing, rows)
        for i, array in enumerate(ins):
            given = array.at[0, pl.ds(span.start + row, rows), tokens]
            loads[step, i] = pltpu.make_async_copy(given, held.at[step, i], arrived.at[step, i])
            loads[step, i].start()
    for step in far_first(len(outs)):
        for i in range(len(ins)):
            loads[step, i].wait()
        stores.append(pltpu.make_async_copy(held.at[step], outs[step], sent.at[step]))
        stores[-1].start()
    for copy in stores:
        copy.wait()


def split(arrays, span, n, sharing):
    rows = (span.stop - span.start) // sharing
    hbm = pl.BlockSpec(memory_space=pltpu.HBM)
    return pl.pallas_call(
        functools.partial(split_kernel, sharing, rows, span),
        in_specs=[hbm] * 4,
        out_specs=[hbm] * n,
        out_shape=[jax.ShapeDtypeStruct((4, rows, LANES), jnp.bfloat16)] * n,
        scratch_shapes=[
            pltpu.VMEM((n, 4, rows, LANES), jnp.bfloat16),
            pltpu.SemaphoreType.DMA((n, 4)),
            pltpu.SemaphoreType.DMA((n,)),
        ],
        compiler_params=pltpu.CompilerParams(vmem_limit_bytes=60 * 2**20),
        name="pack",
    )(*arrays)


def far_first(n):
    return [*reversed(range(n // 2, n)), *range(n // 2)]


def swap(block, axis, pairs):
    return lax.ppermute(block, axis, [(i, j) for i, j in pairs] + [(j, i) for i, j in pairs])


def exchange(blocks):
    n = len(blocks)
    moved = list(blocks)
    for step in reversed(range(1, n)):
        pairs = [[i, i ^ step] for i in range(n) if i < i ^ step]
        moved[step] = swap(blocks[step], "seq", pairs)
    return moved


def sides_kernel(n, *refs):
    ins, outs = refs[:n], refs[n:]
    is_odd = lax.axis_index("grp") & 1
    for step, ref in enumerate(ins):
        frame = lax.axis_index("seq") ^ step
        for start, out in zip((1, 0), outs):
            at = frame - jnp.where(is_odd == start, 1, 0)

            @pl.when((at >= 0) & (at < n - 1))
            def _():
                out[jnp.clip(at, 0, n - 2)] = ref[...]


def sides(blocks):
    n = len(blocks)
    shape = jax.ShapeDtypeStruct((n - 1, *blocks[0].shape), jnp.bfloat16)
    vmem = pl.BlockSpec(memory_space=pltpu.VMEM)
    return pl.pallas_call(
        functools.partial(sides_kernel, n),
        in_specs=[vmem] * n,
        out_specs=[vmem] * 2,
        out_shape=[shape] * 2,
        compiler_params=pltpu.CompilerParams(vmem_limit_bytes=24 * 2**20),
        name="sides",
    )(*blocks)


def gated(values, *earlier):
    return lax.optimization_barrier((values, *earlier))


def neighbours(block, start):
    count = lax.axis_size("grp")
    return swap(block, "grp", [(i, (i + 1) % count) for i in range(start, count, 2)])


def join_kernel(sharing, span, *refs):
    outs, sent = refs[-4:-1], refs[-1]
    rows = refs[0].shape[1]
    n = sent.shape[0]
    copies = []
    for at, step in enumerate(far_first(n)):
        row, tokens = part_of(lax.axis_index("seq") ^ step, sharing, rows)
        for i, out in enumerate(outs):
            given = out.at[0, pl.ds(span.start + row, rows), tokens]
            copies.append(pltpu.make_async_copy(refs[at].at[i], given, sent.at[step, i]))
            copies[-1].start()
    for copy in copies:
        copy.wait()


def join(blocks, span, tokens, sharing, earlier):
    n = len(blocks)
    shape = jax.ShapeDtypeStruct((1, WIDTH, tokens), jnp.bfloat16)
    hbm = pl.BlockSpec(memory_space=pltpu.HBM)
    earlier = [] if earlier is None else list(earlier)
    return pl.pallas_call(
        functools.partial(join_kernel, sharing, span),
        in_specs=[pl.BlockSpec(memory_space=pltpu.VMEM)] * n + [hbm] * len(earlier),
        out_specs=[hbm] * 3,
        out_shape=[shape] * 3,
        scratch_shapes=[pltpu.SemaphoreType.DMA((n, 3))],
        input_output_aliases={n + i: i for i in range(len(earlier))},
        compiler_params=pltpu.CompilerParams(vmem_limit_bytes=24 * 2**20),
        name="unpack",
    )(*(blocks[step] for step in far_first(n)), *earlier)


def clip_kernel(window, heads, given_bounds, *refs):
    own, sides_of = refs[:window], refs[window : window + 2]
    outs, refs = refs[window + 2 : 2 * window + 2], refs[2 * window + 2 :]
    wide, score_ref, grad_ref, weight_ref, found, bounds, arrived = refs
    copy = pltpu.make_async_copy(given_bounds, bounds, arrived)
    copy.start()
    halo = window - 1
    extent = window + 2 * halo
    queries, keys, values, cotangent = range(4)

    def widen(ref, frame):
        for i in range(4):
            wide[i, frame] = ref[i].astype(jnp.float32)

    for step, ref in enumerate(own):
        widen(ref, halo + (lax.axis_index("seq") ^ step))
    copy.wait()
    lowest, highest = bounds[0, halo], bounds[1, halo + window - 1]
    for start, ref in zip((1, 0), sides_of):
        is_next = (lax.axis_index("grp") & 1) == start
        for at in range(halo):
            frame = at + jnp.where(is_next, halo + window, 0)
            needed = (frame >= lowest) & (frame < highest)
            pl.when(needed)(functools.partial(widen, ref.at[at], frame))

    def partners(frame):
        first, last = bounds[0, frame], bounds[1, frame]
        return first, last - first, [jnp.minimum(first + t, last - 1) for t in range(window)]

    def products(frame, carry):
        first, count, others = partners(frame)
        scores, grads = [[] for _ in others], [[] for _ in others]
        for head in range(heads):
            span = slice(head * HDIM, (head + 1) * HDIM)
            query, cot = wide[queries, frame, span, :], wide[cotangent, frame, span, :]
            for t, other in enumerate(others):
                score = jnp.sum(query * wide[keys, other, span, :], axis=0, keepdims=True)
                grad = jnp.sum(cot * wide[values, other, span, :], axis=0, keepdims=True)
                scores[t].append(score)
                grads[t].append(grad)
        for t in range(window):
            bias = jnp.where(t < count, 0.0, masked_score)
            score_ref[t, frame] = jnp.concatenate(scores[t], axis=0) * SCALING + bias
            grad_ref[t, frame] = jnp.concatenate(grads[t], axis=0)
        return carry

    lax.fori_loop(lowest, highest, products, 0)
    scores, grads = [score_ref[t] for t in range(window)], [grad_ref[t] for t in range(window)]
    peak = functools.reduce(jnp.maximum, scores)
    raised = [jnp.exp(score - peak) for score in scores]
    inverse = 1.0 / functools.reduce(jnp.add, raised)
    weights = [part * inverse for part in raised]
    weights_low = [rounded(part) for part in weights]
    dots = functools.reduce(jnp.add, [w * d for w, d in zip(weights_low, grads)])
    for t in range(window):
        weight_ref[t] = weights_low[t]
        score_ref[t] = rounded(weights[t] * (grads[t] - dots))

    def gradients(at, carry):
        frame = halo + at
        first, count, others = partners(frame)
        place = frame - first
        sums = [[], [], []]
        for head in range(heads):
            span, row = slice(head * HDIM, (head + 1) * HDIM), slice(head, head + 1)
            totals = [None] * 3
            for t, other in enumerate(others):
                score_back = jnp.where(t < count, score_ref[place, other, row, :], 0.0)
                weight_back = jnp.where(t < count, weight_ref[place, other, row, :], 0.0)
                terms = (
                    score_ref[t, frame, row, :] * wide[keys, other, span, :],
                    score_back * wide[queries, other, span, :],
                    weight_back * wide[cotangent, other, span, :],
                )
                totals = [x if y is None else y + x for x, y in zip(terms, totals)]
            for held, total, scale in zip(sums, totals, (SCALING, SCALING, None)):
                held.append(total if scale is None else total * scale)
        for i, parts in enumerate(sums):
            found[at, i] = jnp.concatenate(parts, axis=0).astype(jnp.bfloat16)
        return carry

    lax.fori_loop(0, window, gradients, 0)
    for step, out in enumerate(outs):
        out[...] = found[lax.axis_index("seq") ^ step]


def clip_grads(bounds, own, beside):
    window = len(own)
    _, rows, lanes = own[0].shape
    heads = rows // HDIM
    extent = 3 * window - 2
    vmem = pl.BlockSpec(memory_space=pltpu.VMEM)
    shape = (3, rows, lanes)
    slots = pltpu.VMEM((window, extent, heads, lanes), jnp.float32)
    return pl.pallas_call(
        functools.partial(clip_kernel, window, heads),
        out_shape=[jax.ShapeDtypeStruct(shape, jnp.bfloat16)] * window,
        in_specs=[pl.BlockSpec(memory_space=pl.ANY)] + [vmem] * (window + 2),
        out_specs=[vmem] * window,
        scratch_shapes=[
            pltpu.VMEM((4, extent, rows, lanes), jnp.float32),
            slots,
            slots,
            slots,
            pltpu.VMEM((window, *shape), jnp.bfloat16),
            pltpu.SMEM(bounds.shape, jnp.int32),
            pltpu.SemaphoreType.DMA,
        ],
        compiler_params=pltpu.CompilerParams(vmem_limit_bytes=48 * 2**20),
        cost_estimate=pl.CostEstimate(
            flops=800 * extent * window * rows * lanes,
            bytes_accessed=2 * sum(block.size for block in (*own, *beside)),
            transcendentals=extent * window * heads * lanes,
        ),
        name="clips",
    )(bounds, *own, *beside)


def clip_bounds(clip_len, window):
    halo = window - 1
    extent = window + 2 * halo
    start = lax.axis_index("grp") * window - halo
    frames = start + jnp.arange(extent, dtype=jnp.int32)
    order = jnp.arange(clip_len.shape[0])
    ends = jnp.sum(jnp.where(order[:, None] <= order[None, :], clip_len[:, None], 0), axis=0)
    begins = ends - clip_len
    holds = (begins[None, :] <= frames[:, None]) & (frames[:, None] < ends[None, :])
    first = jnp.sum(jnp.where(holds, begins[None, :], 0), axis=1) - start
    last = jnp.sum(jnp.where(holds, ends[None, :], 0), axis=1) - start
    return jnp.stack([first, last]).astype(jnp.int32)


def tile_shards(q_space, k_space, v_space, cot_space, q_time, k_time, v_time, cot_time, clip_len):
    def turned(*arrays):
        return tuple(array.transpose(0, 2, 1) for array in arrays)

    n = lax.axis_size("seq")
    window = q_time.shape[0] * n
    tokens = q_time.shape[1]
    sharing = n * LANES // tokens
    bounds = clip_bounds(clip_len, window)
    time = turned(q_time, k_time, v_time, cot_time)
    spans = []
    head = 0
    for heads in CHUNKS:
        spans.append(slice(head * HDIM, (head + heads) * HDIM))
        head += heads
    space_in = turned(q_space, k_space, v_space, cot_space)
    packed = [split(time, span, n, sharing) for span in spans]
    own = [exchange(blocks) for blocks in packed]
    space = space_grads(*space_in)
    beside = [
        [neighbours(ends, start) for ends, start in zip(sides(blocks), (1, 0))] for blocks in own
    ]
    back, grads = [], None
    for blocks, near in zip(own, beside):
        back.append(exchange(clip_grads(bounds, blocks, near)))
    for span, blocks in zip(spans, back):
        grads = join(blocks, span, tokens, sharing, grads)
    return turned(*space, *grads)


def whole_tiles(mesh, tokens):
    n = mesh.shape["seq"]
    sharing = n * LANES // tokens
    return (
        tokens % LANES == 0
        and n % 4 == 0
        and n & (n - 1) == 0
        and mesh.shape["grp"] % 2 == 0
        and mesh.shape["grp"] > 2
        and sharing * tokens == n * LANES
        and all(heads % sharing == 0 and heads // sharing * HDIM % 16 == 0 for heads in CHUNKS)
    )


def padded(block, sides, width):
    for axis, dim in sides:
        count = lax.axis_size(axis)
        forward = [(i, i + 1) for i in range(count - 1)]
        backward = [(target, source) for source, target in forward]
        low = lax.ppermute(
            lax.slice_in_dim(block, block.shape[dim] - width, None, axis=dim), axis, forward
        )
        high = lax.ppermute(lax.slice_in_dim(block, 0, width, axis=dim), axis, backward)
        block = jnp.concatenate([low, block, high], axis=dim)
    return block


def shifted(value, axis, by):
    count = lax.axis_size(axis)
    pairs = [(i, i + by) for i in range(count) if 0 <= i + by < count]
    return lax.ppermute(value, axis, pairs)


def clip_labels(clip_len, first_frame, count, frame_total):
    frame_ids = first_frame + jnp.arange(count, dtype=jnp.int32)
    clip_ends = jnp.cumsum(clip_len)
    labels = jnp.sum((clip_ends[None, :] <= frame_ids[:, None]).astype(jnp.int32), axis=1)
    inside = (frame_ids >= 0) & (frame_ids < frame_total)
    return (labels, inside)


def frame_grads(queries, keys, values, cotangent):
    scaling = 1.0 / math.sqrt(HDIM)
    tokens = queries.shape[0]
    q_heads = queries.reshape(tokens, HEADS, HDIM)
    k_heads = keys.reshape(tokens, HEADS, HDIM)
    v_heads = values.reshape(tokens, HEADS, HDIM)
    g_heads = cotangent.reshape(tokens, HEADS, HDIM)
    scores = (
        jnp.einsum("qhd,khd->hqk", q_heads, k_heads, preferred_element_type=jnp.float32) * scaling
    )
    row_max = jnp.max(scores, axis=-1, keepdims=True)
    log_total = row_max + jnp.log(jnp.sum(jnp.exp(scores - row_max), axis=-1, keepdims=True))
    weights = jnp.exp(scores - log_total)
    weights_low = weights.astype(jnp.bfloat16)
    attended = jnp.einsum("hqk,khd->qhd", weights_low, v_heads, preferred_element_type=jnp.float32)
    row_dot = jnp.einsum("qhd,qhd->hq", g_heads.astype(jnp.float32), attended)
    weight_grad = jnp.einsum("qhd,khd->hqk", g_heads, v_heads, preferred_element_type=jnp.float32)
    score_grad = (weights * (weight_grad - row_dot[:, :, None])).astype(jnp.bfloat16)
    grad_query = (
        jnp.einsum("hqk,khd->qhd", score_grad, k_heads, preferred_element_type=jnp.float32)
        * scaling
    )
    grad_key = (
        jnp.einsum("hqk,qhd->khd", score_grad, q_heads, preferred_element_type=jnp.float32)
        * scaling
    )
    grad_value = jnp.einsum(
        "hqk,qhd->khd", weights_low, g_heads, preferred_element_type=jnp.float32
    )
    flat_shape = (1, tokens, HEADS * HDIM)
    return (
        grad_query.reshape(flat_shape).astype(jnp.bfloat16),
        grad_key.reshape(flat_shape).astype(jnp.bfloat16),
        grad_value.reshape(flat_shape).astype(jnp.bfloat16),
    )


def shards(q_space, k_space, v_space, cot_space, q_time, k_time, v_time, cot_time, clip_len):
    scaling = 1.0 / math.sqrt(HDIM)
    grad_qs, grad_ks, grad_vs = frame_grads(q_space[0], k_space[0], v_space[0], cot_space[0])
    moved = (
        lax.all_to_all(q_time, "seq", split_axis=1, concat_axis=0, tiled=True),
        lax.all_to_all(k_time, "seq", split_axis=1, concat_axis=0, tiled=True),
        lax.all_to_all(v_time, "seq", split_axis=1, concat_axis=0, tiled=True),
        lax.all_to_all(cot_time, "seq", split_axis=1, concat_axis=0, tiled=True),
    )
    query_win, key_win, value_win, cot_win = moved
    window = query_win.shape[0]
    places = query_win.shape[1]
    channels = query_win.shape[2]
    group_id = lax.axis_index("grp")
    frame_total = window * lax.axis_size("grp")
    first_frame = group_id * window

    def split_heads(array):
        return array.reshape(array.shape[0], places, HEADS, HDIM)

    key_pair = padded(jnp.stack([key_win, value_win]), (("grp", 1),), window)
    q_own = split_heads(query_win)
    g_own = split_heads(cot_win)
    k_ext = split_heads(key_pair[0])
    v_ext = split_heads(key_pair[1])
    own_label, own_inside = clip_labels(clip_len, first_frame, window, frame_total)
    ext_label, ext_inside = clip_labels(clip_len, first_frame - window, 3 * window, frame_total)
    allowed = (own_label[:, None] == ext_label[None, :]) & ext_inside[None, :]
    scores = (
        jnp.einsum("iphd,jphd->phij", q_own, k_ext, preferred_element_type=jnp.float32) * scaling
    )
    scores = jnp.where(allowed, scores, masked_score)
    row_max = jnp.max(scores, axis=-1)
    log_total = row_max + jnp.log(jnp.sum(jnp.exp(scores - row_max[..., None]), axis=-1))
    weights = jnp.where(allowed, jnp.exp(scores - log_total[..., None]), 0.0)
    weights_low = weights.astype(jnp.bfloat16)
    attended = jnp.einsum("phij,jphd->iphd", weights_low, v_ext, preferred_element_type=jnp.float32)
    row_dot = jnp.einsum("iphd,iphd->phi", g_own.astype(jnp.float32), attended)
    weight_grad = jnp.einsum("iphd,jphd->phij", g_own, v_ext, preferred_element_type=jnp.float32)
    score_grad = (weights * (weight_grad - row_dot[..., None])).astype(jnp.bfloat16)
    grad_query = (
        jnp.einsum("phij,jphd->iphd", score_grad, k_ext, preferred_element_type=jnp.float32)
        * scaling
    )
    key_terms = (
        jnp.einsum("phij,iphd->jphd", score_grad, q_own, preferred_element_type=jnp.float32)
        * scaling
    )
    value_terms = jnp.einsum(
        "phij,iphd->jphd", weights_low, g_own, preferred_element_type=jnp.float32
    )
    both_terms = jnp.stack([key_terms, value_terms]).reshape(2, 3 * window, places, channels)
    from_after = shifted(both_terms[:, :window], "grp", -1)
    from_before = shifted(both_terms[:, 2 * window :], "grp", 1)
    summed = both_terms[:, window : 2 * window] + from_after + from_before
    grad_key = summed[0]
    grad_value = summed[1]
    grad_qt, grad_kt, grad_vt = (
        lax.all_to_all(
            grad_query.reshape(window, places, channels).astype(jnp.bfloat16),
            "seq",
            split_axis=0,
            concat_axis=1,
            tiled=True,
        ),
        lax.all_to_all(
            grad_key.astype(jnp.bfloat16), "seq", split_axis=0, concat_axis=1, tiled=True
        ),
        lax.all_to_all(
            grad_value.astype(jnp.bfloat16), "seq", split_axis=0, concat_axis=1, tiled=True
        ),
    )
    return (grad_qs, grad_ks, grad_vs, grad_qt, grad_kt, grad_vt)


def solution(mesh):
    split_spec = P(("grp", "seq"), None, None)

    def mapped(body):
        return jax.shard_map(
            body,
            mesh=mesh,
            in_specs=(split_spec,) * 8 + (P(),),
            out_specs=(split_spec,) * 6,
            check_vma=False,
        )

    def grads(*arrays):
        return mapped(tile_shards if whole_tiles(mesh, arrays[0].shape[1]) else shards)(*arrays)

    return grads
```

```python
import functools
import math

import jax
import jax.numpy as jnp
from jax import lax
from jax.experimental import pallas as pl
from jax.experimental.pallas import tpu as pltpu
from jax.sharding import PartitionSpec as P

HEADS = 8
HDIM = 72
WIDTH = HEADS * HDIM
LANES = 128
SCALING = 1.0 / math.sqrt(HDIM)
CHUNKS = (4, 4)
masked_score = -1e30


def dot(left, right, left_dim, right_dim):
    dims = (((left_dim,), (right_dim,)), ((), ()))
    return lax.dot_general(left, right, dims, preferred_element_type=jnp.float32)


def rounded(value):
    return value.astype(jnp.bfloat16).astype(jnp.float32)


def frame_kernel(q_ref, k_ref, v_ref, g_ref, dq_ref, dk_ref, dv_ref):
    pair = 2 * HDIM
    reach = -(-HDIM // 16) * 16
    row = lax.broadcasted_iota(jnp.int32, (reach, 1), 0)
    for begin in range(0, WIDTH, pair):
        found = [[], [], []]
        for low, own in ((0, 0), (pair - reach, reach - HDIM)):
            span = slice(begin + low, begin + low + reach)
            mask = ((row >= own) & (row < own + HDIM)).astype(jnp.float32).astype(jnp.bfloat16)
            queries, keys = q_ref[0, span, :], k_ref[0, span, :]
            cotangent = g_ref[0, span, :]
            scores = dot(keys * mask, queries, 0, 0) * SCALING
            weight_grad = dot(v_ref[0, span, :] * mask, cotangent, 0, 0)
            raised = jnp.exp(scores - jnp.max(scores, axis=0, keepdims=True))
            weights = raised * (1.0 / jnp.sum(raised, axis=0, keepdims=True))
            weights_low = weights.astype(jnp.bfloat16)
            dots = jnp.sum(weights_low.astype(jnp.float32) * weight_grad, axis=0, keepdims=True)
            score_grad = (weights * (weight_grad - dots)).astype(jnp.bfloat16)
            rows = slice(own, own + HDIM)
            found[0].append(dot(keys, score_grad, 1, 0)[rows] * SCALING)
            found[1].append(dot(queries, score_grad, 1, 1)[rows] * SCALING)
            found[2].append(dot(cotangent, weights_low, 1, 1)[rows])
        for out, parts in zip((dq_ref, dk_ref, dv_ref), found):
            out[0, begin : begin + pair, :] = jnp.concatenate(parts, axis=0).astype(jnp.bfloat16)


def space_grads(queries, keys, values, cotangent):
    tokens = queries.shape[2]
    shape = jax.ShapeDtypeStruct(queries.shape, jnp.bfloat16)
    return pl.pallas_call(
        frame_kernel,
        out_shape=(shape, shape, shape),
        compiler_params=pltpu.CompilerParams(vmem_limit_bytes=60 * 2**20),
        cost_estimate=pl.CostEstimate(
            flops=12 * tokens * tokens * 256 * HEADS,
            bytes_accessed=14 * tokens * WIDTH,
            transcendentals=tokens * tokens * HEADS,
        ),
        name="space",
    )(queries, keys, values, cotangent)


def part_of(device, sharing, rows):
    row = pl.multiple_of(device % sharing * rows, 16)
    return row, pl.ds(pl.multiple_of(device // sharing * LANES, LANES), LANES)


def split_kernel(sharing, rows, span, *refs):
    ins, outs, (held, arrived, sent) = refs[:4], refs[4:-3], refs[-3:]
    loads, stores = {}, []
    for step in far_first(len(outs)):
        row, tokens = part_of(lax.axis_index("seq") ^ step, sharing, rows)
        for i, array in enumerate(ins):
            given = array.at[0, pl.ds(span.start + row, rows), tokens]
            loads[step, i] = pltpu.make_async_copy(given, held.at[step, i], arrived.at[step, i])
            loads[step, i].start()
    for step in far_first(len(outs)):
        for i in range(len(ins)):
            loads[step, i].wait()
        stores.append(pltpu.make_async_copy(held.at[step], outs[step], sent.at[step]))
        stores[-1].start()
    for copy in stores:
        copy.wait()


def split(arrays, span, n, sharing):
    rows = (span.stop - span.start) // sharing
    hbm = pl.BlockSpec(memory_space=pltpu.HBM)
    return pl.pallas_call(
        functools.partial(split_kernel, sharing, rows, span),
        in_specs=[hbm] * 4,
        out_specs=[hbm] * n,
        out_shape=[jax.ShapeDtypeStruct((4, rows, LANES), jnp.bfloat16)] * n,
        scratch_shapes=[
            pltpu.VMEM((n, 4, rows, LANES), jnp.bfloat16),
            pltpu.SemaphoreType.DMA((n, 4)),
            pltpu.SemaphoreType.DMA((n,)),
        ],
        compiler_params=pltpu.CompilerParams(vmem_limit_bytes=60 * 2**20),
        name="pack",
    )(*arrays)


def far_first(n):
    return [*reversed(range(n // 2, n)), *range(n // 2)]


def swap(block, axis, pairs):
    return lax.ppermute(block, axis, [(i, j) for i, j in pairs] + [(j, i) for i, j in pairs])


def exchange(blocks):
    n = len(blocks)
    moved = list(blocks)
    for step in reversed(range(1, n)):
        pairs = [[i, i ^ step] for i in range(n) if i < i ^ step]
        moved[step] = swap(blocks[step], "seq", pairs)
    return moved


def sides_kernel(n, *refs):
    ins, outs = refs[:n], refs[n:]
    is_odd = lax.axis_index("grp") & 1
    for step, ref in enumerate(ins):
        frame = lax.axis_index("seq") ^ step
        for start, out in zip((1, 0), outs):
            at = frame - jnp.where(is_odd == start, 1, 0)

            @pl.when((at >= 0) & (at < n - 1))
            def _():
                out[jnp.clip(at, 0, n - 2)] = ref[...]


def sides(blocks):
    n = len(blocks)
    shape = jax.ShapeDtypeStruct((n - 1, *blocks[0].shape), jnp.bfloat16)
    vmem = pl.BlockSpec(memory_space=pltpu.VMEM)
    return pl.pallas_call(
        functools.partial(sides_kernel, n),
        in_specs=[vmem] * n,
        out_specs=[vmem] * 2,
        out_shape=[shape] * 2,
        compiler_params=pltpu.CompilerParams(vmem_limit_bytes=24 * 2**20),
        name="sides",
    )(*blocks)


def gated(values, *earlier):
    return lax.optimization_barrier((values, *earlier))


def neighbours(block, start):
    count = lax.axis_size("grp")
    return swap(block, "grp", [(i, (i + 1) % count) for i in range(start, count, 2)])


def join_kernel(sharing, span, *refs):
    outs, sent = refs[-4:-1], refs[-1]
    rows = refs[0].shape[1]
    n = sent.shape[0]
    copies = []
    for at, step in enumerate(far_first(n)):
        row, tokens = part_of(lax.axis_index("seq") ^ step, sharing, rows)
        for i, out in enumerate(outs):
            given = out.at[0, pl.ds(span.start + row, rows), tokens]
            copies.append(pltpu.make_async_copy(refs[at].at[i], given, sent.at[step, i]))
            copies[-1].start()
    for copy in copies:
        copy.wait()


def join(blocks, span, tokens, sharing, earlier):
    n = len(blocks)
    shape = jax.ShapeDtypeStruct((1, WIDTH, tokens), jnp.bfloat16)
    hbm = pl.BlockSpec(memory_space=pltpu.HBM)
    earlier = [] if earlier is None else list(earlier)
    return pl.pallas_call(
        functools.partial(join_kernel, sharing, span),
        in_specs=[pl.BlockSpec(memory_space=pltpu.VMEM)] * n + [hbm] * len(earlier),
        out_specs=[hbm] * 3,
        out_shape=[shape] * 3,
        scratch_shapes=[pltpu.SemaphoreType.DMA((n, 3))],
        input_output_aliases={n + i: i for i in range(len(earlier))},
        compiler_params=pltpu.CompilerParams(vmem_limit_bytes=24 * 2**20),
        name="unpack",
    )(*(blocks[step] for step in far_first(n)), *earlier)


def clip_kernel(window, heads, given_bounds, *refs):
    own, sides_of = refs[:window], refs[window : window + 2]
    outs, refs = refs[window + 2 : 2 * window + 2], refs[2 * window + 2 :]
    wide, score_ref, grad_ref, weight_ref, found, bounds, arrived = refs
    copy = pltpu.make_async_copy(given_bounds, bounds, arrived)
    copy.start()
    halo = window - 1
    extent = window + 2 * halo
    queries, keys, values, cotangent = range(4)

    def widen(ref, frame):
        for i in range(4):
            wide[i, frame] = ref[i].astype(jnp.float32)

    for step, ref in enumerate(own):
        widen(ref, halo + (lax.axis_index("seq") ^ step))
    for start, ref in zip((1, 0), sides_of):
        is_next = (lax.axis_index("grp") & 1) == start
        for at in range(halo):
            widen(ref.at[at], at + jnp.where(is_next, halo + window, 0))
    copy.wait()
    lowest, highest = bounds[0, halo], bounds[1, halo + window - 1]

    def partners(frame):
        first, last = bounds[0, frame], bounds[1, frame]
        return first, last - first, [jnp.minimum(first + t, last - 1) for t in range(window)]

    def products(frame, carry):
        first, count, others = partners(frame)
        scores, grads = [[] for _ in others], [[] for _ in others]
        for head in range(heads):
            span = slice(head * HDIM, (head + 1) * HDIM)
            query, cot = wide[queries, frame, span, :], wide[cotangent, frame, span, :]
            for t, other in enumerate(others):
                score = jnp.sum(query * wide[keys, other, span, :], axis=0, keepdims=True)
                grad = jnp.sum(cot * wide[values, other, span, :], axis=0, keepdims=True)
                scores[t].append(score)
                grads[t].append(grad)
        for t in range(window):
            bias = jnp.where(t < count, 0.0, masked_score)
            score_ref[t, frame] = jnp.concatenate(scores[t], axis=0) * SCALING + bias
            grad_ref[t, frame] = jnp.concatenate(grads[t], axis=0)
        return carry

    lax.fori_loop(lowest, highest, products, 0)
    scores, grads = [score_ref[t] for t in range(window)], [grad_ref[t] for t in range(window)]
    peak = functools.reduce(jnp.maximum, scores)
    raised = [jnp.exp(score - peak) for score in scores]
    inverse = 1.0 / functools.reduce(jnp.add, raised)
    weights = [part * inverse for part in raised]
    weights_low = [rounded(part) for part in weights]
    dots = functools.reduce(jnp.add, [w * d for w, d in zip(weights_low, grads)])
    for t in range(window):
        weight_ref[t] = weights_low[t]
        score_ref[t] = rounded(weights[t] * (grads[t] - dots))

    def gradients(at, carry):
        frame = halo + at
        first, count, others = partners(frame)
        place = frame - first
        sums = [[], [], []]
        for head in range(heads):
            span, row = slice(head * HDIM, (head + 1) * HDIM), slice(head, head + 1)
            totals = [None] * 3
            for t, other in enumerate(others):
                score_back = jnp.where(t < count, score_ref[place, other, row, :], 0.0)
                weight_back = jnp.where(t < count, weight_ref[place, other, row, :], 0.0)
                terms = (
                    score_ref[t, frame, row, :] * wide[keys, other, span, :],
                    score_back * wide[queries, other, span, :],
                    weight_back * wide[cotangent, other, span, :],
                )
                totals = [x if y is None else y + x for x, y in zip(terms, totals)]
            for held, total, scale in zip(sums, totals, (SCALING, SCALING, None)):
                held.append(total if scale is None else total * scale)
        for i, parts in enumerate(sums):
            found[at, i] = jnp.concatenate(parts, axis=0).astype(jnp.bfloat16)
        return carry

    lax.fori_loop(0, window, gradients, 0)
    for step, out in enumerate(outs):
        out[...] = found[lax.axis_index("seq") ^ step]


def clip_grads(bounds, own, beside):
    window = len(own)
    _, rows, lanes = own[0].shape
    heads = rows // HDIM
    extent = 3 * window - 2
    vmem = pl.BlockSpec(memory_space=pltpu.VMEM)
    shape = (3, rows, lanes)
    slots = pltpu.VMEM((window, extent, heads, lanes), jnp.float32)
    return pl.pallas_call(
        functools.partial(clip_kernel, window, heads),
        out_shape=[jax.ShapeDtypeStruct(shape, jnp.bfloat16)] * window,
        in_specs=[pl.BlockSpec(memory_space=pl.ANY)] + [vmem] * (window + 2),
        out_specs=[vmem] * window,
        scratch_shapes=[
            pltpu.VMEM((4, extent, rows, lanes), jnp.float32),
            slots,
            slots,
            slots,
            pltpu.VMEM((window, *shape), jnp.bfloat16),
            pltpu.SMEM(bounds.shape, jnp.int32),
            pltpu.SemaphoreType.DMA,
        ],
        compiler_params=pltpu.CompilerParams(vmem_limit_bytes=48 * 2**20),
        cost_estimate=pl.CostEstimate(
            flops=800 * extent * window * rows * lanes,
            bytes_accessed=2 * sum(block.size for block in (*own, *beside)),
            transcendentals=extent * window * heads * lanes,
        ),
        name="clips",
    )(bounds, *own, *beside)


def clip_bounds(clip_len, window):
    halo = window - 1
    extent = window + 2 * halo
    start = lax.axis_index("grp") * window - halo
    frames = start + jnp.arange(extent, dtype=jnp.int32)
    order = jnp.arange(clip_len.shape[0])
    ends = jnp.sum(jnp.where(order[:, None] <= order[None, :], clip_len[:, None], 0), axis=0)
    begins = ends - clip_len
    holds = (begins[None, :] <= frames[:, None]) & (frames[:, None] < ends[None, :])
    first = jnp.sum(jnp.where(holds, begins[None, :], 0), axis=1) - start
    last = jnp.sum(jnp.where(holds, ends[None, :], 0), axis=1) - start
    return jnp.stack([first, last]).astype(jnp.int32)


def tile_shards(q_space, k_space, v_space, cot_space, q_time, k_time, v_time, cot_time, clip_len):
    def turned(*arrays):
        return tuple(array.transpose(0, 2, 1) for array in arrays)

    n = lax.axis_size("seq")
    window = q_time.shape[0] * n
    tokens = q_time.shape[1]
    sharing = n * LANES // tokens
    bounds = clip_bounds(clip_len, window)
    time = turned(q_time, k_time, v_time, cot_time)
    spans = []
    head = 0
    for heads in CHUNKS:
        spans.append(slice(head * HDIM, (head + heads) * HDIM))
        head += heads
    space_in = turned(q_space, k_space, v_space, cot_space)
    packed = [list(split(time, span, n, sharing)) for span in spans]
    own = [exchange(packed[0])]
    packed[1][n // 2 :], own[0][-1] = gated(packed[1][n // 2 :], own[0][-1])
    own.append(exchange(packed[1]))
    space = space_grads(*space_in)
    beside = [
        [neighbours(ends, start) for ends, start in zip(sides(blocks), (1, 0))] for blocks in own
    ]
    back, grads = [], None
    for blocks, near in zip(own, beside):
        back.append(exchange(clip_grads(bounds, blocks, near)))
    for span, blocks in zip(spans, back):
        grads = join(blocks, span, tokens, sharing, grads)
    return turned(*space, *grads)


def whole_tiles(mesh, tokens):
    n = mesh.shape["seq"]
    sharing = n * LANES // tokens
    return (
        tokens % LANES == 0
        and n % 4 == 0
        and n & (n - 1) == 0
        and mesh.shape["grp"] % 2 == 0
        and mesh.shape["grp"] > 2
        and sharing * tokens == n * LANES
        and all(heads % sharing == 0 and heads // sharing * HDIM % 16 == 0 for heads in CHUNKS)
    )


def padded(block, sides, width):
    for axis, dim in sides:
        count = lax.axis_size(axis)
        forward = [(i, i + 1) for i in range(count - 1)]
        backward = [(target, source) for source, target in forward]
        low = lax.ppermute(
            lax.slice_in_dim(block, block.shape[dim] - width, None, axis=dim), axis, forward
        )
        high = lax.ppermute(lax.slice_in_dim(block, 0, width, axis=dim), axis, backward)
        block = jnp.concatenate([low, block, high], axis=dim)
    return block


def shifted(value, axis, by):
    count = lax.axis_size(axis)
    pairs = [(i, i + by) for i in range(count) if 0 <= i + by < count]
    return lax.ppermute(value, axis, pairs)


def clip_labels(clip_len, first_frame, count, frame_total):
    frame_ids = first_frame + jnp.arange(count, dtype=jnp.int32)
    clip_ends = jnp.cumsum(clip_len)
    labels = jnp.sum((clip_ends[None, :] <= frame_ids[:, None]).astype(jnp.int32), axis=1)
    inside = (frame_ids >= 0) & (frame_ids < frame_total)
    return (labels, inside)


def frame_grads(queries, keys, values, cotangent):
    scaling = 1.0 / math.sqrt(HDIM)
    tokens = queries.shape[0]
    q_heads = queries.reshape(tokens, HEADS, HDIM)
    k_heads = keys.reshape(tokens, HEADS, HDIM)
    v_heads = values.reshape(tokens, HEADS, HDIM)
    g_heads = cotangent.reshape(tokens, HEADS, HDIM)
    scores = (
        jnp.einsum("qhd,khd->hqk", q_heads, k_heads, preferred_element_type=jnp.float32) * scaling
    )
    row_max = jnp.max(scores, axis=-1, keepdims=True)
    log_total = row_max + jnp.log(jnp.sum(jnp.exp(scores - row_max), axis=-1, keepdims=True))
    weights = jnp.exp(scores - log_total)
    weights_low = weights.astype(jnp.bfloat16)
    attended = jnp.einsum("hqk,khd->qhd", weights_low, v_heads, preferred_element_type=jnp.float32)
    row_dot = jnp.einsum("qhd,qhd->hq", g_heads.astype(jnp.float32), attended)
    weight_grad = jnp.einsum("qhd,khd->hqk", g_heads, v_heads, preferred_element_type=jnp.float32)
    score_grad = (weights * (weight_grad - row_dot[:, :, None])).astype(jnp.bfloat16)
    grad_query = (
        jnp.einsum("hqk,khd->qhd", score_grad, k_heads, preferred_element_type=jnp.float32)
        * scaling
    )
    grad_key = (
        jnp.einsum("hqk,qhd->khd", score_grad, q_heads, preferred_element_type=jnp.float32)
        * scaling
    )
    grad_value = jnp.einsum(
        "hqk,qhd->khd", weights_low, g_heads, preferred_element_type=jnp.float32
    )
    flat_shape = (1, tokens, HEADS * HDIM)
    return (
        grad_query.reshape(flat_shape).astype(jnp.bfloat16),
        grad_key.reshape(flat_shape).astype(jnp.bfloat16),
        grad_value.reshape(flat_shape).astype(jnp.bfloat16),
    )


def shards(q_space, k_space, v_space, cot_space, q_time, k_time, v_time, cot_time, clip_len):
    scaling = 1.0 / math.sqrt(HDIM)
    grad_qs, grad_ks, grad_vs = frame_grads(q_space[0], k_space[0], v_space[0], cot_space[0])
    moved = (
        lax.all_to_all(q_time, "seq", split_axis=1, concat_axis=0, tiled=True),
        lax.all_to_all(k_time, "seq", split_axis=1, concat_axis=0, tiled=True),
        lax.all_to_all(v_time, "seq", split_axis=1, concat_axis=0, tiled=True),
        lax.all_to_all(cot_time, "seq", split_axis=1, concat_axis=0, tiled=True),
    )
    query_win, key_win, value_win, cot_win = moved
    window = query_win.shape[0]
    places = query_win.shape[1]
    channels = query_win.shape[2]
    group_id = lax.axis_index("grp")
    frame_total = window * lax.axis_size("grp")
    first_frame = group_id * window

    def split_heads(array):
        return array.reshape(array.shape[0], places, HEADS, HDIM)

    key_pair = padded(jnp.stack([key_win, value_win]), (("grp", 1),), window)
    q_own = split_heads(query_win)
    g_own = split_heads(cot_win)
    k_ext = split_heads(key_pair[0])
    v_ext = split_heads(key_pair[1])
    own_label, own_inside = clip_labels(clip_len, first_frame, window, frame_total)
    ext_label, ext_inside = clip_labels(clip_len, first_frame - window, 3 * window, frame_total)
    allowed = (own_label[:, None] == ext_label[None, :]) & ext_inside[None, :]
    scores = (
        jnp.einsum("iphd,jphd->phij", q_own, k_ext, preferred_element_type=jnp.float32) * scaling
    )
    scores = jnp.where(allowed, scores, masked_score)
    row_max = jnp.max(scores, axis=-1)
    log_total = row_max + jnp.log(jnp.sum(jnp.exp(scores - row_max[..., None]), axis=-1))
    weights = jnp.where(allowed, jnp.exp(scores - log_total[..., None]), 0.0)
    weights_low = weights.astype(jnp.bfloat16)
    attended = jnp.einsum("phij,jphd->iphd", weights_low, v_ext, preferred_element_type=jnp.float32)
    row_dot = jnp.einsum("iphd,iphd->phi", g_own.astype(jnp.float32), attended)
    weight_grad = jnp.einsum("iphd,jphd->phij", g_own, v_ext, preferred_element_type=jnp.float32)
    score_grad = (weights * (weight_grad - row_dot[..., None])).astype(jnp.bfloat16)
    grad_query = (
        jnp.einsum("phij,jphd->iphd", score_grad, k_ext, preferred_element_type=jnp.float32)
        * scaling
    )
    key_terms = (
        jnp.einsum("phij,iphd->jphd", score_grad, q_own, preferred_element_type=jnp.float32)
        * scaling
    )
    value_terms = jnp.einsum(
        "phij,iphd->jphd", weights_low, g_own, preferred_element_type=jnp.float32
    )
    both_terms = jnp.stack([key_terms, value_terms]).reshape(2, 3 * window, places, channels)
    from_after = shifted(both_terms[:, :window], "grp", -1)
    from_before = shifted(both_terms[:, 2 * window :], "grp", 1)
    summed = both_terms[:, window : 2 * window] + from_after + from_before
    grad_key = summed[0]
    grad_value = summed[1]
    grad_qt, grad_kt, grad_vt = (
        lax.all_to_all(
            grad_query.reshape(window, places, channels).astype(jnp.bfloat16),
            "seq",
            split_axis=0,
            concat_axis=1,
            tiled=True,
        ),
        lax.all_to_all(
            grad_key.astype(jnp.bfloat16), "seq", split_axis=0, concat_axis=1, tiled=True
        ),
        lax.all_to_all(
            grad_value.astype(jnp.bfloat16), "seq", split_axis=0, concat_axis=1, tiled=True
        ),
    )
    return (grad_qs, grad_ks, grad_vs, grad_qt, grad_kt, grad_vt)


def solution(mesh):
    split_spec = P(("grp", "seq"), None, None)

    def mapped(body):
        return jax.shard_map(
            body,
            mesh=mesh,
            in_specs=(split_spec,) * 8 + (P(),),
            out_specs=(split_spec,) * 6,
            check_vma=False,
        )

    def grads(*arrays):
        return mapped(tile_shards if whole_tiles(mesh, arrays[0].shape[1]) else shards)(*arrays)

    return grads
```

```python
import functools
import math

import jax
import jax.numpy as jnp
from jax import lax
from jax.experimental import pallas as pl
from jax.experimental.pallas import tpu as pltpu
from jax.sharding import PartitionSpec as P

HEADS = 8
HDIM = 72
WIDTH = HEADS * HDIM
LANES = 128
SCALING = 1.0 / math.sqrt(HDIM)
CHUNKS = (4, 4)
masked_score = -1e30


def dot(left, right, left_dim, right_dim):
    dims = (((left_dim,), (right_dim,)), ((), ()))
    return lax.dot_general(left, right, dims, preferred_element_type=jnp.float32)


def rounded(value):
    return value.astype(jnp.bfloat16).astype(jnp.float32)


def frame_kernel(q_ref, k_ref, v_ref, g_ref, dq_ref, dk_ref, dv_ref):
    pair = 2 * HDIM
    reach = -(-HDIM // 16) * 16
    row = lax.broadcasted_iota(jnp.int32, (reach, 1), 0)
    for begin in range(0, WIDTH, pair):
        found = [[], [], []]
        for low, own in ((0, 0), (pair - reach, reach - HDIM)):
            span = slice(begin + low, begin + low + reach)
            mask = ((row >= own) & (row < own + HDIM)).astype(jnp.float32).astype(jnp.bfloat16)
            queries, keys = q_ref[0, span, :], k_ref[0, span, :]
            cotangent = g_ref[0, span, :]
            scores = dot(keys * mask, queries, 0, 0) * SCALING
            weight_grad = dot(v_ref[0, span, :] * mask, cotangent, 0, 0)
            raised = jnp.exp(scores - jnp.max(scores, axis=0, keepdims=True))
            weights = raised * (1.0 / jnp.sum(raised, axis=0, keepdims=True))
            weights_low = weights.astype(jnp.bfloat16)
            dots = jnp.sum(weights_low.astype(jnp.float32) * weight_grad, axis=0, keepdims=True)
            score_grad = (weights * (weight_grad - dots)).astype(jnp.bfloat16)
            rows = slice(own, own + HDIM)
            found[0].append(dot(keys, score_grad, 1, 0)[rows] * SCALING)
            found[1].append(dot(queries, score_grad, 1, 1)[rows] * SCALING)
            found[2].append(dot(cotangent, weights_low, 1, 1)[rows])
        for out, parts in zip((dq_ref, dk_ref, dv_ref), found):
            out[0, begin : begin + pair, :] = jnp.concatenate(parts, axis=0).astype(jnp.bfloat16)


def space_grads(queries, keys, values, cotangent):
    tokens = queries.shape[2]
    shape = jax.ShapeDtypeStruct(queries.shape, jnp.bfloat16)
    return pl.pallas_call(
        frame_kernel,
        out_shape=(shape, shape, shape),
        compiler_params=pltpu.CompilerParams(vmem_limit_bytes=60 * 2**20),
        cost_estimate=pl.CostEstimate(
            flops=12 * tokens * tokens * 256 * HEADS,
            bytes_accessed=14 * tokens * WIDTH,
            transcendentals=tokens * tokens * HEADS,
        ),
        name="space",
    )(queries, keys, values, cotangent)


def part_of(device, sharing, rows):
    row = pl.multiple_of(device % sharing * rows, 16)
    return row, pl.ds(pl.multiple_of(device // sharing * LANES, LANES), LANES)


def split_kernel(sharing, rows, span, *refs):
    ins, outs, (held, arrived, sent) = refs[:4], refs[4:-3], refs[-3:]
    loads, stores = {}, []
    for step in far_first(len(outs)):
        row, tokens = part_of(lax.axis_index("seq") ^ step, sharing, rows)
        for i, array in enumerate(ins):
            given = array.at[0, pl.ds(span.start + row, rows), tokens]
            loads[step, i] = pltpu.make_async_copy(given, held.at[step, i], arrived.at[step, i])
            loads[step, i].start()
    for step in far_first(len(outs)):
        for i in range(len(ins)):
            loads[step, i].wait()
        stores.append(pltpu.make_async_copy(held.at[step], outs[step], sent.at[step]))
        stores[-1].start()
    for copy in stores:
        copy.wait()


def split(arrays, span, n, sharing):
    rows = (span.stop - span.start) // sharing
    hbm = pl.BlockSpec(memory_space=pltpu.HBM)
    return pl.pallas_call(
        functools.partial(split_kernel, sharing, rows, span),
        in_specs=[hbm] * 4,
        out_specs=[hbm] * n,
        out_shape=[jax.ShapeDtypeStruct((4, rows, LANES), jnp.bfloat16)] * n,
        scratch_shapes=[
            pltpu.VMEM((n, 4, rows, LANES), jnp.bfloat16),
            pltpu.SemaphoreType.DMA((n, 4)),
            pltpu.SemaphoreType.DMA((n,)),
        ],
        compiler_params=pltpu.CompilerParams(vmem_limit_bytes=60 * 2**20),
        name="pack",
    )(*arrays)


def far_first(n):
    return [*reversed(range(n // 2, n)), *range(n // 2)]


def swap(block, axis, pairs):
    return lax.ppermute(block, axis, [(i, j) for i, j in pairs] + [(j, i) for i, j in pairs])


def exchange(blocks):
    n = len(blocks)
    moved = list(blocks)
    for step in reversed(range(1, n)):
        pairs = [[i, i ^ step] for i in range(n) if i < i ^ step]
        moved[step] = swap(blocks[step], "seq", pairs)
    return moved


def sides_kernel(n, *refs):
    ins, outs = refs[:n], refs[n:]
    is_odd = lax.axis_index("grp") & 1
    for step, ref in zip(far_first(n), ins):
        frame = lax.axis_index("seq") ^ step
        for start, out in zip((1, 0), outs):
            at = frame - jnp.where(is_odd == start, 1, 0)

            @pl.when((at >= 0) & (at < n - 1))
            def _():
                out[jnp.clip(at, 0, n - 2)] = ref[...]


def sides(blocks):
    n = len(blocks)
    shape = jax.ShapeDtypeStruct((n - 1, *blocks[0].shape), jnp.bfloat16)
    vmem = pl.BlockSpec(memory_space=pltpu.VMEM)
    return pl.pallas_call(
        functools.partial(sides_kernel, n),
        in_specs=[vmem] * n,
        out_specs=[vmem] * 2,
        out_shape=[shape] * 2,
        compiler_params=pltpu.CompilerParams(vmem_limit_bytes=24 * 2**20),
        name="sides",
    )(*(blocks[step] for step in far_first(n)))


def gated(values, *earlier):
    return lax.optimization_barrier((values, *earlier))


def neighbours(block, start):
    count = lax.axis_size("grp")
    return swap(block, "grp", [(i, (i + 1) % count) for i in range(start, count, 2)])


def join_kernel(sharing, span, *refs):
    outs, sent = refs[-4:-1], refs[-1]
    rows = refs[0].shape[1]
    n = sent.shape[0]
    copies = []
    for at, step in enumerate(far_first(n)):
        row, tokens = part_of(lax.axis_index("seq") ^ step, sharing, rows)
        for i, out in enumerate(outs):
            given = out.at[0, pl.ds(span.start + row, rows), tokens]
            copies.append(pltpu.make_async_copy(refs[at].at[i], given, sent.at[step, i]))
            copies[-1].start()
    for copy in copies:
        copy.wait()


def join(blocks, span, tokens, sharing, earlier):
    n = len(blocks)
    shape = jax.ShapeDtypeStruct((1, WIDTH, tokens), jnp.bfloat16)
    hbm = pl.BlockSpec(memory_space=pltpu.HBM)
    earlier = [] if earlier is None else list(earlier)
    return pl.pallas_call(
        functools.partial(join_kernel, sharing, span),
        in_specs=[pl.BlockSpec(memory_space=pltpu.VMEM)] * n + [hbm] * len(earlier),
        out_specs=[hbm] * 3,
        out_shape=[shape] * 3,
        scratch_shapes=[pltpu.SemaphoreType.DMA((n, 3))],
        input_output_aliases={n + i: i for i in range(len(earlier))},
        compiler_params=pltpu.CompilerParams(vmem_limit_bytes=24 * 2**20),
        name="unpack",
    )(*(blocks[step] for step in far_first(n)), *earlier)


def clip_kernel(window, heads, given_bounds, *refs):
    own, sides_of = refs[:window], refs[window : window + 2]
    outs, refs = refs[window + 2 : 2 * window + 2], refs[2 * window + 2 :]
    wide, score_ref, grad_ref, weight_ref, found, bounds, arrived = refs
    copy = pltpu.make_async_copy(given_bounds, bounds, arrived)
    copy.start()
    halo = window - 1
    extent = window + 2 * halo
    queries, keys, values, cotangent = range(4)

    def widen(ref, frame):
        for i in range(4):
            wide[i, frame] = ref[i].astype(jnp.float32)

    for step, ref in zip(far_first(window), own):
        widen(ref, halo + (lax.axis_index("seq") ^ step))
    for start, ref in zip((1, 0), sides_of):
        is_next = (lax.axis_index("grp") & 1) == start
        for at in range(halo):
            widen(ref.at[at], at + jnp.where(is_next, halo + window, 0))
    copy.wait()
    lowest, highest = bounds[0, halo], bounds[1, halo + window - 1]

    def partners(frame):
        first, last = bounds[0, frame], bounds[1, frame]
        return first, last - first, [jnp.minimum(first + t, last - 1) for t in range(window)]

    def products(frame, carry):
        first, count, others = partners(frame)
        scores, grads = [[] for _ in others], [[] for _ in others]
        for head in range(heads):
            span = slice(head * HDIM, (head + 1) * HDIM)
            query, cot = wide[queries, frame, span, :], wide[cotangent, frame, span, :]
            for t, other in enumerate(others):
                score = jnp.sum(query * wide[keys, other, span, :], axis=0, keepdims=True)
                grad = jnp.sum(cot * wide[values, other, span, :], axis=0, keepdims=True)
                scores[t].append(score)
                grads[t].append(grad)
        for t in range(window):
            bias = jnp.where(t < count, 0.0, masked_score)
            score_ref[t, frame] = jnp.concatenate(scores[t], axis=0) * SCALING + bias
            grad_ref[t, frame] = jnp.concatenate(grads[t], axis=0)
        return carry

    lax.fori_loop(lowest, highest, products, 0)
    scores, grads = [score_ref[t] for t in range(window)], [grad_ref[t] for t in range(window)]
    peak = functools.reduce(jnp.maximum, scores)
    raised = [jnp.exp(score - peak) for score in scores]
    inverse = 1.0 / functools.reduce(jnp.add, raised)
    weights = [part * inverse for part in raised]
    weights_low = [rounded(part) for part in weights]
    dots = functools.reduce(jnp.add, [w * d for w, d in zip(weights_low, grads)])
    for t in range(window):
        weight_ref[t] = weights_low[t]
        score_ref[t] = rounded(weights[t] * (grads[t] - dots))

    def gradients(at, carry):
        frame = halo + at
        first, count, others = partners(frame)
        place = frame - first
        sums = [[], [], []]
        for head in range(heads):
            span, row = slice(head * HDIM, (head + 1) * HDIM), slice(head, head + 1)
            totals = [None] * 3
            for t, other in enumerate(others):
                score_back = jnp.where(t < count, score_ref[place, other, row, :], 0.0)
                weight_back = jnp.where(t < count, weight_ref[place, other, row, :], 0.0)
                terms = (
                    score_ref[t, frame, row, :] * wide[keys, other, span, :],
                    score_back * wide[queries, other, span, :],
                    weight_back * wide[cotangent, other, span, :],
                )
                totals = [x if y is None else y + x for x, y in zip(terms, totals)]
            for held, total, scale in zip(sums, totals, (SCALING, SCALING, None)):
                held.append(total if scale is None else total * scale)
        for i, parts in enumerate(sums):
            found[at, i] = jnp.concatenate(parts, axis=0).astype(jnp.bfloat16)
        return carry

    lax.fori_loop(0, window, gradients, 0)
    for step, out in enumerate(outs):
        out[...] = found[lax.axis_index("seq") ^ step]


def clip_grads(bounds, own, beside):
    window = len(own)
    _, rows, lanes = own[0].shape
    heads = rows // HDIM
    extent = 3 * window - 2
    vmem = pl.BlockSpec(memory_space=pltpu.VMEM)
    shape = (3, rows, lanes)
    slots = pltpu.VMEM((window, extent, heads, lanes), jnp.float32)
    return pl.pallas_call(
        functools.partial(clip_kernel, window, heads),
        out_shape=[jax.ShapeDtypeStruct(shape, jnp.bfloat16)] * window,
        in_specs=[pl.BlockSpec(memory_space=pl.ANY)] + [vmem] * (window + 2),
        out_specs=[vmem] * window,
        scratch_shapes=[
            pltpu.VMEM((4, extent, rows, lanes), jnp.float32),
            slots,
            slots,
            slots,
            pltpu.VMEM((window, *shape), jnp.bfloat16),
            pltpu.SMEM(bounds.shape, jnp.int32),
            pltpu.SemaphoreType.DMA,
        ],
        compiler_params=pltpu.CompilerParams(vmem_limit_bytes=48 * 2**20),
        cost_estimate=pl.CostEstimate(
            flops=800 * extent * window * rows * lanes,
            bytes_accessed=2 * sum(block.size for block in (*own, *beside)),
            transcendentals=extent * window * heads * lanes,
        ),
        name="clips",
    )(bounds, *(own[step] for step in far_first(window)), *beside)


def clip_bounds(clip_len, window):
    halo = window - 1
    extent = window + 2 * halo
    start = lax.axis_index("grp") * window - halo
    frames = start + jnp.arange(extent, dtype=jnp.int32)
    order = jnp.arange(clip_len.shape[0])
    ends = jnp.sum(jnp.where(order[:, None] <= order[None, :], clip_len[:, None], 0), axis=0)
    begins = ends - clip_len
    holds = (begins[None, :] <= frames[:, None]) & (frames[:, None] < ends[None, :])
    first = jnp.sum(jnp.where(holds, begins[None, :], 0), axis=1) - start
    last = jnp.sum(jnp.where(holds, ends[None, :], 0), axis=1) - start
    return jnp.stack([first, last]).astype(jnp.int32)


def tile_shards(q_space, k_space, v_space, cot_space, q_time, k_time, v_time, cot_time, clip_len):
    def turned(*arrays):
        return tuple(array.transpose(0, 2, 1) for array in arrays)

    n = lax.axis_size("seq")
    window = q_time.shape[0] * n
    tokens = q_time.shape[1]
    sharing = n * LANES // tokens
    bounds = clip_bounds(clip_len, window)
    time = turned(q_time, k_time, v_time, cot_time)
    spans = []
    head = 0
    for heads in CHUNKS:
        spans.append(slice(head * HDIM, (head + heads) * HDIM))
        head += heads
    space_in = turned(q_space, k_space, v_space, cot_space)
    packed = [list(split(time, span, n, sharing)) for span in spans]
    own = [exchange(packed[0])]
    space = space_grads(*space_in)
    packed[1][2:], own[0][2], space = gated(packed[1][2:], own[0][2], space)
    own.append(exchange(packed[1]))
    beside = [
        [neighbours(ends, start) for ends, start in zip(sides(blocks), (1, 0))] for blocks in own
    ]
    back, grads = [], None
    for blocks, near in zip(own, beside):
        back.append(exchange(clip_grads(bounds, blocks, near)))
    for span, blocks in zip(spans, back):
        grads = join(blocks, span, tokens, sharing, grads)
    return turned(*space, *grads)


def whole_tiles(mesh, tokens):
    n = mesh.shape["seq"]
    sharing = n * LANES // tokens
    return (
        tokens % LANES == 0
        and n % 4 == 0
        and n & (n - 1) == 0
        and mesh.shape["grp"] % 2 == 0
        and mesh.shape["grp"] > 2
        and sharing * tokens == n * LANES
        and all(heads % sharing == 0 and heads // sharing * HDIM % 16 == 0 for heads in CHUNKS)
    )


def padded(block, sides, width):
    for axis, dim in sides:
        count = lax.axis_size(axis)
        forward = [(i, i + 1) for i in range(count - 1)]
        backward = [(target, source) for source, target in forward]
        low = lax.ppermute(
            lax.slice_in_dim(block, block.shape[dim] - width, None, axis=dim), axis, forward
        )
        high = lax.ppermute(lax.slice_in_dim(block, 0, width, axis=dim), axis, backward)
        block = jnp.concatenate([low, block, high], axis=dim)
    return block


def shifted(value, axis, by):
    count = lax.axis_size(axis)
    pairs = [(i, i + by) for i in range(count) if 0 <= i + by < count]
    return lax.ppermute(value, axis, pairs)


def clip_labels(clip_len, first_frame, count, frame_total):
    frame_ids = first_frame + jnp.arange(count, dtype=jnp.int32)
    clip_ends = jnp.cumsum(clip_len)
    labels = jnp.sum((clip_ends[None, :] <= frame_ids[:, None]).astype(jnp.int32), axis=1)
    inside = (frame_ids >= 0) & (frame_ids < frame_total)
    return (labels, inside)


def frame_grads(queries, keys, values, cotangent):
    scaling = 1.0 / math.sqrt(HDIM)
    tokens = queries.shape[0]
    q_heads = queries.reshape(tokens, HEADS, HDIM)
    k_heads = keys.reshape(tokens, HEADS, HDIM)
    v_heads = values.reshape(tokens, HEADS, HDIM)
    g_heads = cotangent.reshape(tokens, HEADS, HDIM)
    scores = (
        jnp.einsum("qhd,khd->hqk", q_heads, k_heads, preferred_element_type=jnp.float32) * scaling
    )
    row_max = jnp.max(scores, axis=-1, keepdims=True)
    log_total = row_max + jnp.log(jnp.sum(jnp.exp(scores - row_max), axis=-1, keepdims=True))
    weights = jnp.exp(scores - log_total)
    weights_low = weights.astype(jnp.bfloat16)
    attended = jnp.einsum("hqk,khd->qhd", weights_low, v_heads, preferred_element_type=jnp.float32)
    row_dot = jnp.einsum("qhd,qhd->hq", g_heads.astype(jnp.float32), attended)
    weight_grad = jnp.einsum("qhd,khd->hqk", g_heads, v_heads, preferred_element_type=jnp.float32)
    score_grad = (weights * (weight_grad - row_dot[:, :, None])).astype(jnp.bfloat16)
    grad_query = (
        jnp.einsum("hqk,khd->qhd", score_grad, k_heads, preferred_element_type=jnp.float32)
        * scaling
    )
    grad_key = (
        jnp.einsum("hqk,qhd->khd", score_grad, q_heads, preferred_element_type=jnp.float32)
        * scaling
    )
    grad_value = jnp.einsum(
        "hqk,qhd->khd", weights_low, g_heads, preferred_element_type=jnp.float32
    )
    flat_shape = (1, tokens, HEADS * HDIM)
    return (
        grad_query.reshape(flat_shape).astype(jnp.bfloat16),
        grad_key.reshape(flat_shape).astype(jnp.bfloat16),
        grad_value.reshape(flat_shape).astype(jnp.bfloat16),
    )


def shards(q_space, k_space, v_space, cot_space, q_time, k_time, v_time, cot_time, clip_len):
    scaling = 1.0 / math.sqrt(HDIM)
    grad_qs, grad_ks, grad_vs = frame_grads(q_space[0], k_space[0], v_space[0], cot_space[0])
    moved = (
        lax.all_to_all(q_time, "seq", split_axis=1, concat_axis=0, tiled=True),
        lax.all_to_all(k_time, "seq", split_axis=1, concat_axis=0, tiled=True),
        lax.all_to_all(v_time, "seq", split_axis=1, concat_axis=0, tiled=True),
        lax.all_to_all(cot_time, "seq", split_axis=1, concat_axis=0, tiled=True),
    )
    query_win, key_win, value_win, cot_win = moved
    window = query_win.shape[0]
    places = query_win.shape[1]
    channels = query_win.shape[2]
    group_id = lax.axis_index("grp")
    frame_total = window * lax.axis_size("grp")
    first_frame = group_id * window

    def split_heads(array):
        return array.reshape(array.shape[0], places, HEADS, HDIM)

    key_pair = padded(jnp.stack([key_win, value_win]), (("grp", 1),), window)
    q_own = split_heads(query_win)
    g_own = split_heads(cot_win)
    k_ext = split_heads(key_pair[0])
    v_ext = split_heads(key_pair[1])
    own_label, own_inside = clip_labels(clip_len, first_frame, window, frame_total)
    ext_label, ext_inside = clip_labels(clip_len, first_frame - window, 3 * window, frame_total)
    allowed = (own_label[:, None] == ext_label[None, :]) & ext_inside[None, :]
    scores = (
        jnp.einsum("iphd,jphd->phij", q_own, k_ext, preferred_element_type=jnp.float32) * scaling
    )
    scores = jnp.where(allowed, scores, masked_score)
    row_max = jnp.max(scores, axis=-1)
    log_total = row_max + jnp.log(jnp.sum(jnp.exp(scores - row_max[..., None]), axis=-1))
    weights = jnp.where(allowed, jnp.exp(scores - log_total[..., None]), 0.0)
    weights_low = weights.astype(jnp.bfloat16)
    attended = jnp.einsum("phij,jphd->iphd", weights_low, v_ext, preferred_element_type=jnp.float32)
    row_dot = jnp.einsum("iphd,iphd->phi", g_own.astype(jnp.float32), attended)
    weight_grad = jnp.einsum("iphd,jphd->phij", g_own, v_ext, preferred_element_type=jnp.float32)
    score_grad = (weights * (weight_grad - row_dot[..., None])).astype(jnp.bfloat16)
    grad_query = (
        jnp.einsum("phij,jphd->iphd", score_grad, k_ext, preferred_element_type=jnp.float32)
        * scaling
    )
    key_terms = (
        jnp.einsum("phij,iphd->jphd", score_grad, q_own, preferred_element_type=jnp.float32)
        * scaling
    )
    value_terms = jnp.einsum(
        "phij,iphd->jphd", weights_low, g_own, preferred_element_type=jnp.float32
    )
    both_terms = jnp.stack([key_terms, value_terms]).reshape(2, 3 * window, places, channels)
    from_after = shifted(both_terms[:, :window], "grp", -1)
    from_before = shifted(both_terms[:, 2 * window :], "grp", 1)
    summed = both_terms[:, window : 2 * window] + from_after + from_before
    grad_key = summed[0]
    grad_value = summed[1]
    grad_qt, grad_kt, grad_vt = (
        lax.all_to_all(
            grad_query.reshape(window, places, channels).astype(jnp.bfloat16),
            "seq",
            split_axis=0,
            concat_axis=1,
            tiled=True,
        ),
        lax.all_to_all(
            grad_key.astype(jnp.bfloat16), "seq", split_axis=0, concat_axis=1, tiled=True
        ),
        lax.all_to_all(
            grad_value.astype(jnp.bfloat16), "seq", split_axis=0, concat_axis=1, tiled=True
        ),
    )
    return (grad_qs, grad_ks, grad_vs, grad_qt, grad_kt, grad_vt)


def solution(mesh):
    split_spec = P(("grp", "seq"), None, None)

    def mapped(body):
        return jax.shard_map(
            body,
            mesh=mesh,
            in_specs=(split_spec,) * 8 + (P(),),
            out_specs=(split_spec,) * 6,
            check_vma=False,
        )

    def grads(*arrays):
        return mapped(tile_shards if whole_tiles(mesh, arrays[0].shape[1]) else shards)(*arrays)

    return grads
```

```python
import functools
import math

import jax
import jax.numpy as jnp
from jax import lax
from jax.experimental import pallas as pl
from jax.experimental.pallas import tpu as pltpu
from jax.sharding import PartitionSpec as P

HEADS = 8
HDIM = 72
WIDTH = HEADS * HDIM
LANES = 128
SCALING = 1.0 / math.sqrt(HDIM)
CHUNKS = (4, 4)
masked_score = -1e30


def dot(left, right, left_dim, right_dim):
    dims = (((left_dim,), (right_dim,)), ((), ()))
    return lax.dot_general(left, right, dims, preferred_element_type=jnp.float32)


def rounded(value):
    return value.astype(jnp.bfloat16).astype(jnp.float32)


def frame_kernel(q_ref, k_ref, v_ref, g_ref, dq_ref, dk_ref, dv_ref):
    pair = 2 * HDIM
    reach = -(-HDIM // 16) * 16
    row = lax.broadcasted_iota(jnp.int32, (reach, 1), 0)
    for begin in range(0, WIDTH, pair):
        found = [[], [], []]
        for low, own in ((0, 0), (pair - reach, reach - HDIM)):
            span = slice(begin + low, begin + low + reach)
            mask = ((row >= own) & (row < own + HDIM)).astype(jnp.float32).astype(jnp.bfloat16)
            queries, keys = q_ref[0, span, :], k_ref[0, span, :]
            cotangent = g_ref[0, span, :]
            scores = dot(keys * mask, queries, 0, 0) * SCALING
            weight_grad = dot(v_ref[0, span, :] * mask, cotangent, 0, 0)
            raised = jnp.exp(scores - jnp.max(scores, axis=0, keepdims=True))
            weights = raised * (1.0 / jnp.sum(raised, axis=0, keepdims=True))
            weights_low = weights.astype(jnp.bfloat16)
            dots = jnp.sum(weights_low.astype(jnp.float32) * weight_grad, axis=0, keepdims=True)
            score_grad = (weights * (weight_grad - dots)).astype(jnp.bfloat16)
            rows = slice(own, own + HDIM)
            found[0].append(dot(keys, score_grad, 1, 0)[rows] * SCALING)
            found[1].append(dot(queries, score_grad, 1, 1)[rows] * SCALING)
            found[2].append(dot(cotangent, weights_low, 1, 1)[rows])
        for out, parts in zip((dq_ref, dk_ref, dv_ref), found):
            out[0, begin : begin + pair, :] = jnp.concatenate(parts, axis=0).astype(jnp.bfloat16)


def space_grads(queries, keys, values, cotangent):
    tokens = queries.shape[2]
    shape = jax.ShapeDtypeStruct(queries.shape, jnp.bfloat16)
    return pl.pallas_call(
        frame_kernel,
        out_shape=(shape, shape, shape),
        compiler_params=pltpu.CompilerParams(vmem_limit_bytes=60 * 2**20),
        cost_estimate=pl.CostEstimate(
            flops=12 * tokens * tokens * 256 * HEADS,
            bytes_accessed=14 * tokens * WIDTH,
            transcendentals=tokens * tokens * HEADS,
        ),
        name="space",
    )(queries, keys, values, cotangent)


def part_of(device, sharing, rows):
    row = pl.multiple_of(device % sharing * rows, 16)
    return row, pl.ds(pl.multiple_of(device // sharing * LANES, LANES), LANES)


def split_kernel(sharing, rows, span, *refs):
    ins, outs, (held, arrived, sent) = refs[:4], refs[4:-3], refs[-3:]
    loads, stores = {}, []
    for step in far_first(len(outs)):
        row, tokens = part_of(lax.axis_index("seq") ^ step, sharing, rows)
        for i, array in enumerate(ins):
            given = array.at[0, pl.ds(span.start + row, rows), tokens]
            loads[step, i] = pltpu.make_async_copy(given, held.at[step, i], arrived.at[step, i])
            loads[step, i].start()
    for step in far_first(len(outs)):
        for i in range(len(ins)):
            loads[step, i].wait()
        stores.append(pltpu.make_async_copy(held.at[step], outs[step], sent.at[step]))
        stores[-1].start()
    for copy in stores:
        copy.wait()


def split(arrays, span, n, sharing):
    rows = (span.stop - span.start) // sharing
    hbm = pl.BlockSpec(memory_space=pltpu.HBM)
    return pl.pallas_call(
        functools.partial(split_kernel, sharing, rows, span),
        in_specs=[hbm] * 4,
        out_specs=[hbm] * n,
        out_shape=[jax.ShapeDtypeStruct((4, rows, LANES), jnp.bfloat16)] * n,
        scratch_shapes=[
            pltpu.VMEM((n, 4, rows, LANES), jnp.bfloat16),
            pltpu.SemaphoreType.DMA((n, 4)),
            pltpu.SemaphoreType.DMA((n,)),
        ],
        compiler_params=pltpu.CompilerParams(vmem_limit_bytes=60 * 2**20),
        name="pack",
    )(*arrays)


def far_first(n):
    return [*reversed(range(n // 2, n)), *range(n // 2)]


def swap(block, axis, pairs):
    return lax.ppermute(block, axis, [(i, j) for i, j in pairs] + [(j, i) for i, j in pairs])


def exchange(blocks):
    n = len(blocks)
    moved = list(blocks)
    for step in reversed(range(1, n)):
        pairs = [[i, i ^ step] for i in range(n) if i < i ^ step]
        moved[step] = swap(blocks[step], "seq", pairs)
    return moved


def sides_kernel(n, *refs):
    ins, outs = refs[:n], refs[n:]
    is_odd = lax.axis_index("grp") & 1
    for step, ref in enumerate(ins):
        frame = lax.axis_index("seq") ^ step
        for start, out in zip((1, 0), outs):
            at = frame - jnp.where(is_odd == start, 1, 0)

            @pl.when((at >= 0) & (at < n - 1))
            def _():
                out[jnp.clip(at, 0, n - 2)] = ref[...]


def sides(blocks):
    n = len(blocks)
    shape = jax.ShapeDtypeStruct((n - 1, *blocks[0].shape), jnp.bfloat16)
    vmem = pl.BlockSpec(memory_space=pltpu.VMEM)
    return pl.pallas_call(
        functools.partial(sides_kernel, n),
        in_specs=[vmem] * n,
        out_specs=[vmem] * 2,
        out_shape=[shape] * 2,
        compiler_params=pltpu.CompilerParams(vmem_limit_bytes=24 * 2**20),
        name="sides",
    )(*blocks)


def gated(values, *earlier):
    return lax.optimization_barrier((values, *earlier))


def neighbours(block, start):
    count = lax.axis_size("grp")
    pairs = [(i, i + 1) for i in range(start, count - 1, 2)]
    alone = set(range(count)) - {i for pair in pairs for i in pair}
    links = pairs + [(j, i) for i, j in pairs] + [(i, i) for i in sorted(alone)]
    return lax.ppermute(block, "grp", links)


def join_kernel(sharing, span, *refs):
    outs, sent = refs[-4:-1], refs[-1]
    rows = refs[0].shape[1]
    n = sent.shape[0]
    copies = []
    for at, step in enumerate(far_first(n)):
        row, tokens = part_of(lax.axis_index("seq") ^ step, sharing, rows)
        for i, out in enumerate(outs):
            given = out.at[0, pl.ds(span.start + row, rows), tokens]
            copies.append(pltpu.make_async_copy(refs[at].at[i], given, sent.at[step, i]))
            copies[-1].start()
    for copy in copies:
        copy.wait()


def join(blocks, span, tokens, sharing, earlier):
    n = len(blocks)
    shape = jax.ShapeDtypeStruct((1, WIDTH, tokens), jnp.bfloat16)
    hbm = pl.BlockSpec(memory_space=pltpu.HBM)
    earlier = [] if earlier is None else list(earlier)
    return pl.pallas_call(
        functools.partial(join_kernel, sharing, span),
        in_specs=[pl.BlockSpec(memory_space=pltpu.VMEM)] * n + [hbm] * len(earlier),
        out_specs=[hbm] * 3,
        out_shape=[shape] * 3,
        scratch_shapes=[pltpu.SemaphoreType.DMA((n, 3))],
        input_output_aliases={n + i: i for i in range(len(earlier))},
        compiler_params=pltpu.CompilerParams(vmem_limit_bytes=24 * 2**20),
        name="unpack",
    )(*(blocks[step] for step in far_first(n)), *earlier)


def clip_kernel(window, heads, given_bounds, *refs):
    own, sides_of = refs[:window], refs[window : window + 2]
    outs, refs = refs[window + 2 : 2 * window + 2], refs[2 * window + 2 :]
    wide, score_ref, grad_ref, weight_ref, found, bounds, arrived = refs
    copy = pltpu.make_async_copy(given_bounds, bounds, arrived)
    copy.start()
    halo = window - 1
    extent = window + 2 * halo
    queries, keys, values, cotangent = range(4)

    def widen(ref, frame):
        for i in range(4):
            wide[i, frame] = ref[i].astype(jnp.float32)

    for step, ref in enumerate(own):
        widen(ref, halo + (lax.axis_index("seq") ^ step))
    for start, ref in zip((1, 0), sides_of):
        is_next = (lax.axis_index("grp") & 1) == start
        for at in range(halo):
            widen(ref.at[at], at + jnp.where(is_next, halo + window, 0))
    copy.wait()
    lowest, highest = bounds[0, halo], bounds[1, halo + window - 1]

    def partners(frame):
        first, last = bounds[0, frame], bounds[1, frame]
        return first, last - first, [jnp.minimum(first + t, last - 1) for t in range(window)]

    def products(frame, carry):
        first, count, others = partners(frame)
        scores, grads = [[] for _ in others], [[] for _ in others]
        for head in range(heads):
            span = slice(head * HDIM, (head + 1) * HDIM)
            query, cot = wide[queries, frame, span, :], wide[cotangent, frame, span, :]
            for t, other in enumerate(others):
                score = jnp.sum(query * wide[keys, other, span, :], axis=0, keepdims=True)
                grad = jnp.sum(cot * wide[values, other, span, :], axis=0, keepdims=True)
                scores[t].append(score)
                grads[t].append(grad)
        for t in range(window):
            bias = jnp.where(t < count, 0.0, masked_score)
            score_ref[t, frame] = jnp.concatenate(scores[t], axis=0) * SCALING + bias
            grad_ref[t, frame] = jnp.concatenate(grads[t], axis=0)
        return carry

    lax.fori_loop(lowest, highest, products, 0)
    scores, grads = [score_ref[t] for t in range(window)], [grad_ref[t] for t in range(window)]
    peak = functools.reduce(jnp.maximum, scores)
    raised = [jnp.exp(score - peak) for score in scores]
    inverse = 1.0 / functools.reduce(jnp.add, raised)
    weights = [part * inverse for part in raised]
    weights_low = [rounded(part) for part in weights]
    dots = functools.reduce(jnp.add, [w * d for w, d in zip(weights_low, grads)])
    for t in range(window):
        weight_ref[t] = weights_low[t]
        score_ref[t] = rounded(weights[t] * (grads[t] - dots))

    def gradients(at, carry):
        frame = halo + at
        first, count, others = partners(frame)
        place = frame - first
        sums = [[], [], []]
        for head in range(heads):
            span, row = slice(head * HDIM, (head + 1) * HDIM), slice(head, head + 1)
            totals = [None] * 3
            for t, other in enumerate(others):
                score_back = jnp.where(t < count, score_ref[place, other, row, :], 0.0)
                weight_back = jnp.where(t < count, weight_ref[place, other, row, :], 0.0)
                terms = (
                    score_ref[t, frame, row, :] * wide[keys, other, span, :],
                    score_back * wide[queries, other, span, :],
                    weight_back * wide[cotangent, other, span, :],
                )
                totals = [x if y is None else y + x for x, y in zip(terms, totals)]
            for held, total, scale in zip(sums, totals, (SCALING, SCALING, None)):
                held.append(total if scale is None else total * scale)
        for i, parts in enumerate(sums):
            found[at, i] = jnp.concatenate(parts, axis=0).astype(jnp.bfloat16)
        return carry

    lax.fori_loop(0, window, gradients, 0)
    for step, out in enumerate(outs):
        out[...] = found[lax.axis_index("seq") ^ step]


def clip_grads(bounds, own, beside):
    window = len(own)
    _, rows, lanes = own[0].shape
    heads = rows // HDIM
    extent = 3 * window - 2
    vmem = pl.BlockSpec(memory_space=pltpu.VMEM)
    shape = (3, rows, lanes)
    slots = pltpu.VMEM((window, extent, heads, lanes), jnp.float32)
    return pl.pallas_call(
        functools.partial(clip_kernel, window, heads),
        out_shape=[jax.ShapeDtypeStruct(shape, jnp.bfloat16)] * window,
        in_specs=[pl.BlockSpec(memory_space=pl.ANY)] + [vmem] * (window + 2),
        out_specs=[vmem] * window,
        scratch_shapes=[
            pltpu.VMEM((4, extent, rows, lanes), jnp.float32),
            slots,
            slots,
            slots,
            pltpu.VMEM((window, *shape), jnp.bfloat16),
            pltpu.SMEM(bounds.shape, jnp.int32),
            pltpu.SemaphoreType.DMA,
        ],
        compiler_params=pltpu.CompilerParams(vmem_limit_bytes=48 * 2**20),
        cost_estimate=pl.CostEstimate(
            flops=800 * extent * window * rows * lanes,
            bytes_accessed=2 * sum(block.size for block in (*own, *beside)),
            transcendentals=extent * window * heads * lanes,
        ),
        name="clips",
    )(bounds, *own, *beside)


def clip_bounds(clip_len, window):
    halo = window - 1
    extent = window + 2 * halo
    start = lax.axis_index("grp") * window - halo
    frames = start + jnp.arange(extent, dtype=jnp.int32)
    order = jnp.arange(clip_len.shape[0])
    ends = jnp.sum(jnp.where(order[:, None] <= order[None, :], clip_len[:, None], 0), axis=0)
    begins = ends - clip_len
    holds = (begins[None, :] <= frames[:, None]) & (frames[:, None] < ends[None, :])
    first = jnp.sum(jnp.where(holds, begins[None, :], 0), axis=1) - start
    last = jnp.sum(jnp.where(holds, ends[None, :], 0), axis=1) - start
    return jnp.stack([first, last]).astype(jnp.int32)


def tile_shards(q_space, k_space, v_space, cot_space, q_time, k_time, v_time, cot_time, clip_len):
    def turned(*arrays):
        return tuple(array.transpose(0, 2, 1) for array in arrays)

    n = lax.axis_size("seq")
    window = q_time.shape[0] * n
    tokens = q_time.shape[1]
    sharing = n * LANES // tokens
    bounds = clip_bounds(clip_len, window)
    time = turned(q_time, k_time, v_time, cot_time)
    spans = []
    head = 0
    for heads in CHUNKS:
        spans.append(slice(head * HDIM, (head + heads) * HDIM))
        head += heads
    space_in = turned(q_space, k_space, v_space, cot_space)
    packed = [list(split(time, span, n, sharing)) for span in spans]
    own = [exchange(packed[0])]
    space = space_grads(*space_in)
    packed[1][2:], own[0][2], space = gated(packed[1][2:], own[0][2], space)
    own.append(exchange(packed[1]))
    beside = [
        [neighbours(ends, start) for ends, start in zip(sides(blocks), (1, 0))] for blocks in own
    ]
    back, grads = [], None
    for blocks, near in zip(own, beside):
        back.append(exchange(clip_grads(bounds, blocks, near)))
    for span, blocks in zip(spans, back):
        grads = join(blocks, span, tokens, sharing, grads)
    return turned(*space, *grads)


def whole_tiles(mesh, tokens):
    n = mesh.shape["seq"]
    sharing = n * LANES // tokens
    return (
        tokens % LANES == 0
        and n % 4 == 0
        and n & (n - 1) == 0
        and mesh.shape["grp"] % 2 == 0
        and sharing * tokens == n * LANES
        and all(heads % sharing == 0 and heads // sharing * HDIM % 16 == 0 for heads in CHUNKS)
    )


def padded(block, sides, width):
    for axis, dim in sides:
        count = lax.axis_size(axis)
        forward = [(i, i + 1) for i in range(count - 1)]
        backward = [(target, source) for source, target in forward]
        low = lax.ppermute(
            lax.slice_in_dim(block, block.shape[dim] - width, None, axis=dim), axis, forward
        )
        high = lax.ppermute(lax.slice_in_dim(block, 0, width, axis=dim), axis, backward)
        block = jnp.concatenate([low, block, high], axis=dim)
    return block


def shifted(value, axis, by):
    count = lax.axis_size(axis)
    pairs = [(i, i + by) for i in range(count) if 0 <= i + by < count]
    return lax.ppermute(value, axis, pairs)


def clip_labels(clip_len, first_frame, count, frame_total):
    frame_ids = first_frame + jnp.arange(count, dtype=jnp.int32)
    clip_ends = jnp.cumsum(clip_len)
    labels = jnp.sum((clip_ends[None, :] <= frame_ids[:, None]).astype(jnp.int32), axis=1)
    inside = (frame_ids >= 0) & (frame_ids < frame_total)
    return (labels, inside)


def frame_grads(queries, keys, values, cotangent):
    scaling = 1.0 / math.sqrt(HDIM)
    tokens = queries.shape[0]
    q_heads = queries.reshape(tokens, HEADS, HDIM)
    k_heads = keys.reshape(tokens, HEADS, HDIM)
    v_heads = values.reshape(tokens, HEADS, HDIM)
    g_heads = cotangent.reshape(tokens, HEADS, HDIM)
    scores = (
        jnp.einsum("qhd,khd->hqk", q_heads, k_heads, preferred_element_type=jnp.float32) * scaling
    )
    row_max = jnp.max(scores, axis=-1, keepdims=True)
    log_total = row_max + jnp.log(jnp.sum(jnp.exp(scores - row_max), axis=-1, keepdims=True))
    weights = jnp.exp(scores - log_total)
    weights_low = weights.astype(jnp.bfloat16)
    attended = jnp.einsum("hqk,khd->qhd", weights_low, v_heads, preferred_element_type=jnp.float32)
    row_dot = jnp.einsum("qhd,qhd->hq", g_heads.astype(jnp.float32), attended)
    weight_grad = jnp.einsum("qhd,khd->hqk", g_heads, v_heads, preferred_element_type=jnp.float32)
    score_grad = (weights * (weight_grad - row_dot[:, :, None])).astype(jnp.bfloat16)
    grad_query = (
        jnp.einsum("hqk,khd->qhd", score_grad, k_heads, preferred_element_type=jnp.float32)
        * scaling
    )
    grad_key = (
        jnp.einsum("hqk,qhd->khd", score_grad, q_heads, preferred_element_type=jnp.float32)
        * scaling
    )
    grad_value = jnp.einsum(
        "hqk,qhd->khd", weights_low, g_heads, preferred_element_type=jnp.float32
    )
    flat_shape = (1, tokens, HEADS * HDIM)
    return (
        grad_query.reshape(flat_shape).astype(jnp.bfloat16),
        grad_key.reshape(flat_shape).astype(jnp.bfloat16),
        grad_value.reshape(flat_shape).astype(jnp.bfloat16),
    )


def shards(q_space, k_space, v_space, cot_space, q_time, k_time, v_time, cot_time, clip_len):
    scaling = 1.0 / math.sqrt(HDIM)
    grad_qs, grad_ks, grad_vs = frame_grads(q_space[0], k_space[0], v_space[0], cot_space[0])
    moved = (
        lax.all_to_all(q_time, "seq", split_axis=1, concat_axis=0, tiled=True),
        lax.all_to_all(k_time, "seq", split_axis=1, concat_axis=0, tiled=True),
        lax.all_to_all(v_time, "seq", split_axis=1, concat_axis=0, tiled=True),
        lax.all_to_all(cot_time, "seq", split_axis=1, concat_axis=0, tiled=True),
    )
    query_win, key_win, value_win, cot_win = moved
    window = query_win.shape[0]
    places = query_win.shape[1]
    channels = query_win.shape[2]
    group_id = lax.axis_index("grp")
    frame_total = window * lax.axis_size("grp")
    first_frame = group_id * window

    def split_heads(array):
        return array.reshape(array.shape[0], places, HEADS, HDIM)

    key_pair = padded(jnp.stack([key_win, value_win]), (("grp", 1),), window)
    q_own = split_heads(query_win)
    g_own = split_heads(cot_win)
    k_ext = split_heads(key_pair[0])
    v_ext = split_heads(key_pair[1])
    own_label, own_inside = clip_labels(clip_len, first_frame, window, frame_total)
    ext_label, ext_inside = clip_labels(clip_len, first_frame - window, 3 * window, frame_total)
    allowed = (own_label[:, None] == ext_label[None, :]) & ext_inside[None, :]
    scores = (
        jnp.einsum("iphd,jphd->phij", q_own, k_ext, preferred_element_type=jnp.float32) * scaling
    )
    scores = jnp.where(allowed, scores, masked_score)
    row_max = jnp.max(scores, axis=-1)
    log_total = row_max + jnp.log(jnp.sum(jnp.exp(scores - row_max[..., None]), axis=-1))
    weights = jnp.where(allowed, jnp.exp(scores - log_total[..., None]), 0.0)
    weights_low = weights.astype(jnp.bfloat16)
    attended = jnp.einsum("phij,jphd->iphd", weights_low, v_ext, preferred_element_type=jnp.float32)
    row_dot = jnp.einsum("iphd,iphd->phi", g_own.astype(jnp.float32), attended)
    weight_grad = jnp.einsum("iphd,jphd->phij", g_own, v_ext, preferred_element_type=jnp.float32)
    score_grad = (weights * (weight_grad - row_dot[..., None])).astype(jnp.bfloat16)
    grad_query = (
        jnp.einsum("phij,jphd->iphd", score_grad, k_ext, preferred_element_type=jnp.float32)
        * scaling
    )
    key_terms = (
        jnp.einsum("phij,iphd->jphd", score_grad, q_own, preferred_element_type=jnp.float32)
        * scaling
    )
    value_terms = jnp.einsum(
        "phij,iphd->jphd", weights_low, g_own, preferred_element_type=jnp.float32
    )
    both_terms = jnp.stack([key_terms, value_terms]).reshape(2, 3 * window, places, channels)
    from_after = shifted(both_terms[:, :window], "grp", -1)
    from_before = shifted(both_terms[:, 2 * window :], "grp", 1)
    summed = both_terms[:, window : 2 * window] + from_after + from_before
    grad_key = summed[0]
    grad_value = summed[1]
    grad_qt, grad_kt, grad_vt = (
        lax.all_to_all(
            grad_query.reshape(window, places, channels).astype(jnp.bfloat16),
            "seq",
            split_axis=0,
            concat_axis=1,
            tiled=True,
        ),
        lax.all_to_all(
            grad_key.astype(jnp.bfloat16), "seq", split_axis=0, concat_axis=1, tiled=True
        ),
        lax.all_to_all(
            grad_value.astype(jnp.bfloat16), "seq", split_axis=0, concat_axis=1, tiled=True
        ),
    )
    return (grad_qs, grad_ks, grad_vs, grad_qt, grad_kt, grad_vt)


def solution(mesh):
    split_spec = P(("grp", "seq"), None, None)

    def mapped(body):
        return jax.shard_map(
            body,
            mesh=mesh,
            in_specs=(split_spec,) * 8 + (P(),),
            out_specs=(split_spec,) * 6,
            check_vma=False,
        )

    def grads(*arrays):
        return mapped(tile_shards if whole_tiles(mesh, arrays[0].shape[1]) else shards)(*arrays)

    return grads
```

```python
import functools
import math

import jax
import jax.numpy as jnp
from jax import lax
from jax.experimental import pallas as pl
from jax.experimental.pallas import tpu as pltpu
from jax.sharding import PartitionSpec as P

HEADS = 8
HDIM = 72
WIDTH = HEADS * HDIM
LANES = 128
SCALING = 1.0 / math.sqrt(HDIM)
CHUNKS = (4, 4)
masked_score = -1e30


def dot(left, right, left_dim, right_dim):
    dims = (((left_dim,), (right_dim,)), ((), ()))
    return lax.dot_general(left, right, dims, preferred_element_type=jnp.float32)


def rounded(value):
    return value.astype(jnp.bfloat16).astype(jnp.float32)


def frame_kernel(q_ref, k_ref, v_ref, g_ref, dq_ref, dk_ref, dv_ref):
    pair = 2 * HDIM
    reach = -(-HDIM // 16) * 16
    row = lax.broadcasted_iota(jnp.int32, (reach, 1), 0)
    for begin in range(0, WIDTH, pair):
        found = [[], [], []]
        for low, own in ((0, 0), (pair - reach, reach - HDIM)):
            span = slice(begin + low, begin + low + reach)
            mask = ((row >= own) & (row < own + HDIM)).astype(jnp.float32).astype(jnp.bfloat16)
            queries, keys = q_ref[0, span, :], k_ref[0, span, :]
            cotangent = g_ref[0, span, :]
            scores = dot(keys * mask, queries, 0, 0) * SCALING
            weight_grad = dot(v_ref[0, span, :] * mask, cotangent, 0, 0)
            raised = jnp.exp(scores - jnp.max(scores, axis=0, keepdims=True))
            weights = raised * (1.0 / jnp.sum(raised, axis=0, keepdims=True))
            weights_low = weights.astype(jnp.bfloat16)
            dots = jnp.sum(weights_low.astype(jnp.float32) * weight_grad, axis=0, keepdims=True)
            score_grad = (weights * (weight_grad - dots)).astype(jnp.bfloat16)
            rows = slice(own, own + HDIM)
            found[0].append(dot(keys, score_grad, 1, 0)[rows] * SCALING)
            found[1].append(dot(queries, score_grad, 1, 1)[rows] * SCALING)
            found[2].append(dot(cotangent, weights_low, 1, 1)[rows])
        for out, parts in zip((dq_ref, dk_ref, dv_ref), found):
            out[0, begin : begin + pair, :] = jnp.concatenate(parts, axis=0).astype(jnp.bfloat16)


def space_grads(queries, keys, values, cotangent):
    tokens = queries.shape[2]
    shape = jax.ShapeDtypeStruct(queries.shape, jnp.bfloat16)
    return pl.pallas_call(
        frame_kernel,
        out_shape=(shape, shape, shape),
        compiler_params=pltpu.CompilerParams(vmem_limit_bytes=60 * 2**20),
        cost_estimate=pl.CostEstimate(
            flops=12 * tokens * tokens * 256 * HEADS,
            bytes_accessed=14 * tokens * WIDTH,
            transcendentals=tokens * tokens * HEADS,
        ),
        name="space",
    )(queries, keys, values, cotangent)


def part_of(device, sharing, rows):
    row = pl.multiple_of(device % sharing * rows, 16)
    return row, pl.ds(pl.multiple_of(device // sharing * LANES, LANES), LANES)


def split_kernel(sharing, rows, jobs, *refs):
    ins, outs, (held, arrived, sent) = refs[:4], refs[4:-3], refs[-3:]
    loads, stores = {}, []
    for at, (begin, step) in enumerate(jobs):
        row, tokens = part_of(lax.axis_index("seq") ^ step, sharing, rows)
        for i, array in enumerate(ins):
            given = array.at[0, pl.ds(begin + row, rows), tokens]
            loads[at, i] = pltpu.make_async_copy(given, held.at[at, i], arrived.at[at, i])
            loads[at, i].start()
    for at, out in enumerate(outs):
        for i in range(len(ins)):
            loads[at, i].wait()
        stores.append(pltpu.make_async_copy(held.at[at], out, sent.at[at]))
        stores[-1].start()
    for copy in stores:
        copy.wait()


def split(arrays, jobs, rows, sharing):
    count = len(jobs)
    hbm = pl.BlockSpec(memory_space=pltpu.HBM)
    return pl.pallas_call(
        functools.partial(split_kernel, sharing, rows, jobs),
        in_specs=[hbm] * 4,
        out_specs=[hbm] * count,
        out_shape=[jax.ShapeDtypeStruct((4, rows, LANES), jnp.bfloat16)] * count,
        scratch_shapes=[
            pltpu.VMEM((count, 4, rows, LANES), jnp.bfloat16),
            pltpu.SemaphoreType.DMA((count, 4)),
            pltpu.SemaphoreType.DMA((count,)),
        ],
        compiler_params=pltpu.CompilerParams(vmem_limit_bytes=60 * 2**20),
        name="pack",
    )(*arrays)


def far_first(n):
    return [*reversed(range(n // 2, n)), *range(n // 2)]


def swap(block, axis, pairs):
    return lax.ppermute(block, axis, [(i, j) for i, j in pairs] + [(j, i) for i, j in pairs])


def exchange(blocks):
    n = len(blocks)
    moved = list(blocks)
    for step in reversed(range(1, n)):
        pairs = [[i, i ^ step] for i in range(n) if i < i ^ step]
        moved[step] = swap(blocks[step], "seq", pairs)
    return moved


def sides_kernel(n, *refs):
    ins, outs = refs[:n], refs[n:]
    is_odd = lax.axis_index("grp") & 1
    for step, ref in enumerate(ins):
        frame = lax.axis_index("seq") ^ step
        for start, out in zip((1, 0), outs):
            at = frame - jnp.where(is_odd == start, 1, 0)

            @pl.when((at >= 0) & (at < n - 1))
            def _():
                out[jnp.clip(at, 0, n - 2)] = ref[...]


def sides(blocks):
    n = len(blocks)
    shape = jax.ShapeDtypeStruct((n - 1, *blocks[0].shape), jnp.bfloat16)
    vmem = pl.BlockSpec(memory_space=pltpu.VMEM)
    return pl.pallas_call(
        functools.partial(sides_kernel, n),
        in_specs=[vmem] * n,
        out_specs=[vmem] * 2,
        out_shape=[shape] * 2,
        compiler_params=pltpu.CompilerParams(vmem_limit_bytes=24 * 2**20),
        name="sides",
    )(*blocks)


def gated(values, *earlier):
    return lax.optimization_barrier((values, *earlier))


def neighbours(block, start):
    count = lax.axis_size("grp")
    return swap(block, "grp", [(i, (i + 1) % count) for i in range(start, count, 2)])


def join_kernel(sharing, span, *refs):
    outs, sent = refs[-4:-1], refs[-1]
    rows = refs[0].shape[1]
    n = sent.shape[0]
    copies = []
    for at, step in enumerate(far_first(n)):
        row, tokens = part_of(lax.axis_index("seq") ^ step, sharing, rows)
        for i, out in enumerate(outs):
            given = out.at[0, pl.ds(span.start + row, rows), tokens]
            copies.append(pltpu.make_async_copy(refs[at].at[i], given, sent.at[step, i]))
            copies[-1].start()
    for copy in copies:
        copy.wait()


def join(blocks, span, tokens, sharing, earlier):
    n = len(blocks)
    shape = jax.ShapeDtypeStruct((1, WIDTH, tokens), jnp.bfloat16)
    hbm = pl.BlockSpec(memory_space=pltpu.HBM)
    earlier = [] if earlier is None else list(earlier)
    return pl.pallas_call(
        functools.partial(join_kernel, sharing, span),
        in_specs=[pl.BlockSpec(memory_space=pltpu.VMEM)] * n + [hbm] * len(earlier),
        out_specs=[hbm] * 3,
        out_shape=[shape] * 3,
        scratch_shapes=[pltpu.SemaphoreType.DMA((n, 3))],
        input_output_aliases={n + i: i for i in range(len(earlier))},
        compiler_params=pltpu.CompilerParams(vmem_limit_bytes=24 * 2**20),
        name="unpack",
    )(*(blocks[step] for step in far_first(n)), *earlier)


def clip_kernel(window, heads, given_bounds, *refs):
    own, sides_of = refs[:window], refs[window : window + 2]
    outs, refs = refs[window + 2 : 2 * window + 2], refs[2 * window + 2 :]
    wide, score_ref, grad_ref, weight_ref, found, bounds, arrived = refs
    copy = pltpu.make_async_copy(given_bounds, bounds, arrived)
    copy.start()
    halo = window - 1
    extent = window + 2 * halo
    queries, keys, values, cotangent = range(4)

    def widen(ref, frame):
        for i in range(4):
            wide[i, frame] = ref[i].astype(jnp.float32)

    for step, ref in enumerate(own):
        widen(ref, halo + (lax.axis_index("seq") ^ step))
    for start, ref in zip((1, 0), sides_of):
        is_next = (lax.axis_index("grp") & 1) == start
        for at in range(halo):
            widen(ref.at[at], at + jnp.where(is_next, halo + window, 0))
    copy.wait()
    lowest, highest = bounds[0, halo], bounds[1, halo + window - 1]

    def partners(frame):
        first, last = bounds[0, frame], bounds[1, frame]
        return first, last - first, [jnp.minimum(first + t, last - 1) for t in range(window)]

    def products(frame, carry):
        first, count, others = partners(frame)
        scores, grads = [[] for _ in others], [[] for _ in others]
        for head in range(heads):
            span = slice(head * HDIM, (head + 1) * HDIM)
            query, cot = wide[queries, frame, span, :], wide[cotangent, frame, span, :]
            for t, other in enumerate(others):
                score = jnp.sum(query * wide[keys, other, span, :], axis=0, keepdims=True)
                grad = jnp.sum(cot * wide[values, other, span, :], axis=0, keepdims=True)
                scores[t].append(score)
                grads[t].append(grad)
        for t in range(window):
            bias = jnp.where(t < count, 0.0, masked_score)
            score_ref[t, frame] = jnp.concatenate(scores[t], axis=0) * SCALING + bias
            grad_ref[t, frame] = jnp.concatenate(grads[t], axis=0)
        return carry

    lax.fori_loop(lowest, highest, products, 0)
    scores, grads = [score_ref[t] for t in range(window)], [grad_ref[t] for t in range(window)]
    peak = functools.reduce(jnp.maximum, scores)
    raised = [jnp.exp(score - peak) for score in scores]
    inverse = 1.0 / functools.reduce(jnp.add, raised)
    weights = [part * inverse for part in raised]
    weights_low = [rounded(part) for part in weights]
    dots = functools.reduce(jnp.add, [w * d for w, d in zip(weights_low, grads)])
    for t in range(window):
        weight_ref[t] = weights_low[t]
        score_ref[t] = rounded(weights[t] * (grads[t] - dots))

    def gradients(at, carry):
        frame = halo + at
        first, count, others = partners(frame)
        place = frame - first
        sums = [[], [], []]
        for head in range(heads):
            span, row = slice(head * HDIM, (head + 1) * HDIM), slice(head, head + 1)
            totals = [None] * 3
            for t, other in enumerate(others):
                score_back = jnp.where(t < count, score_ref[place, other, row, :], 0.0)
                weight_back = jnp.where(t < count, weight_ref[place, other, row, :], 0.0)
                terms = (
                    score_ref[t, frame, row, :] * wide[keys, other, span, :],
                    score_back * wide[queries, other, span, :],
                    weight_back * wide[cotangent, other, span, :],
                )
                totals = [x if y is None else y + x for x, y in zip(terms, totals)]
            for held, total, scale in zip(sums, totals, (SCALING, SCALING, None)):
                held.append(total if scale is None else total * scale)
        for i, parts in enumerate(sums):
            found[at, i] = jnp.concatenate(parts, axis=0).astype(jnp.bfloat16)
        return carry

    lax.fori_loop(0, window, gradients, 0)
    for step, out in enumerate(outs):
        out[...] = found[lax.axis_index("seq") ^ step]


def clip_grads(bounds, own, beside):
    window = len(own)
    _, rows, lanes = own[0].shape
    heads = rows // HDIM
    extent = 3 * window - 2
    vmem = pl.BlockSpec(memory_space=pltpu.VMEM)
    shape = (3, rows, lanes)
    slots = pltpu.VMEM((window, extent, heads, lanes), jnp.float32)
    return pl.pallas_call(
        functools.partial(clip_kernel, window, heads),
        out_shape=[jax.ShapeDtypeStruct(shape, jnp.bfloat16)] * window,
        in_specs=[pl.BlockSpec(memory_space=pl.ANY)] + [vmem] * (window + 2),
        out_specs=[vmem] * window,
        scratch_shapes=[
            pltpu.VMEM((4, extent, rows, lanes), jnp.float32),
            slots,
            slots,
            slots,
            pltpu.VMEM((window, *shape), jnp.bfloat16),
            pltpu.SMEM(bounds.shape, jnp.int32),
            pltpu.SemaphoreType.DMA,
        ],
        compiler_params=pltpu.CompilerParams(vmem_limit_bytes=48 * 2**20),
        cost_estimate=pl.CostEstimate(
            flops=800 * extent * window * rows * lanes,
            bytes_accessed=2 * sum(block.size for block in (*own, *beside)),
            transcendentals=extent * window * heads * lanes,
        ),
        name="clips",
    )(bounds, *own, *beside)


def clip_bounds(clip_len, window):
    halo = window - 1
    extent = window + 2 * halo
    start = lax.axis_index("grp") * window - halo
    frames = start + jnp.arange(extent, dtype=jnp.int32)
    order = jnp.arange(clip_len.shape[0])
    ends = jnp.sum(jnp.where(order[:, None] <= order[None, :], clip_len[:, None], 0), axis=0)
    begins = ends - clip_len
    holds = (begins[None, :] <= frames[:, None]) & (frames[:, None] < ends[None, :])
    first = jnp.sum(jnp.where(holds, begins[None, :], 0), axis=1) - start
    last = jnp.sum(jnp.where(holds, ends[None, :], 0), axis=1) - start
    return jnp.stack([first, last]).astype(jnp.int32)


def tile_shards(q_space, k_space, v_space, cot_space, q_time, k_time, v_time, cot_time, clip_len):
    def turned(*arrays):
        return tuple(array.transpose(0, 2, 1) for array in arrays)

    n = lax.axis_size("seq")
    window = q_time.shape[0] * n
    tokens = q_time.shape[1]
    sharing = n * LANES // tokens
    bounds = clip_bounds(clip_len, window)
    time = turned(q_time, k_time, v_time, cot_time)
    spans = []
    head = 0
    for heads in CHUNKS:
        spans.append(slice(head * HDIM, (head + heads) * HDIM))
        head += heads
    space_in = turned(q_space, k_space, v_space, cot_space)
    rows = CHUNKS[0] // sharing * HDIM
    jobs = [(span.start, step) for span in spans for step in far_first(n)]
    blocks = {}
    for part in (jobs[: n // 2], jobs[n // 2 :]):
        blocks.update(zip(part, split(time, part, rows, sharing)))
    packed = [[blocks[span.start, step] for step in range(n)] for span in spans]
    own = [exchange(packed[0])]
    space = space_grads(*space_in)
    packed[1][2:], own[0][2], space = gated(packed[1][2:], own[0][2], space)
    own.append(exchange(packed[1]))
    beside = [
        [neighbours(ends, start) for ends, start in zip(sides(blocks), (1, 0))] for blocks in own
    ]
    back, grads = [], None
    for blocks, near in zip(own, beside):
        back.append(exchange(clip_grads(bounds, blocks, near)))
    for span, blocks in zip(spans, back):
        grads = join(blocks, span, tokens, sharing, grads)
    return turned(*space, *grads)


def whole_tiles(mesh, tokens):
    n = mesh.shape["seq"]
    sharing = n * LANES // tokens
    return (
        tokens % LANES == 0
        and n % 4 == 0
        and n & (n - 1) == 0
        and mesh.shape["grp"] % 2 == 0
        and mesh.shape["grp"] > 2
        and sharing * tokens == n * LANES
        and len(set(CHUNKS)) == 1
        and all(heads % sharing == 0 and heads // sharing * HDIM % 16 == 0 for heads in CHUNKS)
    )


def padded(block, sides, width):
    for axis, dim in sides:
        count = lax.axis_size(axis)
        forward = [(i, i + 1) for i in range(count - 1)]
        backward = [(target, source) for source, target in forward]
        low = lax.ppermute(
            lax.slice_in_dim(block, block.shape[dim] - width, None, axis=dim), axis, forward
        )
        high = lax.ppermute(lax.slice_in_dim(block, 0, width, axis=dim), axis, backward)
        block = jnp.concatenate([low, block, high], axis=dim)
    return block


def shifted(value, axis, by):
    count = lax.axis_size(axis)
    pairs = [(i, i + by) for i in range(count) if 0 <= i + by < count]
    return lax.ppermute(value, axis, pairs)


def clip_labels(clip_len, first_frame, count, frame_total):
    frame_ids = first_frame + jnp.arange(count, dtype=jnp.int32)
    clip_ends = jnp.cumsum(clip_len)
    labels = jnp.sum((clip_ends[None, :] <= frame_ids[:, None]).astype(jnp.int32), axis=1)
    inside = (frame_ids >= 0) & (frame_ids < frame_total)
    return (labels, inside)


def frame_grads(queries, keys, values, cotangent):
    scaling = 1.0 / math.sqrt(HDIM)
    tokens = queries.shape[0]
    q_heads = queries.reshape(tokens, HEADS, HDIM)
    k_heads = keys.reshape(tokens, HEADS, HDIM)
    v_heads = values.reshape(tokens, HEADS, HDIM)
    g_heads = cotangent.reshape(tokens, HEADS, HDIM)
    scores = (
        jnp.einsum("qhd,khd->hqk", q_heads, k_heads, preferred_element_type=jnp.float32) * scaling
    )
    row_max = jnp.max(scores, axis=-1, keepdims=True)
    log_total = row_max + jnp.log(jnp.sum(jnp.exp(scores - row_max), axis=-1, keepdims=True))
    weights = jnp.exp(scores - log_total)
    weights_low = weights.astype(jnp.bfloat16)
    attended = jnp.einsum("hqk,khd->qhd", weights_low, v_heads, preferred_element_type=jnp.float32)
    row_dot = jnp.einsum("qhd,qhd->hq", g_heads.astype(jnp.float32), attended)
    weight_grad = jnp.einsum("qhd,khd->hqk", g_heads, v_heads, preferred_element_type=jnp.float32)
    score_grad = (weights * (weight_grad - row_dot[:, :, None])).astype(jnp.bfloat16)
    grad_query = (
        jnp.einsum("hqk,khd->qhd", score_grad, k_heads, preferred_element_type=jnp.float32)
        * scaling
    )
    grad_key = (
        jnp.einsum("hqk,qhd->khd", score_grad, q_heads, preferred_element_type=jnp.float32)
        * scaling
    )
    grad_value = jnp.einsum(
        "hqk,qhd->khd", weights_low, g_heads, preferred_element_type=jnp.float32
    )
    flat_shape = (1, tokens, HEADS * HDIM)
    return (
        grad_query.reshape(flat_shape).astype(jnp.bfloat16),
        grad_key.reshape(flat_shape).astype(jnp.bfloat16),
        grad_value.reshape(flat_shape).astype(jnp.bfloat16),
    )


def shards(q_space, k_space, v_space, cot_space, q_time, k_time, v_time, cot_time, clip_len):
    scaling = 1.0 / math.sqrt(HDIM)
    grad_qs, grad_ks, grad_vs = frame_grads(q_space[0], k_space[0], v_space[0], cot_space[0])
    moved = (
        lax.all_to_all(q_time, "seq", split_axis=1, concat_axis=0, tiled=True),
        lax.all_to_all(k_time, "seq", split_axis=1, concat_axis=0, tiled=True),
        lax.all_to_all(v_time, "seq", split_axis=1, concat_axis=0, tiled=True),
        lax.all_to_all(cot_time, "seq", split_axis=1, concat_axis=0, tiled=True),
    )
    query_win, key_win, value_win, cot_win = moved
    window = query_win.shape[0]
    places = query_win.shape[1]
    channels = query_win.shape[2]
    group_id = lax.axis_index("grp")
    frame_total = window * lax.axis_size("grp")
    first_frame = group_id * window

    def split_heads(array):
        return array.reshape(array.shape[0], places, HEADS, HDIM)

    key_pair = padded(jnp.stack([key_win, value_win]), (("grp", 1),), window)
    q_own = split_heads(query_win)
    g_own = split_heads(cot_win)
    k_ext = split_heads(key_pair[0])
    v_ext = split_heads(key_pair[1])
    own_label, own_inside = clip_labels(clip_len, first_frame, window, frame_total)
    ext_label, ext_inside = clip_labels(clip_len, first_frame - window, 3 * window, frame_total)
    allowed = (own_label[:, None] == ext_label[None, :]) & ext_inside[None, :]
    scores = (
        jnp.einsum("iphd,jphd->phij", q_own, k_ext, preferred_element_type=jnp.float32) * scaling
    )
    scores = jnp.where(allowed, scores, masked_score)
    row_max = jnp.max(scores, axis=-1)
    log_total = row_max + jnp.log(jnp.sum(jnp.exp(scores - row_max[..., None]), axis=-1))
    weights = jnp.where(allowed, jnp.exp(scores - log_total[..., None]), 0.0)
    weights_low = weights.astype(jnp.bfloat16)
    attended = jnp.einsum("phij,jphd->iphd", weights_low, v_ext, preferred_element_type=jnp.float32)
    row_dot = jnp.einsum("iphd,iphd->phi", g_own.astype(jnp.float32), attended)
    weight_grad = jnp.einsum("iphd,jphd->phij", g_own, v_ext, preferred_element_type=jnp.float32)
    score_grad = (weights * (weight_grad - row_dot[..., None])).astype(jnp.bfloat16)
    grad_query = (
        jnp.einsum("phij,jphd->iphd", score_grad, k_ext, preferred_element_type=jnp.float32)
        * scaling
    )
    key_terms = (
        jnp.einsum("phij,iphd->jphd", score_grad, q_own, preferred_element_type=jnp.float32)
        * scaling
    )
    value_terms = jnp.einsum(
        "phij,iphd->jphd", weights_low, g_own, preferred_element_type=jnp.float32
    )
    both_terms = jnp.stack([key_terms, value_terms]).reshape(2, 3 * window, places, channels)
    from_after = shifted(both_terms[:, :window], "grp", -1)
    from_before = shifted(both_terms[:, 2 * window :], "grp", 1)
    summed = both_terms[:, window : 2 * window] + from_after + from_before
    grad_key = summed[0]
    grad_value = summed[1]
    grad_qt, grad_kt, grad_vt = (
        lax.all_to_all(
            grad_query.reshape(window, places, channels).astype(jnp.bfloat16),
            "seq",
            split_axis=0,
            concat_axis=1,
            tiled=True,
        ),
        lax.all_to_all(
            grad_key.astype(jnp.bfloat16), "seq", split_axis=0, concat_axis=1, tiled=True
        ),
        lax.all_to_all(
            grad_value.astype(jnp.bfloat16), "seq", split_axis=0, concat_axis=1, tiled=True
        ),
    )
    return (grad_qs, grad_ks, grad_vs, grad_qt, grad_kt, grad_vt)


def solution(mesh):
    split_spec = P(("grp", "seq"), None, None)

    def mapped(body):
        return jax.shard_map(
            body,
            mesh=mesh,
            in_specs=(split_spec,) * 8 + (P(),),
            out_specs=(split_spec,) * 6,
            check_vma=False,
        )

    def grads(*arrays):
        return mapped(tile_shards if whole_tiles(mesh, arrays[0].shape[1]) else shards)(*arrays)

    return grads
```

```python
import functools
import math

import jax
import jax.numpy as jnp
from jax import lax
from jax.experimental import pallas as pl
from jax.experimental.pallas import tpu as pltpu
from jax.sharding import PartitionSpec as P

HEADS = 8
HDIM = 72
WIDTH = HEADS * HDIM
LANES = 128
SCALING = 1.0 / math.sqrt(HDIM)
CHUNKS = (4, 4)
masked_score = -1e30


def dot(left, right, left_dim, right_dim):
    dims = (((left_dim,), (right_dim,)), ((), ()))
    return lax.dot_general(left, right, dims, preferred_element_type=jnp.float32)


def rounded(value):
    return value.astype(jnp.bfloat16).astype(jnp.float32)


def frame_kernel(q_ref, k_ref, v_ref, g_ref, dq_ref, dk_ref, dv_ref):
    pair = 2 * HDIM
    reach = -(-HDIM // 16) * 16
    row = lax.broadcasted_iota(jnp.int32, (reach, 1), 0)
    for begin in range(0, WIDTH, pair):
        found = [[], [], []]
        for low, own in ((0, 0), (pair - reach, reach - HDIM)):
            span = slice(begin + low, begin + low + reach)
            mask = ((row >= own) & (row < own + HDIM)).astype(jnp.float32).astype(jnp.bfloat16)
            queries, keys = q_ref[0, span, :], k_ref[0, span, :]
            cotangent = g_ref[0, span, :]
            scores = dot(keys * mask, queries, 0, 0) * SCALING
            weight_grad = dot(v_ref[0, span, :] * mask, cotangent, 0, 0)
            raised = jnp.exp(scores - jnp.max(scores, axis=0, keepdims=True))
            weights = raised * (1.0 / jnp.sum(raised, axis=0, keepdims=True))
            weights_low = weights.astype(jnp.bfloat16)
            dots = jnp.sum(weights_low.astype(jnp.float32) * weight_grad, axis=0, keepdims=True)
            score_grad = (weights * (weight_grad - dots)).astype(jnp.bfloat16)
            rows = slice(own, own + HDIM)
            found[0].append(dot(keys, score_grad, 1, 0)[rows] * SCALING)
            found[1].append(dot(queries, score_grad, 1, 1)[rows] * SCALING)
            found[2].append(dot(cotangent, weights_low, 1, 1)[rows])
        for out, parts in zip((dq_ref, dk_ref, dv_ref), found):
            out[0, begin : begin + pair, :] = jnp.concatenate(parts, axis=0).astype(jnp.bfloat16)


def space_grads(queries, keys, values, cotangent):
    tokens = queries.shape[2]
    shape = jax.ShapeDtypeStruct(queries.shape, jnp.bfloat16)
    return pl.pallas_call(
        frame_kernel,
        out_shape=(shape, shape, shape),
        compiler_params=pltpu.CompilerParams(vmem_limit_bytes=60 * 2**20),
        cost_estimate=pl.CostEstimate(
            flops=12 * tokens * tokens * 256 * HEADS,
            bytes_accessed=14 * tokens * WIDTH,
            transcendentals=tokens * tokens * HEADS,
        ),
        name="space",
    )(queries, keys, values, cotangent)


def part_of(device, sharing, rows):
    row = pl.multiple_of(device % sharing * rows, 16)
    return row, pl.ds(pl.multiple_of(device // sharing * LANES, LANES), LANES)


def split_kernel(sharing, rows, span, *refs):
    ins, outs, (held, arrived, sent) = refs[:4], refs[4:-3], refs[-3:]
    loads, stores = {}, []
    for step in far_first(len(outs)):
        row, tokens = part_of(lax.axis_index("seq") ^ step, sharing, rows)
        for i, array in enumerate(ins):
            given = array.at[0, pl.ds(span.start + row, rows), tokens]
            loads[step, i] = pltpu.make_async_copy(given, held.at[step, i], arrived.at[step, i])
            loads[step, i].start()
    for step in far_first(len(outs)):
        for i in range(len(ins)):
            loads[step, i].wait()
        stores.append(pltpu.make_async_copy(held.at[step], outs[step], sent.at[step]))
        stores[-1].start()
    for copy in stores:
        copy.wait()


def split(arrays, span, n, sharing):
    rows = (span.stop - span.start) // sharing
    hbm = pl.BlockSpec(memory_space=pltpu.HBM)
    return pl.pallas_call(
        functools.partial(split_kernel, sharing, rows, span),
        in_specs=[hbm] * 4,
        out_specs=[hbm] * n,
        out_shape=[jax.ShapeDtypeStruct((4, rows, LANES), jnp.bfloat16)] * n,
        scratch_shapes=[
            pltpu.VMEM((n, 4, rows, LANES), jnp.bfloat16),
            pltpu.SemaphoreType.DMA((n, 4)),
            pltpu.SemaphoreType.DMA((n,)),
        ],
        compiler_params=pltpu.CompilerParams(vmem_limit_bytes=60 * 2**20),
        name="pack",
    )(*arrays)


def far_first(n):
    return [*reversed(range(n // 2, n)), *range(n // 2)]


def swap(block, axis, pairs):
    return lax.ppermute(block, axis, [(i, j) for i, j in pairs] + [(j, i) for i, j in pairs])


def exchange(blocks):
    n = len(blocks)
    moved = list(blocks)
    for step in reversed(range(1, n)):
        pairs = [[i, i ^ step] for i in range(n) if i < i ^ step]
        moved[step] = swap(blocks[step], "seq", pairs)
    return moved


def sides_kernel(n, *refs):
    ins, outs = refs[:n], refs[n:]
    is_odd = lax.axis_index("grp") & 1
    for step, ref in enumerate(ins):
        frame = lax.axis_index("seq") ^ step
        for start, out in zip((1, 0), outs):
            at = frame - jnp.where(is_odd == start, 1, 0)

            @pl.when((at >= 0) & (at < n - 1))
            def _():
                out[jnp.clip(at, 0, n - 2)] = ref[...]


def sides(blocks):
    n = len(blocks)
    shape = jax.ShapeDtypeStruct((n - 1, *blocks[0].shape), jnp.bfloat16)
    vmem = pl.BlockSpec(memory_space=pltpu.VMEM)
    return pl.pallas_call(
        functools.partial(sides_kernel, n),
        in_specs=[vmem] * n,
        out_specs=[vmem] * 2,
        out_shape=[shape] * 2,
        compiler_params=pltpu.CompilerParams(vmem_limit_bytes=24 * 2**20),
        name="sides",
    )(*blocks)


def gated(values, *earlier):
    return lax.optimization_barrier((values, *earlier))


def neighbours(block, start):
    count = lax.axis_size("grp")
    return swap(block, "grp", [(i, (i + 1) % count) for i in range(start, count, 2)])


def join_kernel(sharing, span, *refs):
    outs, sent = refs[-4:-1], refs[-1]
    rows = refs[0].shape[1]
    n = sent.shape[0]
    copies = []
    for at, step in enumerate(far_first(n)):
        row, tokens = part_of(lax.axis_index("seq") ^ step, sharing, rows)
        for i, out in enumerate(outs):
            given = out.at[0, pl.ds(span.start + row, rows), tokens]
            copies.append(pltpu.make_async_copy(refs[at].at[i], given, sent.at[step, i]))
            copies[-1].start()
    for copy in copies:
        copy.wait()


def join(blocks, span, tokens, sharing, earlier):
    n = len(blocks)
    shape = jax.ShapeDtypeStruct((1, WIDTH, tokens), jnp.bfloat16)
    hbm = pl.BlockSpec(memory_space=pltpu.HBM)
    earlier = [] if earlier is None else list(earlier)
    return pl.pallas_call(
        functools.partial(join_kernel, sharing, span),
        in_specs=[pl.BlockSpec(memory_space=pltpu.VMEM)] * n + [hbm] * len(earlier),
        out_specs=[hbm] * 3,
        out_shape=[shape] * 3,
        scratch_shapes=[pltpu.SemaphoreType.DMA((n, 3))],
        input_output_aliases={n + i: i for i in range(len(earlier))},
        compiler_params=pltpu.CompilerParams(vmem_limit_bytes=24 * 2**20),
        name="unpack",
    )(*(blocks[step] for step in far_first(n)), *earlier)


def clip_kernel(window, heads, given_bounds, *refs):
    own, sides_of = refs[:window], refs[window : window + 2]
    outs, refs = refs[window + 2 : 2 * window + 2], refs[2 * window + 2 :]
    wide, score_ref, grad_ref, weight_ref, found, bounds, arrived = refs
    copy = pltpu.make_async_copy(given_bounds, bounds, arrived)
    copy.start()
    halo = window - 1
    extent = window + 2 * halo
    queries, keys, values, cotangent = range(4)

    def widen(ref, frame):
        for i in range(4):
            wide[i, frame] = ref[i].astype(jnp.float32)

    for step, ref in enumerate(own):
        widen(ref, halo + (lax.axis_index("seq") ^ step))
    for start, ref in zip((1, 0), sides_of):
        is_next = (lax.axis_index("grp") & 1) == start
        for at in range(halo):
            widen(ref.at[at], at + jnp.where(is_next, halo + window, 0))
    copy.wait()
    lowest, highest = bounds[0, halo], bounds[1, halo + window - 1]

    def partners(frame):
        first, last = bounds[0, frame], bounds[1, frame]
        return first, last - first, [jnp.minimum(first + t, last - 1) for t in range(window)]

    def products(frame, carry):
        first, count, others = partners(frame)
        scores, grads = [[] for _ in others], [[] for _ in others]
        for head in range(heads):
            span = slice(head * HDIM, (head + 1) * HDIM)
            query, cot = wide[queries, frame, span, :], wide[cotangent, frame, span, :]
            for t, other in enumerate(others):
                score = jnp.sum(query * wide[keys, other, span, :], axis=0, keepdims=True)
                grad = jnp.sum(cot * wide[values, other, span, :], axis=0, keepdims=True)
                scores[t].append(score)
                grads[t].append(grad)
        for t in range(window):
            bias = jnp.where(t < count, 0.0, masked_score)
            score_ref[t, frame] = jnp.concatenate(scores[t], axis=0) * SCALING + bias
            grad_ref[t, frame] = jnp.concatenate(grads[t], axis=0)
        return carry

    lax.fori_loop(lowest, highest, products, 0)
    scores, grads = [score_ref[t] for t in range(window)], [grad_ref[t] for t in range(window)]
    peak = functools.reduce(jnp.maximum, scores)
    raised = [jnp.exp(score - peak) for score in scores]
    inverse = 1.0 / functools.reduce(jnp.add, raised)
    weights = [part * inverse for part in raised]
    weights_low = [rounded(part) for part in weights]
    dots = functools.reduce(jnp.add, [w * d for w, d in zip(weights_low, grads)])
    for t in range(window):
        weight_ref[t] = weights_low[t]
        score_ref[t] = rounded(weights[t] * (grads[t] - dots))

    def gradients(at, carry):
        frame = halo + at
        first, count, others = partners(frame)
        place = frame - first
        sums = [[], [], []]
        for head in range(heads):
            span, row = slice(head * HDIM, (head + 1) * HDIM), slice(head, head + 1)
            totals = [None] * 3
            for t, other in enumerate(others):
                score_back = jnp.where(t < count, score_ref[place, other, row, :], 0.0)
                weight_back = jnp.where(t < count, weight_ref[place, other, row, :], 0.0)
                terms = (
                    score_ref[t, frame, row, :] * wide[keys, other, span, :],
                    score_back * wide[queries, other, span, :],
                    weight_back * wide[cotangent, other, span, :],
                )
                totals = [x if y is None else y + x for x, y in zip(terms, totals)]
            for held, total, scale in zip(sums, totals, (SCALING, SCALING, None)):
                held.append(total if scale is None else total * scale)
        for i, parts in enumerate(sums):
            found[at, i] = jnp.concatenate(parts, axis=0).astype(jnp.bfloat16)
        return carry

    lax.fori_loop(0, window, gradients, 0)
    for step, out in enumerate(outs):
        out[...] = found[lax.axis_index("seq") ^ step]


def clip_grads(bounds, own, beside):
    window = len(own)
    _, rows, lanes = own[0].shape
    heads = rows // HDIM
    extent = 3 * window - 2
    vmem = pl.BlockSpec(memory_space=pltpu.VMEM)
    shape = (3, rows, lanes)
    slots = pltpu.VMEM((window, extent, heads, lanes), jnp.float32)
    return pl.pallas_call(
        functools.partial(clip_kernel, window, heads),
        out_shape=[jax.ShapeDtypeStruct(shape, jnp.bfloat16)] * window,
        in_specs=[pl.BlockSpec(memory_space=pl.ANY)] + [vmem] * (window + 2),
        out_specs=[vmem] * window,
        scratch_shapes=[
            pltpu.VMEM((4, extent, rows, lanes), jnp.float32),
            slots,
            slots,
            slots,
            pltpu.VMEM((window, *shape), jnp.bfloat16),
            pltpu.SMEM(bounds.shape, jnp.int32),
            pltpu.SemaphoreType.DMA,
        ],
        compiler_params=pltpu.CompilerParams(vmem_limit_bytes=48 * 2**20),
        cost_estimate=pl.CostEstimate(
            flops=800 * extent * window * rows * lanes,
            bytes_accessed=2 * sum(block.size for block in (*own, *beside)),
            transcendentals=extent * window * heads * lanes,
        ),
        name="clips",
    )(bounds, *own, *beside)


def clip_bounds(clip_len, window):
    halo = window - 1
    extent = window + 2 * halo
    start = lax.axis_index("grp") * window - halo
    frames = start + jnp.arange(extent, dtype=jnp.int32)
    order = jnp.arange(clip_len.shape[0])
    ends = jnp.sum(jnp.where(order[:, None] <= order[None, :], clip_len[:, None], 0), axis=0)
    begins = ends - clip_len
    holds = (begins[None, :] <= frames[:, None]) & (frames[:, None] < ends[None, :])
    first = jnp.sum(jnp.where(holds, begins[None, :], 0), axis=1) - start
    last = jnp.sum(jnp.where(holds, ends[None, :], 0), axis=1) - start
    return jnp.stack([first, last]).astype(jnp.int32)


def tile_shards(q_space, k_space, v_space, cot_space, q_time, k_time, v_time, cot_time, clip_len):
    def turned(*arrays):
        return tuple(array.transpose(0, 2, 1) for array in arrays)

    n = lax.axis_size("seq")
    window = q_time.shape[0] * n
    tokens = q_time.shape[1]
    sharing = n * LANES // tokens
    bounds = clip_bounds(clip_len, window)
    time = turned(q_time, k_time, v_time, cot_time)
    spans = []
    head = 0
    for heads in CHUNKS:
        spans.append(slice(head * HDIM, (head + heads) * HDIM))
        head += heads
    space_in = turned(q_space, k_space, v_space, cot_space)
    packed = [list(split(time, span, n, sharing)) for span in spans]
    own = [exchange(packed[0])]
    space = space_grads(*space_in)
    packed[1][2:], own[0][2], space = gated(packed[1][2:], own[0][2], space)
    own.append(exchange(packed[1]))
    beside = [
        [neighbours(ends, start) for ends, start in zip(sides(blocks), (1, 0))] for blocks in own
    ]
    back, grads = [], None
    for blocks, near in zip(own, beside):
        back.append(exchange(clip_grads(bounds, blocks, near)))
    for span, blocks in zip(spans, back):
        grads = join(blocks, span, tokens, sharing, grads)
    return turned(*space, *grads)


def whole_tiles(mesh, tokens):
    n = mesh.shape["seq"]
    sharing = n * LANES // tokens
    return (
        tokens % LANES == 0
        and n % 4 == 0
        and n & (n - 1) == 0
        and mesh.shape["grp"] % 2 == 0
        and mesh.shape["grp"] > 2
        and sharing * tokens == n * LANES
        and all(heads % sharing == 0 and heads // sharing * HDIM % 16 == 0 for heads in CHUNKS)
    )


def padded(block, sides, width):
    for axis, dim in sides:
        count = lax.axis_size(axis)
        forward = [(i, i + 1) for i in range(count - 1)]
        backward = [(target, source) for source, target in forward]
        low = lax.ppermute(
            lax.slice_in_dim(block, block.shape[dim] - width, None, axis=dim), axis, forward
        )
        high = lax.ppermute(lax.slice_in_dim(block, 0, width, axis=dim), axis, backward)
        block = jnp.concatenate([low, block, high], axis=dim)
    return block


def shifted(value, axis, by):
    count = lax.axis_size(axis)
    pairs = [(i, i + by) for i in range(count) if 0 <= i + by < count]
    return lax.ppermute(value, axis, pairs)


def clip_labels(clip_len, first_frame, count, frame_total):
    frame_ids = first_frame + jnp.arange(count, dtype=jnp.int32)
    clip_ends = jnp.cumsum(clip_len)
    labels = jnp.sum((clip_ends[None, :] <= frame_ids[:, None]).astype(jnp.int32), axis=1)
    inside = (frame_ids >= 0) & (frame_ids < frame_total)
    return (labels, inside)


def frame_grads(queries, keys, values, cotangent):
    scaling = 1.0 / math.sqrt(HDIM)
    tokens = queries.shape[0]
    q_heads = queries.reshape(tokens, HEADS, HDIM)
    k_heads = keys.reshape(tokens, HEADS, HDIM)
    v_heads = values.reshape(tokens, HEADS, HDIM)
    g_heads = cotangent.reshape(tokens, HEADS, HDIM)
    scores = (
        jnp.einsum("qhd,khd->hqk", q_heads, k_heads, preferred_element_type=jnp.float32) * scaling
    )
    row_max = jnp.max(scores, axis=-1, keepdims=True)
    log_total = row_max + jnp.log(jnp.sum(jnp.exp(scores - row_max), axis=-1, keepdims=True))
    weights = jnp.exp(scores - log_total)
    weights_low = weights.astype(jnp.bfloat16)
    attended = jnp.einsum("hqk,khd->qhd", weights_low, v_heads, preferred_element_type=jnp.float32)
    row_dot = jnp.einsum("qhd,qhd->hq", g_heads.astype(jnp.float32), attended)
    weight_grad = jnp.einsum("qhd,khd->hqk", g_heads, v_heads, preferred_element_type=jnp.float32)
    score_grad = (weights * (weight_grad - row_dot[:, :, None])).astype(jnp.bfloat16)
    grad_query = (
        jnp.einsum("hqk,khd->qhd", score_grad, k_heads, preferred_element_type=jnp.float32)
        * scaling
    )
    grad_key = (
        jnp.einsum("hqk,qhd->khd", score_grad, q_heads, preferred_element_type=jnp.float32)
        * scaling
    )
    grad_value = jnp.einsum(
        "hqk,qhd->khd", weights_low, g_heads, preferred_element_type=jnp.float32
    )
    flat_shape = (1, tokens, HEADS * HDIM)
    return (
        grad_query.reshape(flat_shape).astype(jnp.bfloat16),
        grad_key.reshape(flat_shape).astype(jnp.bfloat16),
        grad_value.reshape(flat_shape).astype(jnp.bfloat16),
    )


def shards(q_space, k_space, v_space, cot_space, q_time, k_time, v_time, cot_time, clip_len):
    scaling = 1.0 / math.sqrt(HDIM)
    grad_qs, grad_ks, grad_vs = frame_grads(q_space[0], k_space[0], v_space[0], cot_space[0])
    moved = (
        lax.all_to_all(q_time, "seq", split_axis=1, concat_axis=0, tiled=True),
        lax.all_to_all(k_time, "seq", split_axis=1, concat_axis=0, tiled=True),
        lax.all_to_all(v_time, "seq", split_axis=1, concat_axis=0, tiled=True),
        lax.all_to_all(cot_time, "seq", split_axis=1, concat_axis=0, tiled=True),
    )
    query_win, key_win, value_win, cot_win = moved
    window = query_win.shape[0]
    places = query_win.shape[1]
    channels = query_win.shape[2]
    group_id = lax.axis_index("grp")
    frame_total = window * lax.axis_size("grp")
    first_frame = group_id * window

    def split_heads(array):
        return array.reshape(array.shape[0], places, HEADS, HDIM)

    key_pair = padded(jnp.stack([key_win, value_win]), (("grp", 1),), window)
    q_own = split_heads(query_win)
    g_own = split_heads(cot_win)
    k_ext = split_heads(key_pair[0])
    v_ext = split_heads(key_pair[1])
    own_label, own_inside = clip_labels(clip_len, first_frame, window, frame_total)
    ext_label, ext_inside = clip_labels(clip_len, first_frame - window, 3 * window, frame_total)
    allowed = (own_label[:, None] == ext_label[None, :]) & ext_inside[None, :]
    scores = (
        jnp.einsum("iphd,jphd->phij", q_own, k_ext, preferred_element_type=jnp.float32) * scaling
    )
    scores = jnp.where(allowed, scores, masked_score)
    row_max = jnp.max(scores, axis=-1)
    log_total = row_max + jnp.log(jnp.sum(jnp.exp(scores - row_max[..., None]), axis=-1))
    weights = jnp.where(allowed, jnp.exp(scores - log_total[..., None]), 0.0)
    weights_low = weights.astype(jnp.bfloat16)
    attended = jnp.einsum("phij,jphd->iphd", weights_low, v_ext, preferred_element_type=jnp.float32)
    row_dot = jnp.einsum("iphd,iphd->phi", g_own.astype(jnp.float32), attended)
    weight_grad = jnp.einsum("iphd,jphd->phij", g_own, v_ext, preferred_element_type=jnp.float32)
    score_grad = (weights * (weight_grad - row_dot[..., None])).astype(jnp.bfloat16)
    grad_query = (
        jnp.einsum("phij,jphd->iphd", score_grad, k_ext, preferred_element_type=jnp.float32)
        * scaling
    )
    key_terms = (
        jnp.einsum("phij,iphd->jphd", score_grad, q_own, preferred_element_type=jnp.float32)
        * scaling
    )
    value_terms = jnp.einsum(
        "phij,iphd->jphd", weights_low, g_own, preferred_element_type=jnp.float32
    )
    both_terms = jnp.stack([key_terms, value_terms]).reshape(2, 3 * window, places, channels)
    from_after = shifted(both_terms[:, :window], "grp", -1)
    from_before = shifted(both_terms[:, 2 * window :], "grp", 1)
    summed = both_terms[:, window : 2 * window] + from_after + from_before
    grad_key = summed[0]
    grad_value = summed[1]
    grad_qt, grad_kt, grad_vt = (
        lax.all_to_all(
            grad_query.reshape(window, places, channels).astype(jnp.bfloat16),
            "seq",
            split_axis=0,
            concat_axis=1,
            tiled=True,
        ),
        lax.all_to_all(
            grad_key.astype(jnp.bfloat16), "seq", split_axis=0, concat_axis=1, tiled=True
        ),
        lax.all_to_all(
            grad_value.astype(jnp.bfloat16), "seq", split_axis=0, concat_axis=1, tiled=True
        ),
    )
    return (grad_qs, grad_ks, grad_vs, grad_qt, grad_kt, grad_vt)


def solution(mesh):
    split_spec = P(("grp", "seq"), None, None)

    def mapped(body):
        return jax.shard_map(
            body,
            mesh=mesh,
            in_specs=(split_spec,) * 8 + (P(),),
            out_specs=(split_spec,) * 6,
            check_vma=False,
        )

    def grads(*arrays):
        return mapped(tile_shards if whole_tiles(mesh, arrays[0].shape[1]) else shards)(*arrays)

    return grads
```

```python
import functools
import math

import jax
import jax.numpy as jnp
from jax import lax
from jax.experimental import pallas as pl
from jax.experimental.pallas import tpu as pltpu
from jax.sharding import PartitionSpec as P

HEADS = 8
HDIM = 72
WIDTH = HEADS * HDIM
LANES = 128
SCALING = 1.0 / math.sqrt(HDIM)
CHUNKS = (4, 4)
masked_score = -1e30


def dot(left, right, left_dim, right_dim):
    dims = (((left_dim,), (right_dim,)), ((), ()))
    return lax.dot_general(left, right, dims, preferred_element_type=jnp.float32)


def rounded(value):
    return value.astype(jnp.bfloat16).astype(jnp.float32)


def frame_kernel(q_ref, k_ref, v_ref, g_ref, dq_ref, dk_ref, dv_ref):
    pair = 2 * HDIM
    reach = -(-HDIM // 16) * 16
    row = lax.broadcasted_iota(jnp.int32, (reach, 1), 0)
    for begin in range(0, WIDTH, pair):
        found = [[], [], []]
        for low, own in ((0, 0), (pair - reach, reach - HDIM)):
            span = slice(begin + low, begin + low + reach)
            mask = ((row >= own) & (row < own + HDIM)).astype(jnp.float32).astype(jnp.bfloat16)
            queries, keys = q_ref[0, span, :], k_ref[0, span, :]
            cotangent = g_ref[0, span, :]
            scores = dot(keys * mask, queries, 0, 0) * SCALING
            weight_grad = dot(v_ref[0, span, :] * mask, cotangent, 0, 0)
            raised = jnp.exp(scores - jnp.max(scores, axis=0, keepdims=True))
            weights = raised * (1.0 / jnp.sum(raised, axis=0, keepdims=True))
            weights_low = weights.astype(jnp.bfloat16)
            dots = jnp.sum(weights_low.astype(jnp.float32) * weight_grad, axis=0, keepdims=True)
            score_grad = (weights * (weight_grad - dots)).astype(jnp.bfloat16)
            rows = slice(own, own + HDIM)
            found[0].append(dot(keys, score_grad, 1, 0)[rows] * SCALING)
            found[1].append(dot(queries, score_grad, 1, 1)[rows] * SCALING)
            found[2].append(dot(cotangent, weights_low, 1, 1)[rows])
        for out, parts in zip((dq_ref, dk_ref, dv_ref), found):
            out[0, begin : begin + pair, :] = jnp.concatenate(parts, axis=0).astype(jnp.bfloat16)


def space_grads(queries, keys, values, cotangent):
    tokens = queries.shape[2]
    shape = jax.ShapeDtypeStruct(queries.shape, jnp.bfloat16)
    return pl.pallas_call(
        frame_kernel,
        out_shape=(shape, shape, shape),
        compiler_params=pltpu.CompilerParams(vmem_limit_bytes=60 * 2**20),
        cost_estimate=pl.CostEstimate(
            flops=12 * tokens * tokens * 256 * HEADS,
            bytes_accessed=14 * tokens * WIDTH,
            transcendentals=tokens * tokens * HEADS,
        ),
        name="space",
    )(queries, keys, values, cotangent)


def part_of(device, sharing, rows):
    row = pl.multiple_of(device % sharing * rows, 16)
    return row, pl.ds(pl.multiple_of(device // sharing * LANES, LANES), LANES)


def split_kernel(sharing, rows, span, *refs):
    ins, outs, (held, arrived, sent) = refs[:4], refs[4:-3], refs[-3:]
    loads, stores = {}, []
    for step in far_first(len(outs)):
        row, tokens = part_of(lax.axis_index("seq") ^ step, sharing, rows)
        for i, array in enumerate(ins):
            given = array.at[0, pl.ds(span.start + row, rows), tokens]
            loads[step, i] = pltpu.make_async_copy(given, held.at[step, i], arrived.at[step, i])
            loads[step, i].start()
    for step in far_first(len(outs)):
        for i in range(len(ins)):
            loads[step, i].wait()
        stores.append(pltpu.make_async_copy(held.at[step], outs[step], sent.at[step]))
        stores[-1].start()
    for copy in stores:
        copy.wait()


def split(arrays, span, n, sharing):
    rows = (span.stop - span.start) // sharing
    hbm = pl.BlockSpec(memory_space=pltpu.HBM)
    return pl.pallas_call(
        functools.partial(split_kernel, sharing, rows, span),
        in_specs=[hbm] * 4,
        out_specs=[hbm] * n,
        out_shape=[jax.ShapeDtypeStruct((4, rows, LANES), jnp.bfloat16)] * n,
        scratch_shapes=[
            pltpu.VMEM((n, 4, rows, LANES), jnp.bfloat16),
            pltpu.SemaphoreType.DMA((n, 4)),
            pltpu.SemaphoreType.DMA((n,)),
        ],
        compiler_params=pltpu.CompilerParams(vmem_limit_bytes=60 * 2**20),
        name="pack",
    )(*arrays)


def far_first(n):
    return [*reversed(range(n // 2, n)), *range(n // 2)]


def listed(n):
    return [*range(n // 2, n), *range(n // 2)]


def swap(block, axis, pairs):
    return lax.ppermute(block, axis, [(i, j) for i, j in pairs] + [(j, i) for i, j in pairs])


def exchange(blocks):
    n = len(blocks)
    moved = list(blocks)
    for step in reversed(range(1, n)):
        pairs = [[i, i ^ step] for i in range(n) if i < i ^ step]
        moved[step] = swap(blocks[step], "seq", pairs)
    return moved


def sides_kernel(n, *refs):
    ins, outs = refs[:n], refs[n:]
    is_odd = lax.axis_index("grp") & 1
    for step, ref in enumerate(ins):
        frame = lax.axis_index("seq") ^ step
        for start, out in zip((1, 0), outs):
            at = frame - jnp.where(is_odd == start, 1, 0)

            @pl.when((at >= 0) & (at < n - 1))
            def _():
                out[jnp.clip(at, 0, n - 2)] = ref[...]


def sides(blocks):
    n = len(blocks)
    shape = jax.ShapeDtypeStruct((n - 1, *blocks[0].shape), jnp.bfloat16)
    vmem = pl.BlockSpec(memory_space=pltpu.VMEM)
    return pl.pallas_call(
        functools.partial(sides_kernel, n),
        in_specs=[vmem] * n,
        out_specs=[vmem] * 2,
        out_shape=[shape] * 2,
        compiler_params=pltpu.CompilerParams(vmem_limit_bytes=24 * 2**20),
        name="sides",
    )(*blocks)


def gated(values, *earlier):
    return lax.optimization_barrier((values, *earlier))


def neighbours(block, start):
    count = lax.axis_size("grp")
    return swap(block, "grp", [(i, (i + 1) % count) for i in range(start, count, 2)])


def join_kernel(sharing, span, *refs):
    outs, sent = refs[-4:-1], refs[-1]
    rows = refs[0].shape[1]
    n = sent.shape[0]
    copies = []
    for at, step in enumerate(far_first(n)):
        row, tokens = part_of(lax.axis_index("seq") ^ step, sharing, rows)
        for i, out in enumerate(outs):
            given = out.at[0, pl.ds(span.start + row, rows), tokens]
            copies.append(pltpu.make_async_copy(refs[at].at[i], given, sent.at[step, i]))
            copies[-1].start()
    for copy in copies:
        copy.wait()


def join(blocks, span, tokens, sharing, earlier):
    n = len(blocks)
    shape = jax.ShapeDtypeStruct((1, WIDTH, tokens), jnp.bfloat16)
    hbm = pl.BlockSpec(memory_space=pltpu.HBM)
    earlier = [] if earlier is None else list(earlier)
    return pl.pallas_call(
        functools.partial(join_kernel, sharing, span),
        in_specs=[pl.BlockSpec(memory_space=pltpu.VMEM)] * n + [hbm] * len(earlier),
        out_specs=[hbm] * 3,
        out_shape=[shape] * 3,
        scratch_shapes=[pltpu.SemaphoreType.DMA((n, 3))],
        input_output_aliases={n + i: i for i in range(len(earlier))},
        compiler_params=pltpu.CompilerParams(vmem_limit_bytes=24 * 2**20),
        name="unpack",
    )(*(blocks[step] for step in far_first(n)), *earlier)


def clip_kernel(window, heads, given_bounds, *refs):
    own, sides_of = refs[:window], refs[window : window + 2]
    outs, refs = refs[window + 2 : 2 * window + 2], refs[2 * window + 2 :]
    wide, score_ref, grad_ref, weight_ref, found, bounds, arrived = refs
    copy = pltpu.make_async_copy(given_bounds, bounds, arrived)
    copy.start()
    halo = window - 1
    extent = window + 2 * halo
    queries, keys, values, cotangent = range(4)

    def widen(ref, frame):
        for i in range(4):
            wide[i, frame] = ref[i].astype(jnp.float32)

    for step, ref in zip(listed(window), own):
        widen(ref, halo + (lax.axis_index("seq") ^ step))
    for start, ref in zip((1, 0), sides_of):
        is_next = (lax.axis_index("grp") & 1) == start
        for at in range(halo):
            widen(ref.at[at], at + jnp.where(is_next, halo + window, 0))
    copy.wait()
    lowest, highest = bounds[0, halo], bounds[1, halo + window - 1]

    def partners(frame):
        first, last = bounds[0, frame], bounds[1, frame]
        return first, last - first, [jnp.minimum(first + t, last - 1) for t in range(window)]

    def products(frame, carry):
        first, count, others = partners(frame)
        scores, grads = [[] for _ in others], [[] for _ in others]
        for head in range(heads):
            span = slice(head * HDIM, (head + 1) * HDIM)
            query, cot = wide[queries, frame, span, :], wide[cotangent, frame, span, :]
            for t, other in enumerate(others):
                score = jnp.sum(query * wide[keys, other, span, :], axis=0, keepdims=True)
                grad = jnp.sum(cot * wide[values, other, span, :], axis=0, keepdims=True)
                scores[t].append(score)
                grads[t].append(grad)
        for t in range(window):
            bias = jnp.where(t < count, 0.0, masked_score)
            score_ref[t, frame] = jnp.concatenate(scores[t], axis=0) * SCALING + bias
            grad_ref[t, frame] = jnp.concatenate(grads[t], axis=0)
        return carry

    lax.fori_loop(lowest, highest, products, 0)
    scores, grads = [score_ref[t] for t in range(window)], [grad_ref[t] for t in range(window)]
    peak = functools.reduce(jnp.maximum, scores)
    raised = [jnp.exp(score - peak) for score in scores]
    inverse = 1.0 / functools.reduce(jnp.add, raised)
    weights = [part * inverse for part in raised]
    weights_low = [rounded(part) for part in weights]
    dots = functools.reduce(jnp.add, [w * d for w, d in zip(weights_low, grads)])
    for t in range(window):
        weight_ref[t] = weights_low[t]
        score_ref[t] = rounded(weights[t] * (grads[t] - dots))

    def gradients(at, carry):
        frame = halo + at
        first, count, others = partners(frame)
        place = frame - first
        sums = [[], [], []]
        for head in range(heads):
            span, row = slice(head * HDIM, (head + 1) * HDIM), slice(head, head + 1)
            totals = [None] * 3
            for t, other in enumerate(others):
                score_back = jnp.where(t < count, score_ref[place, other, row, :], 0.0)
                weight_back = jnp.where(t < count, weight_ref[place, other, row, :], 0.0)
                terms = (
                    score_ref[t, frame, row, :] * wide[keys, other, span, :],
                    score_back * wide[queries, other, span, :],
                    weight_back * wide[cotangent, other, span, :],
                )
                totals = [x if y is None else y + x for x, y in zip(terms, totals)]
            for held, total, scale in zip(sums, totals, (SCALING, SCALING, None)):
                held.append(total if scale is None else total * scale)
        for i, parts in enumerate(sums):
            found[at, i] = jnp.concatenate(parts, axis=0).astype(jnp.bfloat16)
        return carry

    lax.fori_loop(0, window, gradients, 0)
    for step, out in enumerate(outs):
        out[...] = found[lax.axis_index("seq") ^ step]


def clip_grads(bounds, own, beside):
    window = len(own)
    _, rows, lanes = own[0].shape
    heads = rows // HDIM
    extent = 3 * window - 2
    vmem = pl.BlockSpec(memory_space=pltpu.VMEM)
    shape = (3, rows, lanes)
    slots = pltpu.VMEM((window, extent, heads, lanes), jnp.float32)
    return pl.pallas_call(
        functools.partial(clip_kernel, window, heads),
        out_shape=[jax.ShapeDtypeStruct(shape, jnp.bfloat16)] * window,
        in_specs=[pl.BlockSpec(memory_space=pl.ANY)] + [vmem] * (window + 2),
        out_specs=[vmem] * window,
        scratch_shapes=[
            pltpu.VMEM((4, extent, rows, lanes), jnp.float32),
            slots,
            slots,
            slots,
            pltpu.VMEM((window, *shape), jnp.bfloat16),
            pltpu.SMEM(bounds.shape, jnp.int32),
            pltpu.SemaphoreType.DMA,
        ],
        compiler_params=pltpu.CompilerParams(vmem_limit_bytes=48 * 2**20),
        cost_estimate=pl.CostEstimate(
            flops=800 * extent * window * rows * lanes,
            bytes_accessed=2 * sum(block.size for block in (*own, *beside)),
            transcendentals=extent * window * heads * lanes,
        ),
        name="clips",
    )(bounds, *(own[step] for step in listed(window)), *beside)


def clip_bounds(clip_len, window):
    halo = window - 1
    extent = window + 2 * halo
    start = lax.axis_index("grp") * window - halo
    frames = start + jnp.arange(extent, dtype=jnp.int32)
    order = jnp.arange(clip_len.shape[0])
    ends = jnp.sum(jnp.where(order[:, None] <= order[None, :], clip_len[:, None], 0), axis=0)
    begins = ends - clip_len
    holds = (begins[None, :] <= frames[:, None]) & (frames[:, None] < ends[None, :])
    first = jnp.sum(jnp.where(holds, begins[None, :], 0), axis=1) - start
    last = jnp.sum(jnp.where(holds, ends[None, :], 0), axis=1) - start
    return jnp.stack([first, last]).astype(jnp.int32)


def tile_shards(q_space, k_space, v_space, cot_space, q_time, k_time, v_time, cot_time, clip_len):
    def turned(*arrays):
        return tuple(array.transpose(0, 2, 1) for array in arrays)

    n = lax.axis_size("seq")
    window = q_time.shape[0] * n
    tokens = q_time.shape[1]
    sharing = n * LANES // tokens
    bounds = clip_bounds(clip_len, window)
    time = turned(q_time, k_time, v_time, cot_time)
    spans = []
    head = 0
    for heads in CHUNKS:
        spans.append(slice(head * HDIM, (head + heads) * HDIM))
        head += heads
    space_in = turned(q_space, k_space, v_space, cot_space)
    packed = [list(split(time, span, n, sharing)) for span in spans]
    own = [exchange(packed[0])]
    space = space_grads(*space_in)
    packed[1][1:], own[0][2], space = gated(packed[1][1:], own[0][2], space)
    own.append(exchange(packed[1]))
    beside = [
        [neighbours(ends, start) for ends, start in zip(sides(blocks), (1, 0))] for blocks in own
    ]
    back, grads = [], None
    for blocks, near in zip(own, beside):
        back.append(exchange(clip_grads(bounds, blocks, near)))
    for span, blocks in zip(spans, back):
        grads = join(blocks, span, tokens, sharing, grads)
    return turned(*space, *grads)


def whole_tiles(mesh, tokens):
    n = mesh.shape["seq"]
    sharing = n * LANES // tokens
    return (
        tokens % LANES == 0
        and n % 4 == 0
        and n & (n - 1) == 0
        and mesh.shape["grp"] % 2 == 0
        and mesh.shape["grp"] > 2
        and sharing * tokens == n * LANES
        and all(heads % sharing == 0 and heads // sharing * HDIM % 16 == 0 for heads in CHUNKS)
    )


def padded(block, sides, width):
    for axis, dim in sides:
        count = lax.axis_size(axis)
        forward = [(i, i + 1) for i in range(count - 1)]
        backward = [(target, source) for source, target in forward]
        low = lax.ppermute(
            lax.slice_in_dim(block, block.shape[dim] - width, None, axis=dim), axis, forward
        )
        high = lax.ppermute(lax.slice_in_dim(block, 0, width, axis=dim), axis, backward)
        block = jnp.concatenate([low, block, high], axis=dim)
    return block


def shifted(value, axis, by):
    count = lax.axis_size(axis)
    pairs = [(i, i + by) for i in range(count) if 0 <= i + by < count]
    return lax.ppermute(value, axis, pairs)


def clip_labels(clip_len, first_frame, count, frame_total):
    frame_ids = first_frame + jnp.arange(count, dtype=jnp.int32)
    clip_ends = jnp.cumsum(clip_len)
    labels = jnp.sum((clip_ends[None, :] <= frame_ids[:, None]).astype(jnp.int32), axis=1)
    inside = (frame_ids >= 0) & (frame_ids < frame_total)
    return (labels, inside)


def frame_grads(queries, keys, values, cotangent):
    scaling = 1.0 / math.sqrt(HDIM)
    tokens = queries.shape[0]
    q_heads = queries.reshape(tokens, HEADS, HDIM)
    k_heads = keys.reshape(tokens, HEADS, HDIM)
    v_heads = values.reshape(tokens, HEADS, HDIM)
    g_heads = cotangent.reshape(tokens, HEADS, HDIM)
    scores = (
        jnp.einsum("qhd,khd->hqk", q_heads, k_heads, preferred_element_type=jnp.float32) * scaling
    )
    row_max = jnp.max(scores, axis=-1, keepdims=True)
    log_total = row_max + jnp.log(jnp.sum(jnp.exp(scores - row_max), axis=-1, keepdims=True))
    weights = jnp.exp(scores - log_total)
    weights_low = weights.astype(jnp.bfloat16)
    attended = jnp.einsum("hqk,khd->qhd", weights_low, v_heads, preferred_element_type=jnp.float32)
    row_dot = jnp.einsum("qhd,qhd->hq", g_heads.astype(jnp.float32), attended)
    weight_grad = jnp.einsum("qhd,khd->hqk", g_heads, v_heads, preferred_element_type=jnp.float32)
    score_grad = (weights * (weight_grad - row_dot[:, :, None])).astype(jnp.bfloat16)
    grad_query = (
        jnp.einsum("hqk,khd->qhd", score_grad, k_heads, preferred_element_type=jnp.float32)
        * scaling
    )
    grad_key = (
        jnp.einsum("hqk,qhd->khd", score_grad, q_heads, preferred_element_type=jnp.float32)
        * scaling
    )
    grad_value = jnp.einsum(
        "hqk,qhd->khd", weights_low, g_heads, preferred_element_type=jnp.float32
    )
    flat_shape = (1, tokens, HEADS * HDIM)
    return (
        grad_query.reshape(flat_shape).astype(jnp.bfloat16),
        grad_key.reshape(flat_shape).astype(jnp.bfloat16),
        grad_value.reshape(flat_shape).astype(jnp.bfloat16),
    )


def shards(q_space, k_space, v_space, cot_space, q_time, k_time, v_time, cot_time, clip_len):
    scaling = 1.0 / math.sqrt(HDIM)
    grad_qs, grad_ks, grad_vs = frame_grads(q_space[0], k_space[0], v_space[0], cot_space[0])
    moved = (
        lax.all_to_all(q_time, "seq", split_axis=1, concat_axis=0, tiled=True),
        lax.all_to_all(k_time, "seq", split_axis=1, concat_axis=0, tiled=True),
        lax.all_to_all(v_time, "seq", split_axis=1, concat_axis=0, tiled=True),
        lax.all_to_all(cot_time, "seq", split_axis=1, concat_axis=0, tiled=True),
    )
    query_win, key_win, value_win, cot_win = moved
    window = query_win.shape[0]
    places = query_win.shape[1]
    channels = query_win.shape[2]
    group_id = lax.axis_index("grp")
    frame_total = window * lax.axis_size("grp")
    first_frame = group_id * window

    def split_heads(array):
        return array.reshape(array.shape[0], places, HEADS, HDIM)

    key_pair = padded(jnp.stack([key_win, value_win]), (("grp", 1),), window)
    q_own = split_heads(query_win)
    g_own = split_heads(cot_win)
    k_ext = split_heads(key_pair[0])
    v_ext = split_heads(key_pair[1])
    own_label, own_inside = clip_labels(clip_len, first_frame, window, frame_total)
    ext_label, ext_inside = clip_labels(clip_len, first_frame - window, 3 * window, frame_total)
    allowed = (own_label[:, None] == ext_label[None, :]) & ext_inside[None, :]
    scores = (
        jnp.einsum("iphd,jphd->phij", q_own, k_ext, preferred_element_type=jnp.float32) * scaling
    )
    scores = jnp.where(allowed, scores, masked_score)
    row_max = jnp.max(scores, axis=-1)
    log_total = row_max + jnp.log(jnp.sum(jnp.exp(scores - row_max[..., None]), axis=-1))
    weights = jnp.where(allowed, jnp.exp(scores - log_total[..., None]), 0.0)
    weights_low = weights.astype(jnp.bfloat16)
    attended = jnp.einsum("phij,jphd->iphd", weights_low, v_ext, preferred_element_type=jnp.float32)
    row_dot = jnp.einsum("iphd,iphd->phi", g_own.astype(jnp.float32), attended)
    weight_grad = jnp.einsum("iphd,jphd->phij", g_own, v_ext, preferred_element_type=jnp.float32)
    score_grad = (weights * (weight_grad - row_dot[..., None])).astype(jnp.bfloat16)
    grad_query = (
        jnp.einsum("phij,jphd->iphd", score_grad, k_ext, preferred_element_type=jnp.float32)
        * scaling
    )
    key_terms = (
        jnp.einsum("phij,iphd->jphd", score_grad, q_own, preferred_element_type=jnp.float32)
        * scaling
    )
    value_terms = jnp.einsum(
        "phij,iphd->jphd", weights_low, g_own, preferred_element_type=jnp.float32
    )
    both_terms = jnp.stack([key_terms, value_terms]).reshape(2, 3 * window, places, channels)
    from_after = shifted(both_terms[:, :window], "grp", -1)
    from_before = shifted(both_terms[:, 2 * window :], "grp", 1)
    summed = both_terms[:, window : 2 * window] + from_after + from_before
    grad_key = summed[0]
    grad_value = summed[1]
    grad_qt, grad_kt, grad_vt = (
        lax.all_to_all(
            grad_query.reshape(window, places, channels).astype(jnp.bfloat16),
            "seq",
            split_axis=0,
            concat_axis=1,
            tiled=True,
        ),
        lax.all_to_all(
            grad_key.astype(jnp.bfloat16), "seq", split_axis=0, concat_axis=1, tiled=True
        ),
        lax.all_to_all(
            grad_value.astype(jnp.bfloat16), "seq", split_axis=0, concat_axis=1, tiled=True
        ),
    )
    return (grad_qs, grad_ks, grad_vs, grad_qt, grad_kt, grad_vt)


def solution(mesh):
    split_spec = P(("grp", "seq"), None, None)

    def mapped(body):
        return jax.shard_map(
            body,
            mesh=mesh,
            in_specs=(split_spec,) * 8 + (P(),),
            out_specs=(split_spec,) * 6,
            check_vma=False,
        )

    def grads(*arrays):
        return mapped(tile_shards if whole_tiles(mesh, arrays[0].shape[1]) else shards)(*arrays)

    return grads
```

```python
import functools
import math

import jax
import jax.numpy as jnp
from jax import lax
from jax.experimental import pallas as pl
from jax.experimental.pallas import tpu as pltpu
from jax.sharding import PartitionSpec as P

HEADS = 8
HDIM = 72
WIDTH = HEADS * HDIM
LANES = 128
SCALING = 1.0 / math.sqrt(HDIM)
CHUNKS = (4, 4)
masked_score = -1e30


def dot(left, right, left_dim, right_dim):
    dims = (((left_dim,), (right_dim,)), ((), ()))
    return lax.dot_general(left, right, dims, preferred_element_type=jnp.float32)


def rounded(value):
    return value.astype(jnp.bfloat16).astype(jnp.float32)


def frame_kernel(q_ref, k_ref, v_ref, g_ref, dq_ref, dk_ref, dv_ref):
    pair = 2 * HDIM
    reach = -(-HDIM // 16) * 16
    row = lax.broadcasted_iota(jnp.int32, (reach, 1), 0)
    for begin in range(0, WIDTH, pair):
        found = [[], [], []]
        for low, own in ((0, 0), (pair - reach, reach - HDIM)):
            span = slice(begin + low, begin + low + reach)
            mask = ((row >= own) & (row < own + HDIM)).astype(jnp.float32).astype(jnp.bfloat16)
            queries, keys = q_ref[0, span, :], k_ref[0, span, :]
            cotangent = g_ref[0, span, :]
            scores = dot(keys * mask, queries, 0, 0) * SCALING
            weight_grad = dot(v_ref[0, span, :] * mask, cotangent, 0, 0)
            raised = jnp.exp(scores - jnp.max(scores, axis=0, keepdims=True))
            weights = raised * (1.0 / jnp.sum(raised, axis=0, keepdims=True))
            weights_low = weights.astype(jnp.bfloat16)
            dots = jnp.sum(weights_low.astype(jnp.float32) * weight_grad, axis=0, keepdims=True)
            score_grad = (weights * (weight_grad - dots)).astype(jnp.bfloat16)
            rows = slice(own, own + HDIM)
            found[0].append(dot(keys, score_grad, 1, 0)[rows] * SCALING)
            found[1].append(dot(queries, score_grad, 1, 1)[rows] * SCALING)
            found[2].append(dot(cotangent, weights_low, 1, 1)[rows])
        for out, parts in zip((dq_ref, dk_ref, dv_ref), found):
            out[0, begin : begin + pair, :] = jnp.concatenate(parts, axis=0).astype(jnp.bfloat16)


def space_grads(queries, keys, values, cotangent):
    tokens = queries.shape[2]
    shape = jax.ShapeDtypeStruct(queries.shape, jnp.bfloat16)
    return pl.pallas_call(
        frame_kernel,
        out_shape=(shape, shape, shape),
        compiler_params=pltpu.CompilerParams(vmem_limit_bytes=60 * 2**20),
        cost_estimate=pl.CostEstimate(
            flops=12 * tokens * tokens * 256 * HEADS,
            bytes_accessed=14 * tokens * WIDTH,
            transcendentals=tokens * tokens * HEADS,
        ),
        name="space",
    )(queries, keys, values, cotangent)


def part_of(device, sharing, rows):
    row = pl.multiple_of(device % sharing * rows, 16)
    return row, pl.ds(pl.multiple_of(device // sharing * LANES, LANES), LANES)


def split_kernel(sharing, rows, span, *refs):
    ins, outs, (held, arrived, sent) = refs[:4], refs[4:-3], refs[-3:]
    loads, stores = {}, []
    for step in far_first(len(outs)):
        row, tokens = part_of(lax.axis_index("seq") ^ step, sharing, rows)
        for i, array in enumerate(ins):
            given = array.at[0, pl.ds(span.start + row, rows), tokens]
            loads[step, i] = pltpu.make_async_copy(given, held.at[step, i], arrived.at[step, i])
            loads[step, i].start()
    for step in far_first(len(outs)):
        for i in range(len(ins)):
            loads[step, i].wait()
        stores.append(pltpu.make_async_copy(held.at[step], outs[step], sent.at[step]))
        stores[-1].start()
    for copy in stores:
        copy.wait()


def split(arrays, span, n, sharing):
    rows = (span.stop - span.start) // sharing
    hbm = pl.BlockSpec(memory_space=pltpu.HBM)
    return pl.pallas_call(
        functools.partial(split_kernel, sharing, rows, span),
        in_specs=[hbm] * 4,
        out_specs=[hbm] * n,
        out_shape=[jax.ShapeDtypeStruct((4, rows, LANES), jnp.bfloat16)] * n,
        scratch_shapes=[
            pltpu.VMEM((n, 4, rows, LANES), jnp.bfloat16),
            pltpu.SemaphoreType.DMA((n, 4)),
            pltpu.SemaphoreType.DMA((n,)),
        ],
        compiler_params=pltpu.CompilerParams(vmem_limit_bytes=60 * 2**20),
        name="pack",
    )(*arrays)


def far_first(n):
    return [*reversed(range(n // 2, n)), *range(n // 2)]


def swap(block, axis, pairs):
    return lax.ppermute(block, axis, [(i, j) for i, j in pairs] + [(j, i) for i, j in pairs])


def exchange(blocks):
    n = len(blocks)
    moved = list(blocks)
    for step in reversed(range(1, n)):
        pairs = [[i, i ^ step] for i in range(n) if i < i ^ step]
        moved[step] = swap(blocks[step], "seq", pairs)
    return moved


def sides_kernel(n, *refs):
    ins, outs = refs[:n], refs[n:]
    is_odd = lax.axis_index("grp") & 1
    for step, ref in enumerate(ins):
        frame = lax.axis_index("seq") ^ step
        for start, out in zip((1, 0), outs):
            at = frame - jnp.where(is_odd == start, 1, 0)

            @pl.when((at >= 0) & (at < n - 1))
            def _():
                out[jnp.clip(at, 0, n - 2)] = ref[...]


def sides(blocks):
    n = len(blocks)
    shape = jax.ShapeDtypeStruct((n - 1, *blocks[0].shape), jnp.bfloat16)
    vmem = pl.BlockSpec(memory_space=pltpu.VMEM)
    return pl.pallas_call(
        functools.partial(sides_kernel, n),
        in_specs=[vmem] * n,
        out_specs=[vmem] * 2,
        out_shape=[shape] * 2,
        compiler_params=pltpu.CompilerParams(vmem_limit_bytes=24 * 2**20),
        name="sides",
    )(*blocks)


def gated(values, *earlier):
    return lax.optimization_barrier((values, *earlier))


def neighbours(block, start):
    count = lax.axis_size("grp")
    return swap(block, "grp", [(i, (i + 1) % count) for i in range(start, count, 2)])


def join_kernel(sharing, span, *refs):
    outs, sent = refs[-4:-1], refs[-1]
    rows = refs[0].shape[1]
    n = sent.shape[0]
    copies = []
    for at, step in enumerate(far_first(n)):
        row, tokens = part_of(lax.axis_index("seq") ^ step, sharing, rows)
        for i, out in enumerate(outs):
            given = out.at[0, pl.ds(span.start + row, rows), tokens]
            copies.append(pltpu.make_async_copy(refs[at].at[i], given, sent.at[step, i]))
            copies[-1].start()
    for copy in copies:
        copy.wait()


def join(blocks, span, tokens, sharing, earlier):
    n = len(blocks)
    shape = jax.ShapeDtypeStruct((1, WIDTH, tokens), jnp.bfloat16)
    hbm = pl.BlockSpec(memory_space=pltpu.HBM)
    earlier = [] if earlier is None else list(earlier)
    return pl.pallas_call(
        functools.partial(join_kernel, sharing, span),
        in_specs=[pl.BlockSpec(memory_space=pltpu.VMEM)] * n + [hbm] * len(earlier),
        out_specs=[hbm] * 3,
        out_shape=[shape] * 3,
        scratch_shapes=[pltpu.SemaphoreType.DMA((n, 3))],
        input_output_aliases={n + i: i for i in range(len(earlier))},
        compiler_params=pltpu.CompilerParams(vmem_limit_bytes=24 * 2**20),
        name="unpack",
    )(*(blocks[step] for step in far_first(n)), *earlier)


def clip_kernel(window, heads, given_bounds, *refs):
    own, sides_of = refs[:window], refs[window : window + 2]
    outs, refs = refs[window + 2 : 2 * window + 2], refs[2 * window + 2 :]
    wide, score_ref, grad_ref, weight_ref, found, bounds, arrived = refs
    copy = pltpu.make_async_copy(given_bounds, bounds, arrived)
    copy.start()
    halo = window - 1
    extent = window + 2 * halo
    queries, keys, values, cotangent = range(4)

    def widen(ref, frame):
        for i in range(4):
            wide[i, frame] = ref[i].astype(jnp.float32)

    for step, ref in enumerate(own):
        widen(ref, halo + (lax.axis_index("seq") ^ step))
    for start, ref in zip((1, 0), sides_of):
        is_next = (lax.axis_index("grp") & 1) == start
        for at in range(halo):
            widen(ref.at[at], at + jnp.where(is_next, halo + window, 0))
    copy.wait()
    lowest, highest = bounds[0, halo], bounds[1, halo + window - 1]

    def partners(frame):
        first, last = bounds[0, frame], bounds[1, frame]
        return first, last - first, [jnp.minimum(first + t, last - 1) for t in range(window)]

    def products(frame, carry):
        first, count, others = partners(frame)
        scores, grads = [[] for _ in others], [[] for _ in others]
        for head in range(heads):
            span = slice(head * HDIM, (head + 1) * HDIM)
            query, cot = wide[queries, frame, span, :], wide[cotangent, frame, span, :]
            for t, other in enumerate(others):
                score = jnp.sum(query * wide[keys, other, span, :], axis=0, keepdims=True)
                grad = jnp.sum(cot * wide[values, other, span, :], axis=0, keepdims=True)
                scores[t].append(score)
                grads[t].append(grad)
        for t in range(window):
            bias = jnp.where(t < count, 0.0, masked_score)
            score_ref[t, frame] = jnp.concatenate(scores[t], axis=0) * SCALING + bias
            grad_ref[t, frame] = jnp.concatenate(grads[t], axis=0)
        return carry

    lax.fori_loop(lowest, highest, products, 0)
    scores, grads = [score_ref[t] for t in range(window)], [grad_ref[t] for t in range(window)]
    peak = functools.reduce(jnp.maximum, scores)
    raised = [jnp.exp(score - peak) for score in scores]
    inverse = 1.0 / functools.reduce(jnp.add, raised)
    weights = [part * inverse for part in raised]
    weights_low = [rounded(part) for part in weights]
    dots = functools.reduce(jnp.add, [w * d for w, d in zip(weights_low, grads)])
    for t in range(window):
        weight_ref[t] = weights_low[t]
        score_ref[t] = rounded(weights[t] * (grads[t] - dots))

    def gradients(at, carry):
        frame = halo + at
        first, count, others = partners(frame)
        place = frame - first
        sums = [[], [], []]
        for head in range(heads):
            span, row = slice(head * HDIM, (head + 1) * HDIM), slice(head, head + 1)
            totals = [None] * 3
            for t, other in enumerate(others):
                score_back = jnp.where(t < count, score_ref[place, other, row, :], 0.0)
                weight_back = jnp.where(t < count, weight_ref[place, other, row, :], 0.0)
                terms = (
                    score_ref[t, frame, row, :] * wide[keys, other, span, :],
                    score_back * wide[queries, other, span, :],
                    weight_back * wide[cotangent, other, span, :],
                )
                totals = [x if y is None else y + x for x, y in zip(terms, totals)]
            for held, total, scale in zip(sums, totals, (SCALING, SCALING, None)):
                held.append(total if scale is None else total * scale)
        for i, parts in enumerate(sums):
            found[at, i] = jnp.concatenate(parts, axis=0).astype(jnp.bfloat16)
        return carry

    lax.fori_loop(0, window, gradients, 0)
    for step, out in enumerate(outs):
        out[...] = found[lax.axis_index("seq") ^ step]


def clip_grads(bounds, own, beside):
    window = len(own)
    _, rows, lanes = own[0].shape
    heads = rows // HDIM
    extent = 3 * window - 2
    vmem = pl.BlockSpec(memory_space=pltpu.VMEM)
    shape = (3, rows, lanes)
    slots = pltpu.VMEM((window, extent, heads, lanes), jnp.float32)
    return pl.pallas_call(
        functools.partial(clip_kernel, window, heads),
        out_shape=[jax.ShapeDtypeStruct(shape, jnp.bfloat16)] * window,
        in_specs=[pl.BlockSpec(memory_space=pl.ANY)] + [vmem] * (window + 2),
        out_specs=[vmem] * window,
        scratch_shapes=[
            pltpu.VMEM((4, extent, rows, lanes), jnp.float32),
            slots,
            slots,
            slots,
            pltpu.VMEM((window, *shape), jnp.bfloat16),
            pltpu.SMEM(bounds.shape, jnp.int32),
            pltpu.SemaphoreType.DMA,
        ],
        compiler_params=pltpu.CompilerParams(vmem_limit_bytes=48 * 2**20),
        cost_estimate=pl.CostEstimate(
            flops=800 * extent * window * rows * lanes,
            bytes_accessed=2 * sum(block.size for block in (*own, *beside)),
            transcendentals=extent * window * heads * lanes,
        ),
        name="clips",
    )(bounds, *own, *beside)


def clip_bounds(clip_len, window):
    halo = window - 1
    extent = window + 2 * halo
    start = lax.axis_index("grp") * window - halo
    frames = start + jnp.arange(extent, dtype=jnp.int32)
    order = jnp.arange(clip_len.shape[0])
    ends = jnp.sum(jnp.where(order[:, None] <= order[None, :], clip_len[:, None], 0), axis=0)
    begins = ends - clip_len
    holds = (begins[None, :] <= frames[:, None]) & (frames[:, None] < ends[None, :])
    first = jnp.sum(jnp.where(holds, begins[None, :], 0), axis=1) - start
    last = jnp.sum(jnp.where(holds, ends[None, :], 0), axis=1) - start
    return jnp.stack([first, last]).astype(jnp.int32)


def tile_shards(q_space, k_space, v_space, cot_space, q_time, k_time, v_time, cot_time, clip_len):
    def turned(*arrays):
        return tuple(array.transpose(0, 2, 1) for array in arrays)

    n = lax.axis_size("seq")
    window = q_time.shape[0] * n
    tokens = q_time.shape[1]
    sharing = n * LANES // tokens
    bounds = clip_bounds(clip_len, window)
    time = turned(q_time, k_time, v_time, cot_time)
    spans = []
    head = 0
    for heads in CHUNKS:
        spans.append(slice(head * HDIM, (head + heads) * HDIM))
        head += heads
    space_in = turned(q_space, k_space, v_space, cot_space)
    packed = [split(time, span, n, sharing) for span in spans]
    own = [exchange(blocks) for blocks in packed]
    space = space_grads(*space_in)
    beside = [
        [neighbours(ends, start) for ends, start in zip(sides(blocks), (1, 0))] for blocks in own
    ]
    back, grads = [], None
    for blocks, near in zip(own, beside):
        back.append(exchange(clip_grads(bounds, blocks, near)))
    for span, blocks in zip(spans, back):
        grads = join(blocks, span, tokens, sharing, grads)
    return turned(*space, *grads)


def whole_tiles(mesh, tokens):
    n = mesh.shape["seq"]
    sharing = n * LANES // tokens
    return (
        tokens % LANES == 0
        and n % 4 == 0
        and n & (n - 1) == 0
        and mesh.shape["grp"] % 2 == 0
        and mesh.shape["grp"] > 2
        and sharing * tokens == n * LANES
        and all(heads % sharing == 0 and heads // sharing * HDIM % 16 == 0 for heads in CHUNKS)
    )


def padded(block, sides, width):
    for axis, dim in sides:
        count = lax.axis_size(axis)
        forward = [(i, i + 1) for i in range(count - 1)]
        backward = [(target, source) for source, target in forward]
        low = lax.ppermute(
            lax.slice_in_dim(block, block.shape[dim] - width, None, axis=dim), axis, forward
        )
        high = lax.ppermute(lax.slice_in_dim(block, 0, width, axis=dim), axis, backward)
        block = jnp.concatenate([low, block, high], axis=dim)
    return block


def shifted(value, axis, by):
    count = lax.axis_size(axis)
    pairs = [(i, i + by) for i in range(count) if 0 <= i + by < count]
    return lax.ppermute(value, axis, pairs)


def clip_labels(clip_len, first_frame, count, frame_total):
    frame_ids = first_frame + jnp.arange(count, dtype=jnp.int32)
    clip_ends = jnp.cumsum(clip_len)
    labels = jnp.sum((clip_ends[None, :] <= frame_ids[:, None]).astype(jnp.int32), axis=1)
    inside = (frame_ids >= 0) & (frame_ids < frame_total)
    return (labels, inside)


def frame_grads(queries, keys, values, cotangent):
    scaling = 1.0 / math.sqrt(HDIM)
    tokens = queries.shape[0]
    q_heads = queries.reshape(tokens, HEADS, HDIM)
    k_heads = keys.reshape(tokens, HEADS, HDIM)
    v_heads = values.reshape(tokens, HEADS, HDIM)
    g_heads = cotangent.reshape(tokens, HEADS, HDIM)
    scores = (
        jnp.einsum("qhd,khd->hqk", q_heads, k_heads, preferred_element_type=jnp.float32) * scaling
    )
    row_max = jnp.max(scores, axis=-1, keepdims=True)
    log_total = row_max + jnp.log(jnp.sum(jnp.exp(scores - row_max), axis=-1, keepdims=True))
    weights = jnp.exp(scores - log_total)
    weights_low = weights.astype(jnp.bfloat16)
    attended = jnp.einsum("hqk,khd->qhd", weights_low, v_heads, preferred_element_type=jnp.float32)
    row_dot = jnp.einsum("qhd,qhd->hq", g_heads.astype(jnp.float32), attended)
    weight_grad = jnp.einsum("qhd,khd->hqk", g_heads, v_heads, preferred_element_type=jnp.float32)
    score_grad = (weights * (weight_grad - row_dot[:, :, None])).astype(jnp.bfloat16)
    grad_query = (
        jnp.einsum("hqk,khd->qhd", score_grad, k_heads, preferred_element_type=jnp.float32)
        * scaling
    )
    grad_key = (
        jnp.einsum("hqk,qhd->khd", score_grad, q_heads, preferred_element_type=jnp.float32)
        * scaling
    )
    grad_value = jnp.einsum(
        "hqk,qhd->khd", weights_low, g_heads, preferred_element_type=jnp.float32
    )
    flat_shape = (1, tokens, HEADS * HDIM)
    return (
        grad_query.reshape(flat_shape).astype(jnp.bfloat16),
        grad_key.reshape(flat_shape).astype(jnp.bfloat16),
        grad_value.reshape(flat_shape).astype(jnp.bfloat16),
    )


def shards(q_space, k_space, v_space, cot_space, q_time, k_time, v_time, cot_time, clip_len):
    scaling = 1.0 / math.sqrt(HDIM)
    grad_qs, grad_ks, grad_vs = frame_grads(q_space[0], k_space[0], v_space[0], cot_space[0])
    moved = (
        lax.all_to_all(q_time, "seq", split_axis=1, concat_axis=0, tiled=True),
        lax.all_to_all(k_time, "seq", split_axis=1, concat_axis=0, tiled=True),
        lax.all_to_all(v_time, "seq", split_axis=1, concat_axis=0, tiled=True),
        lax.all_to_all(cot_time, "seq", split_axis=1, concat_axis=0, tiled=True),
    )
    query_win, key_win, value_win, cot_win = moved
    window = query_win.shape[0]
    places = query_win.shape[1]
    channels = query_win.shape[2]
    group_id = lax.axis_index("grp")
    frame_total = window * lax.axis_size("grp")
    first_frame = group_id * window

    def split_heads(array):
        return array.reshape(array.shape[0], places, HEADS, HDIM)

    key_pair = padded(jnp.stack([key_win, value_win]), (("grp", 1),), window)
    q_own = split_heads(query_win)
    g_own = split_heads(cot_win)
    k_ext = split_heads(key_pair[0])
    v_ext = split_heads(key_pair[1])
    own_label, own_inside = clip_labels(clip_len, first_frame, window, frame_total)
    ext_label, ext_inside = clip_labels(clip_len, first_frame - window, 3 * window, frame_total)
    allowed = (own_label[:, None] == ext_label[None, :]) & ext_inside[None, :]
    scores = (
        jnp.einsum("iphd,jphd->phij", q_own, k_ext, preferred_element_type=jnp.float32) * scaling
    )
    scores = jnp.where(allowed, scores, masked_score)
    row_max = jnp.max(scores, axis=-1)
    log_total = row_max + jnp.log(jnp.sum(jnp.exp(scores - row_max[..., None]), axis=-1))
    weights = jnp.where(allowed, jnp.exp(scores - log_total[..., None]), 0.0)
    weights_low = weights.astype(jnp.bfloat16)
    attended = jnp.einsum("phij,jphd->iphd", weights_low, v_ext, preferred_element_type=jnp.float32)
    row_dot = jnp.einsum("iphd,iphd->phi", g_own.astype(jnp.float32), attended)
    weight_grad = jnp.einsum("iphd,jphd->phij", g_own, v_ext, preferred_element_type=jnp.float32)
    score_grad = (weights * (weight_grad - row_dot[..., None])).astype(jnp.bfloat16)
    grad_query = (
        jnp.einsum("phij,jphd->iphd", score_grad, k_ext, preferred_element_type=jnp.float32)
        * scaling
    )
    key_terms = (
        jnp.einsum("phij,iphd->jphd", score_grad, q_own, preferred_element_type=jnp.float32)
        * scaling
    )
    value_terms = jnp.einsum(
        "phij,iphd->jphd", weights_low, g_own, preferred_element_type=jnp.float32
    )
    both_terms = jnp.stack([key_terms, value_terms]).reshape(2, 3 * window, places, channels)
    from_after = shifted(both_terms[:, :window], "grp", -1)
    from_before = shifted(both_terms[:, 2 * window :], "grp", 1)
    summed = both_terms[:, window : 2 * window] + from_after + from_before
    grad_key = summed[0]
    grad_value = summed[1]
    grad_qt, grad_kt, grad_vt = (
        lax.all_to_all(
            grad_query.reshape(window, places, channels).astype(jnp.bfloat16),
            "seq",
            split_axis=0,
            concat_axis=1,
            tiled=True,
        ),
        lax.all_to_all(
            grad_key.astype(jnp.bfloat16), "seq", split_axis=0, concat_axis=1, tiled=True
        ),
        lax.all_to_all(
            grad_value.astype(jnp.bfloat16), "seq", split_axis=0, concat_axis=1, tiled=True
        ),
    )
    return (grad_qs, grad_ks, grad_vs, grad_qt, grad_kt, grad_vt)


def solution(mesh):
    split_spec = P(("grp", "seq"), None, None)

    def mapped(body):
        return jax.shard_map(
            body,
            mesh=mesh,
            in_specs=(split_spec,) * 8 + (P(),),
            out_specs=(split_spec,) * 6,
            check_vma=False,
        )

    def grads(*arrays):
        return mapped(tile_shards if whole_tiles(mesh, arrays[0].shape[1]) else shards)(*arrays)

    return grads
```

```python
import functools
import math

import jax
import jax.numpy as jnp
from jax import lax
from jax.experimental import pallas as pl
from jax.experimental.pallas import tpu as pltpu
from jax.sharding import PartitionSpec as P

HEADS = 8
HDIM = 72
WIDTH = HEADS * HDIM
LANES = 128
SCALING = 1.0 / math.sqrt(HDIM)
CHUNKS = (4, 4)
masked_score = -1e30


def dot(left, right, left_dim, right_dim):
    dims = (((left_dim,), (right_dim,)), ((), ()))
    return lax.dot_general(left, right, dims, preferred_element_type=jnp.float32)


def rounded(value):
    return value.astype(jnp.bfloat16).astype(jnp.float32)


def frame_kernel(q_ref, k_ref, v_ref, g_ref, dq_ref, dk_ref, dv_ref):
    pair = 2 * HDIM
    reach = -(-HDIM // 16) * 16
    row = lax.broadcasted_iota(jnp.int32, (reach, 1), 0)
    for begin in range(0, WIDTH, pair):
        found = [[], [], []]
        for low, own in ((0, 0), (pair - reach, reach - HDIM)):
            span = slice(begin + low, begin + low + reach)
            mask = ((row >= own) & (row < own + HDIM)).astype(jnp.float32).astype(jnp.bfloat16)
            queries, keys = q_ref[0, span, :], k_ref[0, span, :]
            cotangent = g_ref[0, span, :]
            scores = dot(keys * mask, queries, 0, 0) * SCALING
            weight_grad = dot(v_ref[0, span, :] * mask, cotangent, 0, 0)
            raised = jnp.exp(scores - jnp.max(scores, axis=0, keepdims=True))
            weights = raised * (1.0 / jnp.sum(raised, axis=0, keepdims=True))
            weights_low = weights.astype(jnp.bfloat16)
            dots = jnp.sum(weights_low.astype(jnp.float32) * weight_grad, axis=0, keepdims=True)
            score_grad = (weights * (weight_grad - dots)).astype(jnp.bfloat16)
            rows = slice(own, own + HDIM)
            found[0].append(dot(keys, score_grad, 1, 0)[rows] * SCALING)
            found[1].append(dot(queries, score_grad, 1, 1)[rows] * SCALING)
            found[2].append(dot(cotangent, weights_low, 1, 1)[rows])
        for out, parts in zip((dq_ref, dk_ref, dv_ref), found):
            out[0, begin : begin + pair, :] = jnp.concatenate(parts, axis=0).astype(jnp.bfloat16)


def space_grads(queries, keys, values, cotangent):
    tokens = queries.shape[2]
    shape = jax.ShapeDtypeStruct(queries.shape, jnp.bfloat16)
    return pl.pallas_call(
        frame_kernel,
        out_shape=(shape, shape, shape),
        compiler_params=pltpu.CompilerParams(vmem_limit_bytes=60 * 2**20),
        cost_estimate=pl.CostEstimate(
            flops=12 * tokens * tokens * 256 * HEADS,
            bytes_accessed=14 * tokens * WIDTH,
            transcendentals=tokens * tokens * HEADS,
        ),
        name="space",
    )(queries, keys, values, cotangent)


def part_of(device, sharing, rows):
    row = pl.multiple_of(device % sharing * rows, 16)
    return row, pl.ds(pl.multiple_of(device // sharing * LANES, LANES), LANES)


def split_kernel(sharing, rows, span, *refs):
    ins, outs, (held, arrived, sent) = refs[:4], refs[4:-3], refs[-3:]
    loads, stores = {}, []
    for step in far_first(len(outs)):
        row, tokens = part_of(lax.axis_index("seq") ^ step, sharing, rows)
        for i, array in enumerate(ins):
            given = array.at[0, pl.ds(span.start + row, rows), tokens]
            loads[step, i] = pltpu.make_async_copy(given, held.at[step, i], arrived.at[step, i])
            loads[step, i].start()
    for step in far_first(len(outs)):
        for i in range(len(ins)):
            loads[step, i].wait()
        stores.append(pltpu.make_async_copy(held.at[step], outs[step], sent.at[step]))
        stores[-1].start()
    for copy in stores:
        copy.wait()


def split(arrays, span, n, sharing):
    rows = (span.stop - span.start) // sharing
    hbm = pl.BlockSpec(memory_space=pltpu.HBM)
    return pl.pallas_call(
        functools.partial(split_kernel, sharing, rows, span),
        in_specs=[hbm] * 4,
        out_specs=[hbm] * n,
        out_shape=[jax.ShapeDtypeStruct((4, rows, LANES), jnp.bfloat16)] * n,
        scratch_shapes=[
            pltpu.VMEM((n, 4, rows, LANES), jnp.bfloat16),
            pltpu.SemaphoreType.DMA((n, 4)),
            pltpu.SemaphoreType.DMA((n,)),
        ],
        compiler_params=pltpu.CompilerParams(vmem_limit_bytes=60 * 2**20),
        name="pack",
    )(*arrays)


def far_first(n):
    return [*reversed(range(n // 2, n)), *range(n // 2)]


def swap(block, axis, pairs):
    return lax.ppermute(block, axis, [(i, j) for i, j in pairs] + [(j, i) for i, j in pairs])


def exchange(blocks):
    n = len(blocks)
    moved = list(blocks)
    for step in reversed(range(1, n)):
        pairs = [[i, i ^ step] for i in range(n) if i < i ^ step]
        moved[step] = swap(blocks[step], "seq", pairs)
    return moved


def sides_kernel(n, *refs):
    ins, outs = refs[:n], refs[n:]
    is_odd = lax.axis_index("grp") & 1
    for step, ref in enumerate(ins):
        frame = lax.axis_index("seq") ^ step
        for start, out in zip((1, 0), outs):
            at = frame - jnp.where(is_odd == start, 1, 0)

            @pl.when((at >= 0) & (at < n - 1))
            def _():
                out[jnp.clip(at, 0, n - 2)] = ref[...]


def sides(blocks):
    n = len(blocks)
    shape = jax.ShapeDtypeStruct((n - 1, *blocks[0].shape), jnp.bfloat16)
    vmem = pl.BlockSpec(memory_space=pltpu.VMEM)
    return pl.pallas_call(
        functools.partial(sides_kernel, n),
        in_specs=[vmem] * n,
        out_specs=[vmem] * 2,
        out_shape=[shape] * 2,
        compiler_params=pltpu.CompilerParams(vmem_limit_bytes=24 * 2**20),
        name="sides",
    )(*blocks)


def gated(values, *earlier):
    return lax.optimization_barrier((values, *earlier))


def neighbours(block, start):
    count = lax.axis_size("grp")
    return swap(block, "grp", [(i, (i + 1) % count) for i in range(start, count, 2)])


def join_kernel(sharing, span, *refs):
    outs, sent = refs[-4:-1], refs[-1]
    rows = refs[0].shape[1]
    n = sent.shape[0]
    copies = []
    for at, step in enumerate(far_first(n)):
        row, tokens = part_of(lax.axis_index("seq") ^ step, sharing, rows)
        for i, out in enumerate(outs):
            given = out.at[0, pl.ds(span.start + row, rows), tokens]
            copies.append(pltpu.make_async_copy(refs[at].at[i], given, sent.at[step, i]))
            copies[-1].start()
    for copy in copies:
        copy.wait()


def join(blocks, span, tokens, sharing, earlier):
    n = len(blocks)
    shape = jax.ShapeDtypeStruct((1, WIDTH, tokens), jnp.bfloat16)
    hbm = pl.BlockSpec(memory_space=pltpu.HBM)
    earlier = [] if earlier is None else list(earlier)
    return pl.pallas_call(
        functools.partial(join_kernel, sharing, span),
        in_specs=[pl.BlockSpec(memory_space=pltpu.VMEM)] * n + [hbm] * len(earlier),
        out_specs=[hbm] * 3,
        out_shape=[shape] * 3,
        scratch_shapes=[pltpu.SemaphoreType.DMA((n, 3))],
        input_output_aliases={n + i: i for i in range(len(earlier))},
        compiler_params=pltpu.CompilerParams(vmem_limit_bytes=24 * 2**20),
        name="unpack",
    )(*(blocks[step] for step in far_first(n)), *earlier)


def clip_kernel(window, heads, given_bounds, *refs):
    own, sides_of = refs[:window], refs[window : window + 2]
    outs, refs = refs[window + 2 : 2 * window + 2], refs[2 * window + 2 :]
    wide, score_ref, grad_ref, weight_ref, found, bounds, arrived = refs
    copy = pltpu.make_async_copy(given_bounds, bounds, arrived)
    copy.start()
    halo = window - 1
    extent = window + 2 * halo
    queries, keys, values, cotangent = range(4)

    def widen(ref, frame):
        for i in range(4):
            wide[i, frame] = ref[i].astype(jnp.float32)

    for step, ref in enumerate(own):
        widen(ref, halo + (lax.axis_index("seq") ^ step))
    for start, ref in zip((1, 0), sides_of):
        is_next = (lax.axis_index("grp") & 1) == start
        for at in range(halo):
            widen(ref.at[at], at + jnp.where(is_next, halo + window, 0))
    copy.wait()
    lowest, highest = bounds[0, halo], bounds[1, halo + window - 1]

    def partners(frame):
        first, last = bounds[0, frame], bounds[1, frame]
        return first, last - first, [jnp.minimum(first + t, last - 1) for t in range(window)]

    def products(frame, carry):
        first, count, others = partners(frame)
        scores, grads = [[] for _ in others], [[] for _ in others]
        for head in range(heads):
            span = slice(head * HDIM, (head + 1) * HDIM)
            query, cot = wide[queries, frame, span, :], wide[cotangent, frame, span, :]
            for t, other in enumerate(others):
                score = jnp.sum(query * wide[keys, other, span, :], axis=0, keepdims=True)
                grad = jnp.sum(cot * wide[values, other, span, :], axis=0, keepdims=True)
                scores[t].append(score)
                grads[t].append(grad)
        for t in range(window):
            bias = jnp.where(t < count, 0.0, masked_score)
            score_ref[t, frame] = jnp.concatenate(scores[t], axis=0) * SCALING + bias
            grad_ref[t, frame] = jnp.concatenate(grads[t], axis=0)
        return carry

    lax.fori_loop(lowest, highest, products, 0)
    scores, grads = [score_ref[t] for t in range(window)], [grad_ref[t] for t in range(window)]
    peak = functools.reduce(jnp.maximum, scores)
    raised = [jnp.exp(score - peak) for score in scores]
    inverse = 1.0 / functools.reduce(jnp.add, raised)
    weights = [part * inverse for part in raised]
    weights_low = [rounded(part) for part in weights]
    dots = functools.reduce(jnp.add, [w * d for w, d in zip(weights_low, grads)])
    for t in range(window):
        weight_ref[t] = weights_low[t]
        score_ref[t] = rounded(weights[t] * (grads[t] - dots))

    def gradients(at, carry):
        frame = halo + at
        first, count, others = partners(frame)
        place = frame - first
        sums = [[], [], []]
        for head in range(heads):
            span, row = slice(head * HDIM, (head + 1) * HDIM), slice(head, head + 1)
            totals = [None] * 3
            for t, other in enumerate(others):
                score_back = jnp.where(t < count, score_ref[place, other, row, :], 0.0)
                weight_back = jnp.where(t < count, weight_ref[place, other, row, :], 0.0)
                terms = (
                    score_ref[t, frame, row, :] * wide[keys, other, span, :],
                    score_back * wide[queries, other, span, :],
                    weight_back * wide[cotangent, other, span, :],
                )
                totals = [x if y is None else y + x for x, y in zip(terms, totals)]
            for held, total, scale in zip(sums, totals, (SCALING, SCALING, None)):
                held.append(total if scale is None else total * scale)
        for i, parts in enumerate(sums):
            found[at, i] = jnp.concatenate(parts, axis=0).astype(jnp.bfloat16)
        return carry

    lax.fori_loop(0, window, gradients, 0, unroll=2)
    for step, out in enumerate(outs):
        out[...] = found[lax.axis_index("seq") ^ step]


def clip_grads(bounds, own, beside):
    window = len(own)
    _, rows, lanes = own[0].shape
    heads = rows // HDIM
    extent = 3 * window - 2
    vmem = pl.BlockSpec(memory_space=pltpu.VMEM)
    shape = (3, rows, lanes)
    slots = pltpu.VMEM((window, extent, heads, lanes), jnp.float32)
    return pl.pallas_call(
        functools.partial(clip_kernel, window, heads),
        out_shape=[jax.ShapeDtypeStruct(shape, jnp.bfloat16)] * window,
        in_specs=[pl.BlockSpec(memory_space=pl.ANY)] + [vmem] * (window + 2),
        out_specs=[vmem] * window,
        scratch_shapes=[
            pltpu.VMEM((4, extent, rows, lanes), jnp.float32),
            slots,
            slots,
            slots,
            pltpu.VMEM((window, *shape), jnp.bfloat16),
            pltpu.SMEM(bounds.shape, jnp.int32),
            pltpu.SemaphoreType.DMA,
        ],
        compiler_params=pltpu.CompilerParams(vmem_limit_bytes=48 * 2**20),
        cost_estimate=pl.CostEstimate(
            flops=800 * extent * window * rows * lanes,
            bytes_accessed=2 * sum(block.size for block in (*own, *beside)),
            transcendentals=extent * window * heads * lanes,
        ),
        name="clips",
    )(bounds, *own, *beside)


def clip_bounds(clip_len, window):
    halo = window - 1
    extent = window + 2 * halo
    start = lax.axis_index("grp") * window - halo
    frames = start + jnp.arange(extent, dtype=jnp.int32)
    order = jnp.arange(clip_len.shape[0])
    ends = jnp.sum(jnp.where(order[:, None] <= order[None, :], clip_len[:, None], 0), axis=0)
    begins = ends - clip_len
    holds = (begins[None, :] <= frames[:, None]) & (frames[:, None] < ends[None, :])
    first = jnp.sum(jnp.where(holds, begins[None, :], 0), axis=1) - start
    last = jnp.sum(jnp.where(holds, ends[None, :], 0), axis=1) - start
    return jnp.stack([first, last]).astype(jnp.int32)


def tile_shards(q_space, k_space, v_space, cot_space, q_time, k_time, v_time, cot_time, clip_len):
    def turned(*arrays):
        return tuple(array.transpose(0, 2, 1) for array in arrays)

    n = lax.axis_size("seq")
    window = q_time.shape[0] * n
    tokens = q_time.shape[1]
    sharing = n * LANES // tokens
    bounds = clip_bounds(clip_len, window)
    time = turned(q_time, k_time, v_time, cot_time)
    spans = []
    head = 0
    for heads in CHUNKS:
        spans.append(slice(head * HDIM, (head + heads) * HDIM))
        head += heads
    space_in = turned(q_space, k_space, v_space, cot_space)
    packed = [list(split(time, span, n, sharing)) for span in spans]
    own = [exchange(packed[0])]
    space = space_grads(*space_in)
    packed[1][2:], own[0][2], space = gated(packed[1][2:], own[0][2], space)
    own.append(exchange(packed[1]))
    beside = [
        [neighbours(ends, start) for ends, start in zip(sides(blocks), (1, 0))] for blocks in own
    ]
    back, grads = [], None
    for blocks, near in zip(own, beside):
        back.append(exchange(clip_grads(bounds, blocks, near)))
    for span, blocks in zip(spans, back):
        grads = join(blocks, span, tokens, sharing, grads)
    return turned(*space, *grads)


def whole_tiles(mesh, tokens):
    n = mesh.shape["seq"]
    sharing = n * LANES // tokens
    return (
        tokens % LANES == 0
        and n % 4 == 0
        and n & (n - 1) == 0
        and mesh.shape["grp"] % 2 == 0
        and mesh.shape["grp"] > 2
        and sharing * tokens == n * LANES
        and all(heads % sharing == 0 and heads // sharing * HDIM % 16 == 0 for heads in CHUNKS)
    )


def padded(block, sides, width):
    for axis, dim in sides:
        count = lax.axis_size(axis)
        forward = [(i, i + 1) for i in range(count - 1)]
        backward = [(target, source) for source, target in forward]
        low = lax.ppermute(
            lax.slice_in_dim(block, block.shape[dim] - width, None, axis=dim), axis, forward
        )
        high = lax.ppermute(lax.slice_in_dim(block, 0, width, axis=dim), axis, backward)
        block = jnp.concatenate([low, block, high], axis=dim)
    return block


def shifted(value, axis, by):
    count = lax.axis_size(axis)
    pairs = [(i, i + by) for i in range(count) if 0 <= i + by < count]
    return lax.ppermute(value, axis, pairs)


def clip_labels(clip_len, first_frame, count, frame_total):
    frame_ids = first_frame + jnp.arange(count, dtype=jnp.int32)
    clip_ends = jnp.cumsum(clip_len)
    labels = jnp.sum((clip_ends[None, :] <= frame_ids[:, None]).astype(jnp.int32), axis=1)
    inside = (frame_ids >= 0) & (frame_ids < frame_total)
    return (labels, inside)


def frame_grads(queries, keys, values, cotangent):
    scaling = 1.0 / math.sqrt(HDIM)
    tokens = queries.shape[0]
    q_heads = queries.reshape(tokens, HEADS, HDIM)
    k_heads = keys.reshape(tokens, HEADS, HDIM)
    v_heads = values.reshape(tokens, HEADS, HDIM)
    g_heads = cotangent.reshape(tokens, HEADS, HDIM)
    scores = (
        jnp.einsum("qhd,khd->hqk", q_heads, k_heads, preferred_element_type=jnp.float32) * scaling
    )
    row_max = jnp.max(scores, axis=-1, keepdims=True)
    log_total = row_max + jnp.log(jnp.sum(jnp.exp(scores - row_max), axis=-1, keepdims=True))
    weights = jnp.exp(scores - log_total)
    weights_low = weights.astype(jnp.bfloat16)
    attended = jnp.einsum("hqk,khd->qhd", weights_low, v_heads, preferred_element_type=jnp.float32)
    row_dot = jnp.einsum("qhd,qhd->hq", g_heads.astype(jnp.float32), attended)
    weight_grad = jnp.einsum("qhd,khd->hqk", g_heads, v_heads, preferred_element_type=jnp.float32)
    score_grad = (weights * (weight_grad - row_dot[:, :, None])).astype(jnp.bfloat16)
    grad_query = (
        jnp.einsum("hqk,khd->qhd", score_grad, k_heads, preferred_element_type=jnp.float32)
        * scaling
    )
    grad_key = (
        jnp.einsum("hqk,qhd->khd", score_grad, q_heads, preferred_element_type=jnp.float32)
        * scaling
    )
    grad_value = jnp.einsum(
        "hqk,qhd->khd", weights_low, g_heads, preferred_element_type=jnp.float32
    )
    flat_shape = (1, tokens, HEADS * HDIM)
    return (
        grad_query.reshape(flat_shape).astype(jnp.bfloat16),
        grad_key.reshape(flat_shape).astype(jnp.bfloat16),
        grad_value.reshape(flat_shape).astype(jnp.bfloat16),
    )


def shards(q_space, k_space, v_space, cot_space, q_time, k_time, v_time, cot_time, clip_len):
    scaling = 1.0 / math.sqrt(HDIM)
    grad_qs, grad_ks, grad_vs = frame_grads(q_space[0], k_space[0], v_space[0], cot_space[0])
    moved = (
        lax.all_to_all(q_time, "seq", split_axis=1, concat_axis=0, tiled=True),
        lax.all_to_all(k_time, "seq", split_axis=1, concat_axis=0, tiled=True),
        lax.all_to_all(v_time, "seq", split_axis=1, concat_axis=0, tiled=True),
        lax.all_to_all(cot_time, "seq", split_axis=1, concat_axis=0, tiled=True),
    )
    query_win, key_win, value_win, cot_win = moved
    window = query_win.shape[0]
    places = query_win.shape[1]
    channels = query_win.shape[2]
    group_id = lax.axis_index("grp")
    frame_total = window * lax.axis_size("grp")
    first_frame = group_id * window

    def split_heads(array):
        return array.reshape(array.shape[0], places, HEADS, HDIM)

    key_pair = padded(jnp.stack([key_win, value_win]), (("grp", 1),), window)
    q_own = split_heads(query_win)
    g_own = split_heads(cot_win)
    k_ext = split_heads(key_pair[0])
    v_ext = split_heads(key_pair[1])
    own_label, own_inside = clip_labels(clip_len, first_frame, window, frame_total)
    ext_label, ext_inside = clip_labels(clip_len, first_frame - window, 3 * window, frame_total)
    allowed = (own_label[:, None] == ext_label[None, :]) & ext_inside[None, :]
    scores = (
        jnp.einsum("iphd,jphd->phij", q_own, k_ext, preferred_element_type=jnp.float32) * scaling
    )
    scores = jnp.where(allowed, scores, masked_score)
    row_max = jnp.max(scores, axis=-1)
    log_total = row_max + jnp.log(jnp.sum(jnp.exp(scores - row_max[..., None]), axis=-1))
    weights = jnp.where(allowed, jnp.exp(scores - log_total[..., None]), 0.0)
    weights_low = weights.astype(jnp.bfloat16)
    attended = jnp.einsum("phij,jphd->iphd", weights_low, v_ext, preferred_element_type=jnp.float32)
    row_dot = jnp.einsum("iphd,iphd->phi", g_own.astype(jnp.float32), attended)
    weight_grad = jnp.einsum("iphd,jphd->phij", g_own, v_ext, preferred_element_type=jnp.float32)
    score_grad = (weights * (weight_grad - row_dot[..., None])).astype(jnp.bfloat16)
    grad_query = (
        jnp.einsum("phij,jphd->iphd", score_grad, k_ext, preferred_element_type=jnp.float32)
        * scaling
    )
    key_terms = (
        jnp.einsum("phij,iphd->jphd", score_grad, q_own, preferred_element_type=jnp.float32)
        * scaling
    )
    value_terms = jnp.einsum(
        "phij,iphd->jphd", weights_low, g_own, preferred_element_type=jnp.float32
    )
    both_terms = jnp.stack([key_terms, value_terms]).reshape(2, 3 * window, places, channels)
    from_after = shifted(both_terms[:, :window], "grp", -1)
    from_before = shifted(both_terms[:, 2 * window :], "grp", 1)
    summed = both_terms[:, window : 2 * window] + from_after + from_before
    grad_key = summed[0]
    grad_value = summed[1]
    grad_qt, grad_kt, grad_vt = (
        lax.all_to_all(
            grad_query.reshape(window, places, channels).astype(jnp.bfloat16),
            "seq",
            split_axis=0,
            concat_axis=1,
            tiled=True,
        ),
        lax.all_to_all(
            grad_key.astype(jnp.bfloat16), "seq", split_axis=0, concat_axis=1, tiled=True
        ),
        lax.all_to_all(
            grad_value.astype(jnp.bfloat16), "seq", split_axis=0, concat_axis=1, tiled=True
        ),
    )
    return (grad_qs, grad_ks, grad_vs, grad_qt, grad_kt, grad_vt)


def solution(mesh):
    split_spec = P(("grp", "seq"), None, None)

    def mapped(body):
        return jax.shard_map(
            body,
            mesh=mesh,
            in_specs=(split_spec,) * 8 + (P(),),
            out_specs=(split_spec,) * 6,
            check_vma=False,
        )

    def grads(*arrays):
        return mapped(tile_shards if whole_tiles(mesh, arrays[0].shape[1]) else shards)(*arrays)

    return grads
```

```python
import functools
import math

import jax
import jax.numpy as jnp
from jax import lax
from jax.experimental import pallas as pl
from jax.experimental.pallas import tpu as pltpu
from jax.sharding import PartitionSpec as P

HEADS = 8
HDIM = 72
WIDTH = HEADS * HDIM
LANES = 128
SCALING = 1.0 / math.sqrt(HDIM)
CHUNKS = (4, 4)
masked_score = -1e30


def dot(left, right, left_dim, right_dim):
    dims = (((left_dim,), (right_dim,)), ((), ()))
    return lax.dot_general(left, right, dims, preferred_element_type=jnp.float32)


def rounded(value):
    return value.astype(jnp.bfloat16).astype(jnp.float32)


def frame_kernel(q_ref, k_ref, v_ref, g_ref, dq_ref, dk_ref, dv_ref):
    pair = 2 * HDIM
    reach = -(-HDIM // 16) * 16
    row = lax.broadcasted_iota(jnp.int32, (reach, 1), 0)
    for begin in range(0, WIDTH, pair):
        found = [[], [], []]
        for low, own in ((0, 0), (pair - reach, reach - HDIM)):
            span = slice(begin + low, begin + low + reach)
            mask = ((row >= own) & (row < own + HDIM)).astype(jnp.float32).astype(jnp.bfloat16)
            queries, keys = q_ref[0, span, :], k_ref[0, span, :]
            cotangent = g_ref[0, span, :]
            scores = dot(keys * mask, queries, 0, 0) * SCALING
            weight_grad = dot(v_ref[0, span, :] * mask, cotangent, 0, 0)
            raised = jnp.exp(scores - jnp.max(scores, axis=0, keepdims=True))
            weights = raised * (1.0 / jnp.sum(raised, axis=0, keepdims=True))
            weights_low = weights.astype(jnp.bfloat16)
            dots = jnp.sum(weights_low.astype(jnp.float32) * weight_grad, axis=0, keepdims=True)
            score_grad = (weights * (weight_grad - dots)).astype(jnp.bfloat16)
            rows = slice(own, own + HDIM)
            found[0].append(dot(keys, score_grad, 1, 0)[rows] * SCALING)
            found[1].append(dot(queries, score_grad, 1, 1)[rows] * SCALING)
            found[2].append(dot(cotangent, weights_low, 1, 1)[rows])
        for out, parts in zip((dq_ref, dk_ref, dv_ref), found):
            out[0, begin : begin + pair, :] = jnp.concatenate(parts, axis=0).astype(jnp.bfloat16)


def space_grads(queries, keys, values, cotangent):
    tokens = queries.shape[2]
    shape = jax.ShapeDtypeStruct(queries.shape, jnp.bfloat16)
    return pl.pallas_call(
        frame_kernel,
        out_shape=(shape, shape, shape),
        compiler_params=pltpu.CompilerParams(vmem_limit_bytes=60 * 2**20),
        cost_estimate=pl.CostEstimate(
            flops=12 * tokens * tokens * 256 * HEADS,
            bytes_accessed=14 * tokens * WIDTH,
            transcendentals=tokens * tokens * HEADS,
        ),
        name="space",
    )(queries, keys, values, cotangent)


def part_of(device, sharing, rows):
    row = pl.multiple_of(device % sharing * rows, 16)
    return row, pl.ds(pl.multiple_of(device // sharing * LANES, LANES), LANES)


def split_kernel(sharing, rows, span, *refs):
    ins, outs, (held, arrived, sent) = refs[:4], refs[4:-3], refs[-3:]
    loads, stores = {}, []
    for step in far_first(len(outs)):
        row, tokens = part_of(lax.axis_index("seq") ^ step, sharing, rows)
        for i, array in enumerate(ins):
            given = array.at[0, pl.ds(span.start + row, rows), tokens]
            loads[step, i] = pltpu.make_async_copy(given, held.at[step, i], arrived.at[step, i])
            loads[step, i].start()
    for step in far_first(len(outs)):
        for i in range(len(ins)):
            loads[step, i].wait()
        stores.append(pltpu.make_async_copy(held.at[step], outs[step], sent.at[step]))
        stores[-1].start()
    for copy in stores:
        copy.wait()


def split(arrays, span, n, sharing):
    rows = (span.stop - span.start) // sharing
    hbm = pl.BlockSpec(memory_space=pltpu.HBM)
    return pl.pallas_call(
        functools.partial(split_kernel, sharing, rows, span),
        in_specs=[hbm] * 4,
        out_specs=[hbm] * n,
        out_shape=[jax.ShapeDtypeStruct((4, rows, LANES), jnp.bfloat16)] * n,
        scratch_shapes=[
            pltpu.VMEM((n, 4, rows, LANES), jnp.bfloat16),
            pltpu.SemaphoreType.DMA((n, 4)),
            pltpu.SemaphoreType.DMA((n,)),
        ],
        compiler_params=pltpu.CompilerParams(vmem_limit_bytes=60 * 2**20),
        name="pack",
    )(*arrays)


def far_first(n):
    return [*reversed(range(n // 2, n)), *range(n // 2)]


def swap(block, axis, pairs):
    return lax.ppermute(block, axis, [(i, j) for i, j in pairs] + [(j, i) for i, j in pairs])


def exchange(blocks):
    n = len(blocks)
    moved = list(blocks)
    for step in reversed(range(1, n)):
        pairs = [[i, i ^ step] for i in range(n) if i < i ^ step]
        moved[step] = swap(blocks[step], "seq", pairs)
    return moved


def sides_kernel(n, *refs):
    ins, outs = refs[:n], refs[n:]
    is_odd = lax.axis_index("grp") & 1
    for step, ref in enumerate(ins):
        frame = lax.axis_index("seq") ^ step
        for start, out in zip((1, 0), outs):
            at = frame - jnp.where(is_odd == start, 1, 0)

            @pl.when((at >= 0) & (at < n - 1))
            def _():
                out[jnp.clip(at, 0, n - 2)] = ref[...]


def sides(blocks):
    n = len(blocks)
    shape = jax.ShapeDtypeStruct((n - 1, *blocks[0].shape), jnp.bfloat16)
    vmem = pl.BlockSpec(memory_space=pltpu.VMEM)
    return pl.pallas_call(
        functools.partial(sides_kernel, n),
        in_specs=[vmem] * n,
        out_specs=[vmem] * 2,
        out_shape=[shape] * 2,
        compiler_params=pltpu.CompilerParams(vmem_limit_bytes=24 * 2**20),
        name="sides",
    )(*blocks)


def gated(values, *earlier):
    return lax.optimization_barrier((values, *earlier))


def neighbours(block, start):
    count = lax.axis_size("grp")
    return swap(block, "grp", [(i, (i + 1) % count) for i in range(start, count, 2)])


def join_kernel(sharing, span, *refs):
    outs, sent = refs[-4:-1], refs[-1]
    rows = refs[0].shape[1]
    n = sent.shape[0]
    copies = []
    for at, step in enumerate(far_first(n)):
        row, tokens = part_of(lax.axis_index("seq") ^ step, sharing, rows)
        for i, out in enumerate(outs):
            given = out.at[0, pl.ds(span.start + row, rows), tokens]
            copies.append(pltpu.make_async_copy(refs[at].at[i], given, sent.at[step, i]))
            copies[-1].start()
    for copy in copies:
        copy.wait()


def join(blocks, span, tokens, sharing, earlier):
    n = len(blocks)
    shape = jax.ShapeDtypeStruct((1, WIDTH, tokens), jnp.bfloat16)
    hbm = pl.BlockSpec(memory_space=pltpu.HBM)
    earlier = [] if earlier is None else list(earlier)
    return pl.pallas_call(
        functools.partial(join_kernel, sharing, span),
        in_specs=[pl.BlockSpec(memory_space=pltpu.VMEM)] * n + [hbm] * len(earlier),
        out_specs=[hbm] * 3,
        out_shape=[shape] * 3,
        scratch_shapes=[pltpu.SemaphoreType.DMA((n, 3))],
        input_output_aliases={n + i: i for i in range(len(earlier))},
        compiler_params=pltpu.CompilerParams(vmem_limit_bytes=24 * 2**20),
        name="unpack",
    )(*(blocks[step] for step in far_first(n)), *earlier)


def clip_kernel(window, heads, given_bounds, *refs):
    own, sides_of = refs[:window], refs[window : window + 2]
    outs, refs = refs[window + 2 : 2 * window + 2], refs[2 * window + 2 :]
    wide, score_ref, grad_ref, weight_ref, found, bounds, arrived = refs
    copy = pltpu.make_async_copy(given_bounds, bounds, arrived)
    copy.start()
    halo = window - 1
    extent = window + 2 * halo
    queries, keys, values, cotangent = range(4)

    def widen(ref, frame):
        for i in range(4):
            wide[i, frame] = ref[i].astype(jnp.float32)

    for step, ref in enumerate(own):
        widen(ref, halo + (lax.axis_index("seq") ^ step))
    for start, ref in zip((1, 0), sides_of):
        is_next = (lax.axis_index("grp") & 1) == start
        for at in range(halo):
            widen(ref.at[at], at + jnp.where(is_next, halo + window, 0))
    copy.wait()
    lowest, highest = bounds[0, halo], bounds[1, halo + window - 1]

    def partners(frame):
        first, last = bounds[0, frame], bounds[1, frame]
        return first, last - first, [jnp.minimum(first + t, last - 1) for t in range(window)]

    def products(frame, carry):
        first, count, others = partners(frame)
        scores, grads = [[] for _ in others], [[] for _ in others]
        for head in range(heads):
            span = slice(head * HDIM, (head + 1) * HDIM)
            query, cot = wide[queries, frame, span, :], wide[cotangent, frame, span, :]
            for t, other in enumerate(others):
                score = jnp.sum(query * wide[keys, other, span, :], axis=0, keepdims=True)
                grad = jnp.sum(cot * wide[values, other, span, :], axis=0, keepdims=True)
                scores[t].append(score)
                grads[t].append(grad)
        for t in range(window):
            bias = jnp.where(t < count, 0.0, masked_score)
            score_ref[t, frame] = jnp.concatenate(scores[t], axis=0) * SCALING + bias
            grad_ref[t, frame] = jnp.concatenate(grads[t], axis=0)
        return carry

    lax.fori_loop(lowest, highest, products, 0)
    scores, grads = [score_ref[t] for t in range(window)], [grad_ref[t] for t in range(window)]
    peak = functools.reduce(jnp.maximum, scores)
    raised = [jnp.exp(score - peak) for score in scores]
    inverse = 1.0 / functools.reduce(jnp.add, raised)
    weights = [part * inverse for part in raised]
    weights_low = [rounded(part) for part in weights]
    dots = functools.reduce(jnp.add, [w * d for w, d in zip(weights_low, grads)])
    for t in range(window):
        weight_ref[t] = weights_low[t]
        score_ref[t] = rounded(weights[t] * (grads[t] - dots))

    def gradients(at, carry):
        frame = halo + at
        first, count, others = partners(frame)
        place = frame - first
        sums = [[], [], []]
        for head in range(heads):
            span, row = slice(head * HDIM, (head + 1) * HDIM), slice(head, head + 1)
            totals = [None] * 3
            for t, other in enumerate(others):
                score_back = jnp.where(t < count, score_ref[place, other, row, :], 0.0)
                weight_back = jnp.where(t < count, weight_ref[place, other, row, :], 0.0)
                terms = (
                    score_ref[t, frame, row, :] * wide[keys, other, span, :],
                    score_back * wide[queries, other, span, :],
                    weight_back * wide[cotangent, other, span, :],
                )
                totals = [x if y is None else y + x for x, y in zip(terms, totals)]
            for held, total, scale in zip(sums, totals, (SCALING, SCALING, None)):
                held.append(total if scale is None else total * scale)
        for i, parts in enumerate(sums):
            found[at, i] = jnp.concatenate(parts, axis=0).astype(jnp.bfloat16)
        return carry

    lax.fori_loop(0, window, gradients, 0)
    for step, out in enumerate(outs):
        out[...] = found[lax.axis_index("seq") ^ step]


def clip_grads(bounds, own, beside):
    window = len(own)
    _, rows, lanes = own[0].shape
    heads = rows // HDIM
    extent = 3 * window - 2
    vmem = pl.BlockSpec(memory_space=pltpu.VMEM)
    shape = (3, rows, lanes)
    slots = pltpu.VMEM((window, extent, heads, lanes), jnp.float32)
    return pl.pallas_call(
        functools.partial(clip_kernel, window, heads),
        out_shape=[jax.ShapeDtypeStruct(shape, jnp.bfloat16)] * window,
        in_specs=[pl.BlockSpec(memory_space=pl.ANY)] + [vmem] * (window + 2),
        out_specs=[vmem] * window,
        scratch_shapes=[
            pltpu.VMEM((4, extent, rows, lanes), jnp.float32),
            slots,
            slots,
            slots,
            pltpu.VMEM((window, *shape), jnp.bfloat16),
            pltpu.SMEM(bounds.shape, jnp.int32),
            pltpu.SemaphoreType.DMA,
        ],
        compiler_params=pltpu.CompilerParams(vmem_limit_bytes=48 * 2**20),
        cost_estimate=pl.CostEstimate(
            flops=800 * extent * window * rows * lanes,
            bytes_accessed=2 * sum(block.size for block in (*own, *beside)),
            transcendentals=extent * window * heads * lanes,
        ),
        name="clips",
    )(bounds, *own, *beside)


def clip_bounds(clip_len, window):
    halo = window - 1
    extent = window + 2 * halo
    start = lax.axis_index("grp") * window - halo
    frames = start + jnp.arange(extent, dtype=jnp.int32)
    order = jnp.arange(clip_len.shape[0])
    ends = jnp.sum(jnp.where(order[:, None] <= order[None, :], clip_len[:, None], 0), axis=0)
    begins = ends - clip_len
    holds = (begins[None, :] <= frames[:, None]) & (frames[:, None] < ends[None, :])
    first = jnp.sum(jnp.where(holds, begins[None, :], 0), axis=1) - start
    last = jnp.sum(jnp.where(holds, ends[None, :], 0), axis=1) - start
    return jnp.stack([first, last]).astype(jnp.int32)


def tile_shards(q_space, k_space, v_space, cot_space, q_time, k_time, v_time, cot_time, clip_len):
    def turned(*arrays):
        return tuple(array.transpose(0, 2, 1) for array in arrays)

    n = lax.axis_size("seq")
    window = q_time.shape[0] * n
    tokens = q_time.shape[1]
    sharing = n * LANES // tokens
    bounds = clip_bounds(clip_len, window)
    time = turned(q_time, k_time, v_time, cot_time)
    spans = []
    head = 0
    for heads in CHUNKS:
        spans.append(slice(head * HDIM, (head + heads) * HDIM))
        head += heads
    space_in = turned(q_space, k_space, v_space, cot_space)
    packed = [list(split(time, span, n, sharing)) for span in spans]
    own = [exchange(packed[0])]
    space = space_grads(*space_in)
    packed[1][2:], space = gated(packed[1][2:], space)
    own.append(exchange(packed[1]))
    beside = [
        [neighbours(ends, start) for ends, start in zip(sides(blocks), (1, 0))] for blocks in own
    ]
    back, grads = [], None
    for blocks, near in zip(own, beside):
        back.append(exchange(clip_grads(bounds, blocks, near)))
    for span, blocks in zip(spans, back):
        grads = join(blocks, span, tokens, sharing, grads)
    return turned(*space, *grads)


def whole_tiles(mesh, tokens):
    n = mesh.shape["seq"]
    sharing = n * LANES // tokens
    return (
        tokens % LANES == 0
        and n % 4 == 0
        and n & (n - 1) == 0
        and mesh.shape["grp"] % 2 == 0
        and mesh.shape["grp"] > 2
        and sharing * tokens == n * LANES
        and all(heads % sharing == 0 and heads // sharing * HDIM % 16 == 0 for heads in CHUNKS)
    )


def padded(block, sides, width):
    for axis, dim in sides:
        count = lax.axis_size(axis)
        forward = [(i, i + 1) for i in range(count - 1)]
        backward = [(target, source) for source, target in forward]
        low = lax.ppermute(
            lax.slice_in_dim(block, block.shape[dim] - width, None, axis=dim), axis, forward
        )
        high = lax.ppermute(lax.slice_in_dim(block, 0, width, axis=dim), axis, backward)
        block = jnp.concatenate([low, block, high], axis=dim)
    return block


def shifted(value, axis, by):
    count = lax.axis_size(axis)
    pairs = [(i, i + by) for i in range(count) if 0 <= i + by < count]
    return lax.ppermute(value, axis, pairs)


def clip_labels(clip_len, first_frame, count, frame_total):
    frame_ids = first_frame + jnp.arange(count, dtype=jnp.int32)
    clip_ends = jnp.cumsum(clip_len)
    labels = jnp.sum((clip_ends[None, :] <= frame_ids[:, None]).astype(jnp.int32), axis=1)
    inside = (frame_ids >= 0) & (frame_ids < frame_total)
    return (labels, inside)


def frame_grads(queries, keys, values, cotangent):
    scaling = 1.0 / math.sqrt(HDIM)
    tokens = queries.shape[0]
    q_heads = queries.reshape(tokens, HEADS, HDIM)
    k_heads = keys.reshape(tokens, HEADS, HDIM)
    v_heads = values.reshape(tokens, HEADS, HDIM)
    g_heads = cotangent.reshape(tokens, HEADS, HDIM)
    scores = (
        jnp.einsum("qhd,khd->hqk", q_heads, k_heads, preferred_element_type=jnp.float32) * scaling
    )
    row_max = jnp.max(scores, axis=-1, keepdims=True)
    log_total = row_max + jnp.log(jnp.sum(jnp.exp(scores - row_max), axis=-1, keepdims=True))
    weights = jnp.exp(scores - log_total)
    weights_low = weights.astype(jnp.bfloat16)
    attended = jnp.einsum("hqk,khd->qhd", weights_low, v_heads, preferred_element_type=jnp.float32)
    row_dot = jnp.einsum("qhd,qhd->hq", g_heads.astype(jnp.float32), attended)
    weight_grad = jnp.einsum("qhd,khd->hqk", g_heads, v_heads, preferred_element_type=jnp.float32)
    score_grad = (weights * (weight_grad - row_dot[:, :, None])).astype(jnp.bfloat16)
    grad_query = (
        jnp.einsum("hqk,khd->qhd", score_grad, k_heads, preferred_element_type=jnp.float32)
        * scaling
    )
    grad_key = (
        jnp.einsum("hqk,qhd->khd", score_grad, q_heads, preferred_element_type=jnp.float32)
        * scaling
    )
    grad_value = jnp.einsum(
        "hqk,qhd->khd", weights_low, g_heads, preferred_element_type=jnp.float32
    )
    flat_shape = (1, tokens, HEADS * HDIM)
    return (
        grad_query.reshape(flat_shape).astype(jnp.bfloat16),
        grad_key.reshape(flat_shape).astype(jnp.bfloat16),
        grad_value.reshape(flat_shape).astype(jnp.bfloat16),
    )


def shards(q_space, k_space, v_space, cot_space, q_time, k_time, v_time, cot_time, clip_len):
    scaling = 1.0 / math.sqrt(HDIM)
    grad_qs, grad_ks, grad_vs = frame_grads(q_space[0], k_space[0], v_space[0], cot_space[0])
    moved = (
        lax.all_to_all(q_time, "seq", split_axis=1, concat_axis=0, tiled=True),
        lax.all_to_all(k_time, "seq", split_axis=1, concat_axis=0, tiled=True),
        lax.all_to_all(v_time, "seq", split_axis=1, concat_axis=0, tiled=True),
        lax.all_to_all(cot_time, "seq", split_axis=1, concat_axis=0, tiled=True),
    )
    query_win, key_win, value_win, cot_win = moved
    window = query_win.shape[0]
    places = query_win.shape[1]
    channels = query_win.shape[2]
    group_id = lax.axis_index("grp")
    frame_total = window * lax.axis_size("grp")
    first_frame = group_id * window

    def split_heads(array):
        return array.reshape(array.shape[0], places, HEADS, HDIM)

    key_pair = padded(jnp.stack([key_win, value_win]), (("grp", 1),), window)
    q_own = split_heads(query_win)
    g_own = split_heads(cot_win)
    k_ext = split_heads(key_pair[0])
    v_ext = split_heads(key_pair[1])
    own_label, own_inside = clip_labels(clip_len, first_frame, window, frame_total)
    ext_label, ext_inside = clip_labels(clip_len, first_frame - window, 3 * window, frame_total)
    allowed = (own_label[:, None] == ext_label[None, :]) & ext_inside[None, :]
    scores = (
        jnp.einsum("iphd,jphd->phij", q_own, k_ext, preferred_element_type=jnp.float32) * scaling
    )
    scores = jnp.where(allowed, scores, masked_score)
    row_max = jnp.max(scores, axis=-1)
    log_total = row_max + jnp.log(jnp.sum(jnp.exp(scores - row_max[..., None]), axis=-1))
    weights = jnp.where(allowed, jnp.exp(scores - log_total[..., None]), 0.0)
    weights_low = weights.astype(jnp.bfloat16)
    attended = jnp.einsum("phij,jphd->iphd", weights_low, v_ext, preferred_element_type=jnp.float32)
    row_dot = jnp.einsum("iphd,iphd->phi", g_own.astype(jnp.float32), attended)
    weight_grad = jnp.einsum("iphd,jphd->phij", g_own, v_ext, preferred_element_type=jnp.float32)
    score_grad = (weights * (weight_grad - row_dot[..., None])).astype(jnp.bfloat16)
    grad_query = (
        jnp.einsum("phij,jphd->iphd", score_grad, k_ext, preferred_element_type=jnp.float32)
        * scaling
    )
    key_terms = (
        jnp.einsum("phij,iphd->jphd", score_grad, q_own, preferred_element_type=jnp.float32)
        * scaling
    )
    value_terms = jnp.einsum(
        "phij,iphd->jphd", weights_low, g_own, preferred_element_type=jnp.float32
    )
    both_terms = jnp.stack([key_terms, value_terms]).reshape(2, 3 * window, places, channels)
    from_after = shifted(both_terms[:, :window], "grp", -1)
    from_before = shifted(both_terms[:, 2 * window :], "grp", 1)
    summed = both_terms[:, window : 2 * window] + from_after + from_before
    grad_key = summed[0]
    grad_value = summed[1]
    grad_qt, grad_kt, grad_vt = (
        lax.all_to_all(
            grad_query.reshape(window, places, channels).astype(jnp.bfloat16),
            "seq",
            split_axis=0,
            concat_axis=1,
            tiled=True,
        ),
        lax.all_to_all(
            grad_key.astype(jnp.bfloat16), "seq", split_axis=0, concat_axis=1, tiled=True
        ),
        lax.all_to_all(
            grad_value.astype(jnp.bfloat16), "seq", split_axis=0, concat_axis=1, tiled=True
        ),
    )
    return (grad_qs, grad_ks, grad_vs, grad_qt, grad_kt, grad_vt)


def solution(mesh):
    split_spec = P(("grp", "seq"), None, None)

    def mapped(body):
        return jax.shard_map(
            body,
            mesh=mesh,
            in_specs=(split_spec,) * 8 + (P(),),
            out_specs=(split_spec,) * 6,
            check_vma=False,
        )

    def grads(*arrays):
        return mapped(tile_shards if whole_tiles(mesh, arrays[0].shape[1]) else shards)(*arrays)

    return grads
```
